32 devices in a mesh: seq: 8 (over z, y), state: 4 (over x, core).
Axes of the slice: x: 2, y: 2, z: 4, core: 2. Of those that a mesh axis runs over, the one named last changes fastest.
Arguments:
- tokens: bfloat16 [2048, 16, 512], P('state', 'seq'), may hold values from -6 to 6
- norm_gain: float32 [512], replicated, may hold values from 0.5 to 1.5
- norm_bias: float32 [512], replicated, may hold values from -2 to 2
- input_weight: bfloat16 [512, 256, 2], P(None, 'state'), may hold values from -0.25 to 0.25
- output_weight: bfloat16 [256, 2, 512], P('state'), may hold values from -0.25 to 0.25
- log_rate: float32 [256], P('state'), may hold values from -9.91 to -2.99
- log_angle: float32 [256], P('state'), may hold values from -4.5 to 1
- log_gain: float32 [256], P('state'), may hold values from -4.91 to -0.87
- skip_gain: float32 [512], replicated, may hold values from -4 to 4
- glu_weight: bfloat16 [512, 1024], replicated, may hold values from -0.25 to 0.25
- lengths: int32 [16], P('seq'), may hold values from 1024 to 2048, as said below
- cotangent: bfloat16 [2048, 16, 512], P('state', 'seq'), may hold values from -6 to 6
Outputs:
- output: bfloat16 [2048, 16, 512], P('state', 'seq')
- grad_tokens: float32 [2048, 16, 512], P('state', 'seq')
- grad_norm_gain: float32 [512], replicated
- grad_norm_bias: float32 [512], replicated
- grad_input_weight: float32 [512, 256, 2], P(None, 'state')
- grad_output_weight: float32 [256, 2, 512], P('state')
- grad_log_rate: float32 [256], P('state')
- grad_log_angle: float32 [256], P('state')
- grad_log_gain: float32 [256], P('state')
- grad_skip_gain: float32 [512], replicated
- grad_glu_weight: float32 [512, 1024], replicated
The draws below stay inside these ranges and needn't reach their ends.
Inputs may be any that keep to these rules, and one draw needn't show every extreme that they name: `lengths`: valid positions of each sequence counted from its start; of the 2 sequences on each index of seq, one is valid over all 2048 positions.
All inputs are finite; a program needn't handle non-finite values.
Results may differ from the reference program's by a relative error of at most 0.008.
Values may be sent and summed in bfloat16 or wider, within the bound.
No kernel may reach another device: no remote copies, remote signals or barrier semaphores. Data moves between devices by JAX's collectives and lax.ppermute only.
A program may use at most 128 MiB of HBM per device.

```python
import math
import jax
import jax.numpy as jnp
from jax import lax

D = 512
NS = 256
SEQS = 2
MIN_LEN = 1024
BLK = 256
SLOT = 2048
BATCH = 16
N_SEQ = 8


def decay_rates(key, slow_share):
    flag_key, slow_key, fast_key = jax.random.split(key, 3)
    slow = jax.random.bernoulli(flag_key, slow_share, (NS,))
    slow_rate = jnp.exp(jax.random.uniform(slow_key, (NS,), jnp.float32, math.log(5e-05), math.log(0.0005)))
    fast_rate = jnp.exp(jax.random.uniform(fast_key, (NS,), jnp.float32, math.log(0.02), math.log(0.05)))
    return jnp.where(slow, slow_rate, fast_rate)


def draw_log_rate(key, part):
    share = 0.5
    rates = decay_rates(key, share)
    return jnp.log(rates).astype(jnp.float32)


def draw_log_gain(key, part):
    share = 0.5
    rates = decay_rates(key, share)
    key = jax.random.fold_in(key, 7)
    noise = jax.random.uniform(key, (NS,), jnp.float32, -0.3, 0.3)
    return (0.5 * jnp.log(1.0 - jnp.exp(-2.0 * rates)) + noise).astype(jnp.float32)


def draw_lengths(key, part):
    key = jax.random.fold_in(key, 11)
    length_key, pick_key = jax.random.split(key)
    lengths_drawn = jax.random.randint(length_key, (N_SEQ, SEQS), MIN_LEN, SLOT + 1)
    chosen = jax.random.randint(pick_key, (N_SEQ, 1), 0, SEQS)
    full_slot = jnp.arange(SEQS)[None, :] == chosen
    return jnp.where(full_slot, SLOT, lengths_drawn).reshape(N_SEQ * SEQS).astype(jnp.int32)


def shard_levels(own_key, shape, cuts, smallest, largest):
    def one(dim, blocks):
        steps = jax.random.uniform(jax.random.fold_in(jax.random.fold_in(own_key, 6), dim), (blocks,), jnp.float32, smallest / len(cuts), largest / len(cuts))
        return jnp.repeat(jnp.exp(steps), shape[dim] // blocks).reshape((-1,) + (1,) * (len(shape) - dim - 1))

    factor_of = one(*cuts[0])
    for cut in cuts[1:]:
        factor_of = factor_of * one(*cut)
    return factor_of


def scatter_about(own_key, dims, width, most, cuts=(), kind=jnp.bfloat16):
    factor_of = shard_levels(own_key, dims, cuts, -0.22, 0.18) if cuts else 1.0
    entries = jax.random.normal(own_key, dims, jnp.float32) * width * factor_of
    return jnp.minimum(jnp.maximum(entries, -most), most).astype(kind)


def setup_inputs(seed: int = 0) -> dict:
    arg_keys = jax.random.split(jax.random.key(seed), 13)
    return {
        "tokens": scatter_about(arg_keys[0], (SLOT, BATCH, D), 1.0, 6.0, ((0, 4), (1, 8))),
        "norm_gain": jnp.clip(1.0 + 0.1 * jax.random.normal(arg_keys[1], (D,), jnp.float32), 0.5, 1.5),
        "norm_bias": scatter_about(arg_keys[2], (D,), 0.3, 2.0, (), jnp.float32),
        "input_weight": scatter_about(arg_keys[3], (D, NS, 2), D ** -0.5, 0.25, ((1, 4),)),
        "output_weight": scatter_about(arg_keys[4], (NS, 2, D), (2 * NS) ** -0.5, 0.25, ((0, 4),)),
        "log_rate": draw_log_rate(jax.random.fold_in(arg_keys[12], 71), 0),
        "log_angle": jnp.clip(-4.5 + 5.5 * jax.random.uniform(arg_keys[6], (NS,), jnp.float32) ** shard_levels(arg_keys[6], (NS,), ((0, 4),), -0.2, 0.2), -4.5, 1.0),
        "log_gain": draw_log_gain(jax.random.fold_in(arg_keys[12], 71), 0),
        "skip_gain": scatter_about(arg_keys[8], (D,), 1.0, 4.0, (), jnp.float32),
        "glu_weight": scatter_about(arg_keys[9], (D, 2 * D), D ** -0.5, 0.25),
        "lengths": draw_lengths(jax.random.fold_in(arg_keys[12], 71), 0),
        "cotangent": scatter_about(arg_keys[11], (SLOT, BATCH, D), 1.0, 6.0, ((0, 4), (1, 8))),
    }


@jax.custom_vjp
def low(v):
    return lax.optimization_barrier(v.astype(jnp.bfloat16)).astype(jnp.float32)

@jax.custom_vjp
def low_back(v):
    return v

def low_keep(v):
    return (low(v), None)

def low_pass(kept, grad):
    return (grad,)

def back_keep(v):
    return (v, None)

def back_low(kept, grad):
    return (low(grad),)
low.defvjp(low_keep, low_pass)
low_back.defvjp(back_keep, back_low)
epsilon = 1e-05
highest = lax.Precision.HIGHEST

def recurrence(pole_re, pole_im, drive_re, drive_im):
    blocks = SLOT // BLK

    def single(current, term):
        next_re = pole_re * current[0] - pole_im * current[1] + term[0]
        next_im = pole_re * current[1] + pole_im * current[0] + term[1]
        return ((next_re, next_im), (next_re, next_im))

    def block_run(current, terms):
        return lax.scan(single, current, terms)
    zero_state = jnp.zeros((NS,), jnp.float32)
    _, (states_re, states_im) = lax.scan(jax.checkpoint(block_run), (zero_state, zero_state), (drive_re.reshape(blocks, BLK, NS), drive_im.reshape(blocks, BLK, NS)))
    return (states_re.reshape(SLOT, NS), states_im.reshape(SLOT, NS))

def layer_seq(params, values, mask):
    norm_gain, norm_bias, input_weight, output_weight, log_rate, log_angle, log_gain, skip_gain, glu_weight = params
    centred = values - lax.optimization_barrier(jnp.mean(values, axis=-1, keepdims=True))
    inverse = lax.rsqrt(lax.optimization_barrier(jnp.mean(centred * centred, axis=-1, keepdims=True)) + epsilon)
    normed = centred * inverse * norm_gain + norm_bias
    normed_low = low(normed)
    projected = low_back(jnp.dot(normed_low, input_weight.reshape(D, 2 * NS), precision=highest))
    projected = projected.reshape(SLOT, NS, 2)
    scale_in = jnp.exp(log_gain)[None, :] * mask[:, None]
    drive_re = projected[..., 0] * scale_in
    drive_im = projected[..., 1] * scale_in
    decay_rate = jnp.exp(log_rate)
    turn_angle = jnp.exp(log_angle)
    pole_re = jnp.exp(-decay_rate) * jnp.cos(turn_angle)
    pole_im = jnp.exp(-decay_rate) * jnp.sin(turn_angle)
    states_re, states_im = recurrence(pole_re, pole_im, drive_re, drive_im)
    stacked = low(jnp.stack([states_re, -states_im], axis=-1).reshape(SLOT, 2 * NS))
    mixed = low_back(jnp.dot(stacked, output_weight.reshape(2 * NS, D), precision=highest))
    preact = mixed + skip_gain * normed
    activated = low(jax.nn.gelu(preact))
    glu_in = low_back(jnp.dot(activated, glu_weight, precision=highest))
    branch = glu_in[:, :D] * jax.nn.sigmoid(glu_in[:, D:])
    return values + mask[:, None] * branch

def reference(tokens, norm_gain, norm_bias, input_weight, output_weight, log_rate, log_angle, log_gain, skip_gain, glu_weight, lengths, cotangent):
    params = (norm_gain, norm_bias, input_weight.astype(jnp.float32), output_weight.astype(jnp.float32), log_rate, log_angle, log_gain, skip_gain, glu_weight.astype(jnp.float32))
    sequences = jnp.swapaxes(tokens.astype(jnp.float32), 0, 1)
    upstream = jnp.swapaxes(cotangent.astype(jnp.float32), 0, 1)
    positions = jnp.arange(SLOT, dtype=jnp.int32)

    def one_sequence(totals, item):
        values, cot_rows, length = item
        mask = (positions < length).astype(jnp.float32)
        result, pull = jax.vjp(lambda weights, rows: layer_seq(weights, rows, mask), params, values)
        grads, grad_rows = pull(cot_rows)
        totals = jax.tree.map(jnp.add, totals, grads)
        return (totals, (result.astype(jnp.bfloat16), grad_rows))
    initial = jax.tree.map(jnp.zeros_like, params)
    totals, (results, grad_rows) = lax.scan(one_sequence, initial, (sequences, upstream, lengths))
    return (jnp.swapaxes(results, 0, 1), jnp.swapaxes(grad_rows, 0, 1), totals[0], totals[1], totals[2], totals[3], totals[4], totals[5], totals[6], totals[7], totals[8])
```

```python
import functools

import jax
import jax.numpy as jnp
from jax import lax
from jax.experimental import pallas as pl
from jax.experimental.pallas import tpu as pltpu
from jax.sharding import PartitionSpec as P

F32, BF16 = jnp.float32, jnp.bfloat16
EPSILON = 1e-05
SUB = 8
CHUNK = 256
PARAM_ROWS = 16
GELU_A = 0.7978845608028654
GELU_B = 0.044715
MIB = 1 << 20


def cmul(ar, ai, br, bi):
    return ar * br - ai * bi, ar * bi + ai * br


def nn(a, b):
    return lax.dot_general(a, b, (((1,), (0,)), ((), ())), preferred_element_type=F32)


def nt(a, b):
    return lax.dot_general(a, b, (((1,), (1,)), ((), ())), preferred_element_type=F32)


def tn(a, b):
    return lax.dot_general(a, b, (((0,), (0,)), ((), ())), preferred_element_type=F32)


def to_rows(x):
    span, group, feats = x.shape
    segs = SUB // group
    steps = span // segs
    return x.reshape(segs, steps, group, feats).transpose(1, 0, 2, 3).reshape(steps * SUB, feats)


def from_rows(y, group):
    rows, feats = y.shape
    segs, steps = SUB // group, rows // SUB
    return y.reshape(steps, segs, group, feats).transpose(1, 0, 2, 3).reshape(segs * steps, group, feats)


def row_mask(base, rows, group, steps, me, lens_ref):
    segs = SUB // group
    row = lax.broadcasted_iota(jnp.int32, (rows, 128), 0) + base
    place = row & (SUB - 1)
    seq = place & (group - 1)
    position = me * (segs * steps) + (place // group) * steps + (row // SUB)
    length = jnp.full((rows, 128), lens_ref[0], jnp.int32)
    for k in range(1, group):
        length = jnp.where(seq == k, lens_ref[k], length)
    return (position < length).astype(F32)


def wide(column, lanes):
    return jnp.concatenate([column] * (lanes // column.shape[1]), axis=1)


def call(body, outs, ins, smem, scratch, limit_mib, flops, name):
    n_smem = len(smem)
    return pl.pallas_call(
        body,
        out_shape=[jax.ShapeDtypeStruct(s, d) for s, d in outs],
        in_specs=[pl.BlockSpec(memory_space=pltpu.SMEM)] * n_smem
        + [pl.BlockSpec(memory_space=pltpu.VMEM)] * len(ins),
        out_specs=[pl.BlockSpec(memory_space=pltpu.VMEM)] * len(outs),
        scratch_shapes=scratch,
        compiler_params=pltpu.CompilerParams(vmem_limit_bytes=limit_mib * MIB),
        cost_estimate=pl.CostEstimate(flops=flops, bytes_accessed=4 * MIB, transcendentals=0),
        name=name,
    )(*smem, *ins)


def norm_kernel(x_ref, gain_ref, bias_ref, low_ref, unit_ref, inv_ref):
    rows, feats = x_ref.shape

    def chunk(c, carry):
        at = pl.ds(pl.multiple_of(c * CHUNK, CHUNK), CHUNK)
        x = x_ref[at, :].astype(F32)
        centred = x - jnp.mean(x, axis=1, keepdims=True)
        inv = lax.rsqrt(jnp.mean(centred * centred, axis=1, keepdims=True) + EPSILON)
        unit = centred * inv
        unit_ref[at, :] = unit
        low_ref[at, :] = (unit * gain_ref[...] + bias_ref[...]).astype(BF16)
        inv_ref[at, :] = jnp.broadcast_to(inv, (CHUNK, 128))
        return carry

    lax.fori_loop(0, rows // CHUNK, chunk, 0)


def gather_rows(me, blocks, own, channels, dst_ref):
    for m, block in enumerate(blocks):
        off = pl.multiple_of((me ^ m) * own, own)
        dst_ref[pl.ds(off, own), :] = block[0:own, :]
        dst_ref[pl.ds(pl.multiple_of(channels + off, own), own), :] = block[own : 2 * own, :]


def seg_of(group):
    row = lax.broadcasted_iota(jnp.int32, (SUB, 128), 0)
    return row // group


def shift_rows(x, by, keep):
    return jnp.where(wide(keep, x.shape[1]), pltpu.roll(x, by % SUB, 0), 0.0)


def seg_prefix(xr, xi, qr, qi, group, forward):
    seg = seg_of(group)
    segs = SUB // group
    dist = 1
    while dist < segs:
        by = group * dist if forward else SUB - group * dist
        keep = seg >= dist if forward else seg < segs - dist
        sr, si = shift_rows(xr, by, keep), shift_rows(xi, by, keep)
        ar, ai = cmul(qr, qi, sr, si)
        xr, xi = xr + ar, xi + ai
        qr, qi = cmul(qr, qi, qr, qi)
        dist *= 2
    return xr, xi


def seg_enter(xr, xi, qr, qi, dr, di, group, forward):
    seg = seg_of(group)
    segs = SUB // group
    by = group if forward else SUB - group
    keep = seg >= 1 if forward else seg < segs - 1
    er, ei = shift_rows(xr, by, keep), shift_rows(xi, by, keep)
    gap = seg if forward else segs - 1 - seg
    pr, pi = jnp.ones_like(er), jnp.zeros_like(ei)
    bit = 1
    while bit < segs:
        nr, ni = cmul(pr, pi, qr, qi)
        take = wide((gap & bit) != 0, er.shape[1])
        pr, pi = jnp.where(take, nr, pr), jnp.where(take, ni, pi)
        qr, qi = cmul(qr, qi, qr, qi)
        bit *= 2
    ar, ai = cmul(pr, pi, dr, di)
    return er + ar, ei + ai


def device_entry(recvs, channels, qr, qi, group, forward):
    seg = seg_of(group)
    segs = SUB // group
    keep = seg == (segs - 1 if forward else 0)
    total_r = total_i = None
    for recv in reversed(recvs):
        if total_r is not None:
            total_r, total_i = cmul(total_r, total_i, qr, qi)
            total_r, total_i = total_r + recv[:, :channels], total_i + recv[:, channels:]
        else:
            total_r, total_i = recv[:, :channels], recv[:, channels:]
    out = []
    for x in (total_r, total_i):
        x = jnp.where(wide(keep, channels), x, 0.0)
        y = x
        for k in range(1, segs):
            y = y + pltpu.roll(x, group * k, 0)
        out.append(y)
    return out


def project_kernel(parts, own, group, me_ref, lens_ref, low_ref, *refs):
    blocks = refs[:parts]
    drive_ref, end_ref, win_ref, cst_ref = refs[parts:]
    rows = low_ref.shape[0]
    channels = own * parts
    steps = rows // SUB
    me = me_ref[0]
    gather_rows(me, blocks, own, channels, win_ref)
    rows_of = []
    for k in range(3):
        total = None
        for block in blocks:
            tile = block[2 * own : 2 * own + PARAM_ROWS, :].astype(F32)
            for part in range(3):
                piece = tile[3 * k + part : 3 * k + part + 1, :channels]
                total = piece if total is None else total + piece
        rows_of.append(total)
    pr, pi, gain = rows_of
    powers = [(pr, pi)]
    span = steps * (SUB // group)
    ar, ai = pr, pi
    count = 1
    while count < span:
        ar, ai = cmul(ar, ai, ar, ai)
        count *= 2
        if count in (steps, span):
            powers.append((ar, ai))
    while len(powers) < 3:
        powers.append(powers[-1])
    for k, (r, i) in enumerate(powers):
        cst_ref[k : k + 1, :] = jnp.concatenate([r, i], axis=1)
    gains = jnp.concatenate([gain, gain], axis=1)
    cst_ref[3:4, :] = gains
    cst_ref[4:8, :] = jnp.zeros((4, 2 * channels), F32)

    def chunk(c, carry):
        base = pl.multiple_of(c * CHUNK, CHUNK)
        at = pl.ds(base, CHUNK)
        mask = row_mask(base, CHUNK, group, steps, me, lens_ref)
        drive_ref[at, :] = nt(low_ref[at, :], win_ref[...]) * (gains * wide(mask, 2 * channels))
        return carry

    lax.fori_loop(0, rows // CHUNK, chunk, 0)
    br = jnp.broadcast_to(pr, (SUB, channels))
    bi = jnp.broadcast_to(pi, (SUB, channels))

    def step(j, h):
        u = drive_ref[pl.ds(pl.multiple_of(j * SUB, SUB), SUB), :]
        nr, ni = cmul(br, bi, h[0], h[1])
        return nr + u[:, :channels], ni + u[:, channels:]

    zero = jnp.zeros((SUB, channels), F32)
    er, ei = lax.fori_loop(0, steps, step, (zero, zero), unroll=8)
    er, ei = seg_prefix(er, ei, *powers[1], group, True)
    end_ref[...] = jnp.concatenate([er, ei], axis=1)


def mix_kernel(parts, n_recv, own, group, orders, me_ref, place_ref, lens_ref, *refs):
    it = iter(refs)
    take = lambda n: [next(it) for _ in range(n)]
    drive_ref, end_ref, cst_ref = take(3)
    recvs = take(n_recv)
    blocks = take(parts)
    x_ref, unit_ref, cot_ref, gain_ref, bias_ref, skip_ref, glu_ref = take(7)
    states_ref, slow_ref, cw_ref, out_ref, dglu_ref, gp_ref = take(6)
    grads = take(len(orders))
    act_ref, acc_ref = take(2)
    rows, feats = x_ref.shape
    channels = own * parts
    steps = rows // SUB
    me = me_ref[0]
    gather_rows(me, blocks, own, channels, cw_ref)
    pr, pi = cst_ref[0:1, :channels], cst_ref[0:1, channels:]
    qr, qi = cst_ref[1:2, :channels], cst_ref[1:2, channels:]
    wr, wi = cst_ref[2:3, :channels], cst_ref[2:3, channels:]
    dr, di = device_entry(recvs, channels, wr, wi, group, True)
    hr, hi = seg_enter(end_ref[:, :channels], end_ref[:, channels:], qr, qi, dr, di, group, True)
    states_ref[0:SUB, :] = jnp.concatenate([hr, hi], axis=1)
    br = jnp.broadcast_to(pr, (SUB, channels))
    bi = jnp.broadcast_to(pi, (SUB, channels))

    def step(j, h):
        base = pl.multiple_of(j * SUB, SUB)
        u = drive_ref[pl.ds(base, SUB), :]
        nr, ni = cmul(br, bi, h[0], h[1])
        nr, ni = nr + u[:, :channels], ni + u[:, channels:]
        at = pl.ds(pl.multiple_of(base + SUB, SUB), SUB)
        states_ref[at, :channels] = nr
        states_ref[at, channels:] = ni
        return nr, ni

    lax.fori_loop(0, steps, step, (hr, hi), unroll=8)

    def chunk(c, carry):
        base = pl.multiple_of(c * CHUNK, CHUNK)
        at = pl.ds(base, CHUNK)
        states = states_ref[pl.ds(pl.multiple_of(base + SUB, SUB), CHUNK), :]
        slow = jnp.concatenate([states[:, :channels], -states[:, channels:]], axis=1).astype(BF16)
        slow_ref[at, :] = slow
        normed = unit_ref[at, :] * gain_ref[...] + bias_ref[...]
        v = nn(slow, cw_ref[...]) + skip_ref[...] * normed
        t = jnp.tanh(GELU_A * (v + GELU_B * (v * v * v)))
        half = 0.5 * (1.0 + t)
        gp_ref[at, :] = half + (0.5 * GELU_A) * v * (1.0 - t * t) * (1.0 + (3.0 * GELU_B) * (v * v))
        act = (v * half).astype(BF16)
        act_ref[at, :] = act
        glu = nn(act, glu_ref[...])
        mask = wide(row_mask(base, CHUNK, group, steps, me, lens_ref), feats)
        value = glu[:, :feats]
        gate = jax.nn.sigmoid(glu[:, feats:])
        branch = mask * gate
        out_ref[at, :] = (x_ref[at, :].astype(F32) + branch * value).astype(BF16)
        d_value = branch * cot_ref[at, :].astype(F32)
        dglu_ref[at, :feats] = d_value.astype(BF16)
        dglu_ref[at, feats:] = (d_value * value * (1.0 - gate)).astype(BF16)
        return carry

    lax.fori_loop(0, rows // CHUNK, chunk, 0)
    width = 256

    def tile(c, carry):
        at = pl.ds(pl.multiple_of(c * width, width), width)
        acc_ref[:, at] = tn(act_ref[...], dglu_ref[:, at])
        return carry

    lax.fori_loop(0, 2 * feats // width, tile, 0)
    spread(acc_ref, place_ref[0], orders, grads)


def spread(acc_ref, place, orders, grads):
    for order, ref in zip(orders, grads):
        _, size, _ = ref.shape
        for k, m in enumerate(order):
            at = pl.ds(pl.multiple_of((place ^ m) * size, size), size)
            ref[k] = acc_ref[at, :].astype(ref.dtype)


def spread_pairs(acc_ref, place, own, channels, orders, grads):
    for order, ref in zip(orders, grads):
        for k, m in enumerate(order):
            off = pl.multiple_of((place ^ m) * own, own)
            ref[k, 0:own] = acc_ref[pl.ds(off, own), :].astype(ref.dtype)
            also = pl.ds(pl.multiple_of(channels + off, own), own)
            ref[k, own : 2 * own] = acc_ref[also, :].astype(ref.dtype)


def back_kernel(own, group, orders, me_ref, *refs):
    it = iter(refs)
    take = lambda n: [next(it) for _ in range(n)]
    dglu_ref, gp_ref, unit_ref, gain_ref, bias_ref, glu_ref, cw_ref, slow_ref, cst_ref = take(9)
    dpre_ref, dst_ref, start_ref, skip_ref = take(4)
    grads = take(len(orders))
    dmix_ref, acc_ref = take(2)
    rows, feats = gp_ref.shape
    channels = cw_ref.shape[0] // 2
    steps = rows // SUB
    me = me_ref[0]

    def chunk(c, total):
        at = pl.ds(pl.multiple_of(c * CHUNK, CHUNK), CHUNK)
        d_pre = nt(dglu_ref[at, :], glu_ref[...]) * gp_ref[at, :]
        dpre_ref[at, :] = d_pre
        normed = unit_ref[at, :] * gain_ref[...] + bias_ref[...]
        total = total + jnp.sum((d_pre * normed).reshape(CHUNK // SUB, SUB, feats), axis=0)
        d_mixed = d_pre.astype(BF16)
        dmix_ref[at, :] = d_mixed
        dst_ref[at, :] = nt(d_mixed, cw_ref[...])
        return total

    total = lax.fori_loop(0, rows // CHUNK, chunk, jnp.zeros((SUB, feats), F32))
    skip_ref[...] = total
    pr, pi = cst_ref[0:1, :channels], cst_ref[0:1, channels:]
    br = jnp.broadcast_to(pr, (SUB, channels))
    bi = jnp.broadcast_to(-pi, (SUB, channels))

    def step(k, a):
        base = pl.multiple_of((steps - 1 - k) * SUB, SUB)
        u = dst_ref[pl.ds(base, SUB), :]
        nr, ni = cmul(br, bi, a[0], a[1])
        return nr + u[:, :channels], ni - u[:, channels:]

    zero = jnp.zeros((SUB, channels), F32)
    ar, ai = lax.fori_loop(0, steps, step, (zero, zero), unroll=8)
    qr, qi = cst_ref[1:2, :channels], -cst_ref[1:2, channels:]
    ar, ai = seg_prefix(ar, ai, qr, qi, group, False)
    start_ref[...] = jnp.concatenate([ar, ai], axis=1)
    width = 256

    def tile(c, carry):
        at = pl.ds(pl.multiple_of(c * width, width), width)
        acc_ref[:, at] = tn(slow_ref[...], dmix_ref[:, at])
        return carry

    lax.fori_loop(0, feats // width, tile, 0)
    spread_pairs(acc_ref, me, own, channels, orders, grads)


def adjoint_kernel(n_recv, own, group, orders, me_ref, lens_ref, *refs):
    it = iter(refs)
    take = lambda n: [next(it) for _ in range(n)]
    dst_ref, start_ref, cst_ref = take(3)
    recvs = take(n_recv)
    states_ref, drive_ref, low_ref = take(3)
    dproj_ref, sums_ref = take(2)
    grads = take(len(orders))
    adj_ref, acc_ref = take(2)
    rows = dst_ref.shape[0]
    channels = dst_ref.shape[1] // 2
    steps = rows // SUB
    me = me_ref[0]
    pr, pi = cst_ref[0:1, :channels], -cst_ref[0:1, channels:]
    qr, qi = cst_ref[1:2, :channels], -cst_ref[1:2, channels:]
    wr, wi = cst_ref[2:3, :channels], -cst_ref[2:3, channels:]
    dr, di = device_entry(recvs, channels, wr, wi, group, False)
    ar, ai = seg_enter(start_ref[:, :channels], start_ref[:, channels:], qr, qi, dr, di, group, False)
    br = jnp.broadcast_to(pr, (SUB, channels))
    bi = jnp.broadcast_to(pi, (SUB, channels))

    def step(k, carry):
        ar, ai, sr, si, sg = carry
        base = pl.multiple_of((steps - 1 - k) * SUB, SUB)
        at = pl.ds(base, SUB)
        d = dst_ref[at, :]
        nr, ni = cmul(br, bi, ar, ai)
        ar, ai = nr + d[:, :channels], ni - d[:, channels:]
        adj_ref[at, :channels] = ar
        adj_ref[at, channels:] = ai
        h = states_ref[at, :]
        hr, hi = h[:, :channels], h[:, channels:]
        u = drive_ref[at, :]
        sr = sr + (ar * hr + ai * hi)
        si = si + (ai * hr - ar * hi)
        sg = sg + (ar * u[:, :channels] + ai * u[:, channels:])
        return ar, ai, sr, si, sg

    zero = jnp.zeros((SUB, channels), F32)
    out = lax.fori_loop(0, steps, step, (ar, ai, zero, zero, zero), unroll=4)
    sums_ref[:, :channels] = out[2]
    sums_ref[:, channels : 2 * channels] = out[3]
    sums_ref[:, 2 * channels : 3 * channels] = out[4]
    gains = cst_ref[3:4, :]

    def chunk(c, carry):
        base = pl.multiple_of(c * CHUNK, CHUNK)
        at = pl.ds(base, CHUNK)
        mask = row_mask(base, CHUNK, group, steps, me, lens_ref)
        dproj_ref[at, :] = (adj_ref[at, :] * (gains * wide(mask, 2 * channels))).astype(BF16)
        return carry

    lax.fori_loop(0, rows // CHUNK, chunk, 0)
    width = 256
    feats = low_ref.shape[1]

    def tile(c, carry):
        at = pl.ds(pl.multiple_of(c * width, width), width)
        acc_ref[:, at] = tn(dproj_ref[...], low_ref[:, at])
        return carry

    lax.fori_loop(0, feats // width, tile, 0)
    spread_pairs(acc_ref, me, own, channels, orders, grads)


def tokens_kernel(dproj_ref, win_ref, dpre_ref, skip_ref, unit_ref, inv_ref, gain_ref, cot_ref, out_ref, sums_ref):
    rows, feats = dpre_ref.shape

    def chunk(c, carry):
        total_gain, total_bias = carry
        at = pl.ds(pl.multiple_of(c * CHUNK, CHUNK), CHUNK)
        d_normed = dpre_ref[at, :] * skip_ref[...] + nn(dproj_ref[at, :], win_ref[...])
        unit = unit_ref[at, :]
        total_gain = total_gain + jnp.sum((d_normed * unit).reshape(CHUNK // SUB, SUB, feats), axis=0)
        total_bias = total_bias + jnp.sum(d_normed.reshape(CHUNK // SUB, SUB, feats), axis=0)
        d_unit = d_normed * gain_ref[...]
        first = jnp.mean(d_unit, axis=1, keepdims=True)
        second = jnp.mean(d_unit * unit, axis=1, keepdims=True)
        inv = wide(inv_ref[at, :], feats)
        out_ref[at, :] = cot_ref[at, :].astype(F32) + inv * (d_unit - first - unit * second)
        return total_gain, total_bias

    zero = jnp.zeros((SUB, feats), F32)
    total_gain, total_bias = lax.fori_loop(0, rows // CHUNK, chunk, (zero, zero))
    sums_ref[:, :feats] = total_gain
    sums_ref[:, feats:] = total_bias


def place_kernel(n, place_ref, *refs):
    blocks, out_ref = refs[:n], refs[n]
    size = blocks[0].shape[0]
    for m, block in enumerate(blocks):
        at = pl.ds(pl.multiple_of((place_ref[0] ^ m) * size, size), size)
        out_ref[at, :] = block[...].astype(F32)


def exchange(x, axis, bit):
    return lax.ppermute(x, axis, [(i, i ^ bit) for i in range(lax.axis_size(axis))])


def bits_of(n):
    return [1 << k for k in range(n.bit_length() - 1)]


def stage_orders(bits):
    kept = [0]
    orders = [[0]]
    for bit in reversed(bits):
        send = [m ^ bit for m in kept]
        orders.insert(0, send)
        kept = send + kept
    return orders


def halve(parts, stages):
    for axis, bit in stages:
        got = exchange(parts[0].astype(BF16), axis, bit)
        rest, off = [], 0
        for p in parts[1:]:
            n = p.shape[0]
            rest.append(p.astype(F32) + got[off : off + n].astype(F32))
            off += n
        parts = rest
    return parts[0][0]


def double(x, stages):
    for axis, bit in stages:
        low = lax.reduce_precision(x, 8, 7).astype(BF16)
        x = low.astype(F32) + exchange(low, axis, bit).astype(F32)
    return x


def double_f32(x, stages):
    for axis, bit in stages:
        x = x + exchange(x, axis, bit)
    return x


def gather_blocks(own, stages):
    blocks = {0: own}
    for axis, bit, unit in stages:
        for m in list(blocks):
            blocks[m ^ unit] = exchange(blocks[m], axis, bit)
    return [blocks[m] for m in range(len(blocks))]


def three_parts(x):
    high = lax.reduce_precision(x, 8, 7)
    mid = lax.reduce_precision(x - high, 8, 7)
    return [high, mid, x - high - mid]


def shards(
    tokens,
    norm_gain,
    norm_bias,
    input_weight,
    output_weight,
    log_rate,
    log_angle,
    log_gain,
    skip_gain,
    glu_weight,
    lengths,
    cotangent,
):
    span, group, feats = tokens.shape
    own = log_rate.shape[0]
    parts = lax.axis_size("state")
    n_seq = lax.axis_size("seq")
    channels = own * parts
    rows = span * group
    me = lax.axis_index("state")
    seq_index = lax.axis_index("seq")
    me_ref = me.reshape(1)
    state_bits, seq_bits = bits_of(parts), bits_of(n_seq)
    place_ref = (me + parts * (seq_index & 1)).reshape(1)
    gather_stages = [("state", b, b) for b in reversed(state_bits)]

    decay = jnp.exp(log_rate)
    angle = jnp.exp(log_angle)
    pole_re = jnp.exp(-decay) * jnp.cos(angle)
    pole_im = jnp.exp(-decay) * jnp.sin(angle)
    small = jnp.stack(three_parts(pole_re) + three_parts(pole_im) + three_parts(jnp.exp(log_gain)))
    mine = (jnp.arange(feats, dtype=jnp.int32) // own) == me
    reps = feats // own
    small = jnp.where(mine[None, :], jnp.tile(small, (1, reps)), 0.0)
    small = jnp.pad(small, ((0, PARAM_ROWS - small.shape[0]), (0, 0))).astype(BF16)
    b_own = input_weight.transpose(2, 1, 0).reshape(2 * own, feats)
    b_own = jnp.concatenate([b_own, small], axis=0)
    c_own = output_weight.transpose(1, 0, 2).reshape(2 * own, feats)
    b_blocks = gather_blocks(b_own, gather_stages)
    c_blocks = gather_blocks(c_own, gather_stages)

    gain_row, bias_row, skip_row = (v.reshape(1, feats) for v in (norm_gain, norm_bias, skip_gain))
    x = to_rows(tokens)
    cot = to_rows(cotangent)
    low, unit, inv = call(
        norm_kernel,
        [((rows, feats), BF16), ((rows, feats), F32), ((rows, 128), F32)],
        [x, gain_row, bias_row],
        [],
        [],
        8,
        rows * feats * 10,
        "norm",
    )
    full = rows * feats * 2 * channels * 2
    drive, end, win, cst = call(
        functools.partial(project_kernel, parts, own, group),
        [
            ((rows, 2 * channels), F32),
            ((SUB, 2 * channels), F32),
            ((2 * channels, feats), BF16),
            ((SUB, 2 * channels), F32),
        ],
        [low] + b_blocks,
        [me_ref, lengths],
        [],
        12,
        full,
        "project",
    )
    forward = [
        lax.ppermute(end, "state", [(i, i + k) for i in range(parts - k)]) for k in range(1, parts)
    ]
    glu_bits = state_bits + [parts]
    glu_orders = stage_orders(glu_bits)
    glu_stages = [("state", b) for b in state_bits] + [("seq", 1)]
    glu_blocks = 2 * parts
    glu_rows = feats // glu_blocks
    glu_outs = [
        ((len(o), glu_rows, 2 * feats), BF16 if k == 0 else F32) for k, o in enumerate(glu_orders)
    ]
    states, slow, cw, out_rows, d_glu, slope, *glu_parts = call(
        functools.partial(mix_kernel, parts, len(forward), own, group, glu_orders),
        [
            ((rows + SUB, 2 * channels), F32),
            ((rows, 2 * channels), BF16),
            ((2 * channels, feats), BF16),
            ((rows, feats), BF16),
            ((rows, 2 * feats), BF16),
            ((rows, feats), F32),
        ]
        + glu_outs,
        [drive, end, cst]
        + forward
        + c_blocks
        + [x, unit, cot, gain_row, bias_row, skip_row, glu_weight],
        [me_ref, place_ref, lengths],
        [pltpu.VMEM((rows, feats), BF16), pltpu.VMEM((feats, 2 * feats), F32)],
        20,
        5 * full,
        "mix",
    )
    state_orders = stage_orders(state_bits)
    state_stages = [("state", b) for b in state_bits]
    seq_stages = [("seq", b) for b in seq_bits]
    pair_outs = [
        ((len(o), 2 * own, feats), BF16 if k == 0 else F32) for k, o in enumerate(state_orders)
    ]
    d_pre, d_states, start, skip_sum, *out_parts = call(
        functools.partial(back_kernel, own, group, state_orders),
        [
            ((rows, feats), F32),
            ((rows, 2 * channels), F32),
            ((SUB, 2 * channels), F32),
            ((SUB, feats), F32),
        ]
        + pair_outs,
        [d_glu, slope, unit, gain_row, bias_row, glu_weight, cw, slow, cst],
        [me_ref],
        [pltpu.VMEM((rows, feats), BF16), pltpu.VMEM((2 * channels, feats), F32)],
        16,
        4 * full,
        "back",
    )
    backward = [
        lax.ppermute(start, "state", [(i + k, i) for i in range(parts - k)]) for k in range(1, parts)
    ]
    d_proj, channel_sums, *in_parts = call(
        functools.partial(adjoint_kernel, len(backward), own, group, state_orders),
        [((rows, 2 * channels), BF16), ((SUB, 3 * channels), F32)] + pair_outs,
        [d_states, start, cst] + backward + [states, drive, low],
        [me_ref, lengths],
        [pltpu.VMEM((rows, 2 * channels), F32), pltpu.VMEM((2 * channels, feats), F32)],
        16,
        2 * full,
        "adjoint",
    )
    grad_rows, feature_sums = call(
        tokens_kernel,
        [((rows, feats), F32), ((SUB, 2 * feats), F32)],
        [d_proj, win, d_pre, skip_row, unit, inv, gain_row, cot],
        [],
        [],
        12,
        full,
        "tokens",
    )

    glu_own = halve(glu_parts, glu_stages)
    glu_own = double(glu_own, [("seq", b) for b in seq_bits[1:]])
    glu_all = gather_blocks(
        lax.reduce_precision(glu_own, 8, 7).astype(BF16),
        [("seq", 1, parts)] + gather_stages,
    )
    (grad_glu,) = call(
        functools.partial(place_kernel, glu_blocks),
        [((feats, 2 * feats), F32)],
        glu_all,
        [place_ref],
        [],
        8,
        feats * feats,
        "place",
    )
    grad_out = double(halve(out_parts, state_stages), seq_stages)
    grad_in = double(halve(in_parts, state_stages), seq_stages)

    sums = jnp.concatenate([channel_sums, feature_sums, skip_sum], axis=1)
    sums = jnp.sum(sums, axis=0, keepdims=True)
    sums = double_f32(sums, state_stages + seq_stages)[0]
    sum_re, sum_im, gain_sum = (
        lax.dynamic_slice(sums, (k * channels + me * own,), (own,)) for k in range(3)
    )
    base = 3 * channels
    grad_gain, grad_bias, grad_skip = (
        sums[base + k * feats : base + (k + 1) * feats] for k in range(3)
    )
    grad_rate = -decay * (sum_re * pole_re + sum_im * pole_im)
    grad_angle = angle * (sum_im * pole_re - sum_re * pole_im)
    return (
        from_rows(out_rows, group),
        from_rows(grad_rows, group),
        grad_gain,
        grad_bias,
        grad_in.reshape(2, own, feats).transpose(2, 1, 0),
        grad_out.reshape(2, own, feats).transpose(1, 0, 2),
        grad_rate,
        grad_angle,
        gain_sum,
        grad_skip,
        grad_glu,
    )


def solution(mesh):
    placed = (
        P("state", "seq", None),
        P(),
        P(),
        P(None, "state", None),
        P("state", None, None),
        P("state"),
        P("state"),
        P("state"),
        P(),
        P(),
        P("seq"),
        P("state", "seq", None),
    )
    return jax.shard_map(
        shards,
        mesh=mesh,
        in_specs=placed,
        out_specs=(
            P("state", "seq", None),
            P("state", "seq", None),
            P(),
            P(),
            P(None, "state", None),
            P("state", None, None),
            P("state"),
            P("state"),
            P("state"),
            P(),
            P(),
        ),
        check_vma=False,
    )
```

```python
import functools

import jax
import jax.numpy as jnp
from jax import lax
from jax.experimental import pallas as pl
from jax.experimental.pallas import tpu as pltpu
from jax.sharding import PartitionSpec as P

F32, BF16 = jnp.float32, jnp.bfloat16
EPSILON = 1e-05
SUB = 8
CHUNK = 256
PARAM_ROWS = 16
GELU_A = 0.7978845608028654
GELU_B = 0.044715
MIB = 1 << 20


def cmul(ar, ai, br, bi):
    return ar * br - ai * bi, ar * bi + ai * br


def nn(a, b):
    return lax.dot_general(a, b, (((1,), (0,)), ((), ())), preferred_element_type=F32)


def nt(a, b):
    return lax.dot_general(a, b, (((1,), (1,)), ((), ())), preferred_element_type=F32)


def tn(a, b):
    return lax.dot_general(a, b, (((0,), (0,)), ((), ())), preferred_element_type=F32)


def rows_in(ref, first, count):
    segs, _, group, feats = ref.shape
    x = ref[:, pl.ds(first, count)].astype(F32)
    return x.transpose(1, 0, 2, 3).reshape(count * segs * group, feats)


def rows_out(y, ref, first, count):
    segs, _, group, feats = ref.shape
    return y.reshape(count, segs, group, feats).transpose(1, 0, 2, 3)


def row_mask(base, rows, group, steps, me, lens_ref):
    segs = SUB // group
    row = lax.broadcasted_iota(jnp.int32, (rows, 128), 0) + base
    place = row & (SUB - 1)
    seq = place & (group - 1)
    position = me * (segs * steps) + (place // group) * steps + (row // SUB)
    length = jnp.full((rows, 128), lens_ref[0], jnp.int32)
    for k in range(1, group):
        length = jnp.where(seq == k, lens_ref[k], length)
    return (position < length).astype(F32)


def wide(column, lanes):
    return jnp.concatenate([column] * (lanes // column.shape[1]), axis=1)


def call(body, outs, ins, scratch, limit_mib, flops, name, small=()):
    specs = []
    for k, x in enumerate(ins):
        if x.dtype == jnp.int32:
            specs.append(pl.BlockSpec(memory_space=pltpu.SMEM))
        elif k in small:
            specs.append(pl.BlockSpec(x.shape, lambda *_, n=x.ndim: (0,) * n))
        else:
            specs.append(pl.BlockSpec(memory_space=pltpu.VMEM))
    return pl.pallas_call(
        body,
        out_shape=[jax.ShapeDtypeStruct(s, d) for s, d in outs],
        in_specs=specs,
        out_specs=[pl.BlockSpec(memory_space=pltpu.VMEM)] * len(outs),
        scratch_shapes=scratch,
        compiler_params=pltpu.CompilerParams(vmem_limit_bytes=limit_mib * MIB),
        cost_estimate=pl.CostEstimate(flops=flops, bytes_accessed=4 * MIB, transcendentals=0),
        name=name,
    )(*ins)


def split_pairs(pairs_ref, flat_ref):
    own, _, feats = pairs_ref.shape
    flat = pairs_ref[...].astype(F32).reshape(2 * own, feats)
    for c in range(feats // 128):
        flat_ref[c] = flat[:, c * 128 : (c + 1) * 128]
    take = lambda k: [flat_ref[c, pl.ds(k, own, stride=2), :] for c in range(feats // 128)]
    return [jnp.concatenate(take(k), axis=1).astype(BF16) for k in range(2)]


def three_parts(x):
    high = x.astype(BF16)
    rest = x - high.astype(F32)
    mid = rest.astype(BF16)
    return [high, mid, (rest - mid.astype(F32)).astype(BF16)]


def prep_kernel(weight_ref, rate_ref, angle_ref, level_ref, gain_ref, bias_ref, skip_ref, pay_ref, vec_ref, flat_ref):
    own, _, feats = weight_ref.shape
    for k, rows in enumerate(split_pairs(weight_ref, flat_ref)):
        pay_ref[k * own : (k + 1) * own, :] = rows
    me = lax.axis_index("state")
    lane = lax.broadcasted_iota(jnp.int32, (1, feats), 1)
    mine = (lane // own) == me
    over = lambda ref: jnp.concatenate([ref[...]] * (feats // own), axis=1)
    size = jnp.exp(-jnp.exp(over(rate_ref)))
    angle = jnp.exp(over(angle_ref))
    parts = []
    for v in (size * jnp.cos(angle), size * jnp.sin(angle), jnp.exp(over(level_ref))):
        parts += three_parts(jnp.where(mine, v, 0.0))
    parts += [jnp.zeros((PARAM_ROWS - len(parts), feats), BF16)]
    pay_ref[2 * own :, :] = jnp.concatenate([p.astype(F32) for p in parts], axis=0).astype(BF16)
    vec_ref[0:1, :] = gain_ref[...]
    vec_ref[1:2, :] = bias_ref[...]
    vec_ref[2:3, :] = skip_ref[...]


def norm_kernel(x_ref, cot_ref, weight_ref, vec_ref, lens_ref, low_ref, unit_ref, inv_ref, mask_ref, rows_ref, pay_ref, flat_ref):
    segs, steps, group, feats = x_ref.shape
    rows = steps * SUB
    own = weight_ref.shape[0]
    me = lax.axis_index("state")
    size = 128
    gain, bias = vec_ref[0:1, :], vec_ref[1:2, :]

    def chunk(c, carry):
        base = pl.multiple_of(c * size, size)
        at = pl.ds(base, size)
        first = pl.multiple_of(c * (size // SUB), size // SUB)
        x = rows_in(x_ref, first, size // SUB)
        centred = x - jnp.mean(x, axis=1, keepdims=True)
        inv = lax.rsqrt(jnp.mean(centred * centred, axis=1, keepdims=True) + EPSILON)
        unit = centred * inv
        unit_ref[at, :] = unit
        low_ref[at, :] = (unit * gain + bias).astype(BF16)
        inv_ref[at, :] = jnp.broadcast_to(inv, (size, 128))
        mask_ref[at, :] = row_mask(base, size, group, steps, me, lens_ref)
        rows_ref[at, :] = rows_in(cot_ref, first, size // SUB).astype(BF16)
        return carry

    lax.fori_loop(0, rows // size, chunk, 0)
    for k, part in enumerate(split_pairs(weight_ref, flat_ref)):
        pay_ref[k * own : (k + 1) * own, :] = part


def gather_rows(me, blocks, own, channels, dst_ref):
    for m, block in enumerate(blocks):
        off = pl.multiple_of((me ^ m) * own, own)
        dst_ref[pl.ds(off, own), :] = block[0:own, :]
        dst_ref[pl.ds(pl.multiple_of(channels + off, own), own), :] = block[own : 2 * own, :]


def seg_of(group):
    row = lax.broadcasted_iota(jnp.int32, (SUB, 128), 0)
    return row // group


def shift_rows(x, by, keep):
    return jnp.where(wide(keep, x.shape[1]), pltpu.roll(x, by % SUB, 0), 0.0)


def seg_prefix(xr, xi, qr, qi, group, forward):
    seg = seg_of(group)
    segs = SUB // group
    dist = 1
    while dist < segs:
        by = group * dist if forward else SUB - group * dist
        keep = seg >= dist if forward else seg < segs - dist
        sr, si = shift_rows(xr, by, keep), shift_rows(xi, by, keep)
        ar, ai = cmul(qr, qi, sr, si)
        xr, xi = xr + ar, xi + ai
        qr, qi = cmul(qr, qi, qr, qi)
        dist *= 2
    return xr, xi


def seg_enter(xr, xi, qr, qi, dr, di, group, forward):
    seg = seg_of(group)
    segs = SUB // group
    by = group if forward else SUB - group
    keep = seg >= 1 if forward else seg < segs - 1
    er, ei = shift_rows(xr, by, keep), shift_rows(xi, by, keep)
    gap = seg if forward else segs - 1 - seg
    pr, pi = jnp.ones_like(er), jnp.zeros_like(ei)
    bit = 1
    while bit < segs:
        nr, ni = cmul(pr, pi, qr, qi)
        take = wide((gap & bit) != 0, er.shape[1])
        pr, pi = jnp.where(take, nr, pr), jnp.where(take, ni, pi)
        qr, qi = cmul(qr, qi, qr, qi)
        bit *= 2
    ar, ai = cmul(pr, pi, dr, di)
    return er + ar, ei + ai


def device_entry(ends_ref, me, channels, qr, qi, group, forward):
    seg = seg_of(group)
    segs = SUB // group
    parts = ends_ref.shape[0]
    keep = wide(seg == (segs - 1 if forward else 0), channels)
    tr = ti = jnp.zeros((SUB, channels), F32)
    for device in range(parts - 1) if forward else range(parts - 1, 0, -1):
        end = ends_ref[me ^ device]
        nr, ni = cmul(tr, ti, qr, qi)
        counts = device < me if forward else device > me
        tr = jnp.where(counts, nr + end[:, :channels], tr)
        ti = jnp.where(counts, ni + end[:, channels:], ti)
    out = []
    for x in (tr, ti):
        x = jnp.where(keep, x, 0.0)
        y = x
        for k in range(1, segs):
            y = y + pltpu.roll(x, group * k, 0)
        out.append(y)
    return out


def project_kernel(parts, own, group, low_ref, mask_ref, *refs):
    blocks = refs[:parts]
    drive_ref, end_ref, win_ref, cst_ref = refs[parts:]
    rows = low_ref.shape[0]
    channels = own * parts
    steps = rows // SUB
    me = lax.axis_index("state")
    gather_rows(me, blocks, own, channels, win_ref)
    rows_of = []
    for k in range(3):
        total = None
        for block in blocks:
            tile = block[2 * own : 2 * own + PARAM_ROWS, :].astype(F32)
            for part in range(3):
                piece = tile[3 * k + part : 3 * k + part + 1, :channels]
                total = piece if total is None else total + piece
        rows_of.append(total)
    pr, pi, gain = rows_of
    powers = [(pr, pi)]
    span = steps * (SUB // group)
    ar, ai = pr, pi
    count = 1
    while count < span:
        ar, ai = cmul(ar, ai, ar, ai)
        count *= 2
        if count in (steps, span):
            powers.append((ar, ai))
    while len(powers) < 3:
        powers.append(powers[-1])
    for k, (r, i) in enumerate(powers):
        cst_ref[k : k + 1, :] = jnp.concatenate([r, i], axis=1)
    gains = jnp.concatenate([gain, gain], axis=1)
    cst_ref[3:4, :] = gains
    cst_ref[4:8, :] = jnp.zeros((4, 2 * channels), F32)

    def chunk(c, carry):
        base = pl.multiple_of(c * CHUNK, CHUNK)
        at = pl.ds(base, CHUNK)
        mask = mask_ref[at, :]
        drive_ref[at, :] = nt(low_ref[at, :], win_ref[...]) * (gains * wide(mask, 2 * channels))
        return carry

    lax.fori_loop(0, rows // CHUNK, chunk, 0)
    br = jnp.broadcast_to(pr, (SUB, channels))
    bi = jnp.broadcast_to(pi, (SUB, channels))

    def step(j, h):
        u = drive_ref[pl.ds(pl.multiple_of(j * SUB, SUB), SUB), :]
        nr, ni = cmul(br, bi, h[0], h[1])
        return nr + u[:, :channels], ni + u[:, channels:]

    zero = jnp.zeros((SUB, channels), F32)
    er, ei = lax.fori_loop(0, steps, step, (zero, zero), unroll=8)
    er, ei = seg_prefix(er, ei, *powers[1], group, True)
    end_ref[...] = jnp.concatenate([er, ei], axis=1)


def mix_kernel(parts, own, group, orders, *refs):
    it = iter(refs)
    take = lambda n: [next(it) for _ in range(n)]
    drive_ref, end_ref, cst_ref, ends_ref = take(4)
    blocks = take(parts)
    unit_ref, cot_ref, mask_ref, vec_ref, glu_ref = take(5)
    states_ref, slow_ref, cw_ref, branch_ref, dglu_ref, gp_ref = take(6)
    grads = take(len(orders))
    act_ref, acc_ref = take(2)
    rows, feats = unit_ref.shape
    channels = own * parts
    steps = rows // SUB
    me = lax.axis_index("state")
    place = me + parts * (lax.axis_index("seq") & 1)
    gather_rows(me, blocks, own, channels, cw_ref)
    gain, bias, skip = (vec_ref[k : k + 1, :] for k in range(3))
    pr, pi = cst_ref[0:1, :channels], cst_ref[0:1, channels:]
    qr, qi = cst_ref[1:2, :channels], cst_ref[1:2, channels:]
    wr, wi = cst_ref[2:3, :channels], cst_ref[2:3, channels:]
    dr, di = device_entry(ends_ref, me, channels, wr, wi, group, True)
    hr, hi = seg_enter(end_ref[:, :channels], end_ref[:, channels:], qr, qi, dr, di, group, True)
    states_ref[0:SUB, :] = jnp.concatenate([hr, hi], axis=1)
    br = jnp.broadcast_to(pr, (SUB, channels))
    bi = jnp.broadcast_to(pi, (SUB, channels))

    def step(j, h):
        base = pl.multiple_of(j * SUB, SUB)
        u = drive_ref[pl.ds(base, SUB), :]
        nr, ni = cmul(br, bi, h[0], h[1])
        nr, ni = nr + u[:, :channels], ni + u[:, channels:]
        at = pl.ds(pl.multiple_of(base + SUB, SUB), SUB)
        states_ref[at, :channels] = nr
        states_ref[at, channels:] = ni
        return nr, ni

    lax.fori_loop(0, steps, step, (hr, hi), unroll=8)

    def chunk(c, carry):
        base = pl.multiple_of(c * CHUNK, CHUNK)
        at = pl.ds(base, CHUNK)
        states = states_ref[pl.ds(pl.multiple_of(base + SUB, SUB), CHUNK), :]
        slow = jnp.concatenate([states[:, :channels], -states[:, channels:]], axis=1).astype(BF16)
        slow_ref[at, :] = slow
        normed = unit_ref[at, :] * gain + bias
        v = nn(slow, cw_ref[...]) + skip * normed
        t = jnp.tanh(GELU_A * (v + GELU_B * (v * v * v)))
        half = 0.5 * (1.0 + t)
        gp_ref[at, :] = half + (0.5 * GELU_A) * v * (1.0 - t * t) * (1.0 + (3.0 * GELU_B) * (v * v))
        act = (v * half).astype(BF16)
        act_ref[at, :] = act
        glu = nn(act, glu_ref[...])
        mask = wide(mask_ref[at, :], feats)
        value = glu[:, :feats]
        gate = jax.nn.sigmoid(glu[:, feats:])
        branch = mask * gate
        branch_ref[at, :] = branch * value
        d_value = branch * cot_ref[at, :].astype(F32)
        dglu_ref[at, :feats] = d_value.astype(BF16)
        dglu_ref[at, feats:] = (d_value * value * (1.0 - gate)).astype(BF16)
        return carry

    lax.fori_loop(0, rows // CHUNK, chunk, 0)
    width = 256

    def tile(c, carry):
        at = pl.ds(pl.multiple_of(c * width, width), width)
        acc_ref[:, at] = tn(act_ref[...], dglu_ref[:, at])
        return carry

    lax.fori_loop(0, 2 * feats // width, tile, 0)
    spread(acc_ref, place, orders, grads)


def spread(acc_ref, place, orders, grads):
    for order, ref in zip(orders, grads):
        _, size, _ = ref.shape
        for k, m in enumerate(order):
            at = pl.ds(pl.multiple_of((place ^ m) * size, size), size)
            ref[k] = acc_ref[at, :].astype(ref.dtype)


def spread_pairs(acc_ref, place, own, channels, orders, grads):
    for order, ref in zip(orders, grads):
        for k, m in enumerate(order):
            off = pl.multiple_of((place ^ m) * own, own)
            ref[k, 0:own] = acc_ref[pl.ds(off, own), :].astype(ref.dtype)
            also = pl.ds(pl.multiple_of(channels + off, own), own)
            ref[k, own : 2 * own] = acc_ref[also, :].astype(ref.dtype)


def back_kernel(own, group, orders, *refs):
    it = iter(refs)
    take = lambda n: [next(it) for _ in range(n)]
    dglu_ref, gp_ref, unit_ref, vec_ref, glu_ref, cw_ref, slow_ref, cst_ref = take(8)
    dpre_ref, dst_ref, start_ref, skip_ref = take(4)
    grads = take(len(orders))
    dmix_ref, acc_ref = take(2)
    rows, feats = gp_ref.shape
    channels = cw_ref.shape[0] // 2
    steps = rows // SUB
    me = lax.axis_index("state")
    gain, bias = vec_ref[0:1, :], vec_ref[1:2, :]

    def chunk(c, total):
        at = pl.ds(pl.multiple_of(c * CHUNK, CHUNK), CHUNK)
        d_pre = nt(dglu_ref[at, :], glu_ref[...]) * gp_ref[at, :]
        dpre_ref[at, :] = d_pre
        normed = unit_ref[at, :] * gain + bias
        total = total + jnp.sum((d_pre * normed).reshape(CHUNK // SUB, SUB, feats), axis=0)
        d_mixed = d_pre.astype(BF16)
        dmix_ref[at, :] = d_mixed
        dst_ref[at, :] = nt(d_mixed, cw_ref[...])
        return total

    total = lax.fori_loop(0, rows // CHUNK, chunk, jnp.zeros((SUB, feats), F32))
    skip_ref[...] = total
    pr, pi = cst_ref[0:1, :channels], cst_ref[0:1, channels:]
    br = jnp.broadcast_to(pr, (SUB, channels))
    bi = jnp.broadcast_to(-pi, (SUB, channels))

    def step(k, a):
        base = pl.multiple_of((steps - 1 - k) * SUB, SUB)
        u = dst_ref[pl.ds(base, SUB), :]
        nr, ni = cmul(br, bi, a[0], a[1])
        return nr + u[:, :channels], ni - u[:, channels:]

    zero = jnp.zeros((SUB, channels), F32)
    ar, ai = lax.fori_loop(0, steps, step, (zero, zero), unroll=8)
    qr, qi = cst_ref[1:2, :channels], -cst_ref[1:2, channels:]
    ar, ai = seg_prefix(ar, ai, qr, qi, group, False)
    start_ref[...] = jnp.concatenate([ar, ai], axis=1)
    width = 256

    def tile(c, carry):
        at = pl.ds(pl.multiple_of(c * width, width), width)
        acc_ref[:, at] = tn(slow_ref[...], dmix_ref[:, at])
        return carry

    lax.fori_loop(0, feats // width, tile, 0)
    spread_pairs(acc_ref, me, own, channels, orders, grads)


def adjoint_kernel(own, group, orders, *refs):
    it = iter(refs)
    take = lambda n: [next(it) for _ in range(n)]
    dst_ref, start_ref, cst_ref, ends_ref = take(4)
    states_ref, drive_ref, low_ref, mask_ref = take(4)
    dproj_ref, sums_ref = take(2)
    grads = take(len(orders))
    adj_ref, acc_ref = take(2)
    rows = dst_ref.shape[0]
    channels = dst_ref.shape[1] // 2
    steps = rows // SUB
    me = lax.axis_index("state")
    pr, pi = cst_ref[0:1, :channels], -cst_ref[0:1, channels:]
    qr, qi = cst_ref[1:2, :channels], -cst_ref[1:2, channels:]
    wr, wi = cst_ref[2:3, :channels], -cst_ref[2:3, channels:]
    dr, di = device_entry(ends_ref, me, channels, wr, wi, group, False)
    ar, ai = seg_enter(start_ref[:, :channels], start_ref[:, channels:], qr, qi, dr, di, group, False)
    br = jnp.broadcast_to(pr, (SUB, channels))
    bi = jnp.broadcast_to(pi, (SUB, channels))

    def step(k, carry):
        ar, ai, sr, si, sg = carry
        base = pl.multiple_of((steps - 1 - k) * SUB, SUB)
        at = pl.ds(base, SUB)
        d = dst_ref[at, :]
        nr, ni = cmul(br, bi, ar, ai)
        ar, ai = nr + d[:, :channels], ni - d[:, channels:]
        adj_ref[at, :channels] = ar
        adj_ref[at, channels:] = ai
        h = states_ref[at, :]
        hr, hi = h[:, :channels], h[:, channels:]
        u = drive_ref[at, :]
        sr = sr + (ar * hr + ai * hi)
        si = si + (ai * hr - ar * hi)
        sg = sg + (ar * u[:, :channels] + ai * u[:, channels:])
        return ar, ai, sr, si, sg

    zero = jnp.zeros((SUB, channels), F32)
    out = lax.fori_loop(0, steps, step, (ar, ai, zero, zero, zero), unroll=4)
    sums_ref[:, :channels] = out[2]
    sums_ref[:, channels : 2 * channels] = out[3]
    sums_ref[:, 2 * channels : 3 * channels] = out[4]
    gains = cst_ref[3:4, :]

    def chunk(c, carry):
        base = pl.multiple_of(c * CHUNK, CHUNK)
        at = pl.ds(base, CHUNK)
        mask = mask_ref[at, :]
        dproj_ref[at, :] = (adj_ref[at, :] * (gains * wide(mask, 2 * channels))).astype(BF16)
        return carry

    lax.fori_loop(0, rows // CHUNK, chunk, 0)
    width = 256
    feats = low_ref.shape[1]

    def tile(c, carry):
        at = pl.ds(pl.multiple_of(c * width, width), width)
        acc_ref[:, at] = tn(dproj_ref[...], low_ref[:, at])
        return carry

    lax.fori_loop(0, feats // width, tile, 0)
    spread_pairs(acc_ref, me, own, channels, orders, grads)


def out_kernel(branch_ref, x_ref, out_ref):
    segs, steps, _, _ = x_ref.shape
    size = 16

    def chunk(c, carry):
        first = pl.multiple_of(c * size, size)
        rows = branch_ref[pl.ds(pl.multiple_of(first * SUB, size * SUB), size * SUB), :]
        at = pl.ds(first, size)
        out_ref[:, at] = (x_ref[:, at].astype(F32) + rows_out(rows, x_ref, first, size)).astype(BF16)
        return carry

    lax.fori_loop(0, steps // size, chunk, 0)


def tokens_kernel(dproj_ref, win_ref, dpre_ref, unit_ref, inv_ref, vec_ref, cot_ref, out_ref, sums_ref):
    rows, feats = dpre_ref.shape
    gain, skip = vec_ref[0:1, :], vec_ref[2:3, :]
    size = 128
    steps = size // SUB

    def chunk(c, carry):
        total_gain, total_bias = carry
        at = pl.ds(pl.multiple_of(c * size, size), size)
        d_normed = dpre_ref[at, :] * skip + nn(dproj_ref[at, :], win_ref[...])
        unit = unit_ref[at, :]
        total_gain = total_gain + jnp.sum((d_normed * unit).reshape(steps, SUB, feats), axis=0)
        total_bias = total_bias + jnp.sum(d_normed.reshape(steps, SUB, feats), axis=0)
        d_unit = d_normed * gain
        first = jnp.mean(d_unit, axis=1, keepdims=True)
        second = jnp.mean(d_unit * unit, axis=1, keepdims=True)
        inv = wide(inv_ref[at, :], feats)
        rows = inv * (d_unit - first - unit * second)
        place = pl.multiple_of(c * steps, steps)
        step_at = pl.ds(place, steps)
        out_ref[:, step_at] = cot_ref[:, step_at].astype(F32) + rows_out(rows, cot_ref, place, steps)
        return total_gain, total_bias

    zero = jnp.zeros((SUB, feats), F32)
    total_gain, total_bias = lax.fori_loop(0, rows // size, chunk, (zero, zero))
    sums_ref[:, :feats] = total_gain
    sums_ref[:, feats:] = total_bias


def place_kernel(masks, parts, *refs):
    arrays, out_ref = refs[:-1], refs[-1]
    place = lax.axis_index("state") + parts * (lax.axis_index("seq") & 1)
    size = arrays[0].shape[1]
    for ms, ref in zip(masks, arrays):
        for k, m in enumerate(ms):
            at = pl.ds(pl.multiple_of((place ^ m) * size, size), size)
            out_ref[at, :] = ref[k].astype(F32)


def exchange(x, mask):
    count = lax.axis_size("seq") * lax.axis_size("state")
    return lax.ppermute(x, ("seq", "state"), [(i, i ^ mask) for i in range(count)])


def tie(x, *after):
    return lax.optimization_barrier((x, after))[0]


def bits_of(n):
    return [1 << k for k in range(n.bit_length() - 1)]


def submasks(group):
    out = [0]
    for bit in group:
        out += [m | bit for m in out]
    return out[1:]


def stage_orders(groups):
    kept = [0]
    stages = []
    for group in reversed(groups):
        sends = [[m ^ p for m in kept] for p in submasks(group)]
        stages.insert(0, sends)
        kept = sum(sends, []) + kept
    return [o for sends in stages for o in sends] + [[0]]


def halve(parts, group):
    masks = submasks(group)
    got = [exchange(p.astype(BF16), m) for p, m in zip(parts, masks)]
    rest, off = [], 0
    for p in parts[len(masks) :]:
        n = p.shape[0]
        total = p.astype(F32)
        for g in got:
            total = total + g[off : off + n].astype(F32)
        rest.append(total)
        off += n
    return rest


def double(x, mask):
    low = lax.reduce_precision(x, 8, 7).astype(BF16)
    return low.astype(F32) + exchange(low, mask).astype(F32)


def double_f32(x, mask):
    return x + exchange(x, mask)


def gather_ends(end, bits):
    g = end[None]
    for bit in reversed(bits):
        g = jnp.stack([g, exchange(g, bit)], axis=1).reshape((2 * g.shape[0],) + end.shape)
    return g


def gather_blocks(own, bits):
    blocks = {0: own}
    for bit in reversed(bits):
        for m in list(blocks):
            blocks[m ^ bit] = exchange(blocks[m], bit)
    return [blocks[m] for m in range(len(blocks))]


def shards(
    tokens,
    norm_gain,
    norm_bias,
    input_weight,
    output_weight,
    log_rate,
    log_angle,
    log_gain,
    skip_gain,
    glu_weight,
    lengths,
    cotangent,
):
    span, group, feats = tokens.shape
    own = log_rate.shape[0]
    parts = lax.axis_size("state")
    n_seq = lax.axis_size("seq")
    channels = own * parts
    rows = span * group
    segs = SUB // group
    me = lax.axis_index("state")
    state_bits = bits_of(parts)
    seq_masks = [parts * b for b in bits_of(n_seq)]
    if len(seq_masks) > 2:
        seq_masks[-1] |= seq_masks[-2]
    full = rows * feats * 2 * channels * 2

    as_row = lambda v: v.reshape(1, -1)
    x4 = tokens.reshape(segs, span // segs, group, feats)
    cot4 = cotangent.reshape(segs, span // segs, group, feats)
    b_own, vec = call(
        prep_kernel,
        [((2 * own + PARAM_ROWS, feats), BF16), ((SUB, feats), F32)],
        [input_weight.transpose(1, 2, 0)]
        + [as_row(v) for v in (log_rate, log_angle, log_gain, norm_gain, norm_bias, skip_gain)],
        [pltpu.VMEM((feats // 128, 2 * own, 128), F32)],
        8,
        MIB,
        "prep",
        small=range(7),
    )
    b_blocks = gather_blocks(b_own, state_bits)
    low, unit, inv, mask, cot, c_own = call(
        norm_kernel,
        [
            ((rows, feats), BF16),
            ((rows, feats), F32),
            ((rows, 128), F32),
            ((rows, 128), F32),
            ((rows, feats), BF16),
            ((2 * own, feats), BF16),
        ],
        [x4, cot4, output_weight, vec, lengths],
        [pltpu.VMEM((feats // 128, 2 * own, 128), F32)],
        8,
        rows * feats * 20,
        "norm",
        small=(2,),
    )
    c_blocks = gather_blocks(c_own, state_bits)
    drive, end, win, cst = call(
        functools.partial(project_kernel, parts, own, group),
        [
            ((rows, 2 * channels), F32),
            ((SUB, 2 * channels), F32),
            ((2 * channels, feats), BF16),
            ((SUB, 2 * channels), F32),
        ],
        [low, mask] + b_blocks,
        [],
        12,
        full,
        "project",
    )
    ends = gather_ends(end, state_bits)
    glu_bits = state_bits + [parts]
    glu_groups = [glu_bits[:1]] + [glu_bits[k : k + 2] for k in range(1, len(glu_bits), 2)]
    glu_orders = stage_orders(glu_groups)
    glu_rows = feats // (2 * parts)
    glu_outs = [
        ((len(o), glu_rows, 2 * feats), BF16 if k == 0 else F32) for k, o in enumerate(glu_orders)
    ]
    states, slow, cw, branch, d_glu, slope, *glu_parts = call(
        functools.partial(mix_kernel, parts, own, group, glu_orders),
        [
            ((rows + SUB, 2 * channels), F32),
            ((rows, 2 * channels), BF16),
            ((2 * channels, feats), BF16),
            ((rows, feats), F32),
            ((rows, 2 * feats), BF16),
            ((rows, feats), F32),
        ]
        + glu_outs,
        [drive, end, cst, ends] + c_blocks + [unit, cot, mask, vec, glu_weight],
        [pltpu.VMEM((rows, feats), BF16), pltpu.VMEM((feats, 2 * feats), F32)],
        20,
        5 * full,
        "mix",
    )
    glu_parts = halve(glu_parts, glu_groups[0])
    state_groups = [[b] for b in state_bits]
    pair_orders = stage_orders(state_groups)
    pair_outs = [
        ((len(o), 2 * own, feats), BF16 if k == 0 else F32) for k, o in enumerate(pair_orders)
    ]
    d_pre, d_states, start, skip_sum, *out_parts = call(
        functools.partial(back_kernel, own, group, pair_orders),
        [
            ((rows, feats), F32),
            ((rows, 2 * channels), F32),
            ((SUB, 2 * channels), F32),
            ((SUB, feats), F32),
        ]
        + pair_outs,
        [d_glu, slope, unit, vec, glu_weight, cw, slow, cst],
        [pltpu.VMEM((rows, feats), BF16), pltpu.VMEM((2 * channels, feats), F32)],
        16,
        4 * full,
        "back",
    )
    starts = gather_ends(tie(start, glu_parts), state_bits)
    for g in glu_groups[1:]:
        glu_parts = halve(glu_parts, g)
    glu_own = glu_parts[0][0]
    out_parts = halve(out_parts, state_groups[0])
    (out4,) = call(
        out_kernel,
        [(x4.shape, BF16)],
        [tie(branch, start), x4],
        [],
        8,
        MIB,
        "out",
    )
    d_proj, channel_sums, *in_parts = call(
        functools.partial(adjoint_kernel, own, group, pair_orders),
        [((rows, 2 * channels), BF16), ((SUB, 3 * channels), F32)] + pair_outs,
        [tie(d_states, out4, out_parts), start, cst, starts, states, drive, low, mask],
        [pltpu.VMEM((rows, 2 * channels), F32), pltpu.VMEM((2 * channels, feats), F32)],
        16,
        2 * full,
        "adjoint",
    )
    in_parts = halve(in_parts, state_groups[0])
    d_proj = tie(d_proj, glu_own, in_parts)
    grad4, feature_sums = call(
        tokens_kernel,
        [(cot4.shape, F32), ((SUB, 2 * feats), F32)],
        [d_proj, win, d_pre, unit, inv, vec, cot4],
        [],
        12,
        full,
        "tokens",
    )
    sums = jnp.concatenate([channel_sums, feature_sums, skip_sum], axis=1)
    sums = jnp.sum(sums, axis=0, keepdims=True)
    for g in state_groups[1:]:
        out_parts = halve(out_parts, g)
        in_parts = halve(in_parts, g)
    grad_out, grad_in = out_parts[0][0], in_parts[0][0]
    for m in state_bits:
        sums = double_f32(sums, m)
    for m in seq_masks:
        grad_out = double(grad_out, m)
        grad_in = double(grad_in, m)
        sums = double_f32(sums, m)
    sums = sums[0]

    for m in seq_masks[1:]:
        glu_own = double(glu_own, m)
    held = {0: lax.reduce_precision(glu_own, 8, 7).astype(BF16)}
    for g in reversed(glu_groups[1:]):
        for m in list(held):
            for p in submasks(g):
                held[m ^ p] = exchange(held[m], p)
    rest = [m for m in held if m]
    arrays = [held[0][None], jnp.stack([held[m] for m in rest])]
    masks = [[0], rest]
    for p in submasks(glu_groups[0]):
        arrays += [exchange(a, p) for a in arrays[:2]]
        masks += [[m ^ p for m in ms] for ms in masks[:2]]
    (grad_glu,) = call(
        functools.partial(place_kernel, masks, parts),
        [((feats, 2 * feats), F32)],
        arrays,
        [],
        8,
        feats * feats,
        "place",
    )
    sum_re, sum_im, gain_sum = (
        lax.dynamic_slice(sums, (k * channels + me * own,), (own,)) for k in range(3)
    )
    base = 3 * channels
    grad_gain, grad_bias, grad_skip = (
        sums[base + k * feats : base + (k + 1) * feats] for k in range(3)
    )
    decay = jnp.exp(log_rate)
    angle = jnp.exp(log_angle)
    pole_re = jnp.exp(-decay) * jnp.cos(angle)
    pole_im = jnp.exp(-decay) * jnp.sin(angle)
    grad_rate = -decay * (sum_re * pole_re + sum_im * pole_im)
    grad_angle = angle * (sum_im * pole_re - sum_re * pole_im)
    return (
        out4.reshape(tokens.shape),
        grad4.reshape(tokens.shape),
        grad_gain,
        grad_bias,
        grad_in.reshape(2, own, feats).transpose(2, 1, 0),
        grad_out.reshape(2, own, feats).transpose(1, 0, 2),
        grad_rate,
        grad_angle,
        gain_sum,
        grad_skip,
        grad_glu,
    )


def solution(mesh):
    placed = (
        P("state", "seq", None),
        P(),
        P(),
        P(None, "state", None),
        P("state", None, None),
        P("state"),
        P("state"),
        P("state"),
        P(),
        P(),
        P("seq"),
        P("state", "seq", None),
    )
    return jax.shard_map(
        shards,
        mesh=mesh,
        in_specs=placed,
        out_specs=(
            P("state", "seq", None),
            P("state", "seq", None),
            P(),
            P(),
            P(None, "state", None),
            P("state", None, None),
            P("state"),
            P("state"),
            P("state"),
            P(),
            P(),
        ),
        check_vma=False,
    )
```

```python
import functools

import jax
import jax.numpy as jnp
from jax import lax
from jax.experimental import pallas as pl
from jax.experimental.pallas import tpu as pltpu
from jax.sharding import PartitionSpec as P

F32, BF16 = jnp.float32, jnp.bfloat16
EPSILON = 1e-05
SUB = 8
CHUNK = 256
PARAM_ROWS = 16
GELU_A = 0.7978845608028654
GELU_B = 0.044715
MIB = 1 << 20


def cmul(ar, ai, br, bi):
    return ar * br - ai * bi, ar * bi + ai * br


def nn(a, b):
    return lax.dot_general(a, b, (((1,), (0,)), ((), ())), preferred_element_type=F32)


def nt(a, b):
    return lax.dot_general(a, b, (((1,), (1,)), ((), ())), preferred_element_type=F32)


def tn(a, b):
    return lax.dot_general(a, b, (((0,), (0,)), ((), ())), preferred_element_type=F32)


def rows_in(ref, first, count):
    segs, _, group, feats = ref.shape
    x = ref[:, pl.ds(first, count)].astype(F32)
    return x.transpose(1, 0, 2, 3).reshape(count * segs * group, feats)


def rows_out(y, ref):
    segs, _, group, feats = ref.shape
    return y.reshape(y.shape[0] // SUB, segs, group, feats).transpose(1, 0, 2, 3)


def row_mask(base, rows, group, steps, me, lens_ref):
    segs = SUB // group
    row = lax.broadcasted_iota(jnp.int32, (rows, 128), 0) + base
    place = row & (SUB - 1)
    seq = place & (group - 1)
    position = me * (segs * steps) + (place // group) * steps + (row // SUB)
    length = jnp.full((rows, 128), lens_ref[0], jnp.int32)
    for k in range(1, group):
        length = jnp.where(seq == k, lens_ref[k], length)
    return (position < length).astype(F32)


def wide(column, lanes):
    return jnp.concatenate([column] * (lanes // column.shape[1]), axis=1)


def call(body, outs, ins, scratch, limit_mib, flops, name, fetched=()):
    specs = [
        pl.BlockSpec(memory_space=pltpu.HBM if k in fetched else pltpu.VMEM) for k in range(len(ins))
    ]
    return pl.pallas_call(
        body,
        out_shape=[jax.ShapeDtypeStruct(s, d) for s, d in outs],
        in_specs=specs,
        out_specs=[pl.BlockSpec(memory_space=pltpu.VMEM)] * len(outs),
        scratch_shapes=scratch,
        compiler_params=pltpu.CompilerParams(vmem_limit_bytes=limit_mib * MIB),
        cost_estimate=pl.CostEstimate(flops=flops, bytes_accessed=4 * MIB, transcendentals=0),
        name=name,
    )(*ins)


def start_copies(sources, targets, sems):
    copies = [pltpu.make_async_copy(a, b, sems.at[k]) for k, (a, b) in enumerate(zip(sources, targets))]
    for c in copies:
        c.start()
    return copies


def held(x):
    return pltpu.VMEM(x.shape, x.dtype)


def split_pairs(pairs_ref, flat_ref):
    own, _, feats = pairs_ref.shape
    flat = pairs_ref[...].astype(F32).reshape(2 * own, feats)
    for c in range(feats // 128):
        flat_ref[c] = flat[:, c * 128 : (c + 1) * 128]
    take = lambda k: [flat_ref[c, pl.ds(k, own, stride=2), :] for c in range(feats // 128)]
    return [jnp.concatenate(take(k), axis=1).astype(BF16) for k in range(2)]


def three_parts(x):
    high = x.astype(BF16)
    rest = x - high.astype(F32)
    mid = rest.astype(BF16)
    return [high, mid, (rest - mid.astype(F32)).astype(BF16)]


def prep_kernel(*refs):
    sources, (pay_ref, vec_ref) = refs[:7], refs[7:9]
    targets, flat_ref, sems = refs[9:16], refs[16], refs[17]
    weight_ref, rate_ref, angle_ref, level_ref = targets[:4]
    own, _, feats = weight_ref.shape
    copies = start_copies(sources, targets, sems)
    for c in copies[1:]:
        c.wait()
    me = lax.axis_index("state")
    lane = lax.broadcasted_iota(jnp.int32, (1, feats), 1)
    mine = (lane // own) == me
    over = lambda ref: jnp.concatenate([ref[...]] * (feats // own), axis=1)
    decay = jnp.exp(over(rate_ref))
    size = jnp.exp(-decay)
    angle = jnp.exp(over(angle_ref))
    pole_re, pole_im = size * jnp.cos(angle), size * jnp.sin(angle)
    parts = []
    for v in (pole_re, pole_im, jnp.exp(over(level_ref))):
        parts += three_parts(jnp.where(mine, v, 0.0))
    parts += [jnp.zeros((PARAM_ROWS - len(parts), feats), BF16)]
    pay_ref[2 * own :, :] = jnp.concatenate([p.astype(F32) for p in parts], axis=0).astype(BF16)
    rows = [t[...] for t in targets[4:]] + [pole_re, pole_im, decay, angle]
    for k, row in enumerate(rows):
        vec_ref[k : k + 1, :] = row
    vec_ref[len(rows) :, :] = jnp.zeros((SUB - len(rows), feats), F32)
    copies[0].wait()
    for k, part in enumerate(split_pairs(weight_ref, flat_ref)):
        pay_ref[k * own : (k + 1) * own, :] = part


def norm_kernel(x_hbm, cot_hbm, weight_hbm, lens_hbm, vec_ref, low_ref, unit_ref, inv_ref, mask_ref, rows_ref, pay_ref, *scratch):
    x_ref, cot_ref, weight_ref, lens_ref, flat_ref, sems = scratch
    segs, steps, group, feats = x_ref.shape
    rows = steps * SUB
    own = weight_ref.shape[0]
    me = lax.axis_index("state")
    size = 128
    cut = steps // 4
    gain, bias = vec_ref[0:1, :], vec_ref[1:2, :]
    sources, targets = [lens_hbm], [lens_ref]
    for k in range(4):
        at = pl.ds(k * cut, cut)
        sources += [x_hbm.at[:, at], cot_hbm.at[:, at]]
        targets += [x_ref.at[:, at], cot_ref.at[:, at]]
    copies = start_copies(sources + [weight_hbm], targets + [weight_ref], sems)
    copies[0].wait()

    def chunk(c, carry):
        base = pl.multiple_of(c * size, size)
        at = pl.ds(base, size)
        first = pl.multiple_of(c * (size // SUB), size // SUB)
        x = rows_in(x_ref, first, size // SUB)
        centred = x - jnp.mean(x, axis=1, keepdims=True)
        inv = lax.rsqrt(jnp.mean(centred * centred, axis=1, keepdims=True) + EPSILON)
        unit = centred * inv
        unit_ref[at, :] = unit
        low_ref[at, :] = (unit * gain + bias).astype(BF16)
        inv_ref[at, :] = jnp.broadcast_to(inv, (size, 128))
        mask_ref[at, :] = row_mask(base, size, group, steps, me, lens_ref)
        rows_ref[at, :] = rows_in(cot_ref, first, size // SUB).astype(BF16)
        return carry

    turns = rows // size // 4
    for k in range(4):
        copies[1 + 2 * k].wait()
        copies[2 + 2 * k].wait()
        lax.fori_loop(k * turns, (k + 1) * turns, chunk, 0)
    copies[9].wait()
    for k, part in enumerate(split_pairs(weight_ref, flat_ref)):
        pay_ref[k * own : (k + 1) * own, :] = part


def gather_rows(me, blocks, own, channels, dst_ref):
    for m, block in enumerate(blocks):
        off = pl.multiple_of((me ^ m) * own, own)
        dst_ref[pl.ds(off, own), :] = block[0:own, :]
        dst_ref[pl.ds(pl.multiple_of(channels + off, own), own), :] = block[own : 2 * own, :]


def seg_of(group):
    row = lax.broadcasted_iota(jnp.int32, (SUB, 128), 0)
    return row // group


def shift_rows(x, by, keep):
    return jnp.where(wide(keep, x.shape[1]), pltpu.roll(x, by % SUB, 0), 0.0)


def seg_prefix(xr, xi, qr, qi, group, forward):
    seg = seg_of(group)
    segs = SUB // group
    dist = 1
    while dist < segs:
        by = group * dist if forward else SUB - group * dist
        keep = seg >= dist if forward else seg < segs - dist
        sr, si = shift_rows(xr, by, keep), shift_rows(xi, by, keep)
        ar, ai = cmul(qr, qi, sr, si)
        xr, xi = xr + ar, xi + ai
        qr, qi = cmul(qr, qi, qr, qi)
        dist *= 2
    return xr, xi


def seg_enter(xr, xi, qr, qi, dr, di, group, forward):
    seg = seg_of(group)
    segs = SUB // group
    by = group if forward else SUB - group
    keep = seg >= 1 if forward else seg < segs - 1
    er, ei = shift_rows(xr, by, keep), shift_rows(xi, by, keep)
    gap = seg if forward else segs - 1 - seg
    pr, pi = jnp.ones_like(er), jnp.zeros_like(ei)
    bit = 1
    while bit < segs:
        nr, ni = cmul(pr, pi, qr, qi)
        take = wide((gap & bit) != 0, er.shape[1])
        pr, pi = jnp.where(take, nr, pr), jnp.where(take, ni, pi)
        qr, qi = cmul(qr, qi, qr, qi)
        bit *= 2
    ar, ai = cmul(pr, pi, dr, di)
    return er + ar, ei + ai


def device_entry(ends_ref, me, channels, qr, qi, group, forward):
    seg = seg_of(group)
    segs = SUB // group
    parts = ends_ref.shape[0]
    keep = wide(seg == (segs - 1 if forward else 0), channels)
    tr = ti = jnp.zeros((SUB, channels), F32)
    for device in range(parts - 1) if forward else range(parts - 1, 0, -1):
        end = ends_ref[me ^ device]
        nr, ni = cmul(tr, ti, qr, qi)
        counts = device < me if forward else device > me
        tr = jnp.where(counts, nr + end[:, :channels], tr)
        ti = jnp.where(counts, ni + end[:, channels:], ti)
    out = []
    for x in (tr, ti):
        x = jnp.where(keep, x, 0.0)
        y = x
        for k in range(1, segs):
            y = y + pltpu.roll(x, group * k, 0)
        out.append(y)
    return out


def project_kernel(parts, own, group, low_ref, mask_ref, *refs):
    blocks = refs[:parts]
    drive_ref, end_ref, win_ref, cst_ref = refs[parts:]
    rows = low_ref.shape[0]
    channels = own * parts
    steps = rows // SUB
    me = lax.axis_index("state")
    gather_rows(me, blocks, own, channels, win_ref)
    rows_of = []
    for k in range(3):
        total = None
        for block in blocks:
            tile = block[2 * own : 2 * own + PARAM_ROWS, :].astype(F32)
            for part in range(3):
                piece = tile[3 * k + part : 3 * k + part + 1, :channels]
                total = piece if total is None else total + piece
        rows_of.append(total)
    pr, pi, gain = rows_of
    powers = [(pr, pi)]
    span = steps * (SUB // group)
    ar, ai = pr, pi
    count = 1
    while count < span:
        ar, ai = cmul(ar, ai, ar, ai)
        count *= 2
        if count in (steps, span):
            powers.append((ar, ai))
    while len(powers) < 3:
        powers.append(powers[-1])
    for k, (r, i) in enumerate(powers):
        cst_ref[k : k + 1, :] = jnp.concatenate([r, i], axis=1)
    gains = jnp.concatenate([gain, gain], axis=1)
    cst_ref[3:4, :] = gains
    cst_ref[4:8, :] = jnp.zeros((4, 2 * channels), F32)

    def chunk(c, carry):
        base = pl.multiple_of(c * CHUNK, CHUNK)
        at = pl.ds(base, CHUNK)
        mask = mask_ref[at, :]
        drive_ref[at, :] = nt(low_ref[at, :], win_ref[...]) * (gains * wide(mask, 2 * channels))
        return carry

    lax.fori_loop(0, rows // CHUNK, chunk, 0)
    br = jnp.broadcast_to(pr, (SUB, channels))
    bi = jnp.broadcast_to(pi, (SUB, channels))

    def step(j, h):
        u = drive_ref[pl.ds(pl.multiple_of(j * SUB, SUB), SUB), :]
        nr, ni = cmul(br, bi, h[0], h[1])
        return nr + u[:, :channels], ni + u[:, channels:]

    zero = jnp.zeros((SUB, channels), F32)
    er, ei = lax.fori_loop(0, steps, step, (zero, zero), unroll=8)
    er, ei = seg_prefix(er, ei, *powers[1], group, True)
    end_ref[...] = jnp.concatenate([er, ei], axis=1)


def mix_kernel(parts, own, group, orders, *refs):
    it = iter(refs)
    take = lambda n: [next(it) for _ in range(n)]
    drive_ref, end_ref, cst_ref, ends_ref = take(4)
    blocks = take(parts)
    unit_ref, cot_ref, mask_ref, vec_ref, glu_ref = take(5)
    states_ref, slow_ref, cw_ref, branch_ref, dglu_ref, gp_ref = take(6)
    grads = take(len(orders))
    act_ref, acc_ref = take(2)
    rows, feats = unit_ref.shape
    channels = own * parts
    steps = rows // SUB
    me = lax.axis_index("state")
    place = me + parts * (lax.axis_index("seq") & 1)
    gather_rows(me, blocks, own, channels, cw_ref)
    gain, bias, skip = (vec_ref[k : k + 1, :] for k in range(3))
    pr, pi = cst_ref[0:1, :channels], cst_ref[0:1, channels:]
    qr, qi = cst_ref[1:2, :channels], cst_ref[1:2, channels:]
    wr, wi = cst_ref[2:3, :channels], cst_ref[2:3, channels:]
    dr, di = device_entry(ends_ref, me, channels, wr, wi, group, True)
    hr, hi = seg_enter(end_ref[:, :channels], end_ref[:, channels:], qr, qi, dr, di, group, True)
    states_ref[0:SUB, :] = jnp.concatenate([hr, hi], axis=1)
    br = jnp.broadcast_to(pr, (SUB, channels))
    bi = jnp.broadcast_to(pi, (SUB, channels))

    def step(j, h):
        base = pl.multiple_of(j * SUB, SUB)
        u = drive_ref[pl.ds(base, SUB), :]
        nr, ni = cmul(br, bi, h[0], h[1])
        nr, ni = nr + u[:, :channels], ni + u[:, channels:]
        at = pl.ds(pl.multiple_of(base + SUB, SUB), SUB)
        states_ref[at, :channels] = nr
        states_ref[at, channels:] = ni
        return nr, ni

    lax.fori_loop(0, steps, step, (hr, hi), unroll=8)

    def chunk(c, carry):
        base = pl.multiple_of(c * CHUNK, CHUNK)
        at = pl.ds(base, CHUNK)
        states = states_ref[pl.ds(pl.multiple_of(base + SUB, SUB), CHUNK), :]
        slow = jnp.concatenate([states[:, :channels], -states[:, channels:]], axis=1).astype(BF16)
        slow_ref[at, :] = slow
        normed = unit_ref[at, :] * gain + bias
        v = nn(slow, cw_ref[...]) + skip * normed
        t = jnp.tanh(GELU_A * (v + GELU_B * (v * v * v)))
        half = 0.5 * (1.0 + t)
        gp_ref[at, :] = half + (0.5 * GELU_A) * v * (1.0 - t * t) * (1.0 + (3.0 * GELU_B) * (v * v))
        act = (v * half).astype(BF16)
        act_ref[at, :] = act
        glu = nn(act, glu_ref[...])
        mask = wide(mask_ref[at, :], feats)
        value = glu[:, :feats]
        gate = jax.nn.sigmoid(glu[:, feats:])
        branch = mask * gate
        branch_ref[at, :] = branch * value
        d_value = branch * cot_ref[at, :].astype(F32)
        dglu_ref[at, :feats] = d_value.astype(BF16)
        dglu_ref[at, feats:] = (d_value * value * (1.0 - gate)).astype(BF16)
        return carry

    lax.fori_loop(0, rows // CHUNK, chunk, 0)
    width = 256

    def tile(c, carry):
        at = pl.ds(pl.multiple_of(c * width, width), width)
        acc_ref[:, at] = tn(act_ref[...], dglu_ref[:, at])
        return carry

    lax.fori_loop(0, 2 * feats // width, tile, 0)
    spread(acc_ref, place, orders, grads)


def spread(acc_ref, place, orders, grads):
    for order, ref in zip(orders, grads):
        _, size, _ = ref.shape
        for k, m in enumerate(order):
            at = pl.ds(pl.multiple_of((place ^ m) * size, size), size)
            ref[k] = acc_ref[at, :].astype(ref.dtype)


def spread_pairs(acc_ref, place, own, channels, orders, grads):
    for order, ref in zip(orders, grads):
        for k, m in enumerate(order):
            off = pl.multiple_of((place ^ m) * own, own)
            ref[k, 0:own] = acc_ref[pl.ds(off, own), :].astype(ref.dtype)
            also = pl.ds(pl.multiple_of(channels + off, own), own)
            ref[k, own : 2 * own] = acc_ref[also, :].astype(ref.dtype)


def back_kernel(own, group, orders, *refs):
    it = iter(refs)
    take = lambda n: [next(it) for _ in range(n)]
    dglu_ref, gp_ref, unit_ref, vec_ref, glu_ref, cw_ref, slow_ref, cst_ref = take(8)
    dpre_ref, dst_ref, start_ref, skip_ref = take(4)
    grads = take(len(orders))
    dmix_ref, acc_ref = take(2)
    rows, feats = gp_ref.shape
    channels = cw_ref.shape[0] // 2
    steps = rows // SUB
    place = lax.axis_index("state") + lax.axis_size("state") * (lax.axis_index("seq") & 1)
    gain, bias = vec_ref[0:1, :], vec_ref[1:2, :]

    def chunk(c, total):
        at = pl.ds(pl.multiple_of(c * CHUNK, CHUNK), CHUNK)
        d_pre = nt(dglu_ref[at, :], glu_ref[...]) * gp_ref[at, :]
        dpre_ref[at, :] = d_pre
        normed = unit_ref[at, :] * gain + bias
        total = total + jnp.sum((d_pre * normed).reshape(CHUNK // SUB, SUB, feats), axis=0)
        d_mixed = d_pre.astype(BF16)
        dmix_ref[at, :] = d_mixed
        dst_ref[at, :] = nt(d_mixed, cw_ref[...])
        return total

    total = lax.fori_loop(0, rows // CHUNK, chunk, jnp.zeros((SUB, feats), F32))
    skip_ref[...] = total
    pr, pi = cst_ref[0:1, :channels], cst_ref[0:1, channels:]
    br = jnp.broadcast_to(pr, (SUB, channels))
    bi = jnp.broadcast_to(-pi, (SUB, channels))

    def step(k, a):
        base = pl.multiple_of((steps - 1 - k) * SUB, SUB)
        u = dst_ref[pl.ds(base, SUB), :]
        nr, ni = cmul(br, bi, a[0], a[1])
        return nr + u[:, :channels], ni - u[:, channels:]

    zero = jnp.zeros((SUB, channels), F32)
    ar, ai = lax.fori_loop(0, steps, step, (zero, zero), unroll=8)
    qr, qi = cst_ref[1:2, :channels], -cst_ref[1:2, channels:]
    ar, ai = seg_prefix(ar, ai, qr, qi, group, False)
    start_ref[...] = jnp.concatenate([ar, ai], axis=1)
    width = 256

    def tile(c, carry):
        at = pl.ds(pl.multiple_of(c * width, width), width)
        acc_ref[:, at] = tn(slow_ref[...], dmix_ref[:, at])
        return carry

    lax.fori_loop(0, feats // width, tile, 0)
    spread(acc_ref, place, orders, grads)


def adjoint_kernel(own, group, orders, *refs):
    it = iter(refs)
    take = lambda n: [next(it) for _ in range(n)]
    dst_ref, start_ref, cst_ref, ends_ref = take(4)
    states_ref, drive_ref, low_ref, mask_ref = take(4)
    dproj_ref, sums_ref = take(2)
    grads = take(len(orders))
    adj_ref, acc_ref = take(2)
    rows = dst_ref.shape[0]
    channels = dst_ref.shape[1] // 2
    steps = rows // SUB
    me = lax.axis_index("state")
    pr, pi = cst_ref[0:1, :channels], -cst_ref[0:1, channels:]
    qr, qi = cst_ref[1:2, :channels], -cst_ref[1:2, channels:]
    wr, wi = cst_ref[2:3, :channels], -cst_ref[2:3, channels:]
    dr, di = device_entry(ends_ref, me, channels, wr, wi, group, False)
    ar, ai = seg_enter(start_ref[:, :channels], start_ref[:, channels:], qr, qi, dr, di, group, False)
    br = jnp.broadcast_to(pr, (SUB, channels))
    bi = jnp.broadcast_to(pi, (SUB, channels))

    def step(k, carry):
        ar, ai, sr, si, sg = carry
        base = pl.multiple_of((steps - 1 - k) * SUB, SUB)
        at = pl.ds(base, SUB)
        d = dst_ref[at, :]
        nr, ni = cmul(br, bi, ar, ai)
        ar, ai = nr + d[:, :channels], ni - d[:, channels:]
        adj_ref[at, :channels] = ar
        adj_ref[at, channels:] = ai
        h = states_ref[at, :]
        hr, hi = h[:, :channels], h[:, channels:]
        u = drive_ref[at, :]
        sr = sr + (ar * hr + ai * hi)
        si = si + (ai * hr - ar * hi)
        sg = sg + (ar * u[:, :channels] + ai * u[:, channels:])
        return ar, ai, sr, si, sg

    zero = jnp.zeros((SUB, channels), F32)
    out = lax.fori_loop(0, steps, step, (ar, ai, zero, zero, zero), unroll=4)
    sums_ref[:, :channels] = out[2]
    sums_ref[:, channels : 2 * channels] = out[3]
    sums_ref[:, 2 * channels : 3 * channels] = out[4]
    gains = cst_ref[3:4, :]

    def chunk(c, carry):
        base = pl.multiple_of(c * CHUNK, CHUNK)
        at = pl.ds(base, CHUNK)
        mask = mask_ref[at, :]
        dproj_ref[at, :] = (adj_ref[at, :] * (gains * wide(mask, 2 * channels))).astype(BF16)
        return carry

    lax.fori_loop(0, rows // CHUNK, chunk, 0)
    width = 256
    feats = low_ref.shape[1]

    def tile(c, carry):
        at = pl.ds(pl.multiple_of(c * width, width), width)
        acc_ref[:, at] = tn(dproj_ref[...], low_ref[:, at])
        return carry

    lax.fori_loop(0, feats // width, tile, 0)
    spread_pairs(acc_ref, me, own, channels, orders, grads)


def out_kernel(x_hbm, branch_ref, out_ref, x_ref, sems):
    segs, steps, _, _ = x_ref.shape
    size = 16
    cut = steps // 4
    places = [pl.ds(k * cut, cut) for k in range(4)]
    copies = start_copies([x_hbm.at[:, p] for p in places], [x_ref.at[:, p] for p in places], sems)

    def chunk(c, carry):
        first = pl.multiple_of(c * size, size)
        rows = branch_ref[pl.ds(pl.multiple_of(first * SUB, size * SUB), size * SUB), :]
        at = pl.ds(first, size)
        out_ref[:, at] = (x_ref[:, at].astype(F32) + rows_out(rows, x_ref)).astype(BF16)
        return carry

    for k in range(4):
        copies[k].wait()
        lax.fori_loop(k * cut // size, (k + 1) * cut // size, chunk, 0)


def normed_kernel(dproj_ref, win_ref, dpre_ref, unit_ref, vec_ref, channel_ref, skip_ref, dnorm_ref, sums_ref):
    rows, feats = dpre_ref.shape
    skip = vec_ref[2:3, :]

    def chunk(c, carry):
        total_gain, total_bias = carry
        at = pl.ds(pl.multiple_of(c * CHUNK, CHUNK), CHUNK)
        d_normed = dpre_ref[at, :] * skip + nn(dproj_ref[at, :], win_ref[...])
        dnorm_ref[at, :] = d_normed
        folded = lambda v: jnp.sum(v.reshape(CHUNK // SUB, SUB, feats), axis=0)
        return total_gain + folded(d_normed * unit_ref[at, :]), total_bias + folded(d_normed)

    zero = jnp.zeros((SUB, feats), F32)
    total_gain, total_bias = lax.fori_loop(0, rows // CHUNK, chunk, (zero, zero))
    over = lambda v: jnp.sum(v, axis=0, keepdims=True)
    channel = over(channel_ref[...])
    wide_at = channel.shape[1] - feats
    sums_ref[0:1, :] = channel[:, :feats]
    sums_ref[1:2, :] = jnp.zeros((1, feats), F32)
    sums_ref[1:2, :wide_at] = channel[:, feats:]
    sums_ref[2:3, :] = over(total_gain)
    sums_ref[3:4, :] = over(total_bias)
    sums_ref[4:5, :] = over(skip_ref[...])
    sums_ref[5:8, :] = jnp.zeros((3, feats), F32)


def tokens_kernel(cot_hbm, dnorm_ref, unit_ref, inv_ref, vec_ref, out_ref, cot_ref, sems):
    rows, feats = dnorm_ref.shape
    gain = vec_ref[0:1, :]
    size = 128
    steps = size // SUB
    cut = cot_ref.shape[1] // 4
    places = [pl.ds(k * cut, cut) for k in range(4)]
    copies = start_copies([cot_hbm.at[:, p] for p in places], [cot_ref.at[:, p] for p in places], sems)

    def chunk(c, carry):
        at = pl.ds(pl.multiple_of(c * size, size), size)
        unit = unit_ref[at, :]
        d_unit = dnorm_ref[at, :] * gain
        first = jnp.mean(d_unit, axis=1, keepdims=True)
        second = jnp.mean(d_unit * unit, axis=1, keepdims=True)
        rows = wide(inv_ref[at, :], feats) * (d_unit - first - unit * second)
        step_at = pl.ds(pl.multiple_of(c * steps, steps), steps)
        out_ref[:, step_at] = cot_ref[:, step_at].astype(F32) + rows_out(rows, cot_ref)
        return carry

    for k in range(4):
        copies[k].wait()
        lax.fori_loop(k * cut // steps, (k + 1) * cut // steps, chunk, 0)


def join_pairs(parts, flat_ref, out_ref):
    own, _, feats = out_ref.shape
    for k, part in enumerate(parts):
        for c in range(feats // 128):
            flat_ref[c, pl.ds(k, own, stride=2), :] = part[:, c * 128 : (c + 1) * 128]
    rows = jnp.concatenate([flat_ref[c] for c in range(feats // 128)], axis=1)
    out_ref[...] = rows.reshape(own, 2, feats)


def halves_kernel(mine_ref, other_ref, out_ref, flat_ref):
    own = out_ref.shape[0]
    first = (lax.axis_index("seq") & 1) == 0
    a, b = mine_ref[...].astype(F32), other_ref[...].astype(F32)
    join_pairs([jnp.where(first, a, b), jnp.where(first, b, a)], flat_ref, out_ref)


def finish_kernel(low_ref, got_ref, sums_ref, more_ref, vec_ref, in_ref, feat_ref, rate_ref, angle_ref, level_ref, flat_ref):
    own, _, feats = in_ref.shape
    total = low_ref[...].astype(F32) + got_ref[0 : 2 * own, :].astype(F32)
    join_pairs([total[:own, :], total[own:, :]], flat_ref, in_ref)
    sums = sums_ref[...] + more_ref[...]
    feat_ref[...] = sums[2:5, :]
    me = lax.axis_index("state")
    channels = lax.axis_size("state") * own
    pick = lambda row: sum(
        jnp.where(me == d, row[:, d * own : (d + 1) * own], 0.0) for d in range(channels // own)
    )
    sum_re, sum_im = pick(sums[0:1, :channels]), pick(sums[0:1, channels:])
    pole_re, pole_im, decay, angle = (vec_ref[k : k + 1, :own] for k in range(3, 7))
    rate_ref[...] = -decay * (sum_re * pole_re + sum_im * pole_im)
    angle_ref[...] = angle * (sum_im * pole_re - sum_re * pole_im)
    level_ref[...] = pick(sums[1:2, :channels])


def place_kernel(masks, parts, *refs):
    arrays, out_ref = refs[:-1], refs[-1]
    place = lax.axis_index("state") + parts * (lax.axis_index("seq") & 1)
    size = arrays[0].shape[1]
    for ms, ref in zip(masks, arrays):
        for k, m in enumerate(ms):
            at = pl.ds(pl.multiple_of((place ^ m) * size, size), size)
            out_ref[at, :] = ref[k].astype(F32)


def exchange(x, mask):
    count = lax.axis_size("seq") * lax.axis_size("state")
    return lax.ppermute(x, ("seq", "state"), [(i, i ^ mask) for i in range(count)])


def tie(x, *after):
    return lax.optimization_barrier((x, after))[0]


def bits_of(n):
    return [1 << k for k in range(n.bit_length() - 1)]


def submasks(group):
    out = [0]
    for bit in group:
        out += [m | bit for m in out]
    return out[1:]


def stage_orders(groups):
    kept = [0]
    stages = []
    for group in reversed(groups):
        sends = [[m ^ p for m in kept] for p in submasks(group)]
        stages.insert(0, sends)
        kept = sum(sends, []) + kept
    return [o for sends in stages for o in sends] + [[0]]


def halve(parts, group, after=None):
    masks = submasks(group)
    sends = [p.astype(BF16) for p in parts[: len(masks)]]
    got = [exchange(p, m) for p, m in zip(sends, masks)]
    if after is not None:
        got = tie(got, after)
    rest, off = [], 0
    for p in parts[len(masks) :]:
        n = p.shape[0]
        total = p.astype(F32)
        for g in got:
            total = total + g[off : off + n].astype(F32)
        rest.append(total)
        off += n
    return rest


def rounded(x):
    return lax.reduce_precision(x, 8, 7)


def double(x, mask):
    low = rounded(x).astype(BF16)
    return low.astype(F32) + exchange(low, mask).astype(F32)


def two_parts(x):
    high = rounded(x)
    return [high.astype(BF16), rounded(x - high).astype(BF16)]


def sum_of(parts):
    return parts[0].astype(F32) + parts[1].astype(F32)


def gather_ends(end, bits):
    g = end[None]
    for bit in reversed(bits):
        g = jnp.stack([g, exchange(g, bit)], axis=1).reshape((2 * g.shape[0],) + end.shape)
    return g


def gather_blocks(own, bits):
    blocks = {0: own}
    for bit in reversed(bits):
        for m in list(blocks):
            blocks[m ^ bit] = exchange(blocks[m], bit)
    return [blocks[m] for m in range(len(blocks))]


def shards(
    tokens,
    norm_gain,
    norm_bias,
    input_weight,
    output_weight,
    log_rate,
    log_angle,
    log_gain,
    skip_gain,
    glu_weight,
    lengths,
    cotangent,
):
    span, group, feats = tokens.shape
    own = log_rate.shape[0]
    parts = lax.axis_size("state")
    n_seq = lax.axis_size("seq")
    channels = own * parts
    rows = span * group
    segs = SUB // group
    me = lax.axis_index("state")
    state_bits = bits_of(parts)
    seq_masks = [parts * b for b in bits_of(n_seq)]
    if len(seq_masks) > 2:
        seq_masks[-1] |= seq_masks[-2]
    full = rows * feats * 2 * channels * 2

    as_row = lambda v: v.reshape(1, -1)
    flat = pltpu.VMEM((feats // 128, 2 * own, 128), F32)
    x4 = tokens.reshape(segs, span // segs, group, feats)
    cot4 = cotangent.reshape(segs, span // segs, group, feats)
    ins = [input_weight.transpose(1, 2, 0)]
    ins += [as_row(v) for v in (log_rate, log_angle, log_gain, norm_gain, norm_bias, skip_gain)]
    b_own, vec = call(
        prep_kernel,
        [((2 * own + PARAM_ROWS, feats), BF16), ((SUB, feats), F32)],
        ins,
        [held(x) for x in ins] + [flat, pltpu.SemaphoreType.DMA((7,))],
        8,
        MIB,
        "prep",
        fetched=range(7),
    )
    b_blocks = gather_blocks(b_own, state_bits)
    low, unit, inv, mask, cot, c_own = call(
        norm_kernel,
        [
            ((rows, feats), BF16),
            ((rows, feats), F32),
            ((rows, 128), F32),
            ((rows, 128), F32),
            ((rows, feats), BF16),
            ((2 * own, feats), BF16),
        ],
        [x4, cot4, output_weight, lengths, vec],
        [held(x4), held(cot4), held(output_weight), pltpu.SMEM(lengths.shape, jnp.int32)]
        + [flat, pltpu.SemaphoreType.DMA((10,))],
        12,
        rows * feats * 20,
        "norm",
        fetched=range(4),
    )
    c_blocks = gather_blocks(c_own, state_bits)
    drive, end, win, cst = call(
        functools.partial(project_kernel, parts, own, group),
        [
            ((rows, 2 * channels), F32),
            ((SUB, 2 * channels), F32),
            ((2 * channels, feats), BF16),
            ((SUB, 2 * channels), F32),
        ],
        [low, mask] + b_blocks,
        [],
        12,
        full,
        "project",
    )
    ends = gather_ends(end, state_bits)
    all_bits = state_bits + [parts]
    all_groups = [all_bits[:1]] + [all_bits[k : k + 2] for k in range(1, len(all_bits), 2)]
    all_orders = stage_orders(all_groups)
    glu_rows = feats // (2 * parts)
    block_outs = lambda rows, width, orders: [
        ((len(o), rows, width), BF16 if k == 0 else F32) for k, o in enumerate(orders)
    ]
    states, slow, cw, branch, d_glu, slope, *glu_parts = call(
        functools.partial(mix_kernel, parts, own, group, all_orders),
        [
            ((rows + SUB, 2 * channels), F32),
            ((rows, 2 * channels), BF16),
            ((2 * channels, feats), BF16),
            ((rows, feats), F32),
            ((rows, 2 * feats), BF16),
            ((rows, feats), F32),
        ]
        + block_outs(glu_rows, 2 * feats, all_orders),
        [drive, end, cst, ends] + c_blocks + [unit, cot, mask, vec, glu_weight],
        [pltpu.VMEM((rows, feats), BF16), pltpu.VMEM((feats, 2 * feats), F32)],
        20,
        5 * full,
        "mix",
    )
    d_pre, d_states, start, skip_sum, *out_parts = call(
        functools.partial(back_kernel, own, group, all_orders),
        [
            ((rows, feats), F32),
            ((rows, 2 * channels), F32),
            ((SUB, 2 * channels), F32),
            ((SUB, feats), F32),
        ]
        + block_outs(own, feats, all_orders),
        [d_glu, slope, unit, vec, glu_weight, cw, slow, cst],
        [pltpu.VMEM((rows, feats), BF16), pltpu.VMEM((2 * channels, feats), F32)],
        16,
        4 * full,
        "back",
    )
    starts = gather_ends(start, state_bits)
    (out4,) = call(
        out_kernel,
        [(x4.shape, BF16)],
        [x4, tie(branch, start)],
        [held(x4), pltpu.SemaphoreType.DMA((4,))],
        8,
        MIB,
        "out",
        fetched=(0,),
    )
    glu_parts = halve(glu_parts, all_groups[0], after=start)
    out_parts = halve(out_parts, all_groups[0])
    both = [jnp.concatenate(p, axis=-1) for p in zip(glu_parts, out_parts)]
    state_groups = [[b] for b in state_bits]
    pair_orders = stage_orders(state_groups)
    d_proj, channel_sums, *in_parts = call(
        functools.partial(adjoint_kernel, own, group, pair_orders),
        [((rows, 2 * channels), BF16), ((SUB, 3 * channels), F32)]
        + block_outs(2 * own, feats, pair_orders),
        [tie(d_states, out4), start, cst, starts, states, drive, low, mask],
        [pltpu.VMEM((rows, 2 * channels), F32), pltpu.VMEM((2 * channels, feats), F32)],
        16,
        2 * full,
        "adjoint",
    )
    for g in all_groups[1:]:
        both = halve(both, g, after=channel_sums)
    both = both[0][0]
    in_parts = halve(in_parts, state_groups[0])
    d_normed, sums = call(
        normed_kernel,
        [((rows, feats), F32), ((SUB, feats), F32)],
        [d_proj, win, d_pre, unit, vec, channel_sums, skip_sum],
        [],
        12,
        full,
        "normed",
    )
    for g in state_groups[1:]:
        keep = in_parts[1:]
        own_sums = two_parts(sums)
        send = jnp.concatenate([in_parts[0].astype(BF16).reshape(-1, feats)] + own_sums, axis=0)
        got = exchange(send, g[0])
        in_parts, off = [], 0
        for p in keep:
            n = p.shape[0] * p.shape[1]
            in_parts.append(p + got[off : off + n].reshape(p.shape).astype(F32))
            off += n
        sums = sum_of(own_sums) + sum_of([got[off : off + SUB], got[off + SUB :]])
        send = in_parts[0]
    total = in_parts[0][0]
    (grad4,) = call(
        tokens_kernel,
        [(cot4.shape, F32)],
        [cot4, tie(d_normed, both, send), unit, inv, vec],
        [held(cot4), pltpu.SemaphoreType.DMA((4,))],
        12,
        full,
        "tokens",
        fetched=(0,),
    )
    for m in seq_masks:
        low_total = rounded(total).astype(BF16)
        own_sums = two_parts(sums)
        got = exchange(jnp.concatenate([low_total] + own_sums, axis=0), m)
        total = low_total.astype(F32) + got[: 2 * own].astype(F32)
        got_sums = [got[2 * own : 2 * own + SUB], got[2 * own + SUB :]]
        sums = sum_of(own_sums) + sum_of(got_sums)
    grad_in, feature_grads, grad_rate, grad_angle, grad_level = call(
        finish_kernel,
        [((own, 2, feats), F32), ((3, feats), F32)] + [((1, own), F32)] * 3,
        [low_total, got, sums, exchange(sums, state_bits[0]), vec],
        [flat],
        8,
        MIB,
        "finish",
    )

    for m in seq_masks[1:]:
        both = double(both, m)
    both = rounded(both).astype(BF16)
    blocks = {0: both[:, : 2 * feats]}
    for g in reversed(all_groups[1:]):
        for m in list(blocks):
            for p in submasks(g):
                if m == 0 and p == parts:
                    got = exchange(both, p)
                    blocks[p] = got[:, : 2 * feats]
                    other_half = got[:, 2 * feats :]
                else:
                    blocks[m ^ p] = exchange(blocks[m], p)
    rest = [m for m in blocks if m]
    arrays = [blocks[0][None], jnp.stack([blocks[m] for m in rest])]
    masks = [[0], rest]
    for p in submasks(all_groups[0]):
        arrays += [exchange(a, p) for a in arrays[:2]]
        masks += [[m ^ p for m in ms] for ms in masks[:2]]
    (grad_out,) = call(
        halves_kernel,
        [((own, 2, feats), F32)],
        [both[:, 2 * feats :], other_half],
        [flat],
        8,
        MIB,
        "halves",
    )
    (grad_glu,) = call(
        functools.partial(place_kernel, masks, parts),
        [((feats, 2 * feats), F32)],
        arrays,
        [],
        8,
        feats * feats,
        "place",
    )
    return (
        out4.reshape(tokens.shape),
        grad4.reshape(tokens.shape),
        feature_grads[0],
        feature_grads[1],
        grad_in.transpose(2, 0, 1),
        grad_out,
        grad_rate.reshape(own),
        grad_angle.reshape(own),
        grad_level.reshape(own),
        feature_grads[2],
        grad_glu,
    )


def solution(mesh):
    placed = (
        P("state", "seq", None),
        P(),
        P(),
        P(None, "state", None),
        P("state", None, None),
        P("state"),
        P("state"),
        P("state"),
        P(),
        P(),
        P("seq"),
        P("state", "seq", None),
    )
    return jax.shard_map(
        shards,
        mesh=mesh,
        in_specs=placed,
        out_specs=(
            P("state", "seq", None),
            P("state", "seq", None),
            P(),
            P(),
            P(None, "state", None),
            P("state", None, None),
            P("state"),
            P("state"),
            P("state"),
            P(),
            P(),
        ),
        check_vma=False,
    )
```

```python
import functools

import jax
import jax.numpy as jnp
from jax import lax
from jax.experimental import pallas as pl
from jax.experimental.pallas import tpu as pltpu
from jax.sharding import PartitionSpec as P

F32, BF16 = jnp.float32, jnp.bfloat16
EPSILON = 1e-05
SUB = 8
CHUNK = 256
PARAM_ROWS = 16
GELU_A = 0.7978845608028654
GELU_B = 0.044715
MIB = 1 << 20


def cmul(ar, ai, br, bi):
    return ar * br - ai * bi, ar * bi + ai * br


def nn(a, b):
    return lax.dot_general(a, b, (((1,), (0,)), ((), ())), preferred_element_type=F32)


def nt(a, b):
    return lax.dot_general(a, b, (((1,), (1,)), ((), ())), preferred_element_type=F32)


def tn(a, b):
    return lax.dot_general(a, b, (((0,), (0,)), ((), ())), preferred_element_type=F32)


def rows_in(ref, first, count):
    segs, _, group, feats = ref.shape
    x = ref[:, pl.ds(first, count)].astype(F32)
    return x.transpose(1, 0, 2, 3).reshape(count * segs * group, feats)


def rows_out(y, ref):
    segs, _, group, feats = ref.shape
    return y.reshape(y.shape[0] // SUB, segs, group, feats).transpose(1, 0, 2, 3)


def row_mask(base, rows, group, steps, me, lengths):
    segs = SUB // group
    row = lax.broadcasted_iota(jnp.int32, (rows, 128), 0) + base
    place = row & (SUB - 1)
    seq = place & (group - 1)
    position = (me * (segs * steps) + (place // group) * steps + (row // SUB)).astype(F32)
    length = jnp.broadcast_to(lengths[:, 0:1], (rows, 128))
    for k in range(1, group):
        length = jnp.where(seq == k, lengths[:, k : k + 1], length)
    return (position < length).astype(F32)


def wide(column, lanes):
    return jnp.concatenate([column] * (lanes // column.shape[1]), axis=1)


def call(body, outs, ins, scratch, limit_mib, flops, name, fetched=()):
    specs = []
    for k, x in enumerate(ins):
        space = pltpu.SMEM if x.dtype == jnp.int32 else pltpu.HBM if k in fetched else pltpu.VMEM
        specs.append(pl.BlockSpec(memory_space=space))
    return pl.pallas_call(
        body,
        out_shape=[jax.ShapeDtypeStruct(s, d) for s, d in outs],
        in_specs=specs,
        out_specs=[pl.BlockSpec(memory_space=pltpu.VMEM)] * len(outs),
        scratch_shapes=scratch,
        compiler_params=pltpu.CompilerParams(vmem_limit_bytes=limit_mib * MIB),
        cost_estimate=pl.CostEstimate(flops=flops, bytes_accessed=4 * MIB, transcendentals=0),
        name=name,
    )(*ins)


def start_copies(sources, targets, sems):
    copies = [pltpu.make_async_copy(a, b, sems.at[k]) for k, (a, b) in enumerate(zip(sources, targets))]
    for c in copies:
        c.start()
    return copies


def held(x):
    return pltpu.VMEM(x.shape, x.dtype)


def split_pairs(pairs_ref, flat_ref):
    own, _, feats = pairs_ref.shape
    flat = pairs_ref[...].astype(F32).reshape(2 * own, feats)
    for c in range(feats // 128):
        flat_ref[c] = flat[:, c * 128 : (c + 1) * 128]
    take = lambda k: [flat_ref[c, pl.ds(k, own, stride=2), :] for c in range(feats // 128)]
    return [jnp.concatenate(take(k), axis=1).astype(BF16) for k in range(2)]


def three_parts(x):
    high = x.astype(BF16)
    rest = x - high.astype(F32)
    mid = rest.astype(BF16)
    return [high, mid, (rest - mid.astype(F32)).astype(BF16)]


def prep_kernel(own, group, small_ref, pay_ref, vec_ref):
    feats = vec_ref.shape[1]
    me = lax.axis_index("state")
    lane = lax.broadcasted_iota(jnp.int32, (1, feats), 1)
    mine = (lane // own) == me
    base = 3 * feats
    logs = [small_ref[:, base + k * own : base + (k + 1) * own] for k in range(3)]
    rate, turn, level = (jnp.concatenate([v] * (feats // own), axis=1) for v in logs)
    decay = jnp.exp(rate)
    size = jnp.exp(-decay)
    angle = jnp.exp(turn)
    pole_re, pole_im = size * jnp.cos(angle), size * jnp.sin(angle)
    parts = []
    for v in (pole_re, pole_im, jnp.exp(level)):
        parts += three_parts(jnp.where(mine, v, 0.0))
    parts += [jnp.zeros((PARAM_ROWS - len(parts), feats), BF16)]
    flat = jnp.concatenate([p.astype(F32) for p in parts], axis=0)
    pay_ref[...] = flat.reshape(PARAM_ROWS // 2, 2, feats).astype(BF16)
    rows = [small_ref[:, k * feats : (k + 1) * feats] for k in range(3)] + [pole_re, pole_im, decay, angle]
    for k, row in enumerate(rows):
        vec_ref[k : k + 1, :] = row
    base += 3 * own
    vec_ref[len(rows) :, :] = jnp.zeros((SUB - len(rows), feats), F32)
    vec_ref[7:8, :group] = small_ref[:, base : base + group]


def cotangent_kernel(cot_ref, rows_ref):
    steps = 16
    for c in range(cot_ref.shape[1] // steps):
        at = pl.ds(c * steps * SUB, steps * SUB)
        rows_ref[at, :] = rows_in(cot_ref, c * steps, steps).astype(BF16)


def weights_kernel(*refs):
    blocks, (out_ref, flat_ref) = refs[:-2], refs[-2:]
    gather_rows(lax.axis_index("state"), blocks, flat_ref, out_ref)


def norm_kernel(x_ref, vec_ref, low_ref, unit_ref, inv_ref, mask_ref):
    segs, steps, group, feats = x_ref.shape
    rows = steps * SUB
    me = lax.axis_index("state")
    size = 128
    gain, bias = vec_ref[0:1, :], vec_ref[1:2, :]

    def chunk(c, carry):
        base = pl.multiple_of(c * size, size)
        at = pl.ds(base, size)
        x = rows_in(x_ref, pl.multiple_of(c * (size // SUB), size // SUB), size // SUB)
        centred = x - jnp.mean(x, axis=1, keepdims=True)
        inv = lax.rsqrt(jnp.mean(centred * centred, axis=1, keepdims=True) + EPSILON)
        unit = centred * inv
        unit_ref[at, :] = unit
        low_ref[at, :] = (unit * gain + bias).astype(BF16)
        inv_ref[at, :] = jnp.broadcast_to(inv, (size, 128))
        mask_ref[at, :] = row_mask(base, size, group, steps, me, vec_ref[7:8, :])
        return carry

    lax.fori_loop(0, rows // size, chunk, 0)


def gather_rows(me, blocks, flat_ref, dst_ref):
    own = flat_ref.shape[1] // 2
    channels = own * len(blocks)
    for m, block in enumerate(blocks):
        for k, part in enumerate(split_pairs(block.at[0:own], flat_ref)):
            at = pl.multiple_of(k * channels + (me ^ m) * own, own)
            dst_ref[pl.ds(at, own), :] = part


def seg_of(group):
    row = lax.broadcasted_iota(jnp.int32, (SUB, 128), 0)
    return row // group


def shift_rows(x, by, keep):
    return jnp.where(wide(keep, x.shape[1]), pltpu.roll(x, by % SUB, 0), 0.0)


def seg_prefix(xr, xi, qr, qi, group, forward):
    seg = seg_of(group)
    segs = SUB // group
    dist = 1
    while dist < segs:
        by = group * dist if forward else SUB - group * dist
        keep = seg >= dist if forward else seg < segs - dist
        sr, si = shift_rows(xr, by, keep), shift_rows(xi, by, keep)
        ar, ai = cmul(qr, qi, sr, si)
        xr, xi = xr + ar, xi + ai
        qr, qi = cmul(qr, qi, qr, qi)
        dist *= 2
    return xr, xi


def seg_enter(xr, xi, qr, qi, dr, di, group, forward):
    seg = seg_of(group)
    segs = SUB // group
    by = group if forward else SUB - group
    keep = seg >= 1 if forward else seg < segs - 1
    er, ei = shift_rows(xr, by, keep), shift_rows(xi, by, keep)
    gap = seg if forward else segs - 1 - seg
    pr, pi = jnp.ones_like(er), jnp.zeros_like(ei)
    bit = 1
    while bit < segs:
        nr, ni = cmul(pr, pi, qr, qi)
        take = wide((gap & bit) != 0, er.shape[1])
        pr, pi = jnp.where(take, nr, pr), jnp.where(take, ni, pi)
        qr, qi = cmul(qr, qi, qr, qi)
        bit *= 2
    ar, ai = cmul(pr, pi, dr, di)
    return er + ar, ei + ai


def device_entry(ends_ref, me, channels, qr, qi, group, forward):
    seg = seg_of(group)
    segs = SUB // group
    parts = ends_ref.shape[0]
    keep = wide(seg == (segs - 1 if forward else 0), channels)
    tr = ti = jnp.zeros((SUB, channels), F32)
    for device in range(parts - 1) if forward else range(parts - 1, 0, -1):
        end = ends_ref[me ^ device]
        nr, ni = cmul(tr, ti, qr, qi)
        counts = device < me if forward else device > me
        tr = jnp.where(counts, nr + end[:, :channels], tr)
        ti = jnp.where(counts, ni + end[:, channels:], ti)
    out = []
    for x in (tr, ti):
        x = jnp.where(keep, x, 0.0)
        y = x
        for k in range(1, segs):
            y = y + pltpu.roll(x, group * k, 0)
        out.append(y)
    return out


def project_kernel(parts, own, group, low_ref, mask_ref, *refs):
    blocks = refs[:parts]
    drive_ref, end_ref, win_ref, cst_ref, flat_ref = refs[parts:]
    rows = low_ref.shape[0]
    channels = own * parts
    steps = rows // SUB
    me = lax.axis_index("state")
    gather_rows(me, blocks, flat_ref, win_ref)
    rows_of = []
    for k in range(3):
        total = None
        for block in blocks:
            tile = block[own : own + PARAM_ROWS // 2].astype(F32).reshape(PARAM_ROWS, -1)
            for part in range(3):
                piece = tile[3 * k + part : 3 * k + part + 1, :channels]
                total = piece if total is None else total + piece
        rows_of.append(total)
    pr, pi, gain = rows_of
    powers = [(pr, pi)]
    span = steps * (SUB // group)
    ar, ai = pr, pi
    count = 1
    while count < span:
        ar, ai = cmul(ar, ai, ar, ai)
        count *= 2
        if count in (steps, span):
            powers.append((ar, ai))
    while len(powers) < 3:
        powers.append(powers[-1])
    for k, (r, i) in enumerate(powers):
        cst_ref[k : k + 1, :] = jnp.concatenate([r, i], axis=1)
    gains = jnp.concatenate([gain, gain], axis=1)
    cst_ref[3:4, :] = gains
    cst_ref[4:8, :] = jnp.zeros((4, 2 * channels), F32)

    def chunk(c, carry):
        base = pl.multiple_of(c * CHUNK, CHUNK)
        at = pl.ds(base, CHUNK)
        mask = mask_ref[at, :]
        drive_ref[at, :] = nt(low_ref[at, :], win_ref[...]) * (gains * wide(mask, 2 * channels))
        return carry

    lax.fori_loop(0, rows // CHUNK, chunk, 0)
    br = jnp.broadcast_to(pr, (SUB, channels))
    bi = jnp.broadcast_to(pi, (SUB, channels))

    def step(j, h):
        u = drive_ref[pl.ds(pl.multiple_of(j * SUB, SUB), SUB), :]
        nr, ni = cmul(br, bi, h[0], h[1])
        return nr + u[:, :channels], ni + u[:, channels:]

    zero = jnp.zeros((SUB, channels), F32)
    er, ei = lax.fori_loop(0, steps, step, (zero, zero), unroll=8)
    er, ei = seg_prefix(er, ei, *powers[1], group, True)
    end_ref[...] = jnp.concatenate([er, ei], axis=1)


def mix_kernel(parts, own, group, orders, *refs):
    it = iter(refs)
    take = lambda n: [next(it) for _ in range(n)]
    drive_ref, end_ref, cst_ref, ends_ref = take(4)
    cw_ref, unit_ref, cot_ref, mask_ref, vec_ref, glu_ref = take(6)
    states_ref, slow_ref, branch_ref, dglu_ref, gp_ref = take(5)
    grads = take(len(orders))
    act_ref, acc_ref = take(2)
    rows, feats = unit_ref.shape
    channels = own * parts
    steps = rows // SUB
    me = lax.axis_index("state")
    place = me + parts * (lax.axis_index("seq") & 1)
    gain, bias, skip = (vec_ref[k : k + 1, :] for k in range(3))
    pr, pi = cst_ref[0:1, :channels], cst_ref[0:1, channels:]
    qr, qi = cst_ref[1:2, :channels], cst_ref[1:2, channels:]
    wr, wi = cst_ref[2:3, :channels], cst_ref[2:3, channels:]
    dr, di = device_entry(ends_ref, me, channels, wr, wi, group, True)
    hr, hi = seg_enter(end_ref[:, :channels], end_ref[:, channels:], qr, qi, dr, di, group, True)
    states_ref[0:SUB, :] = jnp.concatenate([hr, hi], axis=1)
    br = jnp.broadcast_to(pr, (SUB, channels))
    bi = jnp.broadcast_to(pi, (SUB, channels))

    def step(j, h):
        base = pl.multiple_of(j * SUB, SUB)
        u = drive_ref[pl.ds(base, SUB), :]
        nr, ni = cmul(br, bi, h[0], h[1])
        nr, ni = nr + u[:, :channels], ni + u[:, channels:]
        at = pl.ds(pl.multiple_of(base + SUB, SUB), SUB)
        states_ref[at, :channels] = nr
        states_ref[at, channels:] = ni
        return nr, ni

    lax.fori_loop(0, steps, step, (hr, hi), unroll=8)

    def chunk(c, carry):
        base = pl.multiple_of(c * CHUNK, CHUNK)
        at = pl.ds(base, CHUNK)
        states = states_ref[pl.ds(pl.multiple_of(base + SUB, SUB), CHUNK), :]
        slow = jnp.concatenate([states[:, :channels], -states[:, channels:]], axis=1).astype(BF16)
        slow_ref[at, :] = slow
        normed = unit_ref[at, :] * gain + bias
        v = nn(slow, cw_ref[...]) + skip * normed
        t = jnp.tanh(GELU_A * (v + GELU_B * (v * v * v)))
        half = 0.5 * (1.0 + t)
        gp_ref[at, :] = half + (0.5 * GELU_A) * v * (1.0 - t * t) * (1.0 + (3.0 * GELU_B) * (v * v))
        act = (v * half).astype(BF16)
        act_ref[at, :] = act
        glu = nn(act, glu_ref[...])
        mask = wide(mask_ref[at, :], feats)
        value = glu[:, :feats]
        gate = jax.nn.sigmoid(glu[:, feats:])
        branch = mask * gate
        branch_ref[at, :] = branch * value
        d_value = branch * cot_ref[at, :].astype(F32)
        dglu_ref[at, :feats] = d_value.astype(BF16)
        dglu_ref[at, feats:] = (d_value * value * (1.0 - gate)).astype(BF16)
        return carry

    lax.fori_loop(0, rows // CHUNK, chunk, 0)
    width = 256

    def tile(c, carry):
        at = pl.ds(pl.multiple_of(c * width, width), width)
        acc_ref[:, at] = tn(act_ref[...], dglu_ref[:, at])
        return carry

    lax.fori_loop(0, 2 * feats // width, tile, 0)
    spread(acc_ref, place, orders, grads)


def spread(acc_ref, place, orders, grads):
    for order, ref in zip(orders, grads):
        _, size, _ = ref.shape
        for k, m in enumerate(order):
            at = pl.ds(pl.multiple_of((place ^ m) * size, size), size)
            ref[k] = acc_ref[at, :].astype(ref.dtype)


def spread_pairs(acc_ref, place, own, channels, orders, grads):
    for order, ref in zip(orders, grads):
        for k, m in enumerate(order):
            off = pl.multiple_of((place ^ m) * own, own)
            ref[k, 0:own] = acc_ref[pl.ds(off, own), :].astype(ref.dtype)
            also = pl.ds(pl.multiple_of(channels + off, own), own)
            ref[k, own : 2 * own] = acc_ref[also, :].astype(ref.dtype)


def back_kernel(own, group, orders, *refs):
    it = iter(refs)
    take = lambda n: [next(it) for _ in range(n)]
    dglu_ref, gp_ref, unit_ref, vec_ref, glu_ref, cw_ref, slow_ref, cst_ref = take(8)
    dpre_ref, dst_ref, start_ref, skip_ref = take(4)
    grads = take(len(orders))
    dmix_ref, acc_ref = take(2)
    rows, feats = gp_ref.shape
    channels = cw_ref.shape[0] // 2
    steps = rows // SUB
    place = lax.axis_index("state") + lax.axis_size("state") * (lax.axis_index("seq") & 1)
    gain, bias = vec_ref[0:1, :], vec_ref[1:2, :]

    def chunk(c, total):
        at = pl.ds(pl.multiple_of(c * CHUNK, CHUNK), CHUNK)
        d_pre = nt(dglu_ref[at, :], glu_ref[...]) * gp_ref[at, :]
        dpre_ref[at, :] = d_pre
        normed = unit_ref[at, :] * gain + bias
        total = total + jnp.sum((d_pre * normed).reshape(CHUNK // SUB, SUB, feats), axis=0)
        d_mixed = d_pre.astype(BF16)
        dmix_ref[at, :] = d_mixed
        dst_ref[at, :] = nt(d_mixed, cw_ref[...])
        return total

    total = lax.fori_loop(0, rows // CHUNK, chunk, jnp.zeros((SUB, feats), F32))
    skip_ref[...] = total
    pr, pi = cst_ref[0:1, :channels], cst_ref[0:1, channels:]
    br = jnp.broadcast_to(pr, (SUB, channels))
    bi = jnp.broadcast_to(-pi, (SUB, channels))

    def step(k, a):
        base = pl.multiple_of((steps - 1 - k) * SUB, SUB)
        u = dst_ref[pl.ds(base, SUB), :]
        nr, ni = cmul(br, bi, a[0], a[1])
        return nr + u[:, :channels], ni - u[:, channels:]

    zero = jnp.zeros((SUB, channels), F32)
    ar, ai = lax.fori_loop(0, steps, step, (zero, zero), unroll=8)
    qr, qi = cst_ref[1:2, :channels], -cst_ref[1:2, channels:]
    ar, ai = seg_prefix(ar, ai, qr, qi, group, False)
    start_ref[...] = jnp.concatenate([ar, ai], axis=1)
    width = 256

    def tile(c, carry):
        at = pl.ds(pl.multiple_of(c * width, width), width)
        acc_ref[:, at] = tn(slow_ref[...], dmix_ref[:, at])
        return carry

    lax.fori_loop(0, feats // width, tile, 0)
    spread(acc_ref, place, orders, grads)


def adjoint_kernel(own, group, orders, *refs):
    it = iter(refs)
    take = lambda n: [next(it) for _ in range(n)]
    dst_ref, start_ref, cst_ref, ends_ref = take(4)
    states_ref, drive_ref, low_ref, mask_ref = take(4)
    dproj_ref, sums_ref = take(2)
    grads = take(len(orders))
    adj_ref, acc_ref = take(2)
    rows = dst_ref.shape[0]
    channels = dst_ref.shape[1] // 2
    steps = rows // SUB
    me = lax.axis_index("state")
    pr, pi = cst_ref[0:1, :channels], -cst_ref[0:1, channels:]
    qr, qi = cst_ref[1:2, :channels], -cst_ref[1:2, channels:]
    wr, wi = cst_ref[2:3, :channels], -cst_ref[2:3, channels:]
    dr, di = device_entry(ends_ref, me, channels, wr, wi, group, False)
    ar, ai = seg_enter(start_ref[:, :channels], start_ref[:, channels:], qr, qi, dr, di, group, False)
    br = jnp.broadcast_to(pr, (SUB, channels))
    bi = jnp.broadcast_to(pi, (SUB, channels))

    def step(k, carry):
        ar, ai, sr, si, sg = carry
        base = pl.multiple_of((steps - 1 - k) * SUB, SUB)
        at = pl.ds(base, SUB)
        d = dst_ref[at, :]
        nr, ni = cmul(br, bi, ar, ai)
        ar, ai = nr + d[:, :channels], ni - d[:, channels:]
        adj_ref[at, :channels] = ar
        adj_ref[at, channels:] = ai
        h = states_ref[at, :]
        hr, hi = h[:, :channels], h[:, channels:]
        u = drive_ref[at, :]
        sr = sr + (ar * hr + ai * hi)
        si = si + (ai * hr - ar * hi)
        sg = sg + (ar * u[:, :channels] + ai * u[:, channels:])
        return ar, ai, sr, si, sg

    zero = jnp.zeros((SUB, channels), F32)
    out = lax.fori_loop(0, steps, step, (ar, ai, zero, zero, zero), unroll=4)
    sums_ref[:, :channels] = out[2]
    sums_ref[:, channels : 2 * channels] = out[3]
    sums_ref[:, 2 * channels : 3 * channels] = out[4]
    gains = cst_ref[3:4, :]

    def chunk(c, carry):
        base = pl.multiple_of(c * CHUNK, CHUNK)
        at = pl.ds(base, CHUNK)
        mask = mask_ref[at, :]
        dproj_ref[at, :] = (adj_ref[at, :] * (gains * wide(mask, 2 * channels))).astype(BF16)
        return carry

    lax.fori_loop(0, rows // CHUNK, chunk, 0)
    width = 256
    feats = low_ref.shape[1]

    def tile(c, carry):
        at = pl.ds(pl.multiple_of(c * width, width), width)
        acc_ref[:, at] = tn(dproj_ref[...], low_ref[:, at])
        return carry

    lax.fori_loop(0, feats // width, tile, 0)
    spread_pairs(acc_ref, me, own, channels, orders, grads)


def out_kernel(x_hbm, branch_ref, out_ref, x_ref, sems):
    segs, steps, _, _ = x_ref.shape
    size = 16
    cut = steps // 4
    places = [pl.ds(k * cut, cut) for k in range(4)]
    copies = start_copies([x_hbm.at[:, p] for p in places], [x_ref.at[:, p] for p in places], sems)

    def chunk(c, carry):
        first = pl.multiple_of(c * size, size)
        rows = branch_ref[pl.ds(pl.multiple_of(first * SUB, size * SUB), size * SUB), :]
        at = pl.ds(first, size)
        out_ref[:, at] = (x_ref[:, at].astype(F32) + rows_out(rows, x_ref)).astype(BF16)
        return carry

    for k in range(4):
        copies[k].wait()
        lax.fori_loop(k * cut // size, (k + 1) * cut // size, chunk, 0)


def normed_kernel(dproj_ref, win_ref, dpre_ref, unit_ref, vec_ref, channel_ref, skip_ref, dnorm_ref, sums_ref):
    rows, feats = dpre_ref.shape
    skip = vec_ref[2:3, :]

    def chunk(c, carry):
        total_gain, total_bias = carry
        at = pl.ds(pl.multiple_of(c * CHUNK, CHUNK), CHUNK)
        d_normed = dpre_ref[at, :] * skip + nn(dproj_ref[at, :], win_ref[...])
        dnorm_ref[at, :] = d_normed
        folded = lambda v: jnp.sum(v.reshape(CHUNK // SUB, SUB, feats), axis=0)
        return total_gain + folded(d_normed * unit_ref[at, :]), total_bias + folded(d_normed)

    zero = jnp.zeros((SUB, feats), F32)
    total_gain, total_bias = lax.fori_loop(0, rows // CHUNK, chunk, (zero, zero))
    over = lambda v: jnp.sum(v, axis=0, keepdims=True)
    channel = over(channel_ref[...])
    wide_at = channel.shape[1] - feats
    sums_ref[0:1, :] = channel[:, :feats]
    sums_ref[1:2, :] = jnp.zeros((1, feats), F32)
    sums_ref[1:2, :wide_at] = channel[:, feats:]
    sums_ref[2:3, :] = over(total_gain)
    sums_ref[3:4, :] = over(total_bias)
    sums_ref[4:5, :] = over(skip_ref[...])
    sums_ref[5:8, :] = jnp.zeros((3, feats), F32)


def tokens_kernel(cot_hbm, dnorm_ref, unit_ref, inv_ref, vec_ref, out_ref, cot_ref, sems):
    rows, feats = dnorm_ref.shape
    gain = vec_ref[0:1, :]
    size = 128
    steps = size // SUB
    cut = cot_ref.shape[1] // 4
    places = [pl.ds(k * cut, cut) for k in range(4)]
    copies = start_copies([cot_hbm.at[:, p] for p in places], [cot_ref.at[:, p] for p in places], sems)

    def chunk(c, carry):
        at = pl.ds(pl.multiple_of(c * size, size), size)
        unit = unit_ref[at, :]
        d_unit = dnorm_ref[at, :] * gain
        first = jnp.mean(d_unit, axis=1, keepdims=True)
        second = jnp.mean(d_unit * unit, axis=1, keepdims=True)
        rows = wide(inv_ref[at, :], feats) * (d_unit - first - unit * second)
        step_at = pl.ds(pl.multiple_of(c * steps, steps), steps)
        out_ref[:, step_at] = cot_ref[:, step_at].astype(F32) + rows_out(rows, cot_ref)
        return carry

    for k in range(4):
        copies[k].wait()
        lax.fori_loop(k * cut // steps, (k + 1) * cut // steps, chunk, 0)


def join_pairs(parts, flat_ref, out_ref):
    own, _, feats = out_ref.shape
    for k, part in enumerate(parts):
        for c in range(feats // 128):
            flat_ref[c, pl.ds(k, own, stride=2), :] = part[:, c * 128 : (c + 1) * 128]
    rows = jnp.concatenate([flat_ref[c] for c in range(feats // 128)], axis=1)
    out_ref[...] = rows.reshape(own, 2, feats)


def halves_kernel(mine_ref, other_ref, out_ref, flat_ref):
    own = out_ref.shape[0]
    first = (lax.axis_index("seq") & 1) == 0
    a, b = mine_ref[...].astype(F32), other_ref[...].astype(F32)
    join_pairs([jnp.where(first, a, b), jnp.where(first, b, a)], flat_ref, out_ref)


def finish_kernel(low_ref, got_ref, sums_ref, more_ref, vec_ref, in_ref, feat_ref, rate_ref, angle_ref, level_ref, flat_ref):
    own, _, feats = in_ref.shape
    total = low_ref[...].astype(F32) + got_ref[0 : 2 * own, :].astype(F32)
    join_pairs([total[:own, :], total[own:, :]], flat_ref, in_ref)
    sums = sums_ref[...] + more_ref[...]
    feat_ref[...] = sums[2:5, :]
    me = lax.axis_index("state")
    channels = lax.axis_size("state") * own
    pick = lambda row: sum(
        jnp.where(me == d, row[:, d * own : (d + 1) * own], 0.0) for d in range(channels // own)
    )
    sum_re, sum_im = pick(sums[0:1, :channels]), pick(sums[0:1, channels:])
    pole_re, pole_im, decay, angle = (vec_ref[k : k + 1, :own] for k in range(3, 7))
    rate_ref[...] = -decay * (sum_re * pole_re + sum_im * pole_im)
    angle_ref[...] = angle * (sum_im * pole_re - sum_re * pole_im)
    level_ref[...] = pick(sums[1:2, :channels])


def place_kernel(masks, parts, *refs):
    arrays, out_ref = refs[:-1], refs[-1]
    place = lax.axis_index("state") + parts * (lax.axis_index("seq") & 1)
    size = arrays[0].shape[1]
    for ms, ref in zip(masks, arrays):
        for k, m in enumerate(ms):
            at = pl.ds(pl.multiple_of((place ^ m) * size, size), size)
            out_ref[at, :] = ref[k].astype(F32)


def exchange(x, mask):
    count = lax.axis_size("seq") * lax.axis_size("state")
    return lax.ppermute(x, ("seq", "state"), [(i, i ^ mask) for i in range(count)])


def tie(x, *after):
    return lax.optimization_barrier((x, after))[0]


def bits_of(n):
    return [1 << k for k in range(n.bit_length() - 1)]


def submasks(group):
    out = [0]
    for bit in group:
        out += [m | bit for m in out]
    return out[1:]


def stage_orders(groups):
    kept = [0]
    stages = []
    for group in reversed(groups):
        sends = [[m ^ p for m in kept] for p in submasks(group)]
        stages.insert(0, sends)
        kept = sum(sends, []) + kept
    return [o for sends in stages for o in sends] + [[0]]


def swap(parts, group):
    masks = submasks(group)
    return [exchange(p.astype(BF16), m) for p, m in zip(parts, masks)]


def add_up(parts, got):
    rest, off = [], 0
    for p in parts[len(got) :]:
        n = p.shape[0]
        total = p.astype(F32)
        for g in got:
            total = total + g[off : off + n].astype(F32)
        rest.append(total)
        off += n
    return rest


def halve(parts, group):
    return add_up(parts, swap(parts, group))


def rounded(x):
    return lax.reduce_precision(x, 8, 7)


def two_parts(x):
    high = rounded(x)
    return [high.astype(BF16), rounded(x - high).astype(BF16)]


def sum_of(parts):
    return parts[0].astype(F32) + parts[1].astype(F32)


def gather_ends(end, bits):
    g = end[None]
    for bit in reversed(bits):
        g = jnp.stack([g, exchange(g, bit)], axis=1).reshape((2 * g.shape[0],) + end.shape)
    return g


def gather_blocks(arrays, bits, ready=None):
    blocks = [{0: a} for a in arrays]
    for n, bit in enumerate(reversed(bits)):
        for held_blocks in blocks:
            for m in list(held_blocks):
                x = held_blocks[m]
                if m and n and ready is not None:
                    x = tie(x, ready)
                held_blocks[m ^ bit] = exchange(x, bit)
    return [[b[m] for m in range(len(b))] for b in blocks]


def shards(
    tokens,
    norm_gain,
    norm_bias,
    input_weight,
    output_weight,
    log_rate,
    log_angle,
    log_gain,
    skip_gain,
    glu_weight,
    lengths,
    cotangent,
):
    span, group, feats = tokens.shape
    own = log_rate.shape[0]
    parts = lax.axis_size("state")
    n_seq = lax.axis_size("seq")
    channels = own * parts
    rows = span * group
    segs = SUB // group
    me = lax.axis_index("state")
    state_bits = bits_of(parts)
    seq_masks = [parts * b for b in bits_of(n_seq)]
    if len(seq_masks) > 2:
        seq_masks[-1] |= seq_masks[-2]
    full = rows * feats * 2 * channels * 2

    flat = pltpu.VMEM((feats // 128, 2 * own, 128), F32)
    x4 = tokens.reshape(segs, span // segs, group, feats)
    cot4 = cotangent.reshape(segs, span // segs, group, feats)
    small = jnp.concatenate(
        [norm_gain, norm_bias, skip_gain, log_rate, log_angle, log_gain, lengths.astype(F32)]
    )
    small = jnp.pad(small, (0, -small.shape[0] % 128)).reshape(1, -1)
    small_own, vec = call(
        functools.partial(prep_kernel, own, group),
        [((PARAM_ROWS // 2, 2, feats), BF16), ((SUB, feats), F32)],
        [small],
        [],
        8,
        MIB,
        "prep",
    )
    b_own = jnp.concatenate([input_weight.transpose(1, 2, 0), small_own], axis=0)
    low, unit, inv, mask = call(
        norm_kernel,
        [((rows, feats), BF16), ((rows, feats), F32), ((rows, 128), F32), ((rows, 128), F32)],
        [x4, vec],
        [],
        12,
        rows * feats * 20,
        "norm",
    )
    b_blocks, c_blocks = gather_blocks([b_own, tie(output_weight, b_own)], state_bits, low)
    drive, end, win, cst = call(
        functools.partial(project_kernel, parts, own, group),
        [
            ((rows, 2 * channels), F32),
            ((SUB, 2 * channels), F32),
            ((2 * channels, feats), BF16),
            ((SUB, 2 * channels), F32),
        ],
        [low, mask] + b_blocks,
        [flat],
        12,
        full,
        "project",
    )
    ends = gather_ends(end, state_bits)
    (cot,) = call(cotangent_kernel, [((rows, feats), BF16)], [tie(cot4, end)], [], 8, MIB, "cotangent")
    (cw,) = call(
        weights_kernel,
        [((2 * channels, feats), BF16)],
        [tie(c_blocks[0], end)] + c_blocks[1:],
        [flat],
        8,
        MIB,
        "weights",
    )
    all_bits = state_bits + [parts]
    all_groups = [all_bits[:1]] + [all_bits[k : k + 2] for k in range(1, len(all_bits), 2)]
    all_orders = stage_orders(all_groups)
    glu_rows = feats // (2 * parts)
    block_outs = lambda rows, width, orders: [
        ((len(o), rows, width), BF16 if k == 0 else F32) for k, o in enumerate(orders)
    ]
    states, slow, branch, d_glu, slope, *glu_parts = call(
        functools.partial(mix_kernel, parts, own, group, all_orders),
        [
            ((rows + SUB, 2 * channels), F32),
            ((rows, 2 * channels), BF16),
            ((rows, feats), F32),
            ((rows, 2 * feats), BF16),
            ((rows, feats), F32),
        ]
        + block_outs(glu_rows, 2 * feats, all_orders),
        [drive, end, cst, ends, cw, unit, cot, mask, vec, glu_weight],
        [pltpu.VMEM((rows, feats), BF16), pltpu.VMEM((feats, 2 * feats), F32)],
        20,
        5 * full,
        "mix",
    )
    d_pre, d_states, start, skip_sum, *out_parts = call(
        functools.partial(back_kernel, own, group, all_orders),
        [
            ((rows, feats), F32),
            ((rows, 2 * channels), F32),
            ((SUB, 2 * channels), F32),
            ((SUB, feats), F32),
        ]
        + block_outs(own, feats, all_orders),
        [d_glu, slope, unit, vec, glu_weight, cw, slow, cst],
        [pltpu.VMEM((rows, feats), BF16), pltpu.VMEM((2 * channels, feats), F32)],
        16,
        4 * full,
        "back",
    )
    got = swap(glu_parts, all_groups[0])
    starts = gather_ends(tie(start, got), state_bits)
    glu_parts = add_up(glu_parts, tie(got, start))
    out_parts = halve(out_parts, all_groups[0])
    both = [jnp.concatenate(p, axis=-1) for p in zip(glu_parts, out_parts)]
    state_groups = [[b] for b in state_bits]
    pair_orders = stage_orders(state_groups)
    d_proj, channel_sums, *in_parts = call(
        functools.partial(adjoint_kernel, own, group, pair_orders),
        [((rows, 2 * channels), BF16), ((SUB, 3 * channels), F32)]
        + block_outs(2 * own, feats, pair_orders),
        [tie(d_states, both), start, cst, starts, states, drive, low, mask],
        [pltpu.VMEM((rows, 2 * channels), F32), pltpu.VMEM((2 * channels, feats), F32)],
        16,
        2 * full,
        "adjoint",
    )
    in_parts = halve(in_parts, state_groups[0])
    d_normed, sums = call(
        normed_kernel,
        [((rows, feats), F32), ((SUB, feats), F32)],
        [d_proj, win, d_pre, unit, vec, channel_sums, skip_sum],
        [],
        12,
        full,
        "normed",
    )
    sent = []
    for g in state_groups[1:]:
        own_sums = two_parts(sums)
        sent.append(
            jnp.concatenate([in_parts[0].astype(BF16).reshape(-1, feats)] + own_sums, axis=0)
        )
        got = exchange(sent[-1], g[0])
        rest, off = [], 0
        for p in in_parts[1:]:
            n = p.shape[0] * p.shape[1]
            rest.append(p + got[off : off + n].reshape(p.shape).astype(F32))
            off += n
        in_parts = rest
        sums = sum_of(own_sums) + sum_of([got[off : off + SUB], got[off + SUB :]])
    total = in_parts[0][0]
    for m in seq_masks:
        low_total = rounded(total).astype(BF16)
        own_sums = two_parts(sums)
        sent.append(jnp.concatenate([low_total] + own_sums, axis=0))
        got = exchange(sent[-1], m)
        total = low_total.astype(F32) + got[: 2 * own].astype(F32)
        got_sums = [got[2 * own : 2 * own + SUB], got[2 * own + SUB :]]
        sums = sum_of(own_sums) + sum_of(got_sums)
    grad_in, feature_grads, grad_rate, grad_angle, grad_level = call(
        finish_kernel,
        [((own, 2, feats), F32), ((3, feats), F32)] + [((1, own), F32)] * 3,
        [low_total, got, sums, exchange(sums, state_bits[0]), vec],
        [flat],
        8,
        MIB,
        "finish",
    )

    for n, g in enumerate(all_groups[1:]):
        both = add_up(both, tie(swap(both, g), sent[0]))
    both = both[0][0]
    (grad4,) = call(
        tokens_kernel,
        [(cot4.shape, F32)],
        [cot4, tie(d_normed, both, sent[0]), unit, inv, vec],
        [held(cot4), pltpu.SemaphoreType.DMA((4,))],
        12,
        full,
        "tokens",
        fetched=(0,),
    )
    (out4,) = call(
        out_kernel,
        [(x4.shape, BF16)],
        [x4, tie(branch, both, sent[0])],
        [held(x4), pltpu.SemaphoreType.DMA((4,))],
        8,
        MIB,
        "out",
        fetched=(0,),
    )
    at = lambda k: sent[max(0, min(k, len(sent) - 1))]
    for n, m in enumerate(reversed(seq_masks[1:])):
        mine = tie(rounded(both).astype(BF16), at(2 * n - 1))
        got = tie(exchange(mine, m), at(2 * n + 1), grad4, out4)
        both = mine.astype(F32) + got.astype(F32)
    both = tie(rounded(both).astype(BF16), sent[-1])
    blocks = {0: both[:, : 2 * feats]}
    for g in reversed(all_groups[1:]):
        for m in list(blocks):
            for p in submasks(g):
                if m == 0 and p == parts:
                    got = exchange(both, p)
                    blocks[p] = got[:, : 2 * feats]
                    other_half = got[:, 2 * feats :]
                else:
                    blocks[m ^ p] = exchange(blocks[m], p)
    rest = [m for m in blocks if m]
    arrays = [blocks[0][None], jnp.stack([blocks[m] for m in rest])]
    masks = [[0], rest]
    for p in submasks(all_groups[0]):
        arrays += [exchange(a, p) for a in arrays[:2]]
        masks += [[m ^ p for m in ms] for ms in masks[:2]]
    (grad_out,) = call(
        halves_kernel,
        [((own, 2, feats), F32)],
        [both[:, 2 * feats :], other_half],
        [flat],
        8,
        MIB,
        "halves",
    )
    (grad_glu,) = call(
        functools.partial(place_kernel, masks, parts),
        [((feats, 2 * feats), F32)],
        arrays,
        [],
        8,
        feats * feats,
        "place",
    )
    return (
        out4.reshape(tokens.shape),
        grad4.reshape(tokens.shape),
        feature_grads[0],
        feature_grads[1],
        grad_in.transpose(2, 0, 1),
        grad_out,
        grad_rate.reshape(own),
        grad_angle.reshape(own),
        grad_level.reshape(own),
        feature_grads[2],
        grad_glu,
    )


def solution(mesh):
    placed = (
        P("state", "seq", None),
        P(),
        P(),
        P(None, "state", None),
        P("state", None, None),
        P("state"),
        P("state"),
        P("state"),
        P(),
        P(),
        P("seq"),
        P("state", "seq", None),
    )
    return jax.shard_map(
        shards,
        mesh=mesh,
        in_specs=placed,
        out_specs=(
            P("state", "seq", None),
            P("state", "seq", None),
            P(),
            P(),
            P(None, "state", None),
            P("state", None, None),
            P("state"),
            P("state"),
            P("state"),
            P(),
            P(),
        ),
        check_vma=False,
    )
```

```python
import functools

import jax
import jax.numpy as jnp
from jax import lax
from jax.experimental import pallas as pl
from jax.experimental.pallas import tpu as pltpu
from jax.sharding import PartitionSpec as P

F32, BF16 = jnp.float32, jnp.bfloat16
EPSILON = 1e-05
SUB = 8
CHUNK = 256
PARAM_ROWS = 16
GELU_A = 0.7978845608028654
GELU_B = 0.044715
MIB = 1 << 20


def repeat(first, last, body, carry):
    for k in range(first, last):
        carry = body(k, carry)
    return carry


def cmul(ar, ai, br, bi):
    return ar * br - ai * bi, ar * bi + ai * br


def nn(a, b):
    return lax.dot_general(a, b, (((1,), (0,)), ((), ())), preferred_element_type=F32)


def nt(a, b):
    return lax.dot_general(a, b, (((1,), (1,)), ((), ())), preferred_element_type=F32)


def tn(a, b):
    return lax.dot_general(a, b, (((0,), (0,)), ((), ())), preferred_element_type=F32)


def rows_in(ref, first, count):
    segs, _, group, feats = ref.shape
    x = ref[:, pl.ds(first, count)].astype(F32)
    return x.transpose(1, 0, 2, 3).reshape(count * segs * group, feats)


def rows_out(y, ref):
    segs, _, group, feats = ref.shape
    return y.reshape(y.shape[0] // SUB, segs, group, feats).transpose(1, 0, 2, 3)


def row_mask(base, rows, group, steps, me, lengths):
    segs = SUB // group
    row = lax.broadcasted_iota(jnp.int32, (rows, 128), 0) + base
    place = row & (SUB - 1)
    seq = place & (group - 1)
    position = (me * (segs * steps) + (place // group) * steps + (row // SUB)).astype(F32)
    length = jnp.broadcast_to(lengths[:, 0:1], (rows, 128))
    for k in range(1, group):
        length = jnp.where(seq == k, lengths[:, k : k + 1], length)
    return (position < length).astype(F32)


def wide(column, lanes):
    return jnp.concatenate([column] * (lanes // column.shape[1]), axis=1)


def call(body, outs, ins, scratch, limit_mib, flops, name, fetched=()):
    specs = []
    for k, x in enumerate(ins):
        space = pltpu.SMEM if x.dtype == jnp.int32 else pltpu.HBM if k in fetched else pltpu.VMEM
        specs.append(pl.BlockSpec(memory_space=space))
    return pl.pallas_call(
        body,
        out_shape=[jax.ShapeDtypeStruct(s, d) for s, d in outs],
        in_specs=specs,
        out_specs=[pl.BlockSpec(memory_space=pltpu.VMEM)] * len(outs),
        scratch_shapes=scratch,
        compiler_params=pltpu.CompilerParams(vmem_limit_bytes=limit_mib * MIB),
        cost_estimate=pl.CostEstimate(flops=flops, bytes_accessed=4 * MIB, transcendentals=0),
        name=name,
    )(*ins)


def start_copies(sources, targets, sems):
    copies = [pltpu.make_async_copy(a, b, sems.at[k]) for k, (a, b) in enumerate(zip(sources, targets))]
    for c in copies:
        c.start()
    return copies


def held(x):
    return pltpu.VMEM(x.shape, x.dtype)


def split_pairs(pairs_ref, flat_ref):
    own, _, feats = pairs_ref.shape
    flat = pairs_ref[...].astype(F32).reshape(2 * own, feats)
    for c in range(feats // 128):
        flat_ref[c] = flat[:, c * 128 : (c + 1) * 128]
    take = lambda k: [flat_ref[c, pl.ds(k, own, stride=2), :] for c in range(feats // 128)]
    return [jnp.concatenate(take(k), axis=1).astype(BF16) for k in range(2)]


def three_parts(x):
    high = x.astype(BF16)
    rest = x - high.astype(F32)
    mid = rest.astype(BF16)
    return [high, mid, (rest - mid.astype(F32)).astype(BF16)]


def prep_kernel(own, group, small_ref, pay_ref, vec_ref):
    feats = vec_ref.shape[1]
    me = lax.axis_index("state")
    lane = lax.broadcasted_iota(jnp.int32, (1, feats), 1)
    mine = (lane // own) == me
    base = 3 * feats
    logs = [small_ref[:, base + k * own : base + (k + 1) * own] for k in range(3)]
    rate, turn, level = (jnp.concatenate([v] * (feats // own), axis=1) for v in logs)
    decay = jnp.exp(rate)
    size = jnp.exp(-decay)
    angle = jnp.exp(turn)
    pole_re, pole_im = size * jnp.cos(angle), size * jnp.sin(angle)
    parts = []
    for v in (pole_re, pole_im, jnp.exp(level)):
        parts += three_parts(jnp.where(mine, v, 0.0))
    parts += [jnp.zeros((PARAM_ROWS - len(parts), feats), BF16)]
    flat = jnp.concatenate([p.astype(F32) for p in parts], axis=0)
    pay_ref[...] = flat.reshape(PARAM_ROWS // 2, 2, feats).astype(BF16)
    rows = [small_ref[:, k * feats : (k + 1) * feats] for k in range(3)] + [pole_re, pole_im, decay, angle]
    for k, row in enumerate(rows):
        vec_ref[k : k + 1, :] = row
    base += 3 * own
    vec_ref[len(rows) :, :] = jnp.zeros((SUB - len(rows), feats), F32)
    vec_ref[7:8, :group] = small_ref[:, base : base + group]


def cotangent_kernel(cot_ref, rows_ref):
    steps = 16
    for c in range(cot_ref.shape[1] // steps):
        at = pl.ds(c * steps * SUB, steps * SUB)
        rows_ref[at, :] = rows_in(cot_ref, c * steps, steps).astype(BF16)


def weights_kernel(*refs):
    blocks, (out_ref, flat_ref) = refs[:-2], refs[-2:]
    gather_rows(lax.axis_index("state"), blocks, flat_ref, out_ref)


def norm_kernel(x_ref, vec_ref, low_ref, unit_ref, inv_ref, mask_ref):
    segs, steps, group, feats = x_ref.shape
    rows = steps * SUB
    me = lax.axis_index("state")
    size = 128
    gain, bias = vec_ref[0:1, :], vec_ref[1:2, :]

    def chunk(c, carry):
        base = c * size
        at = pl.ds(base, size)
        x = rows_in(x_ref, c * (size // SUB), size // SUB)
        centred = x - jnp.mean(x, axis=1, keepdims=True)
        inv = lax.rsqrt(jnp.mean(centred * centred, axis=1, keepdims=True) + EPSILON)
        unit = centred * inv
        unit_ref[at, :] = unit
        low_ref[at, :] = (unit * gain + bias).astype(BF16)
        inv_ref[at, :] = jnp.broadcast_to(inv, (size, 128))
        mask_ref[at, :] = row_mask(base, size, group, steps, me, vec_ref[7:8, :])
        return carry

    repeat(0, rows // size, chunk, 0)


def gather_rows(me, blocks, flat_ref, dst_ref):
    own = flat_ref.shape[1] // 2
    channels = own * len(blocks)
    for m, block in enumerate(blocks):
        for k, part in enumerate(split_pairs(block.at[0:own], flat_ref)):
            at = pl.multiple_of(k * channels + (me ^ m) * own, own)
            dst_ref[pl.ds(at, own), :] = part


def seg_of(group):
    row = lax.broadcasted_iota(jnp.int32, (SUB, 128), 0)
    return row // group


def shift_rows(x, by, keep):
    return jnp.where(wide(keep, x.shape[1]), pltpu.roll(x, by % SUB, 0), 0.0)


def seg_prefix(xr, xi, qr, qi, group, forward):
    seg = seg_of(group)
    segs = SUB // group
    dist = 1
    while dist < segs:
        by = group * dist if forward else SUB - group * dist
        keep = seg >= dist if forward else seg < segs - dist
        sr, si = shift_rows(xr, by, keep), shift_rows(xi, by, keep)
        ar, ai = cmul(qr, qi, sr, si)
        xr, xi = xr + ar, xi + ai
        qr, qi = cmul(qr, qi, qr, qi)
        dist *= 2
    return xr, xi


def seg_enter(xr, xi, qr, qi, dr, di, group, forward):
    seg = seg_of(group)
    segs = SUB // group
    by = group if forward else SUB - group
    keep = seg >= 1 if forward else seg < segs - 1
    er, ei = shift_rows(xr, by, keep), shift_rows(xi, by, keep)
    gap = seg if forward else segs - 1 - seg
    pr, pi = jnp.ones_like(er), jnp.zeros_like(ei)
    bit = 1
    while bit < segs:
        nr, ni = cmul(pr, pi, qr, qi)
        take = wide((gap & bit) != 0, er.shape[1])
        pr, pi = jnp.where(take, nr, pr), jnp.where(take, ni, pi)
        qr, qi = cmul(qr, qi, qr, qi)
        bit *= 2
    ar, ai = cmul(pr, pi, dr, di)
    return er + ar, ei + ai


def device_entry(ends_ref, me, channels, qr, qi, group, forward):
    seg = seg_of(group)
    segs = SUB // group
    parts = ends_ref.shape[0]
    keep = wide(seg == (segs - 1 if forward else 0), channels)
    tr = ti = jnp.zeros((SUB, channels), F32)
    for device in range(parts - 1) if forward else range(parts - 1, 0, -1):
        end = ends_ref[me ^ device]
        nr, ni = cmul(tr, ti, qr, qi)
        counts = device < me if forward else device > me
        tr = jnp.where(counts, nr + end[:, :channels], tr)
        ti = jnp.where(counts, ni + end[:, channels:], ti)
    out = []
    for x in (tr, ti):
        x = jnp.where(keep, x, 0.0)
        y = x
        for k in range(1, segs):
            y = y + pltpu.roll(x, group * k, 0)
        out.append(y)
    return out


def project_kernel(parts, own, group, low_ref, mask_ref, *refs):
    blocks = refs[:parts]
    drive_ref, end_ref, win_ref, cst_ref, flat_ref = refs[parts:]
    rows = low_ref.shape[0]
    channels = own * parts
    steps = rows // SUB
    me = lax.axis_index("state")
    gather_rows(me, blocks, flat_ref, win_ref)
    rows_of = []
    for k in range(3):
        total = None
        for block in blocks:
            tile = block[own : own + PARAM_ROWS // 2].astype(F32).reshape(PARAM_ROWS, -1)
            for part in range(3):
                piece = tile[3 * k + part : 3 * k + part + 1, :channels]
                total = piece if total is None else total + piece
        rows_of.append(total)
    pr, pi, gain = rows_of
    powers = [(pr, pi)]
    span = steps * (SUB // group)
    ar, ai = pr, pi
    count = 1
    while count < span:
        ar, ai = cmul(ar, ai, ar, ai)
        count *= 2
        if count in (steps, span):
            powers.append((ar, ai))
    while len(powers) < 3:
        powers.append(powers[-1])
    for k, (r, i) in enumerate(powers):
        cst_ref[k : k + 1, :] = jnp.concatenate([r, i], axis=1)
    gains = jnp.concatenate([gain, gain], axis=1)
    cst_ref[3:4, :] = gains
    cst_ref[4:8, :] = jnp.zeros((4, 2 * channels), F32)

    def chunk(c, carry):
        base = c * CHUNK
        at = pl.ds(base, CHUNK)
        mask = mask_ref[at, :]
        drive_ref[at, :] = nt(low_ref[at, :], win_ref[...]) * (gains * wide(mask, 2 * channels))
        return carry

    repeat(0, rows // CHUNK, chunk, 0)
    br = jnp.broadcast_to(pr, (SUB, channels))
    bi = jnp.broadcast_to(pi, (SUB, channels))

    def step(j, h):
        u = drive_ref[pl.ds(pl.multiple_of(j * SUB, SUB), SUB), :]
        nr, ni = cmul(br, bi, h[0], h[1])
        return nr + u[:, :channels], ni + u[:, channels:]

    zero = jnp.zeros((SUB, channels), F32)
    er, ei = lax.fori_loop(0, steps, step, (zero, zero), unroll=8)
    er, ei = seg_prefix(er, ei, *powers[1], group, True)
    end_ref[...] = jnp.concatenate([er, ei], axis=1)


def mix_kernel(parts, own, group, orders, *refs):
    it = iter(refs)
    take = lambda n: [next(it) for _ in range(n)]
    drive_ref, end_ref, cst_ref, ends_ref = take(4)
    cw_ref, unit_ref, cot_ref, mask_ref, vec_ref, glu_ref = take(6)
    states_ref, slow_ref, branch_ref, dglu_ref, gp_ref = take(5)
    grads = take(len(orders))
    act_ref, acc_ref = take(2)
    rows, feats = unit_ref.shape
    channels = own * parts
    steps = rows // SUB
    me = lax.axis_index("state")
    place = me + parts * (lax.axis_index("seq") & 1)
    gain, bias, skip = (vec_ref[k : k + 1, :] for k in range(3))
    pr, pi = cst_ref[0:1, :channels], cst_ref[0:1, channels:]
    qr, qi = cst_ref[1:2, :channels], cst_ref[1:2, channels:]
    wr, wi = cst_ref[2:3, :channels], cst_ref[2:3, channels:]
    dr, di = device_entry(ends_ref, me, channels, wr, wi, group, True)
    hr, hi = seg_enter(end_ref[:, :channels], end_ref[:, channels:], qr, qi, dr, di, group, True)
    states_ref[0:SUB, :] = jnp.concatenate([hr, hi], axis=1)
    br = jnp.broadcast_to(pr, (SUB, channels))
    bi = jnp.broadcast_to(pi, (SUB, channels))

    def step(j, h):
        base = pl.multiple_of(j * SUB, SUB)
        u = drive_ref[pl.ds(base, SUB), :]
        nr, ni = cmul(br, bi, h[0], h[1])
        nr, ni = nr + u[:, :channels], ni + u[:, channels:]
        at = pl.ds(pl.multiple_of(base + SUB, SUB), SUB)
        states_ref[at, :channels] = nr
        states_ref[at, channels:] = ni
        return nr, ni

    lax.fori_loop(0, steps, step, (hr, hi), unroll=8)

    def chunk(c, carry):
        base = c * CHUNK
        at = pl.ds(base, CHUNK)
        states = states_ref[pl.ds(pl.multiple_of(base + SUB, SUB), CHUNK), :]
        slow = jnp.concatenate([states[:, :channels], -states[:, channels:]], axis=1).astype(BF16)
        slow_ref[at, :] = slow
        normed = unit_ref[at, :] * gain + bias
        v = nn(slow, cw_ref[...]) + skip * normed
        t = jnp.tanh(GELU_A * (v + GELU_B * (v * v * v)))
        half = 0.5 * (1.0 + t)
        gp_ref[at, :] = half + (0.5 * GELU_A) * v * (1.0 - t * t) * (1.0 + (3.0 * GELU_B) * (v * v))
        act = (v * half).astype(BF16)
        act_ref[at, :] = act
        glu = nn(act, glu_ref[...])
        mask = wide(mask_ref[at, :], feats)
        value = glu[:, :feats]
        gate = jax.nn.sigmoid(glu[:, feats:])
        branch = mask * gate
        branch_ref[at, :] = branch * value
        d_value = branch * cot_ref[at, :].astype(F32)
        dglu_ref[at, :feats] = d_value.astype(BF16)
        dglu_ref[at, feats:] = (d_value * value * (1.0 - gate)).astype(BF16)
        return carry

    repeat(0, rows // CHUNK, chunk, 0)
    width = 256

    def tile(c, carry):
        at = pl.ds(c * width, width)
        acc_ref[:, at] = tn(act_ref[...], dglu_ref[:, at])
        return carry

    repeat(0, 2 * feats // width, tile, 0)
    spread(acc_ref, place, orders, grads)


def spread(acc_ref, place, orders, grads):
    for order, ref in zip(orders, grads):
        _, size, _ = ref.shape
        for k, m in enumerate(order):
            at = pl.ds(pl.multiple_of((place ^ m) * size, size), size)
            ref[k] = acc_ref[at, :].astype(ref.dtype)


def spread_pairs(acc_ref, place, own, channels, orders, grads):
    for order, ref in zip(orders, grads):
        for k, m in enumerate(order):
            off = pl.multiple_of((place ^ m) * own, own)
            ref[k, 0:own] = acc_ref[pl.ds(off, own), :].astype(ref.dtype)
            also = pl.ds(pl.multiple_of(channels + off, own), own)
            ref[k, own : 2 * own] = acc_ref[also, :].astype(ref.dtype)


def back_kernel(own, group, orders, *refs):
    it = iter(refs)
    take = lambda n: [next(it) for _ in range(n)]
    dglu_ref, gp_ref, unit_ref, vec_ref, glu_ref, cw_ref, slow_ref, cst_ref = take(8)
    dpre_ref, dst_ref, start_ref, skip_ref = take(4)
    grads = take(len(orders))
    dmix_ref, acc_ref = take(2)
    rows, feats = gp_ref.shape
    channels = cw_ref.shape[0] // 2
    steps = rows // SUB
    place = lax.axis_index("state") + lax.axis_size("state") * (lax.axis_index("seq") & 1)
    gain, bias = vec_ref[0:1, :], vec_ref[1:2, :]

    def chunk(c, total):
        at = pl.ds(c * CHUNK, CHUNK)
        d_pre = nt(dglu_ref[at, :], glu_ref[...]) * gp_ref[at, :]
        dpre_ref[at, :] = d_pre
        normed = unit_ref[at, :] * gain + bias
        total = total + jnp.sum((d_pre * normed).reshape(CHUNK // SUB, SUB, feats), axis=0)
        d_mixed = d_pre.astype(BF16)
        dmix_ref[at, :] = d_mixed
        dst_ref[at, :] = nt(d_mixed, cw_ref[...])
        return total

    total = repeat(0, rows // CHUNK, chunk, jnp.zeros((SUB, feats), F32))
    skip_ref[...] = total
    pr, pi = cst_ref[0:1, :channels], cst_ref[0:1, channels:]
    br = jnp.broadcast_to(pr, (SUB, channels))
    bi = jnp.broadcast_to(-pi, (SUB, channels))

    def step(k, a):
        base = pl.multiple_of((steps - 1 - k) * SUB, SUB)
        u = dst_ref[pl.ds(base, SUB), :]
        nr, ni = cmul(br, bi, a[0], a[1])
        return nr + u[:, :channels], ni - u[:, channels:]

    zero = jnp.zeros((SUB, channels), F32)
    ar, ai = lax.fori_loop(0, steps, step, (zero, zero), unroll=8)
    qr, qi = cst_ref[1:2, :channels], -cst_ref[1:2, channels:]
    ar, ai = seg_prefix(ar, ai, qr, qi, group, False)
    start_ref[...] = jnp.concatenate([ar, ai], axis=1)
    width = 256

    def tile(c, carry):
        at = pl.ds(c * width, width)
        acc_ref[:, at] = tn(slow_ref[...], dmix_ref[:, at])
        return carry

    repeat(0, feats // width, tile, 0)
    spread(acc_ref, place, orders, grads)


def adjoint_kernel(own, group, orders, *refs):
    it = iter(refs)
    take = lambda n: [next(it) for _ in range(n)]
    dst_ref, start_ref, cst_ref, ends_ref = take(4)
    states_ref, drive_ref, low_ref, mask_ref = take(4)
    dproj_ref, sums_ref = take(2)
    grads = take(len(orders))
    adj_ref, acc_ref = take(2)
    rows = dst_ref.shape[0]
    channels = dst_ref.shape[1] // 2
    steps = rows // SUB
    me = lax.axis_index("state")
    pr, pi = cst_ref[0:1, :channels], -cst_ref[0:1, channels:]
    qr, qi = cst_ref[1:2, :channels], -cst_ref[1:2, channels:]
    wr, wi = cst_ref[2:3, :channels], -cst_ref[2:3, channels:]
    dr, di = device_entry(ends_ref, me, channels, wr, wi, group, False)
    ar, ai = seg_enter(start_ref[:, :channels], start_ref[:, channels:], qr, qi, dr, di, group, False)
    br = jnp.broadcast_to(pr, (SUB, channels))
    bi = jnp.broadcast_to(pi, (SUB, channels))

    def step(k, carry):
        ar, ai, sr, si, sg = carry
        base = pl.multiple_of((steps - 1 - k) * SUB, SUB)
        at = pl.ds(base, SUB)
        d = dst_ref[at, :]
        nr, ni = cmul(br, bi, ar, ai)
        ar, ai = nr + d[:, :channels], ni - d[:, channels:]
        adj_ref[at, :channels] = ar
        adj_ref[at, channels:] = ai
        h = states_ref[at, :]
        hr, hi = h[:, :channels], h[:, channels:]
        u = drive_ref[at, :]
        sr = sr + (ar * hr + ai * hi)
        si = si + (ai * hr - ar * hi)
        sg = sg + (ar * u[:, :channels] + ai * u[:, channels:])
        return ar, ai, sr, si, sg

    zero = jnp.zeros((SUB, channels), F32)
    out = lax.fori_loop(0, steps, step, (ar, ai, zero, zero, zero), unroll=4)
    sums_ref[:, :channels] = out[2]
    sums_ref[:, channels : 2 * channels] = out[3]
    sums_ref[:, 2 * channels : 3 * channels] = out[4]
    gains = cst_ref[3:4, :]

    def chunk(c, carry):
        base = c * CHUNK
        at = pl.ds(base, CHUNK)
        mask = mask_ref[at, :]
        dproj_ref[at, :] = (adj_ref[at, :] * (gains * wide(mask, 2 * channels))).astype(BF16)
        return carry

    repeat(0, rows // CHUNK, chunk, 0)
    width = 256
    feats = low_ref.shape[1]

    def tile(c, carry):
        at = pl.ds(c * width, width)
        acc_ref[:, at] = tn(dproj_ref[...], low_ref[:, at])
        return carry

    repeat(0, feats // width, tile, 0)
    spread_pairs(acc_ref, me, own, channels, orders, grads)


def out_kernel(x_hbm, branch_ref, out_ref, x_ref, sems):
    segs, steps, _, _ = x_ref.shape
    size = 16
    cut = steps // 4
    places = [pl.ds(k * cut, cut) for k in range(4)]
    copies = start_copies([x_hbm.at[:, p] for p in places], [x_ref.at[:, p] for p in places], sems)

    def chunk(c, carry):
        first = c * size
        rows = branch_ref[pl.ds(pl.multiple_of(first * SUB, size * SUB), size * SUB), :]
        at = pl.ds(first, size)
        out_ref[:, at] = (x_ref[:, at].astype(F32) + rows_out(rows, x_ref)).astype(BF16)
        return carry

    for k in range(4):
        copies[k].wait()
        repeat(k * cut // size, (k + 1) * cut // size, chunk, 0)


def normed_kernel(dproj_ref, win_ref, dpre_ref, unit_ref, vec_ref, channel_ref, skip_ref, dnorm_ref, sums_ref):
    rows, feats = dpre_ref.shape
    skip = vec_ref[2:3, :]

    def chunk(c, carry):
        total_gain, total_bias = carry
        at = pl.ds(c * CHUNK, CHUNK)
        d_normed = dpre_ref[at, :] * skip + nn(dproj_ref[at, :], win_ref[...])
        dnorm_ref[at, :] = d_normed
        folded = lambda v: jnp.sum(v.reshape(CHUNK // SUB, SUB, feats), axis=0)
        return total_gain + folded(d_normed * unit_ref[at, :]), total_bias + folded(d_normed)

    zero = jnp.zeros((SUB, feats), F32)
    total_gain, total_bias = repeat(0, rows // CHUNK, chunk, (zero, zero))
    over = lambda v: jnp.sum(v, axis=0, keepdims=True)
    channel = over(channel_ref[...])
    wide_at = channel.shape[1] - feats
    sums_ref[0:1, :] = channel[:, :feats]
    sums_ref[1:2, :] = jnp.zeros((1, feats), F32)
    sums_ref[1:2, :wide_at] = channel[:, feats:]
    sums_ref[2:3, :] = over(total_gain)
    sums_ref[3:4, :] = over(total_bias)
    sums_ref[4:5, :] = over(skip_ref[...])
    sums_ref[5:8, :] = jnp.zeros((3, feats), F32)


def tokens_kernel(cot_hbm, dnorm_ref, unit_ref, inv_ref, vec_ref, out_ref, cot_ref, sems):
    rows, feats = dnorm_ref.shape
    gain = vec_ref[0:1, :]
    size = 128
    steps = size // SUB
    cut = cot_ref.shape[1] // 4
    places = [pl.ds(k * cut, cut) for k in range(4)]
    copies = start_copies([cot_hbm.at[:, p] for p in places], [cot_ref.at[:, p] for p in places], sems)

    def chunk(c, carry):
        at = pl.ds(c * size, size)
        unit = unit_ref[at, :]
        d_unit = dnorm_ref[at, :] * gain
        first = jnp.mean(d_unit, axis=1, keepdims=True)
        second = jnp.mean(d_unit * unit, axis=1, keepdims=True)
        rows = wide(inv_ref[at, :], feats) * (d_unit - first - unit * second)
        step_at = pl.ds(c * steps, steps)
        out_ref[:, step_at] = cot_ref[:, step_at].astype(F32) + rows_out(rows, cot_ref)
        return carry

    for k in range(4):
        copies[k].wait()
        repeat(k * cut // steps, (k + 1) * cut // steps, chunk, 0)


def join_pairs(parts, flat_ref, out_ref):
    own, _, feats = out_ref.shape
    for k, part in enumerate(parts):
        for c in range(feats // 128):
            flat_ref[c, pl.ds(k, own, stride=2), :] = part[:, c * 128 : (c + 1) * 128]
    rows = jnp.concatenate([flat_ref[c] for c in range(feats // 128)], axis=1)
    out_ref[...] = rows.reshape(own, 2, feats)


def halves_kernel(mine_ref, other_ref, out_ref, flat_ref):
    own = out_ref.shape[0]
    first = (lax.axis_index("seq") & 1) == 0
    a, b = mine_ref[...].astype(F32), other_ref[...].astype(F32)
    join_pairs([jnp.where(first, a, b), jnp.where(first, b, a)], flat_ref, out_ref)


def finish_kernel(low_ref, got_ref, sums_ref, more_ref, vec_ref, in_ref, feat_ref, rate_ref, angle_ref, level_ref, flat_ref):
    own, _, feats = in_ref.shape
    total = low_ref[...].astype(F32) + got_ref[0 : 2 * own, :].astype(F32)
    join_pairs([total[:own, :], total[own:, :]], flat_ref, in_ref)
    sums = sums_ref[...] + more_ref[...]
    feat_ref[...] = sums[2:5, :]
    me = lax.axis_index("state")
    channels = lax.axis_size("state") * own
    pick = lambda row: sum(
        jnp.where(me == d, row[:, d * own : (d + 1) * own], 0.0) for d in range(channels // own)
    )
    sum_re, sum_im = pick(sums[0:1, :channels]), pick(sums[0:1, channels:])
    pole_re, pole_im, decay, angle = (vec_ref[k : k + 1, :own] for k in range(3, 7))
    rate_ref[...] = -decay * (sum_re * pole_re + sum_im * pole_im)
    angle_ref[...] = angle * (sum_im * pole_re - sum_re * pole_im)
    level_ref[...] = pick(sums[1:2, :channels])


def place_kernel(masks, parts, *refs):
    arrays, out_ref = refs[:-1], refs[-1]
    place = lax.axis_index("state") + parts * (lax.axis_index("seq") & 1)
    size = arrays[0].shape[1]
    for ms, ref in zip(masks, arrays):
        for k, m in enumerate(ms):
            at = pl.ds(pl.multiple_of((place ^ m) * size, size), size)
            out_ref[at, :] = ref[k].astype(F32)


def exchange(x, mask):
    count = lax.axis_size("seq") * lax.axis_size("state")
    return lax.ppermute(x, ("seq", "state"), [(i, i ^ mask) for i in range(count)])


def tie(x, *after):
    return lax.optimization_barrier((x, after))[0]


def bits_of(n):
    return [1 << k for k in range(n.bit_length() - 1)]


def submasks(group):
    out = [0]
    for bit in group:
        out += [m | bit for m in out]
    return out[1:]


def stage_orders(groups):
    kept = [0]
    stages = []
    for group in reversed(groups):
        sends = [[m ^ p for m in kept] for p in submasks(group)]
        stages.insert(0, sends)
        kept = sum(sends, []) + kept
    return [o for sends in stages for o in sends] + [[0]]


def swap(parts, group):
    masks = submasks(group)
    return [exchange(p.astype(BF16), m) for p, m in zip(parts, masks)]


def add_up(parts, got):
    rest, off = [], 0
    for p in parts[len(got) :]:
        n = p.shape[0]
        total = p.astype(F32)
        for g in got:
            total = total + g[off : off + n].astype(F32)
        rest.append(total)
        off += n
    return rest


def halve(parts, group):
    return add_up(parts, swap(parts, group))


def rounded(x):
    return lax.reduce_precision(x, 8, 7)


def two_parts(x):
    high = rounded(x)
    return [high.astype(BF16), rounded(x - high).astype(BF16)]


def sum_of(parts):
    return parts[0].astype(F32) + parts[1].astype(F32)


def gather_ends(end, bits):
    g = end[None]
    for bit in reversed(bits):
        g = jnp.stack([g, exchange(g, bit)], axis=1).reshape((2 * g.shape[0],) + end.shape)
    return g


def gather_blocks(arrays, bits, ready=None):
    blocks = [{0: a} for a in arrays]
    for n, bit in enumerate(reversed(bits)):
        for held_blocks in blocks:
            for m in list(held_blocks):
                x = held_blocks[m]
                if m and n and ready is not None:
                    x = tie(x, ready)
                held_blocks[m ^ bit] = exchange(x, bit)
    return [[b[m] for m in range(len(b))] for b in blocks]


def shards(
    tokens,
    norm_gain,
    norm_bias,
    input_weight,
    output_weight,
    log_rate,
    log_angle,
    log_gain,
    skip_gain,
    glu_weight,
    lengths,
    cotangent,
):
    span, group, feats = tokens.shape
    own = log_rate.shape[0]
    parts = lax.axis_size("state")
    n_seq = lax.axis_size("seq")
    channels = own * parts
    rows = span * group
    segs = SUB // group
    me = lax.axis_index("state")
    state_bits = bits_of(parts)
    seq_masks = [parts * b for b in bits_of(n_seq)]
    if len(seq_masks) > 2:
        seq_masks[-1] |= seq_masks[-2]
    full = rows * feats * 2 * channels * 2

    flat = pltpu.VMEM((feats // 128, 2 * own, 128), F32)
    x4 = tokens.reshape(segs, span // segs, group, feats)
    cot4 = cotangent.reshape(segs, span // segs, group, feats)
    small = jnp.concatenate(
        [norm_gain, norm_bias, skip_gain, log_rate, log_angle, log_gain, lengths.astype(F32)]
    )
    small = jnp.pad(small, (0, -small.shape[0] % 128)).reshape(1, -1)
    small_own, vec = call(
        functools.partial(prep_kernel, own, group),
        [((PARAM_ROWS // 2, 2, feats), BF16), ((SUB, feats), F32)],
        [small],
        [],
        8,
        MIB,
        "prep",
    )
    b_own = jnp.concatenate([input_weight.transpose(1, 2, 0), small_own], axis=0)
    low, unit, inv, mask = call(
        norm_kernel,
        [((rows, feats), BF16), ((rows, feats), F32), ((rows, 128), F32), ((rows, 128), F32)],
        [x4, vec],
        [],
        12,
        rows * feats * 20,
        "norm",
    )
    b_blocks, c_blocks = gather_blocks([b_own, tie(output_weight, b_own)], state_bits, low)
    drive, end, win, cst = call(
        functools.partial(project_kernel, parts, own, group),
        [
            ((rows, 2 * channels), F32),
            ((SUB, 2 * channels), F32),
            ((2 * channels, feats), BF16),
            ((SUB, 2 * channels), F32),
        ],
        [low, mask] + b_blocks,
        [flat],
        12,
        full,
        "project",
    )
    ends = gather_ends(end, state_bits)
    (cot,) = call(cotangent_kernel, [((rows, feats), BF16)], [tie(cot4, end)], [], 8, MIB, "cotangent")
    (cw,) = call(
        weights_kernel,
        [((2 * channels, feats), BF16)],
        [tie(c_blocks[0], end)] + c_blocks[1:],
        [flat],
        8,
        MIB,
        "weights",
    )
    all_bits = state_bits + [parts]
    all_groups = [all_bits[:1]] + [all_bits[k : k + 2] for k in range(1, len(all_bits), 2)]
    all_orders = stage_orders(all_groups)
    glu_rows = feats // (2 * parts)
    block_outs = lambda rows, width, orders: [
        ((len(o), rows, width), BF16 if k == 0 else F32) for k, o in enumerate(orders)
    ]
    states, slow, branch, d_glu, slope, *glu_parts = call(
        functools.partial(mix_kernel, parts, own, group, all_orders),
        [
            ((rows + SUB, 2 * channels), F32),
            ((rows, 2 * channels), BF16),
            ((rows, feats), F32),
            ((rows, 2 * feats), BF16),
            ((rows, feats), F32),
        ]
        + block_outs(glu_rows, 2 * feats, all_orders),
        [drive, end, cst, ends, cw, unit, cot, mask, vec, glu_weight],
        [pltpu.VMEM((rows, feats), BF16), pltpu.VMEM((feats, 2 * feats), F32)],
        20,
        5 * full,
        "mix",
    )
    d_pre, d_states, start, skip_sum, *out_parts = call(
        functools.partial(back_kernel, own, group, all_orders),
        [
            ((rows, feats), F32),
            ((rows, 2 * channels), F32),
            ((SUB, 2 * channels), F32),
            ((SUB, feats), F32),
        ]
        + block_outs(own, feats, all_orders),
        [d_glu, slope, unit, vec, glu_weight, cw, slow, cst],
        [pltpu.VMEM((rows, feats), BF16), pltpu.VMEM((2 * channels, feats), F32)],
        16,
        4 * full,
        "back",
    )
    got = swap(glu_parts, all_groups[0])
    starts = gather_ends(tie(start, got), state_bits)
    glu_parts = add_up(glu_parts, tie(got, start))
    out_parts = halve(out_parts, all_groups[0])
    both = [jnp.concatenate(p, axis=-1) for p in zip(glu_parts, out_parts)]
    state_groups = [[b] for b in state_bits]
    pair_orders = stage_orders(state_groups)
    d_proj, channel_sums, *in_parts = call(
        functools.partial(adjoint_kernel, own, group, pair_orders),
        [((rows, 2 * channels), BF16), ((SUB, 3 * channels), F32)]
        + block_outs(2 * own, feats, pair_orders),
        [tie(d_states, both), start, cst, starts, states, drive, low, mask],
        [pltpu.VMEM((rows, 2 * channels), F32), pltpu.VMEM((2 * channels, feats), F32)],
        16,
        2 * full,
        "adjoint",
    )
    in_parts = halve(in_parts, state_groups[0])
    d_normed, sums = call(
        normed_kernel,
        [((rows, feats), F32), ((SUB, feats), F32)],
        [d_proj, win, d_pre, unit, vec, channel_sums, skip_sum],
        [],
        12,
        full,
        "normed",
    )
    sent = []
    for g in state_groups[1:]:
        own_sums = two_parts(sums)
        sent.append(
            jnp.concatenate([in_parts[0].astype(BF16).reshape(-1, feats)] + own_sums, axis=0)
        )
        got = exchange(sent[-1], g[0])
        rest, off = [], 0
        for p in in_parts[1:]:
            n = p.shape[0] * p.shape[1]
            rest.append(p + got[off : off + n].reshape(p.shape).astype(F32))
            off += n
        in_parts = rest
        sums = sum_of(own_sums) + sum_of([got[off : off + SUB], got[off + SUB :]])
    total = in_parts[0][0]
    for m in seq_masks:
        low_total = rounded(total).astype(BF16)
        own_sums = two_parts(sums)
        sent.append(jnp.concatenate([low_total] + own_sums, axis=0))
        got = exchange(sent[-1], m)
        total = low_total.astype(F32) + got[: 2 * own].astype(F32)
        got_sums = [got[2 * own : 2 * own + SUB], got[2 * own + SUB :]]
        sums = sum_of(own_sums) + sum_of(got_sums)
    grad_in, feature_grads, grad_rate, grad_angle, grad_level = call(
        finish_kernel,
        [((own, 2, feats), F32), ((3, feats), F32)] + [((1, own), F32)] * 3,
        [low_total, got, sums, exchange(sums, state_bits[0]), vec],
        [flat],
        8,
        MIB,
        "finish",
    )

    for n, g in enumerate(all_groups[1:]):
        both = add_up(both, tie(swap(both, g), sent[0]))
    both = both[0][0]
    (grad4,) = call(
        tokens_kernel,
        [(cot4.shape, F32)],
        [cot4, tie(d_normed, both, sent[0]), unit, inv, vec],
        [held(cot4), pltpu.SemaphoreType.DMA((4,))],
        12,
        full,
        "tokens",
        fetched=(0,),
    )
    (out4,) = call(
        out_kernel,
        [(x4.shape, BF16)],
        [x4, tie(branch, both, sent[0])],
        [held(x4), pltpu.SemaphoreType.DMA((4,))],
        8,
        MIB,
        "out",
        fetched=(0,),
    )
    at = lambda k: sent[max(0, min(k, len(sent) - 1))]
    for n, m in enumerate(reversed(seq_masks[1:])):
        mine = tie(rounded(both).astype(BF16), at(2 * n - 1))
        got = tie(exchange(mine, m), at(2 * n + 1), grad4, out4)
        both = mine.astype(F32) + got.astype(F32)
    both = tie(rounded(both).astype(BF16), sent[-1])
    blocks = {0: both[:, : 2 * feats]}
    for g in reversed(all_groups[1:]):
        for m in list(blocks):
            for p in submasks(g):
                if m == 0 and p == parts:
                    got = exchange(both, p)
                    blocks[p] = got[:, : 2 * feats]
                    other_half = got[:, 2 * feats :]
                else:
                    blocks[m ^ p] = exchange(blocks[m], p)
    rest = [m for m in blocks if m]
    arrays = [blocks[0][None], jnp.stack([blocks[m] for m in rest])]
    masks = [[0], rest]
    for p in submasks(all_groups[0]):
        arrays += [exchange(a, p) for a in arrays[:2]]
        masks += [[m ^ p for m in ms] for ms in masks[:2]]
    (grad_out,) = call(
        halves_kernel,
        [((own, 2, feats), F32)],
        [both[:, 2 * feats :], other_half],
        [flat],
        8,
        MIB,
        "halves",
    )
    (grad_glu,) = call(
        functools.partial(place_kernel, masks, parts),
        [((feats, 2 * feats), F32)],
        arrays,
        [],
        8,
        feats * feats,
        "place",
    )
    return (
        out4.reshape(tokens.shape),
        grad4.reshape(tokens.shape),
        feature_grads[0],
        feature_grads[1],
        grad_in.transpose(2, 0, 1),
        grad_out,
        grad_rate.reshape(own),
        grad_angle.reshape(own),
        grad_level.reshape(own),
        feature_grads[2],
        grad_glu,
    )


def solution(mesh):
    placed = (
        P("state", "seq", None),
        P(),
        P(),
        P(None, "state", None),
        P("state", None, None),
        P("state"),
        P("state"),
        P("state"),
        P(),
        P(),
        P("seq"),
        P("state", "seq", None),
    )
    return jax.shard_map(
        shards,
        mesh=mesh,
        in_specs=placed,
        out_specs=(
            P("state", "seq", None),
            P("state", "seq", None),
            P(),
            P(),
            P(None, "state", None),
            P("state", None, None),
            P("state"),
            P("state"),
            P("state"),
            P(),
            P(),
        ),
        check_vma=False,
    )
```

```python
import functools

import jax
import jax.numpy as jnp
from jax import lax
from jax.experimental import pallas as pl
from jax.experimental.pallas import tpu as pltpu
from jax.sharding import PartitionSpec as P

F32, BF16 = jnp.float32, jnp.bfloat16
EPSILON = 1e-05
SUB = 8
CHUNK = 512
PARAM_ROWS = 16
GELU_A = 0.7978845608028654
GELU_B = 0.044715
MIB = 1 << 20


def repeat(first, last, body, carry):
    for k in range(first, last):
        carry = body(k, carry)
    return carry


def cmul(ar, ai, br, bi):
    return ar * br - ai * bi, ar * bi + ai * br


def nn(a, b):
    return lax.dot_general(a, b, (((1,), (0,)), ((), ())), preferred_element_type=F32)


def nt(a, b):
    return lax.dot_general(a, b, (((1,), (1,)), ((), ())), preferred_element_type=F32)


def tn(a, b):
    return lax.dot_general(a, b, (((0,), (0,)), ((), ())), preferred_element_type=F32)


def rows_in(ref, first, count):
    segs, _, group, feats = ref.shape
    x = ref[:, pl.ds(first, count)].astype(F32)
    return x.transpose(1, 0, 2, 3).reshape(count * segs * group, feats)


def rows_out(y, ref):
    segs, _, group, feats = ref.shape
    return y.reshape(y.shape[0] // SUB, segs, group, feats).transpose(1, 0, 2, 3)


def valid(first, count, limit_ref):
    step = lax.broadcasted_iota(jnp.int32, (count, SUB, 128), 0) + first
    return (step < limit_ref[...][None]).astype(F32).reshape(count * SUB, 128)


def wide(column, lanes):
    return jnp.concatenate([column] * (lanes // column.shape[1]), axis=1)


def call(body, outs, ins, scratch, limit_mib, flops, name, fetched=()):
    specs = []
    for k, x in enumerate(ins):
        space = pltpu.SMEM if x.ndim == 1 else pltpu.HBM if k in fetched else pltpu.VMEM
        specs.append(pl.BlockSpec(memory_space=space))
    return pl.pallas_call(
        body,
        out_shape=[jax.ShapeDtypeStruct(s, d) for s, d in outs],
        in_specs=specs,
        out_specs=[pl.BlockSpec(memory_space=pltpu.VMEM)] * len(outs),
        scratch_shapes=scratch,
        compiler_params=pltpu.CompilerParams(vmem_limit_bytes=limit_mib * MIB),
        cost_estimate=pl.CostEstimate(flops=flops, bytes_accessed=4 * MIB, transcendentals=0),
        name=name,
    )(*ins)


def start_copies(sources, targets, sems):
    copies = [pltpu.make_async_copy(a, b, sems.at[k]) for k, (a, b) in enumerate(zip(sources, targets))]
    for c in copies:
        c.start()
    return copies


def held(x):
    return pltpu.VMEM(x.shape, x.dtype)


def split_pairs(pairs_ref, flat_ref):
    own, _, feats = pairs_ref.shape
    flat = pairs_ref[...].astype(F32).reshape(2 * own, feats)
    for c in range(feats // 128):
        flat_ref[c] = flat[:, c * 128 : (c + 1) * 128]
    take = lambda k: [flat_ref[c, pl.ds(k, own, stride=2), :] for c in range(feats // 128)]
    return [jnp.concatenate(take(k), axis=1).astype(BF16) for k in range(2)]


def three_parts(x):
    high = x.astype(BF16)
    rest = x - high.astype(F32)
    mid = rest.astype(BF16)
    return [high, mid, (rest - mid.astype(F32)).astype(BF16)]


def prep_kernel(own, small_ref, pay_ref, vec_ref):
    feats = vec_ref.shape[1]
    me = lax.axis_index("state")
    lane = lax.broadcasted_iota(jnp.int32, (1, feats), 1)
    mine = (lane // own) == me
    base = 3 * feats
    logs = [small_ref[:, base + k * own : base + (k + 1) * own] for k in range(3)]
    rate, turn, level = (jnp.concatenate([v] * (feats // own), axis=1) for v in logs)
    decay = jnp.exp(rate)
    size = jnp.exp(-decay)
    angle = jnp.exp(turn)
    pole_re, pole_im = size * jnp.cos(angle), size * jnp.sin(angle)
    parts = []
    for v in (pole_re, pole_im, jnp.exp(level)):
        parts += three_parts(jnp.where(mine, v, 0.0))
    parts += [jnp.zeros((PARAM_ROWS - len(parts), feats), BF16)]
    flat = jnp.concatenate([p.astype(F32) for p in parts], axis=0)
    pay_ref[...] = flat.reshape(PARAM_ROWS // 2, 2, feats).astype(BF16)
    rows = [small_ref[:, k * feats : (k + 1) * feats] for k in range(3)] + [pole_re, pole_im, decay, angle]
    for k, row in enumerate(rows):
        vec_ref[k : k + 1, :] = row
    vec_ref[len(rows) :, :] = jnp.zeros((SUB - len(rows), feats), F32)


def cotangent_kernel(cot_ref, rows_ref):
    steps = 16
    for c in range(cot_ref.shape[1] // steps):
        at = pl.ds(c * steps * SUB, steps * SUB)
        rows_ref[at, :] = rows_in(cot_ref, c * steps, steps).astype(BF16)


def weights_kernel(*refs):
    blocks, (out_ref, flat_ref) = refs[:-2], refs[-2:]
    gather_rows(lax.axis_index("state"), blocks, flat_ref, out_ref)


def limit_kernel(group, steps, lens_ref, limit_ref):
    segs = SUB // group
    place = lax.broadcasted_iota(jnp.int32, (SUB, 128), 0)
    seq = place & (group - 1)
    length = jnp.full((SUB, 128), lens_ref[0], jnp.int32)
    for k in range(1, group):
        length = jnp.where(seq == k, lens_ref[k], length)
    limit_ref[...] = length - (lax.axis_index("state") * segs + place // group) * steps


def norm_kernel(x_ref, vec_ref, low_ref, unit_ref, inv_ref):
    segs, steps, group, feats = x_ref.shape
    rows = steps * SUB
    size = 128
    gain, bias = vec_ref[0:1, :], vec_ref[1:2, :]

    def chunk(c, carry):
        base = c * size
        at = pl.ds(base, size)
        x = rows_in(x_ref, c * (size // SUB), size // SUB)
        centred = x - jnp.mean(x, axis=1, keepdims=True)
        inv = lax.rsqrt(jnp.mean(centred * centred, axis=1, keepdims=True) + EPSILON)
        unit = centred * inv
        unit_ref[at, :] = unit
        low_ref[at, :] = (unit * gain + bias).astype(BF16)
        inv_ref[at, :] = jnp.broadcast_to(inv, (size, 128))
        return carry

    repeat(0, rows // size, chunk, 0)


def gather_rows(me, blocks, flat_ref, dst_ref):
    own = flat_ref.shape[1] // 2
    channels = own * len(blocks)
    for m, block in enumerate(blocks):
        for k, part in enumerate(split_pairs(block.at[0:own], flat_ref)):
            at = pl.multiple_of(k * channels + (me ^ m) * own, own)
            dst_ref[pl.ds(at, own), :] = part


def seg_of(group):
    row = lax.broadcasted_iota(jnp.int32, (SUB, 128), 0)
    return row // group


def shift_rows(x, by, keep):
    return jnp.where(wide(keep, x.shape[1]), pltpu.roll(x, by % SUB, 0), 0.0)


def seg_prefix(xr, xi, qr, qi, group, forward):
    seg = seg_of(group)
    segs = SUB // group
    dist = 1
    while dist < segs:
        by = group * dist if forward else SUB - group * dist
        keep = seg >= dist if forward else seg < segs - dist
        sr, si = shift_rows(xr, by, keep), shift_rows(xi, by, keep)
        ar, ai = cmul(qr, qi, sr, si)
        xr, xi = xr + ar, xi + ai
        qr, qi = cmul(qr, qi, qr, qi)
        dist *= 2
    return xr, xi


def seg_enter(xr, xi, qr, qi, dr, di, group, forward):
    seg = seg_of(group)
    segs = SUB // group
    by = group if forward else SUB - group
    keep = seg >= 1 if forward else seg < segs - 1
    er, ei = shift_rows(xr, by, keep), shift_rows(xi, by, keep)
    gap = seg if forward else segs - 1 - seg
    pr, pi = jnp.ones_like(er), jnp.zeros_like(ei)
    bit = 1
    while bit < segs:
        nr, ni = cmul(pr, pi, qr, qi)
        take = wide((gap & bit) != 0, er.shape[1])
        pr, pi = jnp.where(take, nr, pr), jnp.where(take, ni, pi)
        qr, qi = cmul(qr, qi, qr, qi)
        bit *= 2
    ar, ai = cmul(pr, pi, dr, di)
    return er + ar, ei + ai


def device_entry(ends_ref, me, channels, qr, qi, group, forward):
    seg = seg_of(group)
    segs = SUB // group
    parts = ends_ref.shape[0]
    keep = wide(seg == (segs - 1 if forward else 0), channels)
    tr = ti = jnp.zeros((SUB, channels), F32)
    for device in range(parts - 1) if forward else range(parts - 1, 0, -1):
        end = ends_ref[me ^ device]
        nr, ni = cmul(tr, ti, qr, qi)
        counts = device < me if forward else device > me
        tr = jnp.where(counts, nr + end[:, :channels], tr)
        ti = jnp.where(counts, ni + end[:, channels:], ti)
    out = []
    for x in (tr, ti):
        x = jnp.where(keep, x, 0.0)
        y = x
        for k in range(1, segs):
            y = y + pltpu.roll(x, group * k, 0)
        out.append(y)
    return out


def project_kernel(parts, own, group, low_ref, limit_ref, *refs):
    blocks = refs[:parts]
    drive_ref, end_ref, win_ref, cst_ref, flat_ref = refs[parts:]
    rows = low_ref.shape[0]
    channels = own * parts
    steps = rows // SUB
    me = lax.axis_index("state")
    gather_rows(me, blocks, flat_ref, win_ref)
    rows_of = []
    for k in range(3):
        total = None
        for block in blocks:
            tile = block[own : own + PARAM_ROWS // 2].astype(F32).reshape(PARAM_ROWS, -1)
            for part in range(3):
                piece = tile[3 * k + part : 3 * k + part + 1, :channels]
                total = piece if total is None else total + piece
        rows_of.append(total)
    pr, pi, gain = rows_of
    powers = [(pr, pi)]
    span = steps * (SUB // group)
    ar, ai = pr, pi
    count = 1
    while count < span:
        ar, ai = cmul(ar, ai, ar, ai)
        count *= 2
        if count in (steps, span):
            powers.append((ar, ai))
    while len(powers) < 3:
        powers.append(powers[-1])
    for k, (r, i) in enumerate(powers):
        cst_ref[k : k + 1, :] = jnp.concatenate([r, i], axis=1)
    gains = jnp.concatenate([gain, gain], axis=1)
    cst_ref[3:4, :] = gains
    cst_ref[4:8, :] = jnp.zeros((4, 2 * channels), F32)

    def chunk(c, carry):
        base = c * CHUNK
        at = pl.ds(base, CHUNK)
        mask = valid(base // SUB, CHUNK // SUB, limit_ref)
        drive_ref[at, :] = nt(low_ref[at, :], win_ref[...]) * (gains * wide(mask, 2 * channels))
        return carry

    repeat(0, rows // CHUNK, chunk, 0)
    br = jnp.broadcast_to(pr, (SUB, channels))
    bi = jnp.broadcast_to(pi, (SUB, channels))

    def step(j, h):
        u = drive_ref[pl.ds(pl.multiple_of(j * SUB, SUB), SUB), :]
        nr, ni = cmul(br, bi, h[0], h[1])
        return nr + u[:, :channels], ni + u[:, channels:]

    zero = jnp.zeros((SUB, channels), F32)
    er, ei = lax.fori_loop(0, steps, step, (zero, zero), unroll=16)
    er, ei = seg_prefix(er, ei, *powers[1], group, True)
    end_ref[...] = jnp.concatenate([er, ei], axis=1)


def mix_kernel(parts, own, group, orders, *refs):
    it = iter(refs)
    take = lambda n: [next(it) for _ in range(n)]
    drive_ref, end_ref, cst_ref, ends_ref = take(4)
    cw_ref, unit_ref, cot_ref, limit_ref, vec_ref, glu_ref = take(6)
    states_ref, slow_ref, branch_ref, dglu_ref, gp_ref = take(5)
    grads = take(len(orders))
    act_ref, acc_ref = take(2)
    rows, feats = unit_ref.shape
    channels = own * parts
    steps = rows // SUB
    me = lax.axis_index("state")
    place = me + parts * (lax.axis_index("seq") & 1)
    gain, bias, skip = (vec_ref[k : k + 1, :] for k in range(3))
    pr, pi = cst_ref[0:1, :channels], cst_ref[0:1, channels:]
    qr, qi = cst_ref[1:2, :channels], cst_ref[1:2, channels:]
    wr, wi = cst_ref[2:3, :channels], cst_ref[2:3, channels:]
    dr, di = device_entry(ends_ref, me, channels, wr, wi, group, True)
    hr, hi = seg_enter(end_ref[:, :channels], end_ref[:, channels:], qr, qi, dr, di, group, True)
    states_ref[0:SUB, :] = jnp.concatenate([hr, hi], axis=1)
    br = jnp.broadcast_to(pr, (SUB, channels))
    bi = jnp.broadcast_to(pi, (SUB, channels))

    def step(j, h):
        base = pl.multiple_of(j * SUB, SUB)
        u = drive_ref[pl.ds(base, SUB), :]
        nr, ni = cmul(br, bi, h[0], h[1])
        nr, ni = nr + u[:, :channels], ni + u[:, channels:]
        at = pl.ds(pl.multiple_of(base + SUB, SUB), SUB)
        states_ref[at, :channels] = nr
        states_ref[at, channels:] = ni
        return nr, ni

    lax.fori_loop(0, steps, step, (hr, hi), unroll=16)

    def chunk(c, carry):
        base = c * CHUNK
        at = pl.ds(base, CHUNK)
        states = states_ref[pl.ds(pl.multiple_of(base + SUB, SUB), CHUNK), :]
        slow = jnp.concatenate([states[:, :channels], -states[:, channels:]], axis=1).astype(BF16)
        slow_ref[at, :] = slow
        normed = unit_ref[at, :] * gain + bias
        v = nn(slow, cw_ref[...]) + skip * normed
        t = jnp.tanh(GELU_A * (v + GELU_B * (v * v * v)))
        half = 0.5 * (1.0 + t)
        gp_ref[at, :] = half + (0.5 * GELU_A) * v * (1.0 - t * t) * (1.0 + (3.0 * GELU_B) * (v * v))
        act = (v * half).astype(BF16)
        act_ref[at, :] = act
        glu = nn(act, glu_ref[...])
        mask = wide(valid(base // SUB, CHUNK // SUB, limit_ref), feats)
        value = glu[:, :feats]
        gate = jax.nn.sigmoid(glu[:, feats:])
        branch = mask * gate
        branch_ref[at, :] = branch * value
        d_value = branch * cot_ref[at, :].astype(F32)
        dglu_ref[at, :feats] = d_value.astype(BF16)
        dglu_ref[at, feats:] = (d_value * value * (1.0 - gate)).astype(BF16)
        return carry

    repeat(0, rows // CHUNK, chunk, 0)
    width = 256

    def tile(c, carry):
        at = pl.ds(c * width, width)
        acc_ref[:, at] = tn(act_ref[...], dglu_ref[:, at])
        return carry

    repeat(0, 2 * feats // width, tile, 0)
    spread(acc_ref, place, orders, grads)


def spread(acc_ref, place, orders, grads):
    for order, ref in zip(orders, grads):
        _, size, _ = ref.shape
        for k, m in enumerate(order):
            at = pl.ds(pl.multiple_of((place ^ m) * size, size), size)
            ref[k] = acc_ref[at, :].astype(ref.dtype)


def spread_pairs(acc_ref, place, own, channels, orders, grads):
    for order, ref in zip(orders, grads):
        for k, m in enumerate(order):
            off = pl.multiple_of((place ^ m) * own, own)
            ref[k, 0:own] = acc_ref[pl.ds(off, own), :].astype(ref.dtype)
            also = pl.ds(pl.multiple_of(channels + off, own), own)
            ref[k, own : 2 * own] = acc_ref[also, :].astype(ref.dtype)


def back_kernel(own, orders, *refs):
    it = iter(refs)
    take = lambda n: [next(it) for _ in range(n)]
    dglu_ref, gp_ref, unit_ref, vec_ref, glu_ref, slow_ref = take(6)
    dpre_ref, dmix_ref, skip_ref = take(3)
    grads = take(len(orders))
    (acc_ref,) = take(1)
    rows, feats = gp_ref.shape
    place = lax.axis_index("state") + lax.axis_size("state") * (lax.axis_index("seq") & 1)
    gain, bias = vec_ref[0:1, :], vec_ref[1:2, :]

    def chunk(c, total):
        at = pl.ds(c * CHUNK, CHUNK)
        d_pre = nt(dglu_ref[at, :], glu_ref[...]) * gp_ref[at, :]
        dpre_ref[at, :] = d_pre
        normed = unit_ref[at, :] * gain + bias
        dmix_ref[at, :] = d_pre.astype(BF16)
        return total + jnp.sum((d_pre * normed).reshape(CHUNK // SUB, SUB, feats), axis=0)

    skip_ref[...] = repeat(0, rows // CHUNK, chunk, jnp.zeros((SUB, feats), F32))
    width = 256

    def tile(c, carry):
        at = pl.ds(c * width, width)
        acc_ref[:, at] = tn(slow_ref[...], dmix_ref[:, at])
        return carry

    repeat(0, feats // width, tile, 0)
    spread(acc_ref, place, orders, grads)


def starts_kernel(group, dmix_ref, cw_ref, cst_ref, dst_ref, start_ref):
    rows, feats = dmix_ref.shape
    channels = cw_ref.shape[0] // 2
    steps = rows // SUB

    def chunk(c, carry):
        at = pl.ds(c * CHUNK, CHUNK)
        dst_ref[at, :] = nt(dmix_ref[at, :], cw_ref[...])
        return carry

    repeat(0, rows // CHUNK, chunk, 0)
    br = jnp.broadcast_to(cst_ref[0:1, :channels], (SUB, channels))
    bi = jnp.broadcast_to(-cst_ref[0:1, channels:], (SUB, channels))

    def step(k, a):
        base = pl.multiple_of((steps - 1 - k) * SUB, SUB)
        u = dst_ref[pl.ds(base, SUB), :]
        nr, ni = cmul(br, bi, a[0], a[1])
        return nr + u[:, :channels], ni - u[:, channels:]

    zero = jnp.zeros((SUB, channels), F32)
    ar, ai = lax.fori_loop(0, steps, step, (zero, zero), unroll=16)
    qr, qi = cst_ref[1:2, :channels], -cst_ref[1:2, channels:]
    ar, ai = seg_prefix(ar, ai, qr, qi, group, False)
    start_ref[...] = jnp.concatenate([ar, ai], axis=1)


def adjoint_kernel(own, group, orders, *refs):
    it = iter(refs)
    take = lambda n: [next(it) for _ in range(n)]
    dst_ref, start_ref, cst_ref, ends_ref = take(4)
    states_ref, drive_ref, low_ref, limit_ref = take(4)
    dproj_ref, sums_ref = take(2)
    grads = take(len(orders))
    adj_ref, acc_ref = take(2)
    rows = dst_ref.shape[0]
    channels = dst_ref.shape[1] // 2
    steps = rows // SUB
    me = lax.axis_index("state")
    pr, pi = cst_ref[0:1, :channels], -cst_ref[0:1, channels:]
    qr, qi = cst_ref[1:2, :channels], -cst_ref[1:2, channels:]
    wr, wi = cst_ref[2:3, :channels], -cst_ref[2:3, channels:]
    dr, di = device_entry(ends_ref, me, channels, wr, wi, group, False)
    ar, ai = seg_enter(start_ref[:, :channels], start_ref[:, channels:], qr, qi, dr, di, group, False)
    br = jnp.broadcast_to(pr, (SUB, channels))
    bi = jnp.broadcast_to(pi, (SUB, channels))

    def step(k, carry):
        ar, ai, sr, si, sg = carry
        base = pl.multiple_of((steps - 1 - k) * SUB, SUB)
        at = pl.ds(base, SUB)
        d = dst_ref[at, :]
        nr, ni = cmul(br, bi, ar, ai)
        ar, ai = nr + d[:, :channels], ni - d[:, channels:]
        adj_ref[at, :channels] = ar
        adj_ref[at, channels:] = ai
        h = states_ref[at, :]
        hr, hi = h[:, :channels], h[:, channels:]
        u = drive_ref[at, :]
        sr = sr + (ar * hr + ai * hi)
        si = si + (ai * hr - ar * hi)
        sg = sg + (ar * u[:, :channels] + ai * u[:, channels:])
        return ar, ai, sr, si, sg

    zero = jnp.zeros((SUB, channels), F32)
    out = lax.fori_loop(0, steps, step, (ar, ai, zero, zero, zero), unroll=8)
    sums_ref[:, :channels] = out[2]
    sums_ref[:, channels : 2 * channels] = out[3]
    sums_ref[:, 2 * channels : 3 * channels] = out[4]
    gains = cst_ref[3:4, :]

    def chunk(c, carry):
        base = c * CHUNK
        at = pl.ds(base, CHUNK)
        mask = valid(base // SUB, CHUNK // SUB, limit_ref)
        dproj_ref[at, :] = (adj_ref[at, :] * (gains * wide(mask, 2 * channels))).astype(BF16)
        return carry

    repeat(0, rows // CHUNK, chunk, 0)
    width = 256
    feats = low_ref.shape[1]

    def tile(c, carry):
        at = pl.ds(c * width, width)
        acc_ref[:, at] = tn(dproj_ref[...], low_ref[:, at])
        return carry

    repeat(0, feats // width, tile, 0)
    spread_pairs(acc_ref, me, own, channels, orders, grads)


def out_kernel(x_hbm, branch_ref, out_ref, x_ref, sems):
    segs, steps, _, _ = x_ref.shape
    size = 16
    cut = steps // 4
    places = [pl.ds(k * cut, cut) for k in range(4)]
    copies = start_copies([x_hbm.at[:, p] for p in places], [x_ref.at[:, p] for p in places], sems)

    def chunk(c, carry):
        first = c * size
        rows = branch_ref[pl.ds(pl.multiple_of(first * SUB, size * SUB), size * SUB), :]
        at = pl.ds(first, size)
        out_ref[:, at] = (x_ref[:, at].astype(F32) + rows_out(rows, x_ref)).astype(BF16)
        return carry

    for k in range(4):
        copies[k].wait()
        repeat(k * cut // size, (k + 1) * cut // size, chunk, 0)


def normed_kernel(dproj_ref, win_ref, dpre_ref, unit_ref, vec_ref, channel_ref, skip_ref, dnorm_ref, sums_ref):
    rows, feats = dpre_ref.shape
    skip = vec_ref[2:3, :]

    def chunk(c, carry):
        total_gain, total_bias = carry
        at = pl.ds(c * CHUNK, CHUNK)
        d_normed = dpre_ref[at, :] * skip + nn(dproj_ref[at, :], win_ref[...])
        dnorm_ref[at, :] = d_normed
        folded = lambda v: jnp.sum(v.reshape(CHUNK // SUB, SUB, feats), axis=0)
        return total_gain + folded(d_normed * unit_ref[at, :]), total_bias + folded(d_normed)

    zero = jnp.zeros((SUB, feats), F32)
    total_gain, total_bias = repeat(0, rows // CHUNK, chunk, (zero, zero))
    over = lambda v: jnp.sum(v, axis=0, keepdims=True)
    channel = over(channel_ref[...])
    wide_at = channel.shape[1] - feats
    sums_ref[0:1, :] = channel[:, :feats]
    sums_ref[1:2, :] = jnp.zeros((1, feats), F32)
    sums_ref[1:2, :wide_at] = channel[:, feats:]
    sums_ref[2:3, :] = over(total_gain)
    sums_ref[3:4, :] = over(total_bias)
    sums_ref[4:5, :] = over(skip_ref[...])
    sums_ref[5:8, :] = jnp.zeros((3, feats), F32)


def tokens_kernel(cot_hbm, dnorm_ref, unit_ref, inv_ref, vec_ref, out_ref, cot_ref, sems):
    rows, feats = dnorm_ref.shape
    gain = vec_ref[0:1, :]
    size = 128
    steps = size // SUB
    cut = cot_ref.shape[1] // 4
    places = [pl.ds(k * cut, cut) for k in range(4)]
    copies = start_copies([cot_hbm.at[:, p] for p in places], [cot_ref.at[:, p] for p in places], sems)

    def chunk(c, carry):
        at = pl.ds(c * size, size)
        unit = unit_ref[at, :]
        d_unit = dnorm_ref[at, :] * gain
        first = jnp.mean(d_unit, axis=1, keepdims=True)
        second = jnp.mean(d_unit * unit, axis=1, keepdims=True)
        rows = wide(inv_ref[at, :], feats) * (d_unit - first - unit * second)
        step_at = pl.ds(c * steps, steps)
        out_ref[:, step_at] = cot_ref[:, step_at].astype(F32) + rows_out(rows, cot_ref)
        return carry

    for k in range(4):
        copies[k].wait()
        repeat(k * cut // steps, (k + 1) * cut // steps, chunk, 0)


def join_pairs(parts, flat_ref, out_ref):
    own, _, feats = out_ref.shape
    for k, part in enumerate(parts):
        for c in range(feats // 128):
            flat_ref[c, pl.ds(k, own, stride=2), :] = part[:, c * 128 : (c + 1) * 128]
    rows = jnp.concatenate([flat_ref[c] for c in range(feats // 128)], axis=1)
    out_ref[...] = rows.reshape(own, 2, feats)


def halves_kernel(mine_ref, other_ref, out_ref, flat_ref):
    own = out_ref.shape[0]
    first = (lax.axis_index("seq") & 1) == 0
    a, b = mine_ref[...].astype(F32), other_ref[...].astype(F32)
    join_pairs([jnp.where(first, a, b), jnp.where(first, b, a)], flat_ref, out_ref)


def finish_kernel(total_ref, sums_ref, vec_ref, in_ref, gain_ref, bias_ref, skip_ref, rate_ref, angle_ref, level_ref, flat_ref):
    own, _, feats = in_ref.shape
    join_pairs([total_ref[:own, :], total_ref[own:, :]], flat_ref, in_ref)
    sums = sums_ref[...]
    for k, ref in enumerate((gain_ref, bias_ref, skip_ref)):
        ref[...] = sums[2 + k : 3 + k, :]
    me = lax.axis_index("state")
    channels = lax.axis_size("state") * own
    pick = lambda row: sum(
        jnp.where(me == d, row[:, d * own : (d + 1) * own], 0.0) for d in range(channels // own)
    )
    sum_re, sum_im = pick(sums[0:1, :channels]), pick(sums[0:1, channels:])
    pole_re, pole_im, decay, angle = (vec_ref[k : k + 1, :own] for k in range(3, 7))
    rate_ref[...] = -decay * (sum_re * pole_re + sum_im * pole_im)
    angle_ref[...] = angle * (sum_im * pole_re - sum_re * pole_im)
    level_ref[...] = pick(sums[1:2, :channels])


def place_kernel(masks, parts, *refs):
    arrays, out_ref, wide_ref, sems = refs[: len(masks)], refs[-3], refs[-2], refs[-1]
    place = lax.axis_index("state") + parts * (lax.axis_index("seq") & 1)
    size = arrays[0].shape[1]
    copies = []
    for ms, ref in zip(masks, arrays):
        for k, m in enumerate(ms):
            n = len(copies)
            wide_ref[n] = ref[k].astype(F32)
            at = pl.ds(pl.multiple_of((place ^ m) * size, size), size)
            copies.append(pltpu.make_async_copy(wide_ref.at[n], out_ref.at[at, :], sems.at[n]))
            copies[-1].start()
    for c in copies:
        c.wait()


def place_blocks(arrays, masks, parts, shape, out=None):
    count = sum(len(m) for m in masks)
    _, size, width = arrays[0].shape
    ins = list(arrays) + ([] if out is None else [out])
    specs = [pl.BlockSpec(memory_space=pltpu.VMEM)] * len(arrays)
    specs += [pl.BlockSpec(memory_space=pl.ANY)] * (len(ins) - len(arrays))
    return pl.pallas_call(
        functools.partial(place_kernel, masks, parts),
        out_shape=jax.ShapeDtypeStruct(shape, F32),
        in_specs=specs,
        out_specs=pl.BlockSpec(memory_space=pl.ANY),
        scratch_shapes=[pltpu.VMEM((count, size, width), F32), pltpu.SemaphoreType.DMA((count,))],
        input_output_aliases={} if out is None else {len(arrays): 0},
        compiler_params=pltpu.CompilerParams(vmem_limit_bytes=8 * MIB),
        cost_estimate=pl.CostEstimate(flops=MIB, bytes_accessed=2 * MIB, transcendentals=0),
        name="place",
    )(*ins)


def exchange(x, mask):
    count = lax.axis_size("seq") * lax.axis_size("state")
    return lax.ppermute(x, ("seq", "state"), [(i, i ^ mask) for i in range(count)])


def tie(x, *after):
    return lax.optimization_barrier((x, after))[0]


def bits_of(n):
    return [1 << k for k in range(n.bit_length() - 1)]


def submasks(group):
    out = [0]
    for bit in group:
        out += [m | bit for m in out]
    return out[1:]


def stage_orders(groups):
    kept = [0]
    stages = []
    for group in reversed(groups):
        sends = [[m ^ p for m in kept] for p in submasks(group)]
        stages.insert(0, sends)
        kept = sum(sends, []) + kept
    return [o for sends in stages for o in sends] + [[0]]


def swap(parts, group):
    masks = submasks(group)
    return [exchange(p.astype(BF16), m) for p, m in zip(parts, masks)]


def add_up(parts, got):
    rest, off = [], 0
    for p in parts[len(got) :]:
        n = p.shape[0]
        total = p.astype(F32)
        for g in got:
            total = total + g[off : off + n].astype(F32)
        rest.append(total)
        off += n
    return rest


def halve(parts, group):
    return add_up(parts, swap(parts, group))


def rounded(x):
    return lax.reduce_precision(x, 8, 7)


def two_parts(x):
    high = rounded(x)
    return [high.astype(BF16), rounded(x - high).astype(BF16)]


def sum_of(parts):
    return parts[0].astype(F32) + parts[1].astype(F32)


def gather_ends(end, bits):
    g = end[None]
    for bit in reversed(bits):
        g = jnp.stack([g, exchange(g, bit)], axis=1).reshape((2 * g.shape[0],) + end.shape)
    return g


def gather_blocks(arrays, bits, ready=None):
    blocks = [{0: a} for a in arrays]
    for n, bit in enumerate(reversed(bits)):
        for held_blocks in blocks:
            for m in list(held_blocks):
                x = held_blocks[m]
                if m and n and ready is not None:
                    x = tie(x, ready)
                held_blocks[m ^ bit] = exchange(x, bit)
    return [[b[m] for m in range(len(b))] for b in blocks]


def shards(
    tokens,
    norm_gain,
    norm_bias,
    input_weight,
    output_weight,
    log_rate,
    log_angle,
    log_gain,
    skip_gain,
    glu_weight,
    lengths,
    cotangent,
):
    span, group, feats = tokens.shape
    own = log_rate.shape[0]
    parts = lax.axis_size("state")
    n_seq = lax.axis_size("seq")
    channels = own * parts
    rows = span * group
    segs = SUB // group
    me = lax.axis_index("state")
    state_bits = bits_of(parts)
    seq_masks = [parts * b for b in bits_of(n_seq)]
    if len(seq_masks) > 2:
        seq_masks[-1] |= seq_masks[-2]
    full = rows * feats * 2 * channels * 2

    flat = pltpu.VMEM((feats // 128, 2 * own, 128), F32)
    x4 = tokens.reshape(segs, span // segs, group, feats)
    cot4 = cotangent.reshape(segs, span // segs, group, feats)
    small = jnp.concatenate([norm_gain, norm_bias, skip_gain, log_rate, log_angle, log_gain])
    small = small.reshape(1, -1)
    small_own, vec = call(
        functools.partial(prep_kernel, own),
        [((PARAM_ROWS // 2, 2, feats), BF16), ((SUB, feats), F32)],
        [small],
        [],
        8,
        MIB,
        "prep",
    )
    b_own = jnp.concatenate([input_weight.transpose(1, 2, 0), small_own], axis=0)
    low, unit, inv = call(
        norm_kernel,
        [((rows, feats), BF16), ((rows, feats), F32), ((rows, 128), F32)],
        [x4, vec],
        [],
        12,
        rows * feats * 20,
        "norm",
    )
    (limit,) = call(
        functools.partial(limit_kernel, group, rows // SUB),
        [((SUB, 128), jnp.int32)],
        [tie(lengths, low)],
        [],
        8,
        MIB,
        "limit",
    )
    b_blocks, c_blocks = gather_blocks([b_own, tie(output_weight, b_own)], state_bits, (low, limit))
    drive, end, win, cst = call(
        functools.partial(project_kernel, parts, own, group),
        [
            ((rows, 2 * channels), F32),
            ((SUB, 2 * channels), F32),
            ((2 * channels, feats), BF16),
            ((SUB, 2 * channels), F32),
        ],
        [low, limit] + b_blocks,
        [flat],
        12,
        full,
        "project",
    )
    ends = gather_ends(end, state_bits)
    (cot,) = call(cotangent_kernel, [((rows, feats), BF16)], [tie(cot4, end)], [], 8, MIB, "cotangent")
    (cw,) = call(
        weights_kernel,
        [((2 * channels, feats), BF16)],
        [tie(c_blocks[0], end)] + c_blocks[1:],
        [flat],
        8,
        MIB,
        "weights",
    )
    all_bits = state_bits + [parts]
    all_groups = [all_bits[:1]] + [all_bits[k : k + 2] for k in range(1, len(all_bits), 2)]
    all_orders = stage_orders(all_groups)
    glu_rows = feats // (2 * parts)
    block_outs = lambda rows, width, orders: [
        ((len(o), rows, width), BF16 if k == 0 else F32) for k, o in enumerate(orders)
    ]
    states, slow, branch, d_glu, slope, *glu_parts = call(
        functools.partial(mix_kernel, parts, own, group, all_orders),
        [
            ((rows + SUB, 2 * channels), F32),
            ((rows, 2 * channels), BF16),
            ((rows, feats), F32),
            ((rows, 2 * feats), BF16),
            ((rows, feats), F32),
        ]
        + block_outs(glu_rows, 2 * feats, all_orders),
        [drive, end, cst, ends, cw, unit, cot, limit, vec, glu_weight],
        [pltpu.VMEM((rows, feats), BF16), pltpu.VMEM((feats, 2 * feats), F32)],
        20,
        5 * full,
        "mix",
    )
    d_pre, d_mixed, skip_sum, *out_parts = call(
        functools.partial(back_kernel, own, all_orders),
        [((rows, feats), F32), ((rows, feats), BF16), ((SUB, feats), F32)]
        + block_outs(own, feats, all_orders),
        [d_glu, slope, unit, vec, glu_weight, slow],
        [pltpu.VMEM((2 * channels, feats), F32)],
        16,
        3 * full,
        "back",
    )
    d_states, start = call(
        functools.partial(starts_kernel, group),
        [((rows, 2 * channels), F32), ((SUB, 2 * channels), F32)],
        [d_mixed, cw, cst],
        [],
        12,
        full,
        "starts",
    )
    got = swap(glu_parts, all_groups[0])
    more = swap(out_parts, all_groups[0])
    starts = gather_ends(tie(start, got, more), state_bits)
    got, more = tie((got, more), start)
    glu_parts, out_parts = add_up(glu_parts, got), add_up(out_parts, more)
    both = [jnp.concatenate(p, axis=-1) for p in zip(glu_parts, out_parts)]
    state_groups = [[b] for b in state_bits]
    pair_orders = stage_orders(state_groups)
    d_proj, channel_sums, *in_parts = call(
        functools.partial(adjoint_kernel, own, group, pair_orders),
        [((rows, 2 * channels), BF16), ((SUB, 3 * channels), F32)]
        + block_outs(2 * own, feats, pair_orders),
        [tie(d_states, both), start, cst, starts, states, drive, low, limit],
        [pltpu.VMEM((rows, 2 * channels), F32), pltpu.VMEM((2 * channels, feats), F32)],
        16,
        2 * full,
        "adjoint",
    )
    in_parts = halve(in_parts, state_groups[0])
    d_normed, sums = call(
        normed_kernel,
        [((rows, feats), F32), ((SUB, feats), F32)],
        [d_proj, win, d_pre, unit, vec, channel_sums, skip_sum],
        [],
        12,
        full,
        "normed",
    )
    class chain:
        parts, total, held = in_parts, None, sums
        masks = state_bits[1:] + seq_masks[:1] + seq_masks[:0:-1]
        sent = []

        def send(after=()):
            chain.two = two_parts(chain.held)
            if len(chain.parts) > 1:
                chain.low = chain.parts[0].astype(BF16).reshape(-1, feats)
            else:
                chain.low = rounded(chain.parts[0][0]).astype(BF16)
            chain.sent.append(tie(jnp.concatenate([chain.low] + chain.two, axis=0), after))

        def take():
            got = exchange(chain.sent[-1], chain.masks[len(chain.sent) - 1])
            chain.got, rest, off = got, [], 0
            if len(chain.parts) > 1:
                for p in chain.parts[1:]:
                    n = p.shape[0] * p.shape[1]
                    rest.append(p + got[off : off + n].reshape(p.shape).astype(F32))
                    off += n
            else:
                off = 2 * own
                rest.append((chain.low.astype(F32) + got[:off].astype(F32))[None])
            chain.parts = rest
            chain.held = sum_of(chain.two) + sum_of([got[off : off + SUB], got[off + SUB :]])

    chain.send()
    for g in all_groups[1:]:
        got = swap(both, g)
        both = add_up(both, tie(got, chain.sent[-1]))
    both = both[0][0]
    (grad4,) = call(
        tokens_kernel,
        [(cot4.shape, F32)],
        [cot4, tie(d_normed, both, chain.sent[-1]), unit, inv, vec],
        [held(cot4), pltpu.SemaphoreType.DMA((4,))],
        12,
        full,
        "tokens",
        fetched=(0,),
    )
    (out4,) = call(
        out_kernel,
        [(x4.shape, BF16)],
        [x4, tie(branch, both, chain.sent[-1])],
        [held(x4), pltpu.SemaphoreType.DMA((4,))],
        8,
        MIB,
        "out",
        fetched=(0,),
    )
    chain.take()
    chain.held = chain.held + exchange(chain.held, state_bits[0])
    chain.send()
    glu_masks = seq_masks[:0:-1]
    for n, m in enumerate(glu_masks):
        mine = rounded(both).astype(BF16)
        got = exchange(mine, m)
        if n:
            chain.take()
            chain.send(mine)
        got = tie(got, chain.sent[-1], grad4, out4)
        both = mine.astype(F32) + got.astype(F32)
    both = rounded(both).astype(BF16)
    while len(chain.sent) < len(chain.masks):
        chain.take()
        chain.send(both)
    chain.take()
    last = chain.got
    grad_in, grad_gain, grad_bias, grad_skip, grad_rate, grad_angle, grad_level = call(
        finish_kernel,
        [((own, 2, feats), F32)] + [((1, feats), F32)] * 3 + [((1, own), F32)] * 3,
        [chain.parts[0][0], chain.held, vec],
        [flat],
        8,
        MIB,
        "finish",
    )
    blocks = {0: both[:, : 2 * feats]}
    for g in reversed(all_groups[1:]):
        for m in list(blocks):
            for p in submasks(g):
                if m == 0 and p == parts:
                    got = exchange(both, p)
                    blocks[p] = got[:, : 2 * feats]
                    other_half = got[:, 2 * feats :]
                else:
                    blocks[m ^ p] = exchange(blocks[m], p)
    far_own = [exchange(blocks[0][None], p) for p in submasks(all_groups[0])]
    (grad_out,) = call(
        halves_kernel,
        [((own, 2, feats), F32)],
        [both[:, 2 * feats :], tie(other_half, far_own)],
        [flat],
        8,
        MIB,
        "halves",
    )
    rest = [m for m in blocks if m]
    near = [blocks[0][None], jnp.stack(tie([blocks[m] for m in rest], grad_out, chain.sent[-1]))]
    near_masks = [[0], rest]
    far = [f for p, o in zip(submasks(all_groups[0]), far_own) for f in (o, exchange(near[1], p))]
    far_masks = [[m ^ p for m in ms] for p in submasks(all_groups[0]) for ms in near_masks]
    grad_glu = place_blocks(tie(near, last), near_masks, parts, (feats, 2 * feats))
    grad_glu = place_blocks(tie(far, grad_in), far_masks, parts, (feats, 2 * feats), grad_glu)
    return (
        out4.reshape(tokens.shape),
        grad4.reshape(tokens.shape),
        grad_gain.reshape(feats),
        grad_bias.reshape(feats),
        grad_in.transpose(2, 0, 1),
        grad_out,
        grad_rate.reshape(own),
        grad_angle.reshape(own),
        grad_level.reshape(own),
        grad_skip.reshape(feats),
        grad_glu,
    )


def solution(mesh):
    placed = (
        P("state", "seq", None),
        P(),
        P(),
        P(None, "state", None),
        P("state", None, None),
        P("state"),
        P("state"),
        P("state"),
        P(),
        P(),
        P("seq"),
        P("state", "seq", None),
    )
    return jax.shard_map(
        shards,
        mesh=mesh,
        in_specs=placed,
        out_specs=(
            P("state", "seq", None),
            P("state", "seq", None),
            P(),
            P(),
            P(None, "state", None),
            P("state", None, None),
            P("state"),
            P("state"),
            P("state"),
            P(),
            P(),
        ),
        check_vma=False,
    )
```

```python
import functools

import jax
import jax.numpy as jnp
from jax import lax
from jax.experimental import pallas as pl
from jax.experimental.pallas import tpu as pltpu
from jax.sharding import PartitionSpec as P

F32, BF16 = jnp.float32, jnp.bfloat16
EPSILON = 1e-05
SUB = 8
CHUNK = 512
PARAM_ROWS = 16
GELU_A = 0.7978845608028654
GELU_B = 0.044715
MIB = 1 << 20


def repeat(first, last, body, carry):
    for k in range(first, last):
        carry = body(k, carry)
    return carry


def cmul(ar, ai, br, bi):
    return ar * br - ai * bi, ar * bi + ai * br


def nn(a, b):
    return lax.dot_general(a, b, (((1,), (0,)), ((), ())), preferred_element_type=F32)


def nt(a, b):
    return lax.dot_general(a, b, (((1,), (1,)), ((), ())), preferred_element_type=F32)


def tn(a, b):
    return lax.dot_general(a, b, (((0,), (0,)), ((), ())), preferred_element_type=F32)


def rows_in(ref, first, count):
    segs, _, group, feats = ref.shape
    x = ref[:, pl.ds(first, count)].astype(F32)
    return x.transpose(1, 0, 2, 3).reshape(count * segs * group, feats)


def rows_out(y, ref):
    segs, _, group, feats = ref.shape
    return y.reshape(y.shape[0] // SUB, segs, group, feats).transpose(1, 0, 2, 3)


def valid(first, count, limit_ref):
    step = lax.broadcasted_iota(jnp.int32, (count, SUB, 128), 0) + first
    return (step < limit_ref[...][None]).astype(F32).reshape(count * SUB, 128)


def wide(column, lanes):
    return jnp.concatenate([column] * (lanes // column.shape[1]), axis=1)


def call(body, outs, ins, scratch, limit_mib, flops, name, fetched=(), sent=False):
    specs = []
    for k, x in enumerate(ins):
        space = pltpu.SMEM if x.ndim == 1 else pl.ANY if k in fetched else pltpu.VMEM
        specs.append(pl.BlockSpec(memory_space=space))
    return pl.pallas_call(
        body,
        out_shape=[jax.ShapeDtypeStruct(s, d) for s, d in outs],
        in_specs=specs,
        out_specs=[pl.BlockSpec(memory_space=pl.ANY if sent else pltpu.VMEM)] * len(outs),
        scratch_shapes=scratch,
        compiler_params=pltpu.CompilerParams(vmem_limit_bytes=limit_mib * MIB),
        cost_estimate=pl.CostEstimate(flops=flops, bytes_accessed=4 * MIB, transcendentals=0),
        name=name,
    )(*ins)


def start_copies(sources, targets, sems):
    copies = [pltpu.make_async_copy(a, b, sems.at[k]) for k, (a, b) in enumerate(zip(sources, targets))]
    for c in copies:
        c.start()
    return copies


def held(x):
    return pltpu.VMEM(x.shape, x.dtype)


def split_pairs(pairs_ref, flat_ref):
    own, _, feats = pairs_ref.shape
    flat = pairs_ref[...].astype(F32).reshape(2 * own, feats)
    for c in range(feats // 128):
        flat_ref[c] = flat[:, c * 128 : (c + 1) * 128]
    take = lambda k: [flat_ref[c, pl.ds(k, own, stride=2), :] for c in range(feats // 128)]
    return [jnp.concatenate(take(k), axis=1).astype(BF16) for k in range(2)]


def three_parts(x):
    high = x.astype(BF16)
    rest = x - high.astype(F32)
    mid = rest.astype(BF16)
    return [high, mid, (rest - mid.astype(F32)).astype(BF16)]


def prep_kernel(own, small_ref, pay_ref, vec_ref):
    feats = vec_ref.shape[1]
    me = lax.axis_index("state")
    lane = lax.broadcasted_iota(jnp.int32, (1, feats), 1)
    mine = (lane // own) == me
    base = 3 * feats
    logs = [small_ref[:, base + k * own : base + (k + 1) * own] for k in range(3)]
    rate, turn, level = (jnp.concatenate([v] * (feats // own), axis=1) for v in logs)
    decay = jnp.exp(rate)
    size = jnp.exp(-decay)
    angle = jnp.exp(turn)
    pole_re, pole_im = size * jnp.cos(angle), size * jnp.sin(angle)
    parts = []
    for v in (pole_re, pole_im, jnp.exp(level)):
        parts += three_parts(jnp.where(mine, v, 0.0))
    parts += [jnp.zeros((PARAM_ROWS - len(parts), feats), BF16)]
    flat = jnp.concatenate([p.astype(F32) for p in parts], axis=0)
    pay_ref[...] = flat.reshape(PARAM_ROWS // 2, 2, feats).astype(BF16)
    rows = [small_ref[:, k * feats : (k + 1) * feats] for k in range(3)] + [pole_re, pole_im, decay, angle]
    for k, row in enumerate(rows):
        vec_ref[k : k + 1, :] = row
    vec_ref[len(rows) :, :] = jnp.zeros((SUB - len(rows), feats), F32)


def cotangent_kernel(cot_ref, rows_ref):
    steps = 16
    for c in range(cot_ref.shape[1] // steps):
        at = pl.ds(c * steps * SUB, steps * SUB)
        rows_ref[at, :] = rows_in(cot_ref, c * steps, steps).astype(BF16)


def weights_kernel(*refs):
    blocks, (out_ref, flat_ref) = refs[:-2], refs[-2:]
    gather_rows(lax.axis_index("state"), blocks, flat_ref, out_ref)


def limit_kernel(group, steps, lens_ref, limit_ref):
    segs = SUB // group
    place = lax.broadcasted_iota(jnp.int32, (SUB, 128), 0)
    seq = place & (group - 1)
    length = jnp.full((SUB, 128), lens_ref[0], jnp.int32)
    for k in range(1, group):
        length = jnp.where(seq == k, lens_ref[k], length)
    limit_ref[...] = length - (lax.axis_index("state") * segs + place // group) * steps


def norm_kernel(x_hbm, vec_ref, low_ref, unit_ref, inv_ref, rows_ref, x_ref, sems):
    segs, steps, group, feats = x_ref.shape
    rows = steps * SUB
    size = 128
    gain, bias = vec_ref[0:1, :], vec_ref[1:2, :]
    cut = steps // 4
    places = [pl.ds(k * cut, cut) for k in range(4)]
    copies = start_copies([x_hbm.at[:, p] for p in places], [x_ref.at[:, p] for p in places], sems)

    def chunk(c, carry):
        at = pl.ds(c * size, size)
        x = rows_in(x_ref, c * (size // SUB), size // SUB)
        rows_ref[at, :] = x.astype(BF16)
        centred = x - jnp.mean(x, axis=1, keepdims=True)
        inv = lax.rsqrt(jnp.mean(centred * centred, axis=1, keepdims=True) + EPSILON)
        unit = centred * inv
        unit_ref[at, :] = unit
        low_ref[at, :] = (unit * gain + bias).astype(BF16)
        inv_ref[at, :] = jnp.broadcast_to(inv, (size, 128))
        return carry

    turns = rows // size // 4
    for k in range(4):
        copies[k].wait()
        repeat(k * turns, (k + 1) * turns, chunk, 0)


def gather_rows(me, blocks, flat_ref, dst_ref):
    own = flat_ref.shape[1] // 2
    channels = own * len(blocks)
    for m, block in enumerate(blocks):
        for k, part in enumerate(split_pairs(block.at[0:own], flat_ref)):
            at = pl.multiple_of(k * channels + (me ^ m) * own, own)
            dst_ref[pl.ds(at, own), :] = part


def seg_of(group):
    row = lax.broadcasted_iota(jnp.int32, (SUB, 128), 0)
    return row // group


def shift_rows(x, by, keep):
    return jnp.where(wide(keep, x.shape[1]), pltpu.roll(x, by % SUB, 0), 0.0)


def seg_prefix(xr, xi, qr, qi, group, forward):
    seg = seg_of(group)
    segs = SUB // group
    dist = 1
    while dist < segs:
        by = group * dist if forward else SUB - group * dist
        keep = seg >= dist if forward else seg < segs - dist
        sr, si = shift_rows(xr, by, keep), shift_rows(xi, by, keep)
        ar, ai = cmul(qr, qi, sr, si)
        xr, xi = xr + ar, xi + ai
        qr, qi = cmul(qr, qi, qr, qi)
        dist *= 2
    return xr, xi


def seg_enter(xr, xi, qr, qi, dr, di, group, forward):
    seg = seg_of(group)
    segs = SUB // group
    by = group if forward else SUB - group
    keep = seg >= 1 if forward else seg < segs - 1
    er, ei = shift_rows(xr, by, keep), shift_rows(xi, by, keep)
    gap = seg if forward else segs - 1 - seg
    pr, pi = jnp.ones_like(er), jnp.zeros_like(ei)
    bit = 1
    while bit < segs:
        nr, ni = cmul(pr, pi, qr, qi)
        take = wide((gap & bit) != 0, er.shape[1])
        pr, pi = jnp.where(take, nr, pr), jnp.where(take, ni, pi)
        qr, qi = cmul(qr, qi, qr, qi)
        bit *= 2
    ar, ai = cmul(pr, pi, dr, di)
    return er + ar, ei + ai


def device_entry(ends_ref, me, channels, qr, qi, group, forward):
    seg = seg_of(group)
    segs = SUB // group
    parts = ends_ref.shape[0]
    keep = wide(seg == (segs - 1 if forward else 0), channels)
    tr = ti = jnp.zeros((SUB, channels), F32)
    for device in range(parts - 1) if forward else range(parts - 1, 0, -1):
        end = ends_ref[me ^ device]
        nr, ni = cmul(tr, ti, qr, qi)
        counts = device < me if forward else device > me
        tr = jnp.where(counts, nr + end[:, :channels], tr)
        ti = jnp.where(counts, ni + end[:, channels:], ti)
    out = []
    for x in (tr, ti):
        x = jnp.where(keep, x, 0.0)
        y = x
        for k in range(1, segs):
            y = y + pltpu.roll(x, group * k, 0)
        out.append(y)
    return out


def project_kernel(parts, own, group, low_ref, limit_ref, *refs):
    blocks = refs[:parts]
    drive_ref, end_ref, win_ref, cst_ref, flat_ref = refs[parts:]
    rows = low_ref.shape[0]
    channels = own * parts
    steps = rows // SUB
    me = lax.axis_index("state")
    gather_rows(me, blocks, flat_ref, win_ref)
    rows_of = []
    for k in range(3):
        total = None
        for block in blocks:
            tile = block[own : own + PARAM_ROWS // 2].astype(F32).reshape(PARAM_ROWS, -1)
            for part in range(3):
                piece = tile[3 * k + part : 3 * k + part + 1, :channels]
                total = piece if total is None else total + piece
        rows_of.append(total)
    pr, pi, gain = rows_of
    powers = [(pr, pi)]
    span = steps * (SUB // group)
    ar, ai = pr, pi
    count = 1
    while count < span:
        ar, ai = cmul(ar, ai, ar, ai)
        count *= 2
        if count in (steps, span):
            powers.append((ar, ai))
    while len(powers) < 3:
        powers.append(powers[-1])
    for k, (r, i) in enumerate(powers):
        cst_ref[k : k + 1, :] = jnp.concatenate([r, i], axis=1)
    gains = jnp.concatenate([gain, gain], axis=1)
    cst_ref[3:4, :] = gains
    cst_ref[4:8, :] = jnp.zeros((4, 2 * channels), F32)

    def chunk(c, carry):
        base = c * CHUNK
        at = pl.ds(base, CHUNK)
        mask = valid(base // SUB, CHUNK // SUB, limit_ref)
        drive_ref[at, :] = nt(low_ref[at, :], win_ref[...]) * (gains * wide(mask, 2 * channels))
        return carry

    repeat(0, rows // CHUNK, chunk, 0)
    br = jnp.broadcast_to(pr, (SUB, channels))
    bi = jnp.broadcast_to(pi, (SUB, channels))

    def step(j, h):
        u = drive_ref[pl.ds(pl.multiple_of(j * SUB, SUB), SUB), :]
        nr, ni = cmul(br, bi, h[0], h[1])
        return nr + u[:, :channels], ni + u[:, channels:]

    zero = jnp.zeros((SUB, channels), F32)
    er, ei = lax.fori_loop(0, steps, step, (zero, zero), unroll=16)
    er, ei = seg_prefix(er, ei, *powers[1], group, True)
    end_ref[...] = jnp.concatenate([er, ei], axis=1)


def mix_kernel(parts, own, group, orders, *refs):
    it = iter(refs)
    take = lambda n: [next(it) for _ in range(n)]
    drive_ref, end_ref, cst_ref, ends_ref = take(4)
    cw_ref, unit_ref, cot_ref, limit_ref, vec_ref, glu_ref = take(6)
    states_ref, slow_ref, branch_ref, dglu_ref, gp_ref = take(5)
    grads = take(len(orders))
    act_ref, acc_ref = take(2)
    rows, feats = unit_ref.shape
    channels = own * parts
    steps = rows // SUB
    me = lax.axis_index("state")
    place = me + parts * (lax.axis_index("seq") & 1)
    gain, bias, skip = (vec_ref[k : k + 1, :] for k in range(3))
    pr, pi = cst_ref[0:1, :channels], cst_ref[0:1, channels:]
    qr, qi = cst_ref[1:2, :channels], cst_ref[1:2, channels:]
    wr, wi = cst_ref[2:3, :channels], cst_ref[2:3, channels:]
    dr, di = device_entry(ends_ref, me, channels, wr, wi, group, True)
    hr, hi = seg_enter(end_ref[:, :channels], end_ref[:, channels:], qr, qi, dr, di, group, True)
    states_ref[0:SUB, :] = jnp.concatenate([hr, hi], axis=1)
    br = jnp.broadcast_to(pr, (SUB, channels))
    bi = jnp.broadcast_to(pi, (SUB, channels))

    def step(j, h):
        base = pl.multiple_of(j * SUB, SUB)
        u = drive_ref[pl.ds(base, SUB), :]
        nr, ni = cmul(br, bi, h[0], h[1])
        nr, ni = nr + u[:, :channels], ni + u[:, channels:]
        at = pl.ds(pl.multiple_of(base + SUB, SUB), SUB)
        states_ref[at, :channels] = nr
        states_ref[at, channels:] = ni
        return nr, ni

    lax.fori_loop(0, steps, step, (hr, hi), unroll=16)

    kept = {}

    def mixed(c):
        states = states_ref[pl.ds(c * CHUNK + SUB, CHUNK), :]
        slow = jnp.concatenate([states[:, :channels], -states[:, channels:]], axis=1).astype(BF16)
        slow_ref[pl.ds(c * CHUNK, CHUNK), :] = slow
        kept["mixed", c] = nn(slow, cw_ref[...])

    def activate(c):
        at = pl.ds(c * CHUNK, CHUNK)
        v = kept.pop(("mixed", c)) + skip * (unit_ref[at, :] * gain + bias)
        square = v * v
        t = jnp.tanh(v * (GELU_A + (GELU_A * GELU_B) * square))
        half = 0.5 + 0.5 * t
        slope = (0.5 * GELU_A) + (1.5 * GELU_A * GELU_B) * square
        gp_ref[at, :] = half + v * (1.0 - t * t) * slope
        act = (v * half).astype(BF16)
        act_ref[at, :] = act
        kept["glu", c] = nn(act, glu_ref[...])

    def gated(c):
        at = pl.ds(c * CHUNK, CHUNK)
        glu = kept.pop(("glu", c))
        value = glu[:, :feats]
        gate = jax.nn.sigmoid(glu[:, feats:])
        branch = wide(valid(c * CHUNK // SUB, CHUNK // SUB, limit_ref), feats) * gate
        branch_ref[at, :] = branch * value
        d_value = branch * cot_ref[at, :].astype(F32)
        dglu_ref[at, :feats] = d_value.astype(BF16)
        dglu_ref[at, feats:] = (d_value * value * (1.0 - gate)).astype(BF16)

    count = rows // CHUNK
    for k in range(count + 2):
        for lag, stage in enumerate((mixed, activate, gated)):
            if 0 <= k - lag < count:
                stage(k - lag)
    width = 256

    def tile(c, carry):
        at = pl.ds(c * width, width)
        acc_ref[:, at] = tn(act_ref[...], dglu_ref[:, at])
        return carry

    repeat(0, 2 * feats // width, tile, 0)
    spread(acc_ref, place, orders, grads)


def spread(acc_ref, place, orders, grads):
    for order, ref in zip(orders, grads):
        _, size, _ = ref.shape
        for k, m in enumerate(order):
            at = pl.ds(pl.multiple_of((place ^ m) * size, size), size)
            ref[k] = acc_ref[at, :].astype(ref.dtype)


def spread_pairs(acc_ref, place, own, channels, orders, grads):
    for order, ref in zip(orders, grads):
        for k, m in enumerate(order):
            off = pl.multiple_of((place ^ m) * own, own)
            ref[k, 0:own] = acc_ref[pl.ds(off, own), :].astype(ref.dtype)
            also = pl.ds(pl.multiple_of(channels + off, own), own)
            ref[k, own : 2 * own] = acc_ref[also, :].astype(ref.dtype)


def back_kernel(own, orders, *refs):
    it = iter(refs)
    take = lambda n: [next(it) for _ in range(n)]
    dglu_ref, gp_ref, unit_ref, vec_ref, glu_ref, slow_ref = take(6)
    dpre_ref, dmix_ref, skip_ref = take(3)
    grads = take(len(orders))
    (acc_ref,) = take(1)
    rows, feats = gp_ref.shape
    place = lax.axis_index("state") + lax.axis_size("state") * (lax.axis_index("seq") & 1)
    gain, bias = vec_ref[0:1, :], vec_ref[1:2, :]

    def chunk(c, total):
        at = pl.ds(c * CHUNK, CHUNK)
        d_pre = nt(dglu_ref[at, :], glu_ref[...]) * gp_ref[at, :]
        dpre_ref[at, :] = d_pre
        normed = unit_ref[at, :] * gain + bias
        dmix_ref[at, :] = d_pre.astype(BF16)
        return total + jnp.sum((d_pre * normed).reshape(CHUNK // SUB, SUB, feats), axis=0)

    skip_ref[...] = repeat(0, rows // CHUNK, chunk, jnp.zeros((SUB, feats), F32))
    width = 256

    def tile(c, carry):
        at = pl.ds(c * width, width)
        acc_ref[:, at] = tn(slow_ref[...], dmix_ref[:, at])
        return carry

    repeat(0, feats // width, tile, 0)
    spread(acc_ref, place, orders, grads)


def starts_kernel(group, dmix_ref, cw_ref, cst_ref, dst_ref, start_ref):
    rows, feats = dmix_ref.shape
    channels = cw_ref.shape[0] // 2
    steps = rows // SUB

    def chunk(c, carry):
        at = pl.ds(c * CHUNK, CHUNK)
        dst_ref[at, :] = nt(dmix_ref[at, :], cw_ref[...])
        return carry

    repeat(0, rows // CHUNK, chunk, 0)
    br = jnp.broadcast_to(cst_ref[0:1, :channels], (SUB, channels))
    bi = jnp.broadcast_to(-cst_ref[0:1, channels:], (SUB, channels))

    def step(k, a):
        base = pl.multiple_of((steps - 1 - k) * SUB, SUB)
        u = dst_ref[pl.ds(base, SUB), :]
        nr, ni = cmul(br, bi, a[0], a[1])
        return nr + u[:, :channels], ni - u[:, channels:]

    zero = jnp.zeros((SUB, channels), F32)
    ar, ai = lax.fori_loop(0, steps, step, (zero, zero), unroll=16)
    qr, qi = cst_ref[1:2, :channels], -cst_ref[1:2, channels:]
    ar, ai = seg_prefix(ar, ai, qr, qi, group, False)
    start_ref[...] = jnp.concatenate([ar, ai], axis=1)


def adjoint_kernel(own, group, orders, *refs):
    it = iter(refs)
    take = lambda n: [next(it) for _ in range(n)]
    dst_ref, start_ref, cst_ref, ends_ref = take(4)
    states_ref, drive_ref, low_ref, limit_ref = take(4)
    dproj_ref, sums_ref = take(2)
    grads = take(len(orders))
    adj_ref, acc_ref = take(2)
    rows = dst_ref.shape[0]
    channels = dst_ref.shape[1] // 2
    steps = rows // SUB
    me = lax.axis_index("state")
    pr, pi = cst_ref[0:1, :channels], -cst_ref[0:1, channels:]
    qr, qi = cst_ref[1:2, :channels], -cst_ref[1:2, channels:]
    wr, wi = cst_ref[2:3, :channels], -cst_ref[2:3, channels:]
    dr, di = device_entry(ends_ref, me, channels, wr, wi, group, False)
    ar, ai = seg_enter(start_ref[:, :channels], start_ref[:, channels:], qr, qi, dr, di, group, False)
    br = jnp.broadcast_to(pr, (SUB, channels))
    bi = jnp.broadcast_to(pi, (SUB, channels))

    def step(k, carry):
        ar, ai, sr, si, sg = carry
        base = pl.multiple_of((steps - 1 - k) * SUB, SUB)
        at = pl.ds(base, SUB)
        d = dst_ref[at, :]
        nr, ni = cmul(br, bi, ar, ai)
        ar, ai = nr + d[:, :channels], ni - d[:, channels:]
        adj_ref[at, :channels] = ar
        adj_ref[at, channels:] = ai
        h = states_ref[at, :]
        hr, hi = h[:, :channels], h[:, channels:]
        u = drive_ref[at, :]
        sr = sr + (ar * hr + ai * hi)
        si = si + (ai * hr - ar * hi)
        sg = sg + (ar * u[:, :channels] + ai * u[:, channels:])
        return ar, ai, sr, si, sg

    zero = jnp.zeros((SUB, channels), F32)
    out = lax.fori_loop(0, steps, step, (ar, ai, zero, zero, zero), unroll=8)
    sums_ref[:, :channels] = out[2]
    sums_ref[:, channels : 2 * channels] = out[3]
    sums_ref[:, 2 * channels : 3 * channels] = out[4]
    gains = cst_ref[3:4, :]

    def chunk(c, carry):
        base = c * CHUNK
        at = pl.ds(base, CHUNK)
        mask = valid(base // SUB, CHUNK // SUB, limit_ref)
        dproj_ref[at, :] = (adj_ref[at, :] * (gains * wide(mask, 2 * channels))).astype(BF16)
        return carry

    repeat(0, rows // CHUNK, chunk, 0)
    width = 256
    feats = low_ref.shape[1]

    def tile(c, carry):
        at = pl.ds(c * width, width)
        acc_ref[:, at] = tn(dproj_ref[...], low_ref[:, at])
        return carry

    repeat(0, feats // width, tile, 0)
    spread_pairs(acc_ref, me, own, channels, orders, grads)


def send_steps(rows_of, out_hbm, out_ref, sems):
    steps = out_ref.shape[1]
    count = sems.shape[0]
    cut = steps // count
    copies = []
    for k in range(count):
        at = pl.ds(k * cut, cut)
        out_ref[:, at] = rows_out(rows_of(pl.ds(k * cut * SUB, cut * SUB)), out_ref).astype(out_ref.dtype)
        copies.append(pltpu.make_async_copy(out_ref.at[:, at], out_hbm.at[:, at], sems.at[k]))
        copies[-1].start()
    for c in copies:
        c.wait()


def out_kernel(x_ref, branch_ref, out_hbm, out_ref, sems):
    send_steps(lambda at: x_ref[at, :].astype(F32) + branch_ref[at, :], out_hbm, out_ref, sems)


def normed_kernel(dproj_ref, win_ref, dpre_ref, unit_ref, vec_ref, channel_ref, skip_ref, dnorm_ref, sums_ref):
    rows, feats = dpre_ref.shape
    skip = vec_ref[2:3, :]

    def chunk(c, carry):
        total_gain, total_bias = carry
        at = pl.ds(c * CHUNK, CHUNK)
        d_normed = dpre_ref[at, :] * skip + nn(dproj_ref[at, :], win_ref[...])
        dnorm_ref[at, :] = d_normed
        folded = lambda v: jnp.sum(v.reshape(CHUNK // SUB, SUB, feats), axis=0)
        return total_gain + folded(d_normed * unit_ref[at, :]), total_bias + folded(d_normed)

    zero = jnp.zeros((SUB, feats), F32)
    total_gain, total_bias = repeat(0, rows // CHUNK, chunk, (zero, zero))
    over = lambda v: jnp.sum(v, axis=0, keepdims=True)
    channel = over(channel_ref[...])
    wide_at = channel.shape[1] - feats
    sums_ref[0:1, :] = channel[:, :feats]
    sums_ref[1:2, :] = jnp.zeros((1, feats), F32)
    sums_ref[1:2, :wide_at] = channel[:, feats:]
    sums_ref[2:3, :] = over(total_gain)
    sums_ref[3:4, :] = over(total_bias)
    sums_ref[4:5, :] = over(skip_ref[...])
    sums_ref[5:8, :] = jnp.zeros((3, feats), F32)


def tokens_kernel(cot_ref, dnorm_ref, unit_ref, inv_ref, vec_ref, out_hbm, out_ref, sems):
    feats = dnorm_ref.shape[1]
    gain = vec_ref[0:1, :]

    def rows_of(at):
        unit = unit_ref[at, :]
        d_unit = dnorm_ref[at, :] * gain
        first = jnp.mean(d_unit, axis=1, keepdims=True)
        second = jnp.mean(d_unit * unit, axis=1, keepdims=True)
        return cot_ref[at, :].astype(F32) + wide(inv_ref[at, :], feats) * (d_unit - first - unit * second)

    send_steps(rows_of, out_hbm, out_ref, sems)


def join_pairs(parts, flat_ref, out_ref):
    own, _, feats = out_ref.shape
    for k, part in enumerate(parts):
        for c in range(feats // 128):
            flat_ref[c, pl.ds(k, own, stride=2), :] = part[:, c * 128 : (c + 1) * 128]
    rows = jnp.concatenate([flat_ref[c] for c in range(feats // 128)], axis=1)
    out_ref[...] = rows.reshape(own, 2, feats)


def halves_kernel(mine_ref, other_ref, out_ref, flat_ref):
    own = out_ref.shape[0]
    first = (lax.axis_index("seq") & 1) == 0
    a, b = mine_ref[...].astype(F32), other_ref[...].astype(F32)
    join_pairs([jnp.where(first, a, b), jnp.where(first, b, a)], flat_ref, out_ref)


def finish_kernel(total_ref, sums_ref, vec_ref, in_ref, gain_ref, bias_ref, skip_ref, rate_ref, angle_ref, level_ref, flat_ref):
    own, _, feats = in_ref.shape
    join_pairs([total_ref[:own, :], total_ref[own:, :]], flat_ref, in_ref)
    sums = sums_ref[...]
    for k, ref in enumerate((gain_ref, bias_ref, skip_ref)):
        ref[...] = sums[2 + k : 3 + k, :]
    me = lax.axis_index("state")
    channels = lax.axis_size("state") * own
    pick = lambda row: sum(
        jnp.where(me == d, row[:, d * own : (d + 1) * own], 0.0) for d in range(channels // own)
    )
    sum_re, sum_im = pick(sums[0:1, :channels]), pick(sums[0:1, channels:])
    pole_re, pole_im, decay, angle = (vec_ref[k : k + 1, :own] for k in range(3, 7))
    rate_ref[...] = -decay * (sum_re * pole_re + sum_im * pole_im)
    angle_ref[...] = angle * (sum_im * pole_re - sum_re * pole_im)
    level_ref[...] = pick(sums[1:2, :channels])


def place_kernel(masks, parts, *refs):
    arrays, out_ref, wide_ref, sems = refs[: len(masks)], refs[-3], refs[-2], refs[-1]
    place = lax.axis_index("state") + parts * (lax.axis_index("seq") & 1)
    size = arrays[0].shape[1]
    copies = []
    for ms, ref in zip(masks, arrays):
        for k, m in enumerate(ms):
            n = len(copies)
            wide_ref[n] = ref[k].astype(F32)
            at = pl.ds(pl.multiple_of((place ^ m) * size, size), size)
            copies.append(pltpu.make_async_copy(wide_ref.at[n], out_ref.at[at, :], sems.at[n]))
            copies[-1].start()
    for c in copies:
        c.wait()


def place_blocks(arrays, masks, parts, shape, out=None):
    count = sum(len(m) for m in masks)
    _, size, width = arrays[0].shape
    ins = list(arrays) + ([] if out is None else [out])
    specs = [pl.BlockSpec(memory_space=pltpu.VMEM)] * len(arrays)
    specs += [pl.BlockSpec(memory_space=pl.ANY)] * (len(ins) - len(arrays))
    return pl.pallas_call(
        functools.partial(place_kernel, masks, parts),
        out_shape=jax.ShapeDtypeStruct(shape, F32),
        in_specs=specs,
        out_specs=pl.BlockSpec(memory_space=pl.ANY),
        scratch_shapes=[pltpu.VMEM((count, size, width), F32), pltpu.SemaphoreType.DMA((count,))],
        input_output_aliases={} if out is None else {len(arrays): 0},
        compiler_params=pltpu.CompilerParams(vmem_limit_bytes=8 * MIB),
        cost_estimate=pl.CostEstimate(flops=MIB, bytes_accessed=2 * MIB, transcendentals=0),
        name="place",
    )(*ins)


def exchange(x, mask):
    count = lax.axis_size("seq") * lax.axis_size("state")
    return lax.ppermute(x, ("seq", "state"), [(i, i ^ mask) for i in range(count)])


def tie(x, *after):
    return lax.optimization_barrier((x, after))[0]


def bits_of(n):
    return [1 << k for k in range(n.bit_length() - 1)]


def submasks(group):
    out = [0]
    for bit in group:
        out += [m | bit for m in out]
    return out[1:]


def stage_orders(groups):
    kept = [0]
    stages = []
    for group in reversed(groups):
        sends = [[m ^ p for m in kept] for p in submasks(group)]
        stages.insert(0, sends)
        kept = sum(sends, []) + kept
    return [o for sends in stages for o in sends] + [[0]]


def swap(parts, group):
    masks = submasks(group)
    return [exchange(p.astype(BF16), m) for p, m in zip(parts, masks)]


def add_up(parts, got):
    rest, off = [], 0
    for p in parts[len(got) :]:
        n = p.shape[0]
        total = p.astype(F32)
        for g in got:
            total = total + g[off : off + n].astype(F32)
        rest.append(total)
        off += n
    return rest


def halve(parts, group):
    return add_up(parts, swap(parts, group))


def rounded(x):
    return lax.reduce_precision(x, 8, 7)


def two_parts(x):
    high = rounded(x)
    return [high.astype(BF16), rounded(x - high).astype(BF16)]


def sum_of(parts):
    return parts[0].astype(F32) + parts[1].astype(F32)


def gather_ends(end, bits):
    g = end[None]
    for bit in reversed(bits):
        g = jnp.stack([g, exchange(g, bit)], axis=1).reshape((2 * g.shape[0],) + end.shape)
    return g


def gather_blocks(arrays, bits, ready=None):
    blocks = [{0: a} for a in arrays]
    for n, bit in enumerate(reversed(bits)):
        for held_blocks in blocks:
            for m in list(held_blocks):
                x = held_blocks[m]
                if m and n and ready is not None:
                    x = tie(x, ready)
                held_blocks[m ^ bit] = exchange(x, bit)
    return [[b[m] for m in range(len(b))] for b in blocks]


def shards(
    tokens,
    norm_gain,
    norm_bias,
    input_weight,
    output_weight,
    log_rate,
    log_angle,
    log_gain,
    skip_gain,
    glu_weight,
    lengths,
    cotangent,
):
    span, group, feats = tokens.shape
    own = log_rate.shape[0]
    parts = lax.axis_size("state")
    n_seq = lax.axis_size("seq")
    channels = own * parts
    rows = span * group
    segs = SUB // group
    me = lax.axis_index("state")
    state_bits = bits_of(parts)
    seq_masks = [parts * b for b in bits_of(n_seq)]
    if len(seq_masks) > 2:
        seq_masks[-1] |= seq_masks[-2]
    full = rows * feats * 2 * channels * 2

    flat = pltpu.VMEM((feats // 128, 2 * own, 128), F32)
    x4 = tokens.reshape(segs, span // segs, group, feats)
    cot4 = cotangent.reshape(segs, span // segs, group, feats)
    small = jnp.concatenate([norm_gain, norm_bias, skip_gain, log_rate, log_angle, log_gain])
    small = small.reshape(1, -1)
    small_own, vec = call(
        functools.partial(prep_kernel, own),
        [((PARAM_ROWS // 2, 2, feats), BF16), ((SUB, feats), F32)],
        [small],
        [],
        8,
        MIB,
        "prep",
    )
    b_own = jnp.concatenate([input_weight.transpose(1, 2, 0), small_own], axis=0)
    low, unit, inv, x_rows = call(
        norm_kernel,
        [((rows, feats), BF16), ((rows, feats), F32), ((rows, 128), F32), ((rows, feats), BF16)],
        [x4, vec],
        [held(x4), pltpu.SemaphoreType.DMA((4,))],
        12,
        rows * feats * 20,
        "norm",
        fetched=(0,),
    )
    (limit,) = call(
        functools.partial(limit_kernel, group, rows // SUB),
        [((SUB, 128), jnp.int32)],
        [tie(lengths, low)],
        [],
        8,
        MIB,
        "limit",
    )
    b_blocks, c_blocks = gather_blocks([b_own, tie(output_weight, b_own)], state_bits, (low, limit))
    drive, end, win, cst = call(
        functools.partial(project_kernel, parts, own, group),
        [
            ((rows, 2 * channels), F32),
            ((SUB, 2 * channels), F32),
            ((2 * channels, feats), BF16),
            ((SUB, 2 * channels), F32),
        ],
        [low, limit] + b_blocks,
        [flat],
        12,
        full,
        "project",
    )
    ends = gather_ends(end, state_bits)
    (cot,) = call(cotangent_kernel, [((rows, feats), BF16)], [tie(cot4, end)], [], 8, MIB, "cotangent")
    (cw,) = call(
        weights_kernel,
        [((2 * channels, feats), BF16)],
        [tie(c_blocks[0], end)] + c_blocks[1:],
        [flat],
        8,
        MIB,
        "weights",
    )
    all_bits = state_bits + [parts]
    all_groups = [all_bits[:1]] + [all_bits[k : k + 2] for k in range(1, len(all_bits), 2)]
    all_orders = stage_orders(all_groups)
    glu_rows = feats // (2 * parts)
    block_outs = lambda rows, width, orders: [
        ((len(o), rows, width), BF16 if k == 0 else F32) for k, o in enumerate(orders)
    ]
    states, slow, branch, d_glu, slope, *glu_parts = call(
        functools.partial(mix_kernel, parts, own, group, all_orders),
        [
            ((rows + SUB, 2 * channels), F32),
            ((rows, 2 * channels), BF16),
            ((rows, feats), F32),
            ((rows, 2 * feats), BF16),
            ((rows, feats), F32),
        ]
        + block_outs(glu_rows, 2 * feats, all_orders),
        [drive, end, cst, ends, cw, unit, cot, limit, vec, glu_weight],
        [pltpu.VMEM((rows, feats), BF16), pltpu.VMEM((feats, 2 * feats), F32)],
        20,
        5 * full,
        "mix",
    )
    d_pre, d_mixed, skip_sum, *out_parts = call(
        functools.partial(back_kernel, own, all_orders),
        [((rows, feats), F32), ((rows, feats), BF16), ((SUB, feats), F32)]
        + block_outs(own, feats, all_orders),
        [d_glu, slope, unit, vec, glu_weight, slow],
        [pltpu.VMEM((2 * channels, feats), F32)],
        16,
        3 * full,
        "back",
    )
    d_states, start = call(
        functools.partial(starts_kernel, group),
        [((rows, 2 * channels), F32), ((SUB, 2 * channels), F32)],
        [d_mixed, cw, cst],
        [],
        12,
        full,
        "starts",
    )
    got = swap(glu_parts, all_groups[0])
    more = swap(out_parts, all_groups[0])
    starts = gather_ends(tie(start, got, more), state_bits)
    got, more = tie((got, more), start)
    glu_parts, out_parts = add_up(glu_parts, got), add_up(out_parts, more)
    both = [jnp.concatenate(p, axis=-1) for p in zip(glu_parts, out_parts)]
    state_groups = [[b] for b in state_bits]
    pair_orders = stage_orders(state_groups)
    d_proj, channel_sums, *in_parts = call(
        functools.partial(adjoint_kernel, own, group, pair_orders),
        [((rows, 2 * channels), BF16), ((SUB, 3 * channels), F32)]
        + block_outs(2 * own, feats, pair_orders),
        [tie(d_states, both), start, cst, starts, states, drive, low, limit],
        [pltpu.VMEM((rows, 2 * channels), F32), pltpu.VMEM((2 * channels, feats), F32)],
        16,
        2 * full,
        "adjoint",
    )
    in_parts = halve(in_parts, state_groups[0])
    d_normed, sums = call(
        normed_kernel,
        [((rows, feats), F32), ((SUB, feats), F32)],
        [d_proj, win, d_pre, unit, vec, channel_sums, skip_sum],
        [],
        12,
        full,
        "normed",
    )
    class chain:
        parts, total, held = in_parts, None, sums
        masks = state_bits[1:] + seq_masks[:1] + seq_masks[:0:-1]
        sent = []

        def send(after=()):
            chain.two = two_parts(chain.held)
            if len(chain.parts) > 1:
                chain.low = chain.parts[0].astype(BF16).reshape(-1, feats)
            else:
                chain.low = rounded(chain.parts[0][0]).astype(BF16)
            chain.sent.append(tie(jnp.concatenate([chain.low] + chain.two, axis=0), after))

        def take():
            got = exchange(chain.sent[-1], chain.masks[len(chain.sent) - 1])
            chain.got, rest, off = got, [], 0
            if len(chain.parts) > 1:
                for p in chain.parts[1:]:
                    n = p.shape[0] * p.shape[1]
                    rest.append(p + got[off : off + n].reshape(p.shape).astype(F32))
                    off += n
            else:
                off = 2 * own
                rest.append((chain.low.astype(F32) + got[:off].astype(F32))[None])
            chain.parts = rest
            chain.held = sum_of(chain.two) + sum_of([got[off : off + SUB], got[off + SUB :]])

    chain.send()
    for g in all_groups[1:]:
        got = swap(both, g)
        both = add_up(both, tie(got, chain.sent[-1]))
    both = both[0][0]
    (grad4,) = call(
        tokens_kernel,
        [(cot4.shape, F32)],
        [cot, tie(d_normed, both, chain.sent[-1]), unit, inv, vec],
        [pltpu.VMEM(cot4.shape, F32), pltpu.SemaphoreType.DMA((8,))],
        12,
        full,
        "tokens",
        sent=True,
    )
    (out4,) = call(
        out_kernel,
        [(x4.shape, BF16)],
        [x_rows, tie(branch, both, chain.sent[-1])],
        [held(x4), pltpu.SemaphoreType.DMA((8,))],
        8,
        MIB,
        "out",
        sent=True,
    )
    chain.take()
    chain.held = chain.held + exchange(chain.held, state_bits[0])
    chain.send()
    glu_masks = seq_masks[:0:-1]
    for n, m in enumerate(glu_masks):
        mine = rounded(both).astype(BF16)
        got = exchange(mine, m)
        if n:
            chain.take()
            chain.send(mine)
        got = tie(got, chain.sent[-1], grad4, out4)
        both = mine.astype(F32) + got.astype(F32)
    both = rounded(both).astype(BF16)
    while len(chain.sent) < len(chain.masks):
        chain.take()
        chain.send(both)
    chain.take()
    last = chain.got
    grad_in, grad_gain, grad_bias, grad_skip, grad_rate, grad_angle, grad_level = call(
        finish_kernel,
        [((own, 2, feats), F32)] + [((1, feats), F32)] * 3 + [((1, own), F32)] * 3,
        [chain.parts[0][0], chain.held, vec],
        [flat],
        8,
        MIB,
        "finish",
    )
    blocks = {0: both[:, : 2 * feats]}
    for g in reversed(all_groups[1:]):
        for m in list(blocks):
            for p in submasks(g):
                if m == 0 and p == parts:
                    got = exchange(both, p)
                    blocks[p] = got[:, : 2 * feats]
                    other_half = got[:, 2 * feats :]
                else:
                    blocks[m ^ p] = exchange(blocks[m], p)
    far_own = [exchange(blocks[0][None], p) for p in submasks(all_groups[0])]
    (grad_out,) = call(
        halves_kernel,
        [((own, 2, feats), F32)],
        [both[:, 2 * feats :], tie(other_half, far_own)],
        [flat],
        8,
        MIB,
        "halves",
    )
    rest = [m for m in blocks if m]
    near = [blocks[0][None], jnp.stack(tie([blocks[m] for m in rest], grad_out, chain.sent[-1]))]
    near_masks = [[0], rest]
    far = [f for p, o in zip(submasks(all_groups[0]), far_own) for f in (o, exchange(near[1], p))]
    far_masks = [[m ^ p for m in ms] for p in submasks(all_groups[0]) for ms in near_masks]
    grad_glu = place_blocks(near, near_masks, parts, (feats, 2 * feats))
    grad_glu = place_blocks(tie(far, grad_in), far_masks, parts, (feats, 2 * feats), grad_glu)
    return (
        out4.reshape(tokens.shape),
        grad4.reshape(tokens.shape),
        grad_gain.reshape(feats),
        grad_bias.reshape(feats),
        grad_in.transpose(2, 0, 1),
        grad_out,
        grad_rate.reshape(own),
        grad_angle.reshape(own),
        grad_level.reshape(own),
        grad_skip.reshape(feats),
        grad_glu,
    )


def solution(mesh):
    placed = (
        P("state", "seq", None),
        P(),
        P(),
        P(None, "state", None),
        P("state", None, None),
        P("state"),
        P("state"),
        P("state"),
        P(),
        P(),
        P("seq"),
        P("state", "seq", None),
    )
    return jax.shard_map(
        shards,
        mesh=mesh,
        in_specs=placed,
        out_specs=(
            P("state", "seq", None),
            P("state", "seq", None),
            P(),
            P(),
            P(None, "state", None),
            P("state", None, None),
            P("state"),
            P("state"),
            P("state"),
            P(),
            P(),
        ),
        check_vma=False,
    )
```

```python
import functools

import jax
import jax.numpy as jnp
from jax import lax
from jax.experimental import pallas as pl
from jax.experimental.pallas import tpu as pltpu
from jax.sharding import PartitionSpec as P

F32, BF16 = jnp.float32, jnp.bfloat16
EPSILON = 1e-05
SUB = 8
CHUNK = 512
PARAM_ROWS = 16
GELU_A = 0.7978845608028654
GELU_B = 0.044715
MIB = 1 << 20


def repeat(first, last, body, carry):
    for k in range(first, last):
        carry = body(k, carry)
    return carry


def cmul(ar, ai, br, bi):
    return ar * br - ai * bi, ar * bi + ai * br


def nn(a, b):
    return lax.dot_general(a, b, (((1,), (0,)), ((), ())), preferred_element_type=F32)


def nt(a, b):
    return lax.dot_general(a, b, (((1,), (1,)), ((), ())), preferred_element_type=F32)


def tn(a, b):
    return lax.dot_general(a, b, (((0,), (0,)), ((), ())), preferred_element_type=F32)


def rows_in(ref, first, count):
    segs, _, group, feats = ref.shape
    x = ref[:, pl.ds(first, count)].astype(F32)
    return x.transpose(1, 0, 2, 3).reshape(count * segs * group, feats)


def rows_out(y, ref):
    segs, _, group, feats = ref.shape
    return y.reshape(y.shape[0] // SUB, segs, group, feats).transpose(1, 0, 2, 3)


def valid(first, count, limit_ref):
    step = lax.broadcasted_iota(jnp.int32, (count, SUB, 128), 0) + first
    return (step < limit_ref[...][None]).astype(F32).reshape(count * SUB, 128)


def wide(column, lanes):
    return jnp.concatenate([column] * (lanes // column.shape[1]), axis=1)


def call(body, outs, ins, scratch, limit_mib, flops, name, fetched=(), sent=False):
    specs = []
    for k, x in enumerate(ins):
        space = pltpu.SMEM if x.ndim == 1 else pl.ANY if k in fetched else pltpu.VMEM
        specs.append(pl.BlockSpec(memory_space=space))
    return pl.pallas_call(
        body,
        out_shape=[jax.ShapeDtypeStruct(s, d) for s, d in outs],
        in_specs=specs,
        out_specs=[pl.BlockSpec(memory_space=pl.ANY if sent else pltpu.VMEM)] * len(outs),
        scratch_shapes=scratch,
        compiler_params=pltpu.CompilerParams(vmem_limit_bytes=limit_mib * MIB),
        cost_estimate=pl.CostEstimate(flops=flops, bytes_accessed=4 * MIB, transcendentals=0),
        name=name,
    )(*ins)


def start_copies(sources, targets, sems):
    copies = [pltpu.make_async_copy(a, b, sems.at[k]) for k, (a, b) in enumerate(zip(sources, targets))]
    for c in copies:
        c.start()
    return copies


def held(x):
    return pltpu.VMEM(x.shape, x.dtype)


def split_pairs(pairs_ref, flat_ref):
    own, _, feats = pairs_ref.shape
    flat = pairs_ref[...].astype(F32).reshape(2 * own, feats)
    for c in range(feats // 128):
        flat_ref[c] = flat[:, c * 128 : (c + 1) * 128]
    take = lambda k: [flat_ref[c, pl.ds(k, own, stride=2), :] for c in range(feats // 128)]
    return [jnp.concatenate(take(k), axis=1).astype(BF16) for k in range(2)]


def three_parts(x):
    high = x.astype(BF16)
    rest = x - high.astype(F32)
    mid = rest.astype(BF16)
    return [high, mid, (rest - mid.astype(F32)).astype(BF16)]


def prep_kernel(own, small_ref, pay_ref, vec_ref):
    feats = vec_ref.shape[1]
    me = lax.axis_index("state")
    lane = lax.broadcasted_iota(jnp.int32, (1, feats), 1)
    mine = (lane // own) == me
    base = 3 * feats
    logs = [small_ref[:, base + k * own : base + (k + 1) * own] for k in range(3)]
    rate, turn, level = (jnp.concatenate([v] * (feats // own), axis=1) for v in logs)
    decay = jnp.exp(rate)
    size = jnp.exp(-decay)
    angle = jnp.exp(turn)
    pole_re, pole_im = size * jnp.cos(angle), size * jnp.sin(angle)
    parts = []
    for v in (pole_re, pole_im, jnp.exp(level)):
        parts += three_parts(jnp.where(mine, v, 0.0))
    parts += [jnp.zeros((PARAM_ROWS - len(parts), feats), BF16)]
    flat = jnp.concatenate([p.astype(F32) for p in parts], axis=0)
    pay_ref[...] = flat.reshape(PARAM_ROWS // 2, 2, feats).astype(BF16)
    rows = [small_ref[:, k * feats : (k + 1) * feats] for k in range(3)] + [pole_re, pole_im, decay, angle]
    for k, row in enumerate(rows):
        vec_ref[k : k + 1, :] = row
    vec_ref[len(rows) :, :] = jnp.zeros((SUB - len(rows), feats), F32)


def cotangent_kernel(cot_ref, rows_ref):
    steps = 16
    for c in range(cot_ref.shape[1] // steps):
        at = pl.ds(c * steps * SUB, steps * SUB)
        rows_ref[at, :] = rows_in(cot_ref, c * steps, steps).astype(BF16)


def weights_kernel(*refs):
    blocks, (out_ref, flat_ref) = refs[:-2], refs[-2:]
    gather_rows(lax.axis_index("state"), blocks, flat_ref, out_ref)


def limit_kernel(group, steps, lens_ref, limit_ref):
    segs = SUB // group
    place = lax.broadcasted_iota(jnp.int32, (SUB, 128), 0)
    seq = place & (group - 1)
    length = jnp.full((SUB, 128), lens_ref[0], jnp.int32)
    for k in range(1, group):
        length = jnp.where(seq == k, lens_ref[k], length)
    limit_ref[...] = length - (lax.axis_index("state") * segs + place // group) * steps


def norm_kernel(x_hbm, vec_ref, low_ref, unit_ref, inv_ref, rows_ref, x_ref, sems):
    segs, steps, group, feats = x_ref.shape
    rows = steps * SUB
    size = 128
    gain, bias = vec_ref[0:1, :], vec_ref[1:2, :]
    cut = steps // 4
    places = [pl.ds(k * cut, cut) for k in range(4)]
    copies = start_copies([x_hbm.at[:, p] for p in places], [x_ref.at[:, p] for p in places], sems)

    def chunk(c, carry):
        at = pl.ds(c * size, size)
        x = rows_in(x_ref, c * (size // SUB), size // SUB)
        rows_ref[at, :] = x.astype(BF16)
        centred = x - jnp.mean(x, axis=1, keepdims=True)
        inv = lax.rsqrt(jnp.mean(centred * centred, axis=1, keepdims=True) + EPSILON)
        unit = centred * inv
        unit_ref[at, :] = unit
        low_ref[at, :] = (unit * gain + bias).astype(BF16)
        inv_ref[at, :] = jnp.broadcast_to(inv, (size, 128))
        return carry

    turns = rows // size // 4
    for k in range(4):
        copies[k].wait()
        repeat(k * turns, (k + 1) * turns, chunk, 0)


def gather_rows(me, blocks, flat_ref, dst_ref):
    own = flat_ref.shape[1] // 2
    channels = own * len(blocks)
    for m, block in enumerate(blocks):
        for k, part in enumerate(split_pairs(block.at[0:own], flat_ref)):
            at = pl.multiple_of(k * channels + (me ^ m) * own, own)
            dst_ref[pl.ds(at, own), :] = part


def seg_of(group):
    row = lax.broadcasted_iota(jnp.int32, (SUB, 128), 0)
    return row // group


def shift_rows(x, by, keep):
    return jnp.where(wide(keep, x.shape[1]), pltpu.roll(x, by % SUB, 0), 0.0)


def seg_prefix(xr, xi, qr, qi, group, forward):
    seg = seg_of(group)
    segs = SUB // group
    dist = 1
    while dist < segs:
        by = group * dist if forward else SUB - group * dist
        keep = seg >= dist if forward else seg < segs - dist
        sr, si = shift_rows(xr, by, keep), shift_rows(xi, by, keep)
        ar, ai = cmul(qr, qi, sr, si)
        xr, xi = xr + ar, xi + ai
        qr, qi = cmul(qr, qi, qr, qi)
        dist *= 2
    return xr, xi


def seg_enter(xr, xi, qr, qi, dr, di, group, forward):
    seg = seg_of(group)
    segs = SUB // group
    by = group if forward else SUB - group
    keep = seg >= 1 if forward else seg < segs - 1
    er, ei = shift_rows(xr, by, keep), shift_rows(xi, by, keep)
    gap = seg if forward else segs - 1 - seg
    pr, pi = jnp.ones_like(er), jnp.zeros_like(ei)
    bit = 1
    while bit < segs:
        nr, ni = cmul(pr, pi, qr, qi)
        take = wide((gap & bit) != 0, er.shape[1])
        pr, pi = jnp.where(take, nr, pr), jnp.where(take, ni, pi)
        qr, qi = cmul(qr, qi, qr, qi)
        bit *= 2
    ar, ai = cmul(pr, pi, dr, di)
    return er + ar, ei + ai


def device_entry(ends_ref, me, channels, qr, qi, group, forward):
    seg = seg_of(group)
    segs = SUB // group
    parts = ends_ref.shape[0]
    keep = wide(seg == (segs - 1 if forward else 0), channels)
    tr = ti = jnp.zeros((SUB, channels), F32)
    for device in range(parts - 1) if forward else range(parts - 1, 0, -1):
        end = ends_ref[me ^ device]
        nr, ni = cmul(tr, ti, qr, qi)
        counts = device < me if forward else device > me
        tr = jnp.where(counts, nr + end[:, :channels], tr)
        ti = jnp.where(counts, ni + end[:, channels:], ti)
    out = []
    for x in (tr, ti):
        x = jnp.where(keep, x, 0.0)
        y = x
        for k in range(1, segs):
            y = y + pltpu.roll(x, group * k, 0)
        out.append(y)
    return out


def project_kernel(parts, own, group, low_ref, limit_ref, *refs):
    blocks = refs[:parts]
    drive_ref, end_ref, win_ref, cst_ref, flat_ref = refs[parts:]
    rows = low_ref.shape[0]
    channels = own * parts
    steps = rows // SUB
    me = lax.axis_index("state")
    gather_rows(me, blocks, flat_ref, win_ref)
    rows_of = []
    for k in range(3):
        total = None
        for block in blocks:
            tile = block[own : own + PARAM_ROWS // 2].astype(F32).reshape(PARAM_ROWS, -1)
            for part in range(3):
                piece = tile[3 * k + part : 3 * k + part + 1, :channels]
                total = piece if total is None else total + piece
        rows_of.append(total)
    pr, pi, gain = rows_of
    powers = [(pr, pi)]
    span = steps * (SUB // group)
    ar, ai = pr, pi
    count = 1
    while count < span:
        ar, ai = cmul(ar, ai, ar, ai)
        count *= 2
        if count in (steps, span):
            powers.append((ar, ai))
    while len(powers) < 3:
        powers.append(powers[-1])
    for k, (r, i) in enumerate(powers):
        cst_ref[k : k + 1, :] = jnp.concatenate([r, i], axis=1)
    gains = jnp.concatenate([gain, gain], axis=1)
    cst_ref[3:4, :] = gains
    cst_ref[4:8, :] = jnp.zeros((4, 2 * channels), F32)

    def chunk(c, carry):
        base = c * CHUNK
        at = pl.ds(base, CHUNK)
        mask = valid(base // SUB, CHUNK // SUB, limit_ref)
        drive_ref[at, :] = nt(low_ref[at, :], win_ref[...]) * (gains * wide(mask, 2 * channels))
        return carry

    repeat(0, rows // CHUNK, chunk, 0)
    br = jnp.broadcast_to(pr, (SUB, channels))
    bi = jnp.broadcast_to(pi, (SUB, channels))

    def step(j, h):
        u = drive_ref[pl.ds(pl.multiple_of(j * SUB, SUB), SUB), :]
        nr, ni = cmul(br, bi, h[0], h[1])
        return nr + u[:, :channels], ni + u[:, channels:]

    zero = jnp.zeros((SUB, channels), F32)
    er, ei = lax.fori_loop(0, steps, step, (zero, zero), unroll=16)
    er, ei = seg_prefix(er, ei, *powers[1], group, True)
    end_ref[...] = jnp.concatenate([er, ei], axis=1)


def mix_kernel(parts, own, group, orders, *refs):
    it = iter(refs)
    take = lambda n: [next(it) for _ in range(n)]
    drive_ref, end_ref, cst_ref, ends_ref = take(4)
    cw_ref, unit_ref, cot_ref, limit_ref, vec_ref, glu_ref = take(6)
    states_ref, slow_ref, branch_ref, dglu_ref, gp_ref = take(5)
    grads = take(len(orders))
    act_ref, acc_ref = take(2)
    rows, feats = unit_ref.shape
    channels = own * parts
    steps = rows // SUB
    me = lax.axis_index("state")
    place = me + parts * (lax.axis_index("seq") & 1)
    gain, bias, skip = (vec_ref[k : k + 1, :] for k in range(3))
    pr, pi = cst_ref[0:1, :channels], cst_ref[0:1, channels:]
    qr, qi = cst_ref[1:2, :channels], cst_ref[1:2, channels:]
    wr, wi = cst_ref[2:3, :channels], cst_ref[2:3, channels:]
    dr, di = device_entry(ends_ref, me, channels, wr, wi, group, True)
    hr, hi = seg_enter(end_ref[:, :channels], end_ref[:, channels:], qr, qi, dr, di, group, True)
    states_ref[0:SUB, :] = jnp.concatenate([hr, hi], axis=1)
    br = jnp.broadcast_to(pr, (SUB, channels))
    bi = jnp.broadcast_to(pi, (SUB, channels))

    def step(j, h):
        base = pl.multiple_of(j * SUB, SUB)
        u = drive_ref[pl.ds(base, SUB), :]
        nr, ni = cmul(br, bi, h[0], h[1])
        nr, ni = nr + u[:, :channels], ni + u[:, channels:]
        at = pl.ds(pl.multiple_of(base + SUB, SUB), SUB)
        states_ref[at, :channels] = nr
        states_ref[at, channels:] = ni
        return nr, ni

    lax.fori_loop(0, steps, step, (hr, hi), unroll=16)

    kept = {}

    def mixed(c):
        states = states_ref[pl.ds(c * CHUNK + SUB, CHUNK), :]
        slow = jnp.concatenate([states[:, :channels], -states[:, channels:]], axis=1).astype(BF16)
        slow_ref[pl.ds(c * CHUNK, CHUNK), :] = slow
        kept["mixed", c] = nn(slow, cw_ref[...])

    def activate(c):
        at = pl.ds(c * CHUNK, CHUNK)
        v = kept.pop(("mixed", c)) + skip * (unit_ref[at, :] * gain + bias)
        square = v * v
        t = jnp.tanh(v * (GELU_A + (GELU_A * GELU_B) * square))
        half = 0.5 + 0.5 * t
        slope = (0.5 * GELU_A) + (1.5 * GELU_A * GELU_B) * square
        gp_ref[at, :] = half + v * (1.0 - t * t) * slope
        act = (v * half).astype(BF16)
        act_ref[at, :] = act
        kept["glu", c] = nn(act, glu_ref[...])

    def gated(c):
        at = pl.ds(c * CHUNK, CHUNK)
        glu = kept.pop(("glu", c))
        value = glu[:, :feats]
        gate = jax.nn.sigmoid(glu[:, feats:])
        branch = wide(valid(c * CHUNK // SUB, CHUNK // SUB, limit_ref), feats) * gate
        branch_ref[at, :] = branch * value
        d_value = branch * cot_ref[at, :].astype(F32)
        dglu_ref[at, :feats] = d_value.astype(BF16)
        dglu_ref[at, feats:] = (d_value * value * (1.0 - gate)).astype(BF16)

    count = rows // CHUNK
    for k in range(count + 2):
        for lag, stage in enumerate((mixed, activate, gated)):
            if 0 <= k - lag < count:
                stage(k - lag)
    width = 256

    def tile(c, carry):
        at = pl.ds(c * width, width)
        acc_ref[:, at] = tn(act_ref[...], dglu_ref[:, at])
        return carry

    repeat(0, 2 * feats // width, tile, 0)
    spread(acc_ref, place, orders, grads)


def spread(acc_ref, place, orders, grads):
    for order, ref in zip(orders, grads):
        _, size, _ = ref.shape
        for k, m in enumerate(order):
            at = pl.ds(pl.multiple_of((place ^ m) * size, size), size)
            ref[k] = acc_ref[at, :].astype(ref.dtype)


def spread_pairs(acc_ref, place, own, channels, orders, grads):
    for order, ref in zip(orders, grads):
        for k, m in enumerate(order):
            off = pl.multiple_of((place ^ m) * own, own)
            ref[k, 0:own] = acc_ref[pl.ds(off, own), :].astype(ref.dtype)
            also = pl.ds(pl.multiple_of(channels + off, own), own)
            ref[k, own : 2 * own] = acc_ref[also, :].astype(ref.dtype)


def back_kernel(own, orders, *refs):
    it = iter(refs)
    take = lambda n: [next(it) for _ in range(n)]
    dglu_ref, gp_ref, unit_ref, vec_ref, glu_ref, slow_ref = take(6)
    dpre_ref, dmix_ref, skip_ref = take(3)
    grads = take(len(orders))
    (acc_ref,) = take(1)
    rows, feats = gp_ref.shape
    place = lax.axis_index("state") + lax.axis_size("state") * (lax.axis_index("seq") & 1)
    gain, bias = vec_ref[0:1, :], vec_ref[1:2, :]

    def chunk(c, total):
        at = pl.ds(c * CHUNK, CHUNK)
        d_pre = nt(dglu_ref[at, :], glu_ref[...]) * gp_ref[at, :]
        dpre_ref[at, :] = d_pre
        normed = unit_ref[at, :] * gain + bias
        dmix_ref[at, :] = d_pre.astype(BF16)
        return total + jnp.sum((d_pre * normed).reshape(CHUNK // SUB, SUB, feats), axis=0)

    skip_ref[...] = repeat(0, rows // CHUNK, chunk, jnp.zeros((SUB, feats), F32))
    width = 256

    def tile(c, carry):
        at = pl.ds(c * width, width)
        acc_ref[:, at] = tn(slow_ref[...], dmix_ref[:, at])
        return carry

    repeat(0, feats // width, tile, 0)
    spread(acc_ref, place, orders, grads)


def starts_kernel(group, dmix_ref, cw_ref, cst_ref, dst_ref, start_ref):
    rows, feats = dmix_ref.shape
    channels = cw_ref.shape[0] // 2
    steps = rows // SUB

    def chunk(c, carry):
        at = pl.ds(c * CHUNK, CHUNK)
        dst_ref[at, :] = nt(dmix_ref[at, :], cw_ref[...])
        return carry

    repeat(0, rows // CHUNK, chunk, 0)
    br = jnp.broadcast_to(cst_ref[0:1, :channels], (SUB, channels))
    bi = jnp.broadcast_to(-cst_ref[0:1, channels:], (SUB, channels))

    def step(k, a):
        base = pl.multiple_of((steps - 1 - k) * SUB, SUB)
        u = dst_ref[pl.ds(base, SUB), :]
        nr, ni = cmul(br, bi, a[0], a[1])
        return nr + u[:, :channels], ni - u[:, channels:]

    zero = jnp.zeros((SUB, channels), F32)
    ar, ai = lax.fori_loop(0, steps, step, (zero, zero), unroll=16)
    qr, qi = cst_ref[1:2, :channels], -cst_ref[1:2, channels:]
    ar, ai = seg_prefix(ar, ai, qr, qi, group, False)
    start_ref[...] = jnp.concatenate([ar, ai], axis=1)


def adjoint_kernel(own, group, orders, *refs):
    it = iter(refs)
    take = lambda n: [next(it) for _ in range(n)]
    dst_ref, start_ref, cst_ref, ends_ref = take(4)
    states_ref, drive_ref, low_ref, limit_ref = take(4)
    dproj_ref, sums_ref = take(2)
    grads = take(len(orders))
    adj_ref, acc_ref = take(2)
    rows = dst_ref.shape[0]
    channels = dst_ref.shape[1] // 2
    steps = rows // SUB
    me = lax.axis_index("state")
    pr, pi = cst_ref[0:1, :channels], -cst_ref[0:1, channels:]
    qr, qi = cst_ref[1:2, :channels], -cst_ref[1:2, channels:]
    wr, wi = cst_ref[2:3, :channels], -cst_ref[2:3, channels:]
    dr, di = device_entry(ends_ref, me, channels, wr, wi, group, False)
    ar, ai = seg_enter(start_ref[:, :channels], start_ref[:, channels:], qr, qi, dr, di, group, False)
    br = jnp.broadcast_to(pr, (SUB, channels))
    bi = jnp.broadcast_to(pi, (SUB, channels))

    def step(k, carry):
        ar, ai, sr, si, sg = carry
        base = pl.multiple_of((steps - 1 - k) * SUB, SUB)
        at = pl.ds(base, SUB)
        d = dst_ref[at, :]
        nr, ni = cmul(br, bi, ar, ai)
        ar, ai = nr + d[:, :channels], ni - d[:, channels:]
        adj_ref[at, :channels] = ar
        adj_ref[at, channels:] = ai
        h = states_ref[at, :]
        hr, hi = h[:, :channels], h[:, channels:]
        u = drive_ref[at, :]
        sr = sr + (ar * hr + ai * hi)
        si = si + (ai * hr - ar * hi)
        sg = sg + (ar * u[:, :channels] + ai * u[:, channels:])
        return ar, ai, sr, si, sg

    zero = jnp.zeros((SUB, channels), F32)
    out = lax.fori_loop(0, steps, step, (ar, ai, zero, zero, zero), unroll=8)
    sums_ref[:, :channels] = out[2]
    sums_ref[:, channels : 2 * channels] = out[3]
    sums_ref[:, 2 * channels : 3 * channels] = out[4]
    gains = cst_ref[3:4, :]

    def chunk(c, carry):
        base = c * CHUNK
        at = pl.ds(base, CHUNK)
        mask = valid(base // SUB, CHUNK // SUB, limit_ref)
        dproj_ref[at, :] = (adj_ref[at, :] * (gains * wide(mask, 2 * channels))).astype(BF16)
        return carry

    repeat(0, rows // CHUNK, chunk, 0)
    width = 256
    feats = low_ref.shape[1]

    def tile(c, carry):
        at = pl.ds(c * width, width)
        acc_ref[:, at] = tn(dproj_ref[...], low_ref[:, at])
        return carry

    repeat(0, feats // width, tile, 0)
    spread_pairs(acc_ref, me, own, channels, orders, grads)


def send_steps(rows_of, out_hbm, out_ref, sems):
    steps = out_ref.shape[1]
    count = sems.shape[0]
    cut = steps // count
    copies = []
    for k in range(count):
        at = pl.ds(k * cut, cut)
        out_ref[:, at] = rows_out(rows_of(pl.ds(k * cut * SUB, cut * SUB)), out_ref).astype(out_ref.dtype)
        copies.append(pltpu.make_async_copy(out_ref.at[:, at], out_hbm.at[:, at], sems.at[k]))
        copies[-1].start()
    for c in copies:
        c.wait()


def out_kernel(x_ref, branch_ref, out_hbm, out_ref, sems):
    send_steps(lambda at: x_ref[at, :].astype(F32) + branch_ref[at, :], out_hbm, out_ref, sems)


def normed_kernel(dproj_ref, win_ref, dpre_ref, unit_ref, vec_ref, channel_ref, skip_ref, dnorm_ref, sums_ref):
    rows, feats = dpre_ref.shape
    skip = vec_ref[2:3, :]

    def chunk(c, carry):
        total_gain, total_bias = carry
        at = pl.ds(c * CHUNK, CHUNK)
        d_normed = dpre_ref[at, :] * skip + nn(dproj_ref[at, :], win_ref[...])
        dnorm_ref[at, :] = d_normed
        folded = lambda v: jnp.sum(v.reshape(CHUNK // SUB, SUB, feats), axis=0)
        return total_gain + folded(d_normed * unit_ref[at, :]), total_bias + folded(d_normed)

    zero = jnp.zeros((SUB, feats), F32)
    total_gain, total_bias = repeat(0, rows // CHUNK, chunk, (zero, zero))
    over = lambda v: jnp.sum(v, axis=0, keepdims=True)
    channel = over(channel_ref[...])
    wide_at = channel.shape[1] - feats
    sums_ref[0:1, :] = channel[:, :feats]
    sums_ref[1:2, :] = jnp.zeros((1, feats), F32)
    sums_ref[1:2, :wide_at] = channel[:, feats:]
    sums_ref[2:3, :] = over(total_gain)
    sums_ref[3:4, :] = over(total_bias)
    sums_ref[4:5, :] = over(skip_ref[...])
    sums_ref[5:8, :] = jnp.zeros((3, feats), F32)


def tokens_kernel(cot_ref, dnorm_ref, unit_ref, inv_ref, vec_ref, out_hbm, out_ref, sems):
    feats = dnorm_ref.shape[1]
    gain = vec_ref[0:1, :]

    def rows_of(at):
        unit = unit_ref[at, :]
        d_unit = dnorm_ref[at, :] * gain
        first = jnp.mean(d_unit, axis=1, keepdims=True)
        second = jnp.mean(d_unit * unit, axis=1, keepdims=True)
        return cot_ref[at, :].astype(F32) + wide(inv_ref[at, :], feats) * (d_unit - first - unit * second)

    send_steps(rows_of, out_hbm, out_ref, sems)


def join_pairs(parts, flat_ref, out_ref):
    own, _, feats = out_ref.shape
    for k, part in enumerate(parts):
        for c in range(feats // 128):
            flat_ref[c, pl.ds(k, own, stride=2), :] = part[:, c * 128 : (c + 1) * 128]
    rows = jnp.concatenate([flat_ref[c] for c in range(feats // 128)], axis=1)
    out_ref[...] = rows.reshape(own, 2, feats)


def halves_kernel(mine_ref, other_ref, out_ref, flat_ref):
    own = out_ref.shape[0]
    first = (lax.axis_index("seq") & 1) == 0
    a, b = mine_ref[...].astype(F32), other_ref[...].astype(F32)
    join_pairs([jnp.where(first, a, b), jnp.where(first, b, a)], flat_ref, out_ref)


def finish(total_ref, sums_ref, vec_ref, in_ref, gain_ref, bias_ref, skip_ref, rate_ref, angle_ref, level_ref, flat_ref):
    own, _, feats = in_ref.shape
    join_pairs([total_ref[:own, :], total_ref[own:, :]], flat_ref, in_ref)
    sums = sums_ref[...]
    for k, ref in enumerate((gain_ref, bias_ref, skip_ref)):
        ref[...] = sums[2 + k : 3 + k, :]
    me = lax.axis_index("state")
    channels = lax.axis_size("state") * own
    pick = lambda row: sum(
        jnp.where(me == d, row[:, d * own : (d + 1) * own], 0.0) for d in range(channels // own)
    )
    sum_re, sum_im = pick(sums[0:1, :channels]), pick(sums[0:1, channels:])
    pole_re, pole_im, decay, angle = (vec_ref[k : k + 1, :own] for k in range(3, 7))
    rate_ref[...] = -decay * (sum_re * pole_re + sum_im * pole_im)
    angle_ref[...] = angle * (sum_im * pole_re - sum_re * pole_im)
    level_ref[...] = pick(sums[1:2, :channels])


def start_placing(masks, parts, arrays, out_ref, wide_ref, sems):
    place = lax.axis_index("state") + parts * (lax.axis_index("seq") & 1)
    size = arrays[0].shape[1]
    copies = []
    for ms, ref in zip(masks, arrays):
        for k, m in enumerate(ms):
            n = len(copies)
            wide_ref[n] = ref[k].astype(F32)
            at = pl.ds(pl.multiple_of((place ^ m) * size, size), size)
            copies.append(pltpu.make_async_copy(wide_ref.at[n], out_ref.at[at, :], sems.at[n]))
            copies[-1].start()
    return copies


def place_kernel(masks, parts, *refs):
    for c in start_placing(masks, parts, refs[: len(masks)], *refs[-3:]):
        c.wait()


def place_blocks(arrays, masks, parts, shape):
    count = sum(len(m) for m in masks)
    _, size, width = arrays[0].shape
    return pl.pallas_call(
        functools.partial(place_kernel, masks, parts),
        out_shape=jax.ShapeDtypeStruct(shape, F32),
        in_specs=[pl.BlockSpec(memory_space=pltpu.VMEM)] * len(arrays),
        out_specs=pl.BlockSpec(memory_space=pl.ANY),
        scratch_shapes=[pltpu.VMEM((count, size, width), F32), pltpu.SemaphoreType.DMA((count,))],
        compiler_params=pltpu.CompilerParams(vmem_limit_bytes=8 * MIB),
        cost_estimate=pl.CostEstimate(flops=MIB, bytes_accessed=2 * MIB, transcendentals=0),
        name="place",
    )(*arrays)


def last_kernel(masks, parts, *refs):
    n = len(masks)
    out_ref, in_ref = refs[n + 4 : n + 6]
    wide_ref, sems, flat_ref = refs[-3:]
    copies = start_placing(masks, parts, refs[:n], out_ref, wide_ref, sems)
    finish(*refs[n : n + 3], in_ref, *refs[n + 6 : n + 12], flat_ref)
    for c in copies:
        c.wait()


def last_step(arrays, masks, parts, glu, total, sums, vec, own):
    count = sum(len(m) for m in masks)
    _, size, width = arrays[0].shape
    feats = vec.shape[1]
    shapes = [glu.shape, (own, 2, feats)] + [(1, feats)] * 3 + [(1, own)] * 3
    spaces = [pl.ANY] + [pltpu.VMEM] * 7
    n = len(arrays) + 3
    return pl.pallas_call(
        functools.partial(last_kernel, masks, parts),
        out_shape=[jax.ShapeDtypeStruct(s, F32) for s in shapes],
        in_specs=[pl.BlockSpec(memory_space=pltpu.VMEM)] * n + [pl.BlockSpec(memory_space=pl.ANY)],
        out_specs=[pl.BlockSpec(memory_space=s) for s in spaces],
        scratch_shapes=[
            pltpu.VMEM((count, size, width), F32),
            pltpu.SemaphoreType.DMA((count,)),
            pltpu.VMEM((feats // 128, 2 * own, 128), F32),
        ],
        input_output_aliases={n: 0},
        compiler_params=pltpu.CompilerParams(vmem_limit_bytes=8 * MIB),
        cost_estimate=pl.CostEstimate(flops=MIB, bytes_accessed=2 * MIB, transcendentals=0),
        name="last",
    )(*arrays, total, sums, vec, glu)


def exchange(x, mask):
    count = lax.axis_size("seq") * lax.axis_size("state")
    return lax.ppermute(x, ("seq", "state"), [(i, i ^ mask) for i in range(count)])


def tie(x, *after):
    return lax.optimization_barrier((x, after))[0]


def bits_of(n):
    return [1 << k for k in range(n.bit_length() - 1)]


def submasks(group):
    out = [0]
    for bit in group:
        out += [m | bit for m in out]
    return out[1:]


def stage_orders(groups):
    kept = [0]
    stages = []
    for group in reversed(groups):
        sends = [[m ^ p for m in kept] for p in submasks(group)]
        stages.insert(0, sends)
        kept = sum(sends, []) + kept
    return [o for sends in stages for o in sends] + [[0]]


def swap(parts, group):
    masks = submasks(group)
    return [exchange(p.astype(BF16), m) for p, m in zip(parts, masks)]


def add_up(parts, got):
    rest, off = [], 0
    for p in parts[len(got) :]:
        n = p.shape[0]
        total = p.astype(F32)
        for g in got:
            total = total + g[off : off + n].astype(F32)
        rest.append(total)
        off += n
    return rest


def halve(parts, group):
    return add_up(parts, swap(parts, group))


def rounded(x):
    return lax.reduce_precision(x, 8, 7)


def two_parts(x):
    high = rounded(x)
    return [high.astype(BF16), rounded(x - high).astype(BF16)]


def sum_of(parts):
    return parts[0].astype(F32) + parts[1].astype(F32)


def gather_ends(end, bits):
    g = end[None]
    for bit in reversed(bits):
        g = jnp.stack([g, exchange(g, bit)], axis=1).reshape((2 * g.shape[0],) + end.shape)
    return g


def gather_blocks(arrays, bits, ready=None):
    blocks = [{0: a} for a in arrays]
    for n, bit in enumerate(reversed(bits)):
        for held_blocks in blocks:
            for m in list(held_blocks):
                x = held_blocks[m]
                if m and n and ready is not None:
                    x = tie(x, ready)
                held_blocks[m ^ bit] = exchange(x, bit)
    return [[b[m] for m in range(len(b))] for b in blocks]


def shards(
    tokens,
    norm_gain,
    norm_bias,
    input_weight,
    output_weight,
    log_rate,
    log_angle,
    log_gain,
    skip_gain,
    glu_weight,
    lengths,
    cotangent,
):
    span, group, feats = tokens.shape
    own = log_rate.shape[0]
    parts = lax.axis_size("state")
    n_seq = lax.axis_size("seq")
    channels = own * parts
    rows = span * group
    segs = SUB // group
    me = lax.axis_index("state")
    state_bits = bits_of(parts)
    seq_masks = [parts * b for b in bits_of(n_seq)]
    if len(seq_masks) > 2:
        seq_masks[-1] |= seq_masks[-2]
    full = rows * feats * 2 * channels * 2

    flat = pltpu.VMEM((feats // 128, 2 * own, 128), F32)
    x4 = tokens.reshape(segs, span // segs, group, feats)
    cot4 = cotangent.reshape(segs, span // segs, group, feats)
    small = jnp.concatenate([norm_gain, norm_bias, skip_gain, log_rate, log_angle, log_gain])
    small = small.reshape(1, -1)
    small_own, vec = call(
        functools.partial(prep_kernel, own),
        [((PARAM_ROWS // 2, 2, feats), BF16), ((SUB, feats), F32)],
        [small],
        [],
        8,
        MIB,
        "prep",
    )
    b_own = jnp.concatenate([input_weight.transpose(1, 2, 0), small_own], axis=0)
    low, unit, inv, x_rows = call(
        norm_kernel,
        [((rows, feats), BF16), ((rows, feats), F32), ((rows, 128), F32), ((rows, feats), BF16)],
        [x4, vec],
        [held(x4), pltpu.SemaphoreType.DMA((4,))],
        12,
        rows * feats * 20,
        "norm",
        fetched=(0,),
    )
    (limit,) = call(
        functools.partial(limit_kernel, group, rows // SUB),
        [((SUB, 128), jnp.int32)],
        [tie(lengths, low)],
        [],
        8,
        MIB,
        "limit",
    )
    b_blocks, c_blocks = gather_blocks([b_own, tie(output_weight, b_own)], state_bits, (low, limit))
    drive, end, win, cst = call(
        functools.partial(project_kernel, parts, own, group),
        [
            ((rows, 2 * channels), F32),
            ((SUB, 2 * channels), F32),
            ((2 * channels, feats), BF16),
            ((SUB, 2 * channels), F32),
        ],
        [low, limit] + b_blocks,
        [flat],
        12,
        full,
        "project",
    )
    ends = gather_ends(end, state_bits)
    (cot,) = call(cotangent_kernel, [((rows, feats), BF16)], [tie(cot4, end)], [], 8, MIB, "cotangent")
    (cw,) = call(
        weights_kernel,
        [((2 * channels, feats), BF16)],
        [tie(c_blocks[0], end)] + c_blocks[1:],
        [flat],
        8,
        MIB,
        "weights",
    )
    all_bits = state_bits + [parts]
    all_groups = [all_bits[:1]] + [all_bits[k : k + 2] for k in range(1, len(all_bits), 2)]
    all_orders = stage_orders(all_groups)
    glu_rows = feats // (2 * parts)
    block_outs = lambda rows, width, orders: [
        ((len(o), rows, width), BF16 if k == 0 else F32) for k, o in enumerate(orders)
    ]
    states, slow, branch, d_glu, slope, *glu_parts = call(
        functools.partial(mix_kernel, parts, own, group, all_orders),
        [
            ((rows + SUB, 2 * channels), F32),
            ((rows, 2 * channels), BF16),
            ((rows, feats), F32),
            ((rows, 2 * feats), BF16),
            ((rows, feats), F32),
        ]
        + block_outs(glu_rows, 2 * feats, all_orders),
        [drive, end, cst, ends, cw, unit, cot, limit, vec, glu_weight],
        [pltpu.VMEM((rows, feats), BF16), pltpu.VMEM((feats, 2 * feats), F32)],
        20,
        5 * full,
        "mix",
    )
    d_pre, d_mixed, skip_sum, *out_parts = call(
        functools.partial(back_kernel, own, all_orders),
        [((rows, feats), F32), ((rows, feats), BF16), ((SUB, feats), F32)]
        + block_outs(own, feats, all_orders),
        [d_glu, slope, unit, vec, glu_weight, slow],
        [pltpu.VMEM((2 * channels, feats), F32)],
        16,
        3 * full,
        "back",
    )
    d_states, start = call(
        functools.partial(starts_kernel, group),
        [((rows, 2 * channels), F32), ((SUB, 2 * channels), F32)],
        [d_mixed, cw, cst],
        [],
        12,
        full,
        "starts",
    )
    got = swap(glu_parts, all_groups[0])
    more = swap(out_parts, all_groups[0])
    starts = gather_ends(tie(start, got, more), state_bits)
    got, more = tie((got, more), start)
    glu_parts, out_parts = add_up(glu_parts, got), add_up(out_parts, more)
    both = [jnp.concatenate(p, axis=-1) for p in zip(glu_parts, out_parts)]
    state_groups = [[b] for b in state_bits]
    pair_orders = stage_orders(state_groups)
    d_proj, channel_sums, *in_parts = call(
        functools.partial(adjoint_kernel, own, group, pair_orders),
        [((rows, 2 * channels), BF16), ((SUB, 3 * channels), F32)]
        + block_outs(2 * own, feats, pair_orders),
        [tie(d_states, both), start, cst, starts, states, drive, low, limit],
        [pltpu.VMEM((rows, 2 * channels), F32), pltpu.VMEM((2 * channels, feats), F32)],
        16,
        2 * full,
        "adjoint",
    )
    d_normed, sums = call(
        normed_kernel,
        [((rows, feats), F32), ((SUB, feats), F32)],
        [d_proj, win, d_pre, unit, vec, channel_sums, skip_sum],
        [],
        12,
        full,
        "normed",
    )
    class chain:
        parts, total, held = in_parts, None, sums
        masks = state_bits + seq_masks[:1] + seq_masks[:0:-1]
        sent = []

        def send(after=()):
            chain.two = two_parts(chain.held)
            if len(chain.parts) > 1:
                chain.low = chain.parts[0].astype(BF16).reshape(-1, feats)
            else:
                chain.low = rounded(chain.parts[0][0]).astype(BF16)
            chain.sent.append(tie(jnp.concatenate([chain.low] + chain.two, axis=0), after))

        def take(after=()):
            got = tie(exchange(chain.sent[-1], chain.masks[len(chain.sent) - 1]), after)
            chain.got, rest, off = got, [], 0
            if len(chain.parts) > 1:
                for p in chain.parts[1:]:
                    n = p.shape[0] * p.shape[1]
                    rest.append(p + got[off : off + n].reshape(p.shape).astype(F32))
                    off += n
            else:
                off = 2 * own
                rest.append((chain.low.astype(F32) + got[:off].astype(F32))[None])
            chain.parts = rest
            chain.held = sum_of(chain.two) + sum_of([got[off : off + SUB], got[off + SUB :]])

    chain.send()
    (out4,) = call(
        out_kernel,
        [(x4.shape, BF16)],
        [x_rows, tie(branch, chain.sent[-1])],
        [held(x4), pltpu.SemaphoreType.DMA((8,))],
        8,
        4096 * MIB,
        "out",
        sent=True,
    )
    chain.take(out4)
    chain.send()
    for g in all_groups[1:]:
        got = swap(both, g)
        both = add_up(both, tie(got, chain.sent[-1]))
    both = both[0][0]
    (grad4,) = call(
        tokens_kernel,
        [(cot4.shape, F32)],
        [cot, tie(d_normed, both, chain.sent[-1]), unit, inv, vec],
        [pltpu.VMEM(cot4.shape, F32), pltpu.SemaphoreType.DMA((8,))],
        12,
        4096 * MIB,
        "tokens",
        sent=True,
    )
    chain.take()
    chain.send()
    glu_masks = seq_masks[:0:-1]
    for n, m in enumerate(glu_masks):
        mine = rounded(both).astype(BF16)
        got = exchange(mine, m)
        if n:
            chain.take()
            chain.send(mine)
        got = tie(got, chain.sent[-1], grad4)
        both = mine.astype(F32) + got.astype(F32)
    both = rounded(both).astype(BF16)
    while len(chain.sent) < len(chain.masks):
        chain.take()
        chain.send(both)
    chain.take()
    blocks = {0: both[:, : 2 * feats]}
    for g in reversed(all_groups[1:]):
        for m in list(blocks):
            for p in submasks(g):
                if m == 0 and p == parts:
                    got = exchange(both, p)
                    blocks[p] = got[:, : 2 * feats]
                    other_half = got[:, 2 * feats :]
                else:
                    blocks[m ^ p] = exchange(blocks[m], p)
    far_own = [exchange(blocks[0][None], p) for p in submasks(all_groups[0])]
    (grad_out,) = call(
        halves_kernel,
        [((own, 2, feats), F32)],
        [both[:, 2 * feats :], tie(other_half, far_own)],
        [flat],
        8,
        MIB,
        "halves",
    )
    rest = [m for m in blocks if m]
    near = [blocks[0][None], jnp.stack(tie([blocks[m] for m in rest], grad_out, chain.sent[-1]))]
    outer = submasks(all_groups[0])
    far = [exchange(near[1], p) for p in outer]
    first_masks = [[0], rest] + [[p] for p in outer]
    far_masks = [[m ^ p for m in rest] for p in outer]
    grad_glu = place_blocks(near + far_own, first_masks, parts, (feats, 2 * feats))
    grad_glu, grad_in, grad_gain, grad_bias, grad_skip, grad_rate, grad_angle, grad_level = last_step(
        far, far_masks, parts, grad_glu, chain.parts[0][0], chain.held, vec, own
    )
    return (
        out4.reshape(tokens.shape),
        grad4.reshape(tokens.shape),
        grad_gain.reshape(feats),
        grad_bias.reshape(feats),
        grad_in.transpose(2, 0, 1),
        grad_out,
        grad_rate.reshape(own),
        grad_angle.reshape(own),
        grad_level.reshape(own),
        grad_skip.reshape(feats),
        grad_glu,
    )


def solution(mesh):
    placed = (
        P("state", "seq", None),
        P(),
        P(),
        P(None, "state", None),
        P("state", None, None),
        P("state"),
        P("state"),
        P("state"),
        P(),
        P(),
        P("seq"),
        P("state", "seq", None),
    )
    return jax.shard_map(
        shards,
        mesh=mesh,
        in_specs=placed,
        out_specs=(
            P("state", "seq", None),
            P("state", "seq", None),
            P(),
            P(),
            P(None, "state", None),
            P("state", None, None),
            P("state"),
            P("state"),
            P("state"),
            P(),
            P(),
        ),
        check_vma=False,
    )
```

```python
import functools

import jax
import jax.numpy as jnp
from jax import lax
from jax.experimental import pallas as pl
from jax.experimental.pallas import tpu as pltpu
from jax.sharding import PartitionSpec as P

F32, BF16 = jnp.float32, jnp.bfloat16
EPSILON = 1e-05
SUB = 8
CHUNK = 512
PARAM_ROWS = 16
GELU_A = 0.7978845608028654
GELU_B = 0.044715
MIB = 1 << 20


def repeat(first, last, body, carry):
    for k in range(first, last):
        carry = body(k, carry)
    return carry


def cmul(ar, ai, br, bi):
    return ar * br - ai * bi, ar * bi + ai * br


def nn(a, b):
    return lax.dot_general(a, b, (((1,), (0,)), ((), ())), preferred_element_type=F32)


def nt(a, b):
    return lax.dot_general(a, b, (((1,), (1,)), ((), ())), preferred_element_type=F32)


def tn(a, b):
    return lax.dot_general(a, b, (((0,), (0,)), ((), ())), preferred_element_type=F32)


def rows_in(ref, first, count):
    segs, _, group, feats = ref.shape
    x = ref[:, pl.ds(first, count)].astype(F32)
    return x.transpose(1, 0, 2, 3).reshape(count * segs * group, feats)


def rows_out(y, ref):
    segs, _, group, feats = ref.shape
    return y.reshape(y.shape[0] // SUB, segs, group, feats).transpose(1, 0, 2, 3)


def valid(first, count, limit_ref):
    step = lax.broadcasted_iota(jnp.int32, (count, SUB, 128), 0) + first
    return (step < limit_ref[...][None]).astype(F32).reshape(count * SUB, 128)


def wide(column, lanes):
    return jnp.concatenate([column] * (lanes // column.shape[1]), axis=1)


def call(body, outs, ins, scratch, limit_mib, flops, name, fetched=(), sent=False):
    specs = []
    for k, x in enumerate(ins):
        space = pltpu.SMEM if x.ndim == 1 else pl.ANY if k in fetched else pltpu.VMEM
        specs.append(pl.BlockSpec(memory_space=space))
    return pl.pallas_call(
        body,
        out_shape=[jax.ShapeDtypeStruct(s, d) for s, d in outs],
        in_specs=specs,
        out_specs=[pl.BlockSpec(memory_space=pl.ANY if sent else pltpu.VMEM)] * len(outs),
        scratch_shapes=scratch,
        compiler_params=pltpu.CompilerParams(vmem_limit_bytes=limit_mib * MIB),
        cost_estimate=pl.CostEstimate(flops=flops, bytes_accessed=4 * MIB, transcendentals=0),
        name=name,
    )(*ins)


def start_copies(sources, targets, sems):
    copies = [pltpu.make_async_copy(a, b, sems.at[k]) for k, (a, b) in enumerate(zip(sources, targets))]
    for c in copies:
        c.start()
    return copies


def held(x):
    return pltpu.VMEM(x.shape, x.dtype)


def split_pairs(pairs_ref, flat_ref):
    own, _, feats = pairs_ref.shape
    flat = pairs_ref[...].astype(F32).reshape(2 * own, feats)
    for c in range(feats // 128):
        flat_ref[c] = flat[:, c * 128 : (c + 1) * 128]
    take = lambda k: [flat_ref[c, pl.ds(k, own, stride=2), :] for c in range(feats // 128)]
    return [jnp.concatenate(take(k), axis=1).astype(BF16) for k in range(2)]


def three_parts(x):
    high = x.astype(BF16)
    rest = x - high.astype(F32)
    mid = rest.astype(BF16)
    return [high, mid, (rest - mid.astype(F32)).astype(BF16)]


def prep_kernel(own, small_ref, pay_ref, vec_ref):
    feats = vec_ref.shape[1]
    me = lax.axis_index("state")
    lane = lax.broadcasted_iota(jnp.int32, (1, feats), 1)
    mine = (lane // own) == me
    base = 3 * feats
    logs = [small_ref[:, base + k * own : base + (k + 1) * own] for k in range(3)]
    rate, turn, level = (jnp.concatenate([v] * (feats // own), axis=1) for v in logs)
    decay = jnp.exp(rate)
    size = jnp.exp(-decay)
    angle = jnp.exp(turn)
    pole_re, pole_im = size * jnp.cos(angle), size * jnp.sin(angle)
    parts = []
    for v in (pole_re, pole_im, jnp.exp(level)):
        parts += three_parts(jnp.where(mine, v, 0.0))
    parts += [jnp.zeros((PARAM_ROWS - len(parts), feats), BF16)]
    flat = jnp.concatenate([p.astype(F32) for p in parts], axis=0)
    pay_ref[...] = flat.reshape(PARAM_ROWS // 2, 2, feats).astype(BF16)
    rows = [small_ref[:, k * feats : (k + 1) * feats] for k in range(3)] + [pole_re, pole_im, decay, angle]
    for k, row in enumerate(rows):
        vec_ref[k : k + 1, :] = row
    vec_ref[len(rows) :, :] = jnp.zeros((SUB - len(rows), feats), F32)


def cotangent_kernel(cot_ref, rows_ref):
    steps = 16
    for c in range(cot_ref.shape[1] // steps):
        at = pl.ds(c * steps * SUB, steps * SUB)
        rows_ref[at, :] = rows_in(cot_ref, c * steps, steps).astype(BF16)


def weights_kernel(*refs):
    blocks, (out_ref, flat_ref) = refs[:-2], refs[-2:]
    gather_rows(lax.axis_index("state"), blocks, flat_ref, out_ref)


def limit_kernel(group, steps, lens_ref, limit_ref):
    segs = SUB // group
    place = lax.broadcasted_iota(jnp.int32, (SUB, 128), 0)
    seq = place & (group - 1)
    length = jnp.full((SUB, 128), lens_ref[0], jnp.int32)
    for k in range(1, group):
        length = jnp.where(seq == k, lens_ref[k], length)
    limit_ref[...] = length - (lax.axis_index("state") * segs + place // group) * steps


def norm_kernel(x_hbm, vec_ref, low_ref, unit_ref, inv_ref, rows_ref, x_ref, sems):
    segs, steps, group, feats = x_ref.shape
    rows = steps * SUB
    size = 128
    gain, bias = vec_ref[0:1, :], vec_ref[1:2, :]
    cut = steps // 4
    places = [pl.ds(k * cut, cut) for k in range(4)]
    copies = start_copies([x_hbm.at[:, p] for p in places], [x_ref.at[:, p] for p in places], sems)

    def chunk(c, carry):
        at = pl.ds(c * size, size)
        x = rows_in(x_ref, c * (size // SUB), size // SUB)
        rows_ref[at, :] = x.astype(BF16)
        centred = x - jnp.mean(x, axis=1, keepdims=True)
        inv = lax.rsqrt(jnp.mean(centred * centred, axis=1, keepdims=True) + EPSILON)
        unit = centred * inv
        unit_ref[at, :] = unit
        low_ref[at, :] = (unit * gain + bias).astype(BF16)
        inv_ref[at, :] = jnp.broadcast_to(inv, (size, 128))
        return carry

    turns = rows // size // 4
    for k in range(4):
        copies[k].wait()
        repeat(k * turns, (k + 1) * turns, chunk, 0)


def gather_rows(me, blocks, flat_ref, dst_ref):
    own = flat_ref.shape[1] // 2
    channels = own * len(blocks)
    for m, block in enumerate(blocks):
        for k, part in enumerate(split_pairs(block.at[0:own], flat_ref)):
            at = pl.multiple_of(k * channels + (me ^ m) * own, own)
            dst_ref[pl.ds(at, own), :] = part


def seg_of(group):
    row = lax.broadcasted_iota(jnp.int32, (SUB, 128), 0)
    return row // group


def shift_rows(x, by, keep):
    return jnp.where(wide(keep, x.shape[1]), pltpu.roll(x, by % SUB, 0), 0.0)


def seg_prefix(xr, xi, qr, qi, group, forward):
    seg = seg_of(group)
    segs = SUB // group
    dist = 1
    while dist < segs:
        by = group * dist if forward else SUB - group * dist
        keep = seg >= dist if forward else seg < segs - dist
        sr, si = shift_rows(xr, by, keep), shift_rows(xi, by, keep)
        ar, ai = cmul(qr, qi, sr, si)
        xr, xi = xr + ar, xi + ai
        qr, qi = cmul(qr, qi, qr, qi)
        dist *= 2
    return xr, xi


def seg_enter(xr, xi, qr, qi, dr, di, group, forward):
    seg = seg_of(group)
    segs = SUB // group
    by = group if forward else SUB - group
    keep = seg >= 1 if forward else seg < segs - 1
    er, ei = shift_rows(xr, by, keep), shift_rows(xi, by, keep)
    gap = seg if forward else segs - 1 - seg
    pr, pi = jnp.ones_like(er), jnp.zeros_like(ei)
    bit = 1
    while bit < segs:
        nr, ni = cmul(pr, pi, qr, qi)
        take = wide((gap & bit) != 0, er.shape[1])
        pr, pi = jnp.where(take, nr, pr), jnp.where(take, ni, pi)
        qr, qi = cmul(qr, qi, qr, qi)
        bit *= 2
    ar, ai = cmul(pr, pi, dr, di)
    return er + ar, ei + ai


def device_entry(ends_ref, me, channels, qr, qi, group, forward):
    seg = seg_of(group)
    segs = SUB // group
    parts = ends_ref.shape[0]
    keep = wide(seg == (segs - 1 if forward else 0), channels)
    tr = ti = jnp.zeros((SUB, channels), F32)
    for device in range(parts - 1) if forward else range(parts - 1, 0, -1):
        end = ends_ref[me ^ device]
        nr, ni = cmul(tr, ti, qr, qi)
        counts = device < me if forward else device > me
        tr = jnp.where(counts, nr + end[:, :channels], tr)
        ti = jnp.where(counts, ni + end[:, channels:], ti)
    out = []
    for x in (tr, ti):
        x = jnp.where(keep, x, 0.0)
        y = x
        for k in range(1, segs):
            y = y + pltpu.roll(x, group * k, 0)
        out.append(y)
    return out


def project_kernel(parts, own, group, low_ref, limit_ref, *refs):
    blocks = refs[:parts]
    drive_ref, end_ref, win_ref, cst_ref, flat_ref = refs[parts:]
    rows = low_ref.shape[0]
    channels = own * parts
    steps = rows // SUB
    me = lax.axis_index("state")
    gather_rows(me, blocks, flat_ref, win_ref)
    rows_of = []
    for k in range(3):
        total = None
        for block in blocks:
            tile = block[own : own + PARAM_ROWS // 2].astype(F32).reshape(PARAM_ROWS, -1)
            for part in range(3):
                piece = tile[3 * k + part : 3 * k + part + 1, :channels]
                total = piece if total is None else total + piece
        rows_of.append(total)
    pr, pi, gain = rows_of
    powers = [(pr, pi)]
    span = steps * (SUB // group)
    ar, ai = pr, pi
    count = 1
    while count < span:
        ar, ai = cmul(ar, ai, ar, ai)
        count *= 2
        if count in (steps, span):
            powers.append((ar, ai))
    while len(powers) < 3:
        powers.append(powers[-1])
    for k, (r, i) in enumerate(powers):
        cst_ref[k : k + 1, :] = jnp.concatenate([r, i], axis=1)
    gains = jnp.concatenate([gain, gain], axis=1)
    cst_ref[3:4, :] = gains
    cst_ref[4:8, :] = jnp.zeros((4, 2 * channels), F32)

    def chunk(c, carry):
        base = c * CHUNK
        at = pl.ds(base, CHUNK)
        mask = valid(base // SUB, CHUNK // SUB, limit_ref)
        drive_ref[at, :] = nt(low_ref[at, :], win_ref[...]) * (gains * wide(mask, 2 * channels))
        return carry

    repeat(0, rows // CHUNK, chunk, 0)
    br = jnp.broadcast_to(pr, (SUB, channels))
    bi = jnp.broadcast_to(pi, (SUB, channels))

    def step(j, h):
        u = drive_ref[pl.ds(pl.multiple_of(j * SUB, SUB), SUB), :]
        nr, ni = cmul(br, bi, h[0], h[1])
        return nr + u[:, :channels], ni + u[:, channels:]

    zero = jnp.zeros((SUB, channels), F32)
    er, ei = lax.fori_loop(0, steps, step, (zero, zero), unroll=16)
    er, ei = seg_prefix(er, ei, *powers[1], group, True)
    end_ref[...] = jnp.concatenate([er, ei], axis=1)


def mix_kernel(parts, own, group, orders, *refs):
    it = iter(refs)
    take = lambda n: [next(it) for _ in range(n)]
    drive_ref, end_ref, cst_ref, ends_ref = take(4)
    cw_ref, unit_ref, cot_ref, limit_ref, vec_ref, glu_ref = take(6)
    states_ref, slow_ref, branch_ref, dglu_ref, gp_ref = take(5)
    grads = take(len(orders))
    act_ref, acc_ref = take(2)
    rows, feats = unit_ref.shape
    channels = own * parts
    steps = rows // SUB
    me = lax.axis_index("state")
    place = me + parts * (lax.axis_index("seq") & 1)
    gain, bias, skip = (vec_ref[k : k + 1, :] for k in range(3))
    pr, pi = cst_ref[0:1, :channels], cst_ref[0:1, channels:]
    qr, qi = cst_ref[1:2, :channels], cst_ref[1:2, channels:]
    wr, wi = cst_ref[2:3, :channels], cst_ref[2:3, channels:]
    dr, di = device_entry(ends_ref, me, channels, wr, wi, group, True)
    hr, hi = seg_enter(end_ref[:, :channels], end_ref[:, channels:], qr, qi, dr, di, group, True)
    states_ref[0:SUB, :] = jnp.concatenate([hr, hi], axis=1)
    br = jnp.broadcast_to(pr, (SUB, channels))
    bi = jnp.broadcast_to(pi, (SUB, channels))

    def step(j, h):
        base = pl.multiple_of(j * SUB, SUB)
        u = drive_ref[pl.ds(base, SUB), :]
        nr, ni = cmul(br, bi, h[0], h[1])
        nr, ni = nr + u[:, :channels], ni + u[:, channels:]
        at = pl.ds(pl.multiple_of(base + SUB, SUB), SUB)
        states_ref[at, :channels] = nr
        states_ref[at, channels:] = ni
        return nr, ni

    lax.fori_loop(0, steps, step, (hr, hi), unroll=16)

    kept = {}

    def mixed(c):
        states = states_ref[pl.ds(c * CHUNK + SUB, CHUNK), :]
        slow = jnp.concatenate([states[:, :channels], -states[:, channels:]], axis=1).astype(BF16)
        slow_ref[pl.ds(c * CHUNK, CHUNK), :] = slow
        kept["mixed", c] = nn(slow, cw_ref[...])

    def activate(c):
        at = pl.ds(c * CHUNK, CHUNK)
        v = kept.pop(("mixed", c)) + skip * (unit_ref[at, :] * gain + bias)
        square = v * v
        t = jnp.tanh(v * (GELU_A + (GELU_A * GELU_B) * square))
        half = 0.5 + 0.5 * t
        slope = (0.5 * GELU_A) + (1.5 * GELU_A * GELU_B) * square
        gp_ref[at, :] = half + v * (1.0 - t * t) * slope
        act = (v * half).astype(BF16)
        act_ref[at, :] = act
        kept["glu", c] = nn(act, glu_ref[...])

    def gated(c):
        at = pl.ds(c * CHUNK, CHUNK)
        glu = kept.pop(("glu", c))
        value = glu[:, :feats]
        gate = jax.nn.sigmoid(glu[:, feats:])
        branch = wide(valid(c * CHUNK // SUB, CHUNK // SUB, limit_ref), feats) * gate
        branch_ref[at, :] = branch * value
        d_value = branch * cot_ref[at, :].astype(F32)
        dglu_ref[at, :feats] = d_value.astype(BF16)
        dglu_ref[at, feats:] = (d_value * value * (1.0 - gate)).astype(BF16)

    count = rows // CHUNK
    for k in range(count + 2):
        for lag, stage in enumerate((mixed, activate, gated)):
            if 0 <= k - lag < count:
                stage(k - lag)
    width = 256

    def tile(c, carry):
        at = pl.ds(c * width, width)
        acc_ref[:, at] = tn(act_ref[...], dglu_ref[:, at])
        return carry

    repeat(0, 2 * feats // width, tile, 0)
    spread(acc_ref, place, orders, grads)


def spread(acc_ref, place, orders, grads):
    for order, ref in zip(orders, grads):
        _, size, _ = ref.shape
        for k, m in enumerate(order):
            at = pl.ds(pl.multiple_of((place ^ m) * size, size), size)
            ref[k] = acc_ref[at, :].astype(ref.dtype)


def spread_pairs(acc_ref, place, own, channels, orders, grads):
    for order, ref in zip(orders, grads):
        for k, m in enumerate(order):
            off = pl.multiple_of((place ^ m) * own, own)
            ref[k, 0:own] = acc_ref[pl.ds(off, own), :].astype(ref.dtype)
            also = pl.ds(pl.multiple_of(channels + off, own), own)
            ref[k, own : 2 * own] = acc_ref[also, :].astype(ref.dtype)


def back_kernel(own, orders, *refs):
    it = iter(refs)
    take = lambda n: [next(it) for _ in range(n)]
    dglu_ref, gp_ref, unit_ref, vec_ref, glu_ref, slow_ref = take(6)
    dpre_ref, dmix_ref, skip_ref = take(3)
    grads = take(len(orders))
    (acc_ref,) = take(1)
    rows, feats = gp_ref.shape
    place = lax.axis_index("state") + lax.axis_size("state") * (lax.axis_index("seq") & 1)
    gain, bias = vec_ref[0:1, :], vec_ref[1:2, :]

    def chunk(c, total):
        at = pl.ds(c * CHUNK, CHUNK)
        d_pre = nt(dglu_ref[at, :], glu_ref[...]) * gp_ref[at, :]
        dpre_ref[at, :] = d_pre
        normed = unit_ref[at, :] * gain + bias
        dmix_ref[at, :] = d_pre.astype(BF16)
        return total + jnp.sum((d_pre * normed).reshape(CHUNK // SUB, SUB, feats), axis=0)

    skip_ref[...] = repeat(0, rows // CHUNK, chunk, jnp.zeros((SUB, feats), F32))
    width = 256

    def tile(c, carry):
        at = pl.ds(c * width, width)
        acc_ref[:, at] = tn(slow_ref[...], dmix_ref[:, at])
        return carry

    repeat(0, feats // width, tile, 0)
    spread(acc_ref, place, orders, grads)


def starts_kernel(group, dmix_ref, cw_ref, cst_ref, dst_ref, start_ref):
    rows, feats = dmix_ref.shape
    channels = cw_ref.shape[0] // 2
    steps = rows // SUB

    def chunk(c, carry):
        at = pl.ds(c * CHUNK, CHUNK)
        dst_ref[at, :] = nt(dmix_ref[at, :], cw_ref[...])
        return carry

    repeat(0, rows // CHUNK, chunk, 0)
    br = jnp.broadcast_to(cst_ref[0:1, :channels], (SUB, channels))
    bi = jnp.broadcast_to(-cst_ref[0:1, channels:], (SUB, channels))

    def step(k, a):
        base = pl.multiple_of((steps - 1 - k) * SUB, SUB)
        u = dst_ref[pl.ds(base, SUB), :]
        nr, ni = cmul(br, bi, a[0], a[1])
        return nr + u[:, :channels], ni - u[:, channels:]

    zero = jnp.zeros((SUB, channels), F32)
    ar, ai = lax.fori_loop(0, steps, step, (zero, zero), unroll=16)
    qr, qi = cst_ref[1:2, :channels], -cst_ref[1:2, channels:]
    ar, ai = seg_prefix(ar, ai, qr, qi, group, False)
    start_ref[...] = jnp.concatenate([ar, ai], axis=1)


def adjoint_kernel(own, group, orders, *refs):
    it = iter(refs)
    take = lambda n: [next(it) for _ in range(n)]
    dst_ref, start_ref, cst_ref, ends_ref = take(4)
    states_ref, drive_ref, low_ref, limit_ref = take(4)
    dproj_ref, sums_ref = take(2)
    grads = take(len(orders))
    adj_ref, acc_ref = take(2)
    rows = dst_ref.shape[0]
    channels = dst_ref.shape[1] // 2
    steps = rows // SUB
    me = lax.axis_index("state")
    pr, pi = cst_ref[0:1, :channels], -cst_ref[0:1, channels:]
    qr, qi = cst_ref[1:2, :channels], -cst_ref[1:2, channels:]
    wr, wi = cst_ref[2:3, :channels], -cst_ref[2:3, channels:]
    dr, di = device_entry(ends_ref, me, channels, wr, wi, group, False)
    ar, ai = seg_enter(start_ref[:, :channels], start_ref[:, channels:], qr, qi, dr, di, group, False)
    br = jnp.broadcast_to(pr, (SUB, channels))
    bi = jnp.broadcast_to(pi, (SUB, channels))

    def step(k, carry):
        ar, ai, sr, si, sg = carry
        base = pl.multiple_of((steps - 1 - k) * SUB, SUB)
        at = pl.ds(base, SUB)
        d = dst_ref[at, :]
        nr, ni = cmul(br, bi, ar, ai)
        ar, ai = nr + d[:, :channels], ni - d[:, channels:]
        adj_ref[at, :channels] = ar
        adj_ref[at, channels:] = ai
        h = states_ref[at, :]
        hr, hi = h[:, :channels], h[:, channels:]
        u = drive_ref[at, :]
        sr = sr + (ar * hr + ai * hi)
        si = si + (ai * hr - ar * hi)
        sg = sg + (ar * u[:, :channels] + ai * u[:, channels:])
        return ar, ai, sr, si, sg

    zero = jnp.zeros((SUB, channels), F32)
    out = lax.fori_loop(0, steps, step, (ar, ai, zero, zero, zero), unroll=8)
    sums_ref[:, :channels] = out[2]
    sums_ref[:, channels : 2 * channels] = out[3]
    sums_ref[:, 2 * channels : 3 * channels] = out[4]
    gains = cst_ref[3:4, :]

    def chunk(c, carry):
        base = c * CHUNK
        at = pl.ds(base, CHUNK)
        mask = valid(base // SUB, CHUNK // SUB, limit_ref)
        dproj_ref[at, :] = (adj_ref[at, :] * (gains * wide(mask, 2 * channels))).astype(BF16)
        return carry

    repeat(0, rows // CHUNK, chunk, 0)
    width = 256
    feats = low_ref.shape[1]

    def tile(c, carry):
        at = pl.ds(c * width, width)
        acc_ref[:, at] = tn(dproj_ref[...], low_ref[:, at])
        return carry

    repeat(0, feats // width, tile, 0)
    spread_pairs(acc_ref, me, own, channels, orders, grads)


def send_steps(rows_of, out_hbm, out_ref, sems):
    steps = out_ref.shape[1]
    count = sems.shape[0]
    cut = steps // count
    copies = []
    for k in range(count):
        at = pl.ds(k * cut, cut)
        out_ref[:, at] = rows_out(rows_of(pl.ds(k * cut * SUB, cut * SUB)), out_ref).astype(out_ref.dtype)
        copies.append(pltpu.make_async_copy(out_ref.at[:, at], out_hbm.at[:, at], sems.at[k]))
        copies[-1].start()
    for c in copies:
        c.wait()


def out_kernel(x_ref, branch_ref, out_hbm, out_ref, sems):
    send_steps(lambda at: x_ref[at, :].astype(F32) + branch_ref[at, :], out_hbm, out_ref, sems)


def normed_kernel(dproj_ref, win_ref, dpre_ref, unit_ref, vec_ref, channel_ref, skip_ref, dnorm_ref, sums_ref):
    rows, feats = dpre_ref.shape
    skip = vec_ref[2:3, :]

    def chunk(c, carry):
        total_gain, total_bias = carry
        at = pl.ds(c * CHUNK, CHUNK)
        d_normed = dpre_ref[at, :] * skip + nn(dproj_ref[at, :], win_ref[...])
        dnorm_ref[at, :] = d_normed
        folded = lambda v: jnp.sum(v.reshape(CHUNK // SUB, SUB, feats), axis=0)
        return total_gain + folded(d_normed * unit_ref[at, :]), total_bias + folded(d_normed)

    zero = jnp.zeros((SUB, feats), F32)
    total_gain, total_bias = repeat(0, rows // CHUNK, chunk, (zero, zero))
    over = lambda v: jnp.sum(v, axis=0, keepdims=True)
    channel = over(channel_ref[...])
    wide_at = channel.shape[1] - feats
    sums_ref[0:1, :] = channel[:, :feats]
    sums_ref[1:2, :] = jnp.zeros((1, feats), F32)
    sums_ref[1:2, :wide_at] = channel[:, feats:]
    sums_ref[2:3, :] = over(total_gain)
    sums_ref[3:4, :] = over(total_bias)
    sums_ref[4:5, :] = over(skip_ref[...])
    sums_ref[5:8, :] = jnp.zeros((3, feats), F32)


def tokens_kernel(cot_ref, dnorm_ref, unit_ref, inv_ref, vec_ref, out_hbm, out_ref, sems):
    feats = dnorm_ref.shape[1]
    gain = vec_ref[0:1, :]

    def rows_of(at):
        unit = unit_ref[at, :]
        d_unit = dnorm_ref[at, :] * gain
        first = jnp.mean(d_unit, axis=1, keepdims=True)
        second = jnp.mean(d_unit * unit, axis=1, keepdims=True)
        return cot_ref[at, :].astype(F32) + wide(inv_ref[at, :], feats) * (d_unit - first - unit * second)

    send_steps(rows_of, out_hbm, out_ref, sems)


def join_pairs(parts, flat_ref, out_ref):
    own, _, feats = out_ref.shape
    for k, part in enumerate(parts):
        for c in range(feats // 128):
            flat_ref[c, pl.ds(k, own, stride=2), :] = part[:, c * 128 : (c + 1) * 128]
    rows = jnp.concatenate([flat_ref[c] for c in range(feats // 128)], axis=1)
    out_ref[...] = rows.reshape(own, 2, feats)


def halves_kernel(mine_ref, other_ref, out_ref, flat_ref):
    own = out_ref.shape[0]
    first = (lax.axis_index("seq") & 1) == 0
    a, b = mine_ref[...].astype(F32), other_ref[...].astype(F32)
    join_pairs([jnp.where(first, a, b), jnp.where(first, b, a)], flat_ref, out_ref)


def finish(total_ref, sums_ref, vec_ref, in_ref, gain_ref, bias_ref, skip_ref, rate_ref, angle_ref, level_ref, flat_ref):
    own, _, feats = in_ref.shape
    join_pairs([total_ref[:own, :], total_ref[own:, :]], flat_ref, in_ref)
    sums = sums_ref[...]
    for k, ref in enumerate((gain_ref, bias_ref, skip_ref)):
        ref[...] = sums[2 + k : 3 + k, :]
    me = lax.axis_index("state")
    channels = lax.axis_size("state") * own
    pick = lambda row: sum(
        jnp.where(me == d, row[:, d * own : (d + 1) * own], 0.0) for d in range(channels // own)
    )
    sum_re, sum_im = pick(sums[0:1, :channels]), pick(sums[0:1, channels:])
    pole_re, pole_im, decay, angle = (vec_ref[k : k + 1, :own] for k in range(3, 7))
    rate_ref[...] = -decay * (sum_re * pole_re + sum_im * pole_im)
    angle_ref[...] = angle * (sum_im * pole_re - sum_re * pole_im)
    level_ref[...] = pick(sums[1:2, :channels])


def start_placing(masks, parts, arrays, out_ref, wide_ref, sems):
    place = lax.axis_index("state") + parts * (lax.axis_index("seq") & 1)
    size = arrays[0].shape[1]
    copies = []
    for ms, ref in zip(masks, arrays):
        for k, m in enumerate(ms):
            n = len(copies)
            wide_ref[n] = ref[k].astype(F32)
            at = pl.ds(pl.multiple_of((place ^ m) * size, size), size)
            copies.append(pltpu.make_async_copy(wide_ref.at[n], out_ref.at[at, :], sems.at[n]))
            copies[-1].start()
    return copies


def place_kernel(masks, parts, *refs):
    for c in start_placing(masks, parts, refs[: len(masks)], *refs[-3:]):
        c.wait()


def place_blocks(arrays, masks, parts, shape):
    count = sum(len(m) for m in masks)
    _, size, width = arrays[0].shape
    return pl.pallas_call(
        functools.partial(place_kernel, masks, parts),
        out_shape=jax.ShapeDtypeStruct(shape, F32),
        in_specs=[pl.BlockSpec(memory_space=pltpu.VMEM)] * len(arrays),
        out_specs=pl.BlockSpec(memory_space=pl.ANY),
        scratch_shapes=[pltpu.VMEM((count, size, width), F32), pltpu.SemaphoreType.DMA((count,))],
        compiler_params=pltpu.CompilerParams(vmem_limit_bytes=8 * MIB),
        cost_estimate=pl.CostEstimate(flops=MIB, bytes_accessed=2 * MIB, transcendentals=0),
        name="place",
    )(*arrays)


def last_kernel(masks, parts, *refs):
    n = len(masks)
    out_ref, in_ref = refs[n + 4 : n + 6]
    wide_ref, sems, flat_ref = refs[-3:]
    copies = start_placing(masks, parts, refs[:n], out_ref, wide_ref, sems)
    finish(*refs[n : n + 3], in_ref, *refs[n + 6 : n + 12], flat_ref)
    for c in copies:
        c.wait()


def last_step(arrays, masks, parts, glu, total, sums, vec, own):
    count = sum(len(m) for m in masks)
    _, size, width = arrays[0].shape
    feats = vec.shape[1]
    shapes = [glu.shape, (own, 2, feats)] + [(1, feats)] * 3 + [(1, own)] * 3
    spaces = [pl.ANY] + [pltpu.VMEM] * 7
    n = len(arrays) + 3
    return pl.pallas_call(
        functools.partial(last_kernel, masks, parts),
        out_shape=[jax.ShapeDtypeStruct(s, F32) for s in shapes],
        in_specs=[pl.BlockSpec(memory_space=pltpu.VMEM)] * n + [pl.BlockSpec(memory_space=pl.ANY)],
        out_specs=[pl.BlockSpec(memory_space=s) for s in spaces],
        scratch_shapes=[
            pltpu.VMEM((count, size, width), F32),
            pltpu.SemaphoreType.DMA((count,)),
            pltpu.VMEM((feats // 128, 2 * own, 128), F32),
        ],
        input_output_aliases={n: 0},
        compiler_params=pltpu.CompilerParams(vmem_limit_bytes=8 * MIB),
        cost_estimate=pl.CostEstimate(flops=MIB, bytes_accessed=2 * MIB, transcendentals=0),
        name="last",
    )(*arrays, total, sums, vec, glu)


def exchange(x, mask):
    count = lax.axis_size("seq") * lax.axis_size("state")
    return lax.ppermute(x, ("seq", "state"), [(i, i ^ mask) for i in range(count)])


def tie(x, *after):
    return lax.optimization_barrier((x, after))[0]


def bits_of(n):
    return [1 << k for k in range(n.bit_length() - 1)]


def submasks(group):
    out = [0]
    for bit in group:
        out += [m | bit for m in out]
    return out[1:]


def stage_orders(groups):
    kept = [0]
    stages = []
    for group in reversed(groups):
        sends = [[m ^ p for m in kept] for p in submasks(group)]
        stages.insert(0, sends)
        kept = sum(sends, []) + kept
    return [o for sends in stages for o in sends] + [[0]]


def swap(parts, group):
    masks = submasks(group)
    return [exchange(p.astype(BF16), m) for p, m in zip(parts, masks)]


def add_up(parts, got):
    rest, off = [], 0
    for p in parts[len(got) :]:
        n = p.shape[0]
        total = p.astype(F32)
        for g in got:
            total = total + g[off : off + n].astype(F32)
        rest.append(total)
        off += n
    return rest


def halve(parts, group):
    return add_up(parts, swap(parts, group))


def rounded(x):
    return lax.reduce_precision(x, 8, 7)


def two_parts(x):
    high = rounded(x)
    return [high.astype(BF16), rounded(x - high).astype(BF16)]


def sum_of(parts):
    return parts[0].astype(F32) + parts[1].astype(F32)


def gather_ends(end, bits):
    g = end[None]
    for bit in reversed(bits):
        g = jnp.stack([g, exchange(g, bit)], axis=1).reshape((2 * g.shape[0],) + end.shape)
    return g


def gather_blocks(arrays, bits, ready=None):
    blocks = [{0: a} for a in arrays]
    for n, bit in enumerate(reversed(bits)):
        for held_blocks in blocks:
            for m in list(held_blocks):
                x = held_blocks[m]
                if m and n and ready is not None:
                    x = tie(x, ready)
                held_blocks[m ^ bit] = exchange(x, bit)
    return [[b[m] for m in range(len(b))] for b in blocks]


def shards(
    tokens,
    norm_gain,
    norm_bias,
    input_weight,
    output_weight,
    log_rate,
    log_angle,
    log_gain,
    skip_gain,
    glu_weight,
    lengths,
    cotangent,
):
    span, group, feats = tokens.shape
    own = log_rate.shape[0]
    parts = lax.axis_size("state")
    n_seq = lax.axis_size("seq")
    channels = own * parts
    rows = span * group
    segs = SUB // group
    me = lax.axis_index("state")
    state_bits = bits_of(parts)
    seq_masks = [parts * b for b in bits_of(n_seq)]
    if len(seq_masks) > 2:
        seq_masks[-1] |= seq_masks[-2]
    full = rows * feats * 2 * channels * 2

    flat = pltpu.VMEM((feats // 128, 2 * own, 128), F32)
    x4 = tokens.reshape(segs, span // segs, group, feats)
    cot4 = cotangent.reshape(segs, span // segs, group, feats)
    small = jnp.concatenate([norm_gain, norm_bias, skip_gain, log_rate, log_angle, log_gain])
    small = small.reshape(1, -1)
    small_own, vec = call(
        functools.partial(prep_kernel, own),
        [((PARAM_ROWS // 2, 2, feats), BF16), ((SUB, feats), F32)],
        [small],
        [],
        8,
        MIB,
        "prep",
    )
    b_own = jnp.concatenate([input_weight.transpose(1, 2, 0), small_own], axis=0)
    low, unit, inv, x_rows = call(
        norm_kernel,
        [((rows, feats), BF16), ((rows, feats), F32), ((rows, 128), F32), ((rows, feats), BF16)],
        [x4, vec],
        [held(x4), pltpu.SemaphoreType.DMA((4,))],
        12,
        rows * feats * 20,
        "norm",
        fetched=(0,),
    )
    (limit,) = call(
        functools.partial(limit_kernel, group, rows // SUB),
        [((SUB, 128), jnp.int32)],
        [tie(lengths, low)],
        [],
        8,
        MIB,
        "limit",
    )
    b_blocks, c_blocks = gather_blocks([b_own, tie(output_weight, b_own)], state_bits, (low, limit))
    drive, end, win, cst = call(
        functools.partial(project_kernel, parts, own, group),
        [
            ((rows, 2 * channels), F32),
            ((SUB, 2 * channels), F32),
            ((2 * channels, feats), BF16),
            ((SUB, 2 * channels), F32),
        ],
        [low, limit] + b_blocks,
        [flat],
        12,
        full,
        "project",
    )
    ends = gather_ends(end, state_bits)
    (cot,) = call(cotangent_kernel, [((rows, feats), BF16)], [tie(cot4, end)], [], 8, MIB, "cotangent")
    (cw,) = call(
        weights_kernel,
        [((2 * channels, feats), BF16)],
        [tie(c_blocks[0], end)] + c_blocks[1:],
        [flat],
        8,
        MIB,
        "weights",
    )
    all_bits = state_bits + [parts]
    all_groups = [all_bits[:1]] + [all_bits[k : k + 2] for k in range(1, len(all_bits), 2)]
    all_orders = stage_orders(all_groups)
    glu_rows = feats // (2 * parts)
    block_outs = lambda rows, width, orders: [
        ((len(o), rows, width), BF16 if k == 0 else F32) for k, o in enumerate(orders)
    ]
    states, slow, branch, d_glu, slope, *glu_parts = call(
        functools.partial(mix_kernel, parts, own, group, all_orders),
        [
            ((rows + SUB, 2 * channels), F32),
            ((rows, 2 * channels), BF16),
            ((rows, feats), F32),
            ((rows, 2 * feats), BF16),
            ((rows, feats), F32),
        ]
        + block_outs(glu_rows, 2 * feats, all_orders),
        [drive, end, cst, ends, cw, unit, cot, limit, vec, glu_weight],
        [pltpu.VMEM((rows, feats), BF16), pltpu.VMEM((feats, 2 * feats), F32)],
        20,
        5 * full,
        "mix",
    )
    d_pre, d_mixed, skip_sum, *out_parts = call(
        functools.partial(back_kernel, own, all_orders),
        [((rows, feats), F32), ((rows, feats), BF16), ((SUB, feats), F32)]
        + block_outs(own, feats, all_orders),
        [d_glu, slope, unit, vec, glu_weight, slow],
        [pltpu.VMEM((2 * channels, feats), F32)],
        16,
        3 * full,
        "back",
    )
    d_states, start = call(
        functools.partial(starts_kernel, group),
        [((rows, 2 * channels), F32), ((SUB, 2 * channels), F32)],
        [d_mixed, cw, cst],
        [],
        12,
        full,
        "starts",
    )
    got = swap(glu_parts, all_groups[0])
    more = swap(out_parts, all_groups[0])
    starts = gather_ends(tie(start, got, more), state_bits)
    got, more = tie((got, more), start)
    glu_parts, out_parts = add_up(glu_parts, got), add_up(out_parts, more)
    both = [jnp.concatenate(p, axis=-1) for p in zip(glu_parts, out_parts)]
    state_groups = [[b] for b in state_bits]
    pair_orders = stage_orders(state_groups)
    d_proj, channel_sums, *in_parts = call(
        functools.partial(adjoint_kernel, own, group, pair_orders),
        [((rows, 2 * channels), BF16), ((SUB, 3 * channels), F32)]
        + block_outs(2 * own, feats, pair_orders),
        [tie(d_states, both), start, cst, starts, states, drive, low, limit],
        [pltpu.VMEM((rows, 2 * channels), F32), pltpu.VMEM((2 * channels, feats), F32)],
        16,
        2 * full,
        "adjoint",
    )
    d_normed, sums = call(
        normed_kernel,
        [((rows, feats), F32), ((SUB, feats), F32)],
        [d_proj, win, d_pre, unit, vec, channel_sums, skip_sum],
        [],
        12,
        full,
        "normed",
    )
    class chain:
        parts, total, held = in_parts, None, sums
        masks = state_bits + seq_masks
        sent = []

        def send(after=()):
            chain.two = two_parts(chain.held)
            if len(chain.parts) > 1:
                chain.low = chain.parts[0].astype(BF16).reshape(-1, feats)
            else:
                chain.low = rounded(chain.parts[0][0]).astype(BF16)
            chain.sent.append(tie(jnp.concatenate([chain.low] + chain.two, axis=0), after))

        def take(after=()):
            got = tie(exchange(chain.sent[-1], chain.masks[len(chain.sent) - 1]), after)
            chain.got, rest, off = got, [], 0
            if len(chain.parts) > 1:
                for p in chain.parts[1:]:
                    n = p.shape[0] * p.shape[1]
                    rest.append(p + got[off : off + n].reshape(p.shape).astype(F32))
                    off += n
            else:
                off = 2 * own
                rest.append((chain.low.astype(F32) + got[:off].astype(F32))[None])
            chain.parts = rest
            chain.held = sum_of(chain.two) + sum_of([got[off : off + SUB], got[off + SUB :]])

    chain.send()
    (out4,) = call(
        out_kernel,
        [(x4.shape, BF16)],
        [x_rows, tie(branch, chain.sent[-1])],
        [held(x4), pltpu.SemaphoreType.DMA((8,))],
        8,
        4096 * MIB,
        "out",
        sent=True,
    )
    chain.take(out4)
    chain.send()
    for g in all_groups[1:]:
        got = swap(both, g)
        both = add_up(both, tie(got, chain.sent[-1]))
    both = both[0][0]
    (grad4,) = call(
        tokens_kernel,
        [(cot4.shape, F32)],
        [cot, tie(d_normed, both, chain.sent[-1]), unit, inv, vec],
        [pltpu.VMEM(cot4.shape, F32), pltpu.SemaphoreType.DMA((8,))],
        12,
        4096 * MIB,
        "tokens",
        sent=True,
    )
    chain.take()
    chain.send()
    glu_masks = seq_masks[1:]
    for n, m in enumerate(glu_masks):
        mine = rounded(both).astype(BF16)
        got = exchange(mine, m)
        if n:
            chain.take()
            chain.send(mine)
        got = tie(got, chain.sent[-1], grad4)
        both = mine.astype(F32) + got.astype(F32)
    both = rounded(both).astype(BF16)
    while len(chain.sent) < len(chain.masks):
        chain.take()
        chain.send(both)
    chain.take()
    blocks = {0: both[:, : 2 * feats]}
    for g in reversed(all_groups[1:]):
        for m in list(blocks):
            for p in submasks(g):
                if m == 0 and p == parts:
                    got = exchange(both, p)
                    blocks[p] = got[:, : 2 * feats]
                    other_half = got[:, 2 * feats :]
                else:
                    blocks[m ^ p] = exchange(blocks[m], p)
    far_own = [exchange(blocks[0][None], p) for p in submasks(all_groups[0])]
    (grad_out,) = call(
        halves_kernel,
        [((own, 2, feats), F32)],
        [both[:, 2 * feats :], tie(other_half, far_own)],
        [flat],
        8,
        MIB,
        "halves",
    )
    rest = [m for m in blocks if m]
    near = [blocks[0][None], jnp.stack(tie([blocks[m] for m in rest], grad_out, chain.sent[-1]))]
    outer = submasks(all_groups[0])
    far = [exchange(near[1], p) for p in outer]
    first_masks = [[0], rest] + [[p] for p in outer]
    far_masks = [[m ^ p for m in rest] for p in outer]
    grad_glu = place_blocks(near + far_own, first_masks, parts, (feats, 2 * feats))
    grad_glu, grad_in, grad_gain, grad_bias, grad_skip, grad_rate, grad_angle, grad_level = last_step(
        far, far_masks, parts, grad_glu, chain.parts[0][0], chain.held, vec, own
    )
    return (
        out4.reshape(tokens.shape),
        grad4.reshape(tokens.shape),
        grad_gain.reshape(feats),
        grad_bias.reshape(feats),
        grad_in.transpose(2, 0, 1),
        grad_out,
        grad_rate.reshape(own),
        grad_angle.reshape(own),
        grad_level.reshape(own),
        grad_skip.reshape(feats),
        grad_glu,
    )


def solution(mesh):
    placed = (
        P("state", "seq", None),
        P(),
        P(),
        P(None, "state", None),
        P("state", None, None),
        P("state"),
        P("state"),
        P("state"),
        P(),
        P(),
        P("seq"),
        P("state", "seq", None),
    )
    return jax.shard_map(
        shards,
        mesh=mesh,
        in_specs=placed,
        out_specs=(
            P("state", "seq", None),
            P("state", "seq", None),
            P(),
            P(),
            P(None, "state", None),
            P("state", None, None),
            P("state"),
            P("state"),
            P("state"),
            P(),
            P(),
        ),
        check_vma=False,
    )
```

```python
import functools

import jax
import jax.numpy as jnp
from jax import lax
from jax.experimental import pallas as pl
from jax.experimental.pallas import tpu as pltpu
from jax.sharding import PartitionSpec as P

F32, BF16 = jnp.float32, jnp.bfloat16
EPSILON = 1e-05
SUB = 8
CHUNK = 512
PARAM_ROWS = 16
GELU_A = 0.7978845608028654
GELU_B = 0.044715
MIB = 1 << 20


def repeat(first, last, body, carry):
    for k in range(first, last):
        carry = body(k, carry)
    return carry


def cmul(ar, ai, br, bi):
    return ar * br - ai * bi, ar * bi + ai * br


def nn(a, b):
    return lax.dot_general(a, b, (((1,), (0,)), ((), ())), preferred_element_type=F32)


def nt(a, b):
    return lax.dot_general(a, b, (((1,), (1,)), ((), ())), preferred_element_type=F32)


def tn(a, b):
    return lax.dot_general(a, b, (((0,), (0,)), ((), ())), preferred_element_type=F32)


def rows_in(ref, first, count):
    segs, _, group, feats = ref.shape
    x = ref[:, pl.ds(first, count)].astype(F32)
    return x.transpose(1, 0, 2, 3).reshape(count * segs * group, feats)


def rows_out(y, ref):
    segs, _, group, feats = ref.shape
    return y.reshape(y.shape[0] // SUB, segs, group, feats).transpose(1, 0, 2, 3)


def valid(first, count, limit_ref):
    step = lax.broadcasted_iota(jnp.int32, (count, SUB, 128), 0) + first
    return (step < limit_ref[...][None]).astype(F32).reshape(count * SUB, 128)


def wide(column, lanes):
    return jnp.concatenate([column] * (lanes // column.shape[1]), axis=1)


def call(body, outs, ins, scratch, limit_mib, flops, name, fetched=(), sent=False):
    specs = []
    for k, x in enumerate(ins):
        space = pltpu.SMEM if x.ndim == 1 else pl.ANY if k in fetched else pltpu.VMEM
        specs.append(pl.BlockSpec(memory_space=space))
    return pl.pallas_call(
        body,
        out_shape=[jax.ShapeDtypeStruct(s, d) for s, d in outs],
        in_specs=specs,
        out_specs=[pl.BlockSpec(memory_space=pl.ANY if sent else pltpu.VMEM)] * len(outs),
        scratch_shapes=scratch,
        compiler_params=pltpu.CompilerParams(vmem_limit_bytes=limit_mib * MIB),
        cost_estimate=pl.CostEstimate(flops=flops, bytes_accessed=4 * MIB, transcendentals=0),
        name=name,
    )(*ins)


def start_copies(sources, targets, sems):
    copies = [pltpu.make_async_copy(a, b, sems.at[k]) for k, (a, b) in enumerate(zip(sources, targets))]
    for c in copies:
        c.start()
    return copies


def held(x):
    return pltpu.VMEM(x.shape, x.dtype)


def split_pairs(pairs_ref, flat_ref):
    own, _, feats = pairs_ref.shape
    flat = pairs_ref[...].astype(F32).reshape(2 * own, feats)
    for c in range(feats // 128):
        flat_ref[c] = flat[:, c * 128 : (c + 1) * 128]
    take = lambda k: [flat_ref[c, pl.ds(k, own, stride=2), :] for c in range(feats // 128)]
    return [jnp.concatenate(take(k), axis=1).astype(BF16) for k in range(2)]


def three_parts(x):
    high = x.astype(BF16)
    rest = x - high.astype(F32)
    mid = rest.astype(BF16)
    return [high, mid, (rest - mid.astype(F32)).astype(BF16)]


def prep_kernel(own, small_ref, pay_ref, vec_ref):
    feats = vec_ref.shape[1]
    me = lax.axis_index("state")
    lane = lax.broadcasted_iota(jnp.int32, (1, feats), 1)
    mine = (lane // own) == me
    base = 3 * feats
    logs = [small_ref[:, base + k * own : base + (k + 1) * own] for k in range(3)]
    rate, turn, level = (jnp.concatenate([v] * (feats // own), axis=1) for v in logs)
    decay = jnp.exp(rate)
    size = jnp.exp(-decay)
    angle = jnp.exp(turn)
    pole_re, pole_im = size * jnp.cos(angle), size * jnp.sin(angle)
    parts = []
    for v in (pole_re, pole_im, jnp.exp(level)):
        parts += three_parts(jnp.where(mine, v, 0.0))
    parts += [jnp.zeros((PARAM_ROWS - len(parts), feats), BF16)]
    flat = jnp.concatenate([p.astype(F32) for p in parts], axis=0)
    pay_ref[...] = flat.reshape(PARAM_ROWS // 2, 2, feats).astype(BF16)
    rows = [small_ref[:, k * feats : (k + 1) * feats] for k in range(3)] + [pole_re, pole_im, decay, angle]
    for k, row in enumerate(rows):
        vec_ref[k : k + 1, :] = row
    vec_ref[len(rows) :, :] = jnp.zeros((SUB - len(rows), feats), F32)


def cotangent_kernel(cot_ref, rows_ref):
    steps = 16
    for c in range(cot_ref.shape[1] // steps):
        at = pl.ds(c * steps * SUB, steps * SUB)
        rows_ref[at, :] = rows_in(cot_ref, c * steps, steps).astype(BF16)


def weights_kernel(*refs):
    blocks, (out_ref, flat_ref) = refs[:-2], refs[-2:]
    gather_rows(lax.axis_index("state"), blocks, flat_ref, out_ref)


def limit_kernel(group, steps, lens_ref, limit_ref):
    segs = SUB // group
    place = lax.broadcasted_iota(jnp.int32, (SUB, 128), 0)
    seq = place & (group - 1)
    length = jnp.full((SUB, 128), lens_ref[0], jnp.int32)
    for k in range(1, group):
        length = jnp.where(seq == k, lens_ref[k], length)
    limit_ref[...] = length - (lax.axis_index("state") * segs + place // group) * steps


def norm_kernel(x_hbm, vec_ref, low_ref, unit_ref, inv_ref, rows_ref, x_ref, sems):
    segs, steps, group, feats = x_ref.shape
    rows = steps * SUB
    size = 128
    gain, bias = vec_ref[0:1, :], vec_ref[1:2, :]
    cut = steps // 4
    places = [pl.ds(k * cut, cut) for k in range(4)]
    copies = start_copies([x_hbm.at[:, p] for p in places], [x_ref.at[:, p] for p in places], sems)

    def chunk(c, carry):
        at = pl.ds(c * size, size)
        x = rows_in(x_ref, c * (size // SUB), size // SUB)
        rows_ref[at, :] = x.astype(BF16)
        centred = x - jnp.mean(x, axis=1, keepdims=True)
        inv = lax.rsqrt(jnp.mean(centred * centred, axis=1, keepdims=True) + EPSILON)
        unit = centred * inv
        unit_ref[at, :] = unit
        low_ref[at, :] = (unit * gain + bias).astype(BF16)
        inv_ref[at, :] = jnp.broadcast_to(inv, (size, 128))
        return carry

    turns = rows // size // 4
    for k in range(4):
        copies[k].wait()
        repeat(k * turns, (k + 1) * turns, chunk, 0)


def gather_rows(me, blocks, flat_ref, dst_ref):
    own = flat_ref.shape[1] // 2
    channels = own * len(blocks)
    for m, block in enumerate(blocks):
        for k, part in enumerate(split_pairs(block.at[0:own], flat_ref)):
            at = pl.multiple_of(k * channels + (me ^ m) * own, own)
            dst_ref[pl.ds(at, own), :] = part


def seg_of(group):
    row = lax.broadcasted_iota(jnp.int32, (SUB, 128), 0)
    return row // group


def shift_rows(x, by, keep):
    return jnp.where(wide(keep, x.shape[1]), pltpu.roll(x, by % SUB, 0), 0.0)


def seg_prefix(xr, xi, qr, qi, group, forward):
    seg = seg_of(group)
    segs = SUB // group
    dist = 1
    while dist < segs:
        by = group * dist if forward else SUB - group * dist
        keep = seg >= dist if forward else seg < segs - dist
        sr, si = shift_rows(xr, by, keep), shift_rows(xi, by, keep)
        ar, ai = cmul(qr, qi, sr, si)
        xr, xi = xr + ar, xi + ai
        qr, qi = cmul(qr, qi, qr, qi)
        dist *= 2
    return xr, xi


def seg_enter(xr, xi, qr, qi, dr, di, group, forward):
    seg = seg_of(group)
    segs = SUB // group
    by = group if forward else SUB - group
    keep = seg >= 1 if forward else seg < segs - 1
    er, ei = shift_rows(xr, by, keep), shift_rows(xi, by, keep)
    gap = seg if forward else segs - 1 - seg
    pr, pi = jnp.ones_like(er), jnp.zeros_like(ei)
    bit = 1
    while bit < segs:
        nr, ni = cmul(pr, pi, qr, qi)
        take = wide((gap & bit) != 0, er.shape[1])
        pr, pi = jnp.where(take, nr, pr), jnp.where(take, ni, pi)
        qr, qi = cmul(qr, qi, qr, qi)
        bit *= 2
    ar, ai = cmul(pr, pi, dr, di)
    return er + ar, ei + ai


def device_entry(ends_ref, me, channels, qr, qi, group, forward):
    seg = seg_of(group)
    segs = SUB // group
    parts = ends_ref.shape[0]
    keep = wide(seg == (segs - 1 if forward else 0), channels)
    tr = ti = jnp.zeros((SUB, channels), F32)
    for device in range(parts - 1) if forward else range(parts - 1, 0, -1):
        end = ends_ref[me ^ device]
        nr, ni = cmul(tr, ti, qr, qi)
        counts = device < me if forward else device > me
        tr = jnp.where(counts, nr + end[:, :channels], tr)
        ti = jnp.where(counts, ni + end[:, channels:], ti)
    out = []
    for x in (tr, ti):
        x = jnp.where(keep, x, 0.0)
        y = x
        for k in range(1, segs):
            y = y + pltpu.roll(x, group * k, 0)
        out.append(y)
    return out


def project_kernel(parts, own, group, low_ref, limit_ref, *refs):
    blocks = refs[:parts]
    drive_ref, end_ref, win_ref, cst_ref, flat_ref = refs[parts:]
    rows = low_ref.shape[0]
    channels = own * parts
    steps = rows // SUB
    me = lax.axis_index("state")
    gather_rows(me, blocks, flat_ref, win_ref)
    rows_of = []
    for k in range(3):
        total = None
        for block in blocks:
            tile = block[own : own + PARAM_ROWS // 2].astype(F32).reshape(PARAM_ROWS, -1)
            for part in range(3):
                piece = tile[3 * k + part : 3 * k + part + 1, :channels]
                total = piece if total is None else total + piece
        rows_of.append(total)
    pr, pi, gain = rows_of
    powers = [(pr, pi)]
    span = steps * (SUB // group)
    ar, ai = pr, pi
    count = 1
    while count < span:
        ar, ai = cmul(ar, ai, ar, ai)
        count *= 2
        if count in (steps, span):
            powers.append((ar, ai))
    while len(powers) < 3:
        powers.append(powers[-1])
    for k, (r, i) in enumerate(powers):
        cst_ref[k : k + 1, :] = jnp.concatenate([r, i], axis=1)
    gains = jnp.concatenate([gain, gain], axis=1)
    cst_ref[3:4, :] = gains
    cst_ref[4:8, :] = jnp.zeros((4, 2 * channels), F32)

    def chunk(c, carry):
        base = c * CHUNK
        at = pl.ds(base, CHUNK)
        mask = valid(base // SUB, CHUNK // SUB, limit_ref)
        drive_ref[at, :] = nt(low_ref[at, :], win_ref[...]) * (gains * wide(mask, 2 * channels))
        return carry

    repeat(0, rows // CHUNK, chunk, 0)
    br = jnp.broadcast_to(pr, (SUB, channels))
    bi = jnp.broadcast_to(pi, (SUB, channels))

    def step(j, h):
        u = drive_ref[pl.ds(pl.multiple_of(j * SUB, SUB), SUB), :]
        nr, ni = cmul(br, bi, h[0], h[1])
        return nr + u[:, :channels], ni + u[:, channels:]

    zero = jnp.zeros((SUB, channels), F32)
    er, ei = lax.fori_loop(0, steps, step, (zero, zero), unroll=16)
    er, ei = seg_prefix(er, ei, *powers[1], group, True)
    end_ref[...] = jnp.concatenate([er, ei], axis=1)


def mix_kernel(parts, own, group, orders, *refs):
    it = iter(refs)
    take = lambda n: [next(it) for _ in range(n)]
    drive_ref, end_ref, cst_ref, ends_ref = take(4)
    cw_ref, unit_ref, cot_ref, limit_ref, vec_ref, glu_ref = take(6)
    states_ref, slow_ref, branch_ref, dglu_ref, gp_ref = take(5)
    grads = take(len(orders))
    act_ref, acc_ref = take(2)
    rows, feats = unit_ref.shape
    channels = own * parts
    steps = rows // SUB
    me = lax.axis_index("state")
    place = me + parts * (lax.axis_index("seq") & 1)
    gain, bias, skip = (vec_ref[k : k + 1, :] for k in range(3))
    pr, pi = cst_ref[0:1, :channels], cst_ref[0:1, channels:]
    qr, qi = cst_ref[1:2, :channels], cst_ref[1:2, channels:]
    wr, wi = cst_ref[2:3, :channels], cst_ref[2:3, channels:]
    dr, di = device_entry(ends_ref, me, channels, wr, wi, group, True)
    hr, hi = seg_enter(end_ref[:, :channels], end_ref[:, channels:], qr, qi, dr, di, group, True)
    states_ref[0:SUB, :] = jnp.concatenate([hr, hi], axis=1)
    br = jnp.broadcast_to(pr, (SUB, channels))
    bi = jnp.broadcast_to(pi, (SUB, channels))

    def step(j, h):
        base = pl.multiple_of(j * SUB, SUB)
        u = drive_ref[pl.ds(base, SUB), :]
        nr, ni = cmul(br, bi, h[0], h[1])
        nr, ni = nr + u[:, :channels], ni + u[:, channels:]
        at = pl.ds(pl.multiple_of(base + SUB, SUB), SUB)
        states_ref[at, :channels] = nr
        states_ref[at, channels:] = ni
        return nr, ni

    lax.fori_loop(0, steps, step, (hr, hi), unroll=16)

    kept = {}

    def mixed(c):
        states = states_ref[pl.ds(c * CHUNK + SUB, CHUNK), :]
        slow = jnp.concatenate([states[:, :channels], -states[:, channels:]], axis=1).astype(BF16)
        slow_ref[pl.ds(c * CHUNK, CHUNK), :] = slow
        kept["mixed", c] = nn(slow, cw_ref[...])

    def activate(c):
        at = pl.ds(c * CHUNK, CHUNK)
        v = kept.pop(("mixed", c)) + skip * (unit_ref[at, :] * gain + bias)
        square = v * v
        t = jnp.tanh(v * (GELU_A + (GELU_A * GELU_B) * square))
        half = 0.5 + 0.5 * t
        slope = (0.5 * GELU_A) + (1.5 * GELU_A * GELU_B) * square
        gp_ref[at, :] = half + v * (1.0 - t * t) * slope
        act = (v * half).astype(BF16)
        act_ref[at, :] = act
        kept["glu", c] = nn(act, glu_ref[...])

    def gated(c):
        at = pl.ds(c * CHUNK, CHUNK)
        glu = kept.pop(("glu", c))
        value = glu[:, :feats]
        gate = jax.nn.sigmoid(glu[:, feats:])
        branch = wide(valid(c * CHUNK // SUB, CHUNK // SUB, limit_ref), feats) * gate
        branch_ref[at, :] = branch * value
        d_value = branch * cot_ref[at, :].astype(F32)
        dglu_ref[at, :feats] = d_value.astype(BF16)
        dglu_ref[at, feats:] = (d_value * value * (1.0 - gate)).astype(BF16)

    count = rows // CHUNK
    for k in range(count + 2):
        for lag, stage in enumerate((mixed, activate, gated)):
            if 0 <= k - lag < count:
                stage(k - lag)
    width = 256

    def tile(c, carry):
        at = pl.ds(c * width, width)
        acc_ref[:, at] = tn(act_ref[...], dglu_ref[:, at])
        return carry

    repeat(0, 2 * feats // width, tile, 0)
    spread(acc_ref, place, orders, grads)


def spread(acc_ref, place, orders, grads):
    for order, ref in zip(orders, grads):
        _, size, _ = ref.shape
        for k, m in enumerate(order):
            at = pl.ds(pl.multiple_of((place ^ m) * size, size), size)
            ref[k] = acc_ref[at, :].astype(ref.dtype)


def spread_pairs(acc_ref, place, own, channels, orders, grads):
    for order, ref in zip(orders, grads):
        for k, m in enumerate(order):
            off = pl.multiple_of((place ^ m) * own, own)
            ref[k, 0:own] = acc_ref[pl.ds(off, own), :].astype(ref.dtype)
            also = pl.ds(pl.multiple_of(channels + off, own), own)
            ref[k, own : 2 * own] = acc_ref[also, :].astype(ref.dtype)


def back_kernel(own, orders, *refs):
    it = iter(refs)
    take = lambda n: [next(it) for _ in range(n)]
    dglu_ref, gp_ref, unit_ref, vec_ref, glu_ref, slow_ref = take(6)
    dpre_ref, dmix_ref, skip_ref = take(3)
    grads = take(len(orders))
    (acc_ref,) = take(1)
    rows, feats = gp_ref.shape
    place = lax.axis_index("state") + lax.axis_size("state") * (lax.axis_index("seq") & 1)
    gain, bias = vec_ref[0:1, :], vec_ref[1:2, :]

    def chunk(c, total):
        at = pl.ds(c * CHUNK, CHUNK)
        d_pre = nt(dglu_ref[at, :], glu_ref[...]) * gp_ref[at, :]
        dpre_ref[at, :] = d_pre
        normed = unit_ref[at, :] * gain + bias
        dmix_ref[at, :] = d_pre.astype(BF16)
        return total + jnp.sum((d_pre * normed).reshape(CHUNK // SUB, SUB, feats), axis=0)

    skip_ref[...] = repeat(0, rows // CHUNK, chunk, jnp.zeros((SUB, feats), F32))
    width = 256

    def tile(c, carry):
        at = pl.ds(c * width, width)
        acc_ref[:, at] = tn(slow_ref[...], dmix_ref[:, at])
        return carry

    repeat(0, feats // width, tile, 0)
    spread(acc_ref, place, orders, grads)


def starts_kernel(group, dmix_ref, cw_ref, cst_ref, dst_ref, start_ref):
    rows, feats = dmix_ref.shape
    channels = cw_ref.shape[0] // 2
    steps = rows // SUB

    def chunk(c, carry):
        at = pl.ds(c * CHUNK, CHUNK)
        dst_ref[at, :] = nt(dmix_ref[at, :], cw_ref[...])
        return carry

    repeat(0, rows // CHUNK, chunk, 0)
    br = jnp.broadcast_to(cst_ref[0:1, :channels], (SUB, channels))
    bi = jnp.broadcast_to(-cst_ref[0:1, channels:], (SUB, channels))

    def step(k, a):
        base = pl.multiple_of((steps - 1 - k) * SUB, SUB)
        u = dst_ref[pl.ds(base, SUB), :]
        nr, ni = cmul(br, bi, a[0], a[1])
        return nr + u[:, :channels], ni - u[:, channels:]

    zero = jnp.zeros((SUB, channels), F32)
    ar, ai = lax.fori_loop(0, steps, step, (zero, zero), unroll=16)
    qr, qi = cst_ref[1:2, :channels], -cst_ref[1:2, channels:]
    ar, ai = seg_prefix(ar, ai, qr, qi, group, False)
    start_ref[...] = jnp.concatenate([ar, ai], axis=1)


def adjoint_kernel(own, group, orders, *refs):
    it = iter(refs)
    take = lambda n: [next(it) for _ in range(n)]
    dst_ref, start_ref, cst_ref, ends_ref = take(4)
    states_ref, drive_ref, low_ref, limit_ref = take(4)
    dproj_ref, sums_ref = take(2)
    grads = take(len(orders))
    adj_ref, acc_ref = take(2)
    rows = dst_ref.shape[0]
    channels = dst_ref.shape[1] // 2
    steps = rows // SUB
    me = lax.axis_index("state")
    pr, pi = cst_ref[0:1, :channels], -cst_ref[0:1, channels:]
    qr, qi = cst_ref[1:2, :channels], -cst_ref[1:2, channels:]
    wr, wi = cst_ref[2:3, :channels], -cst_ref[2:3, channels:]
    dr, di = device_entry(ends_ref, me, channels, wr, wi, group, False)
    ar, ai = seg_enter(start_ref[:, :channels], start_ref[:, channels:], qr, qi, dr, di, group, False)
    br = jnp.broadcast_to(pr, (SUB, channels))
    bi = jnp.broadcast_to(pi, (SUB, channels))

    def step(k, carry):
        ar, ai, sr, si, sg = carry
        base = pl.multiple_of((steps - 1 - k) * SUB, SUB)
        at = pl.ds(base, SUB)
        d = dst_ref[at, :]
        nr, ni = cmul(br, bi, ar, ai)
        ar, ai = nr + d[:, :channels], ni - d[:, channels:]
        adj_ref[at, :channels] = ar
        adj_ref[at, channels:] = ai
        h = states_ref[at, :]
        hr, hi = h[:, :channels], h[:, channels:]
        u = drive_ref[at, :]
        sr = sr + (ar * hr + ai * hi)
        si = si + (ai * hr - ar * hi)
        sg = sg + (ar * u[:, :channels] + ai * u[:, channels:])
        return ar, ai, sr, si, sg

    zero = jnp.zeros((SUB, channels), F32)
    out = lax.fori_loop(0, steps, step, (ar, ai, zero, zero, zero), unroll=8)
    sums_ref[:, :channels] = out[2]
    sums_ref[:, channels : 2 * channels] = out[3]
    sums_ref[:, 2 * channels : 3 * channels] = out[4]
    gains = cst_ref[3:4, :]

    def chunk(c, carry):
        base = c * CHUNK
        at = pl.ds(base, CHUNK)
        mask = valid(base // SUB, CHUNK // SUB, limit_ref)
        dproj_ref[at, :] = (adj_ref[at, :] * (gains * wide(mask, 2 * channels))).astype(BF16)
        return carry

    repeat(0, rows // CHUNK, chunk, 0)
    width = 256
    feats = low_ref.shape[1]

    def tile(c, carry):
        at = pl.ds(c * width, width)
        acc_ref[:, at] = tn(dproj_ref[...], low_ref[:, at])
        return carry

    repeat(0, feats // width, tile, 0)
    spread_pairs(acc_ref, me, own, channels, orders, grads)


def send_steps(rows_of, out_hbm, out_ref, sems):
    steps = out_ref.shape[1]
    count = sems.shape[0]
    cut = steps // count
    copies = []
    for k in range(count):
        at = pl.ds(k * cut, cut)
        out_ref[:, at] = rows_out(rows_of(pl.ds(k * cut * SUB, cut * SUB)), out_ref).astype(out_ref.dtype)
        copies.append(pltpu.make_async_copy(out_ref.at[:, at], out_hbm.at[:, at], sems.at[k]))
        copies[-1].start()
    for c in copies:
        c.wait()


def out_kernel(x_ref, branch_ref, out_hbm, out_ref, sems):
    send_steps(lambda at: x_ref[at, :].astype(F32) + branch_ref[at, :], out_hbm, out_ref, sems)


def normed_kernel(dproj_ref, win_ref, dpre_ref, unit_ref, vec_ref, channel_ref, skip_ref, dnorm_ref, sums_ref):
    rows, feats = dpre_ref.shape
    skip = vec_ref[2:3, :]

    def chunk(c, carry):
        total_gain, total_bias = carry
        at = pl.ds(c * CHUNK, CHUNK)
        d_normed = dpre_ref[at, :] * skip + nn(dproj_ref[at, :], win_ref[...])
        dnorm_ref[at, :] = d_normed
        folded = lambda v: jnp.sum(v.reshape(CHUNK // SUB, SUB, feats), axis=0)
        return total_gain + folded(d_normed * unit_ref[at, :]), total_bias + folded(d_normed)

    zero = jnp.zeros((SUB, feats), F32)
    total_gain, total_bias = repeat(0, rows // CHUNK, chunk, (zero, zero))
    over = lambda v: jnp.sum(v, axis=0, keepdims=True)
    channel = over(channel_ref[...])
    wide_at = channel.shape[1] - feats
    sums_ref[0:1, :] = channel[:, :feats]
    sums_ref[1:2, :] = jnp.zeros((1, feats), F32)
    sums_ref[1:2, :wide_at] = channel[:, feats:]
    sums_ref[2:3, :] = over(total_gain)
    sums_ref[3:4, :] = over(total_bias)
    sums_ref[4:5, :] = over(skip_ref[...])
    sums_ref[5:8, :] = jnp.zeros((3, feats), F32)


def tokens_kernel(cot_ref, dnorm_ref, unit_ref, inv_ref, vec_ref, out_hbm, out_ref, sems):
    feats = dnorm_ref.shape[1]
    gain = vec_ref[0:1, :]

    def rows_of(at):
        unit = unit_ref[at, :]
        d_unit = dnorm_ref[at, :] * gain
        first = jnp.mean(d_unit, axis=1, keepdims=True)
        second = jnp.mean(d_unit * unit, axis=1, keepdims=True)
        return cot_ref[at, :].astype(F32) + wide(inv_ref[at, :], feats) * (d_unit - first - unit * second)

    send_steps(rows_of, out_hbm, out_ref, sems)


def join_pairs(parts, flat_ref, out_ref):
    own, _, feats = out_ref.shape
    for k, part in enumerate(parts):
        for c in range(feats // 128):
            flat_ref[c, pl.ds(k, own, stride=2), :] = part[:, c * 128 : (c + 1) * 128]
    rows = jnp.concatenate([flat_ref[c] for c in range(feats // 128)], axis=1)
    out_ref[...] = rows.reshape(own, 2, feats)


def halves_kernel(mine_ref, other_ref, out_ref, flat_ref):
    own = out_ref.shape[0]
    first = (lax.axis_index("seq") & 1) == 0
    a, b = mine_ref[...].astype(F32), other_ref[...].astype(F32)
    join_pairs([jnp.where(first, a, b), jnp.where(first, b, a)], flat_ref, out_ref)


def finish(total_ref, sums_ref, vec_ref, in_ref, gain_ref, bias_ref, skip_ref, rate_ref, angle_ref, level_ref, flat_ref):
    own, _, feats = in_ref.shape
    join_pairs([total_ref[:own, :], total_ref[own:, :]], flat_ref, in_ref)
    sums = sums_ref[...]
    for k, ref in enumerate((gain_ref, bias_ref, skip_ref)):
        ref[...] = sums[2 + k : 3 + k, :]
    me = lax.axis_index("state")
    channels = lax.axis_size("state") * own
    pick = lambda row: sum(
        jnp.where(me == d, row[:, d * own : (d + 1) * own], 0.0) for d in range(channels // own)
    )
    sum_re, sum_im = pick(sums[0:1, :channels]), pick(sums[0:1, channels:])
    pole_re, pole_im, decay, angle = (vec_ref[k : k + 1, :own] for k in range(3, 7))
    rate_ref[...] = -decay * (sum_re * pole_re + sum_im * pole_im)
    angle_ref[...] = angle * (sum_im * pole_re - sum_re * pole_im)
    level_ref[...] = pick(sums[1:2, :channels])


def start_placing(masks, parts, arrays, out_ref, wide_ref, sems):
    place = lax.axis_index("state") + parts * (lax.axis_index("seq") & 1)
    size = arrays[0].shape[1]
    copies = []
    for ms, ref in zip(masks, arrays):
        for k, m in enumerate(ms):
            n = len(copies)
            wide_ref[n] = ref[k].astype(F32)
            at = pl.ds(pl.multiple_of((place ^ m) * size, size), size)
            copies.append(pltpu.make_async_copy(wide_ref.at[n], out_ref.at[at, :], sems.at[n]))
            copies[-1].start()
    return copies


def place_kernel(masks, parts, *refs):
    for c in start_placing(masks, parts, refs[: len(masks)], *refs[-3:]):
        c.wait()


def place_blocks(arrays, masks, parts, shape):
    count = sum(len(m) for m in masks)
    _, size, width = arrays[0].shape
    return pl.pallas_call(
        functools.partial(place_kernel, masks, parts),
        out_shape=jax.ShapeDtypeStruct(shape, F32),
        in_specs=[pl.BlockSpec(memory_space=pltpu.VMEM)] * len(arrays),
        out_specs=pl.BlockSpec(memory_space=pl.ANY),
        scratch_shapes=[pltpu.VMEM((count, size, width), F32), pltpu.SemaphoreType.DMA((count,))],
        compiler_params=pltpu.CompilerParams(vmem_limit_bytes=8 * MIB),
        cost_estimate=pl.CostEstimate(flops=MIB, bytes_accessed=2 * MIB, transcendentals=0),
        name="place",
    )(*arrays)


def last_kernel(masks, parts, *refs):
    n = len(masks)
    out_ref, in_ref = refs[n + 4 : n + 6]
    wide_ref, sems, flat_ref = refs[-3:]
    copies = start_placing(masks, parts, refs[:n], out_ref, wide_ref, sems)
    finish(*refs[n : n + 3], in_ref, *refs[n + 6 : n + 12], flat_ref)
    for c in copies:
        c.wait()


def last_step(arrays, masks, parts, glu, total, sums, vec, own):
    count = sum(len(m) for m in masks)
    _, size, width = arrays[0].shape
    feats = vec.shape[1]
    shapes = [glu.shape, (own, 2, feats)] + [(1, feats)] * 3 + [(1, own)] * 3
    spaces = [pl.ANY] + [pltpu.VMEM] * 7
    n = len(arrays) + 3
    return pl.pallas_call(
        functools.partial(last_kernel, masks, parts),
        out_shape=[jax.ShapeDtypeStruct(s, F32) for s in shapes],
        in_specs=[pl.BlockSpec(memory_space=pltpu.VMEM)] * n + [pl.BlockSpec(memory_space=pl.ANY)],
        out_specs=[pl.BlockSpec(memory_space=s) for s in spaces],
        scratch_shapes=[
            pltpu.VMEM((count, size, width), F32),
            pltpu.SemaphoreType.DMA((count,)),
            pltpu.VMEM((feats // 128, 2 * own, 128), F32),
        ],
        input_output_aliases={n: 0},
        compiler_params=pltpu.CompilerParams(vmem_limit_bytes=8 * MIB),
        cost_estimate=pl.CostEstimate(flops=MIB, bytes_accessed=2 * MIB, transcendentals=0),
        name="last",
    )(*arrays, total, sums, vec, glu)


def exchange(x, mask):
    count = lax.axis_size("seq") * lax.axis_size("state")
    return lax.ppermute(x, ("seq", "state"), [(i, i ^ mask) for i in range(count)])


def tie(x, *after):
    return lax.optimization_barrier((x, after))[0]


def bits_of(n):
    return [1 << k for k in range(n.bit_length() - 1)]


def submasks(group):
    out = [0]
    for bit in group:
        out += [m | bit for m in out]
    return out[1:]


def stage_orders(groups):
    kept = [0]
    stages = []
    for group in reversed(groups):
        sends = [[m ^ p for m in kept] for p in submasks(group)]
        stages.insert(0, sends)
        kept = sum(sends, []) + kept
    return [o for sends in stages for o in sends] + [[0]]


def swap(parts, group):
    masks = submasks(group)
    return [exchange(p.astype(BF16), m) for p, m in zip(parts, masks)]


def add_up(parts, got):
    rest, off = [], 0
    for p in parts[len(got) :]:
        n = p.shape[0]
        total = p.astype(F32)
        for g in got:
            total = total + g[off : off + n].astype(F32)
        rest.append(total)
        off += n
    return rest


def halve(parts, group):
    return add_up(parts, swap(parts, group))


def rounded(x):
    return lax.reduce_precision(x, 8, 7)


def two_parts(x):
    high = rounded(x)
    return [high.astype(BF16), rounded(x - high).astype(BF16)]


def sum_of(parts):
    return parts[0].astype(F32) + parts[1].astype(F32)


def gather_ends(end, bits):
    g = end[None]
    for bit in reversed(bits):
        g = jnp.stack([g, exchange(g, bit)], axis=1).reshape((2 * g.shape[0],) + end.shape)
    return g


def gather_blocks(arrays, bits, ready=None):
    blocks = [{0: a} for a in arrays]
    for n, bit in enumerate(reversed(bits)):
        for held_blocks in blocks:
            for m in list(held_blocks):
                x = held_blocks[m]
                if m and n and ready is not None:
                    x = tie(x, ready)
                held_blocks[m ^ bit] = exchange(x, bit)
    return [[b[m] for m in range(len(b))] for b in blocks]


def shards(
    tokens,
    norm_gain,
    norm_bias,
    input_weight,
    output_weight,
    log_rate,
    log_angle,
    log_gain,
    skip_gain,
    glu_weight,
    lengths,
    cotangent,
):
    span, group, feats = tokens.shape
    own = log_rate.shape[0]
    parts = lax.axis_size("state")
    n_seq = lax.axis_size("seq")
    channels = own * parts
    rows = span * group
    segs = SUB // group
    me = lax.axis_index("state")
    state_bits = bits_of(parts)
    seq_masks = [parts * b for b in bits_of(n_seq)]
    if len(seq_masks) > 2:
        seq_masks[-1] |= seq_masks[-2]
    full = rows * feats * 2 * channels * 2

    flat = pltpu.VMEM((feats // 128, 2 * own, 128), F32)
    x4 = tokens.reshape(segs, span // segs, group, feats)
    cot4 = cotangent.reshape(segs, span // segs, group, feats)
    small = jnp.concatenate([norm_gain, norm_bias, skip_gain, log_rate, log_angle, log_gain])
    small = small.reshape(1, -1)
    small_own, vec = call(
        functools.partial(prep_kernel, own),
        [((PARAM_ROWS // 2, 2, feats), BF16), ((SUB, feats), F32)],
        [small],
        [],
        8,
        MIB,
        "prep",
    )
    b_own = jnp.concatenate([input_weight.transpose(1, 2, 0), small_own], axis=0)
    low, unit, inv, x_rows = call(
        norm_kernel,
        [((rows, feats), BF16), ((rows, feats), F32), ((rows, 128), F32), ((rows, feats), BF16)],
        [x4, vec],
        [held(x4), pltpu.SemaphoreType.DMA((4,))],
        12,
        rows * feats * 20,
        "norm",
        fetched=(0,),
    )
    (limit,) = call(
        functools.partial(limit_kernel, group, rows // SUB),
        [((SUB, 128), jnp.int32)],
        [tie(lengths, low)],
        [],
        8,
        MIB,
        "limit",
    )
    b_blocks, c_blocks = gather_blocks([b_own, tie(output_weight, b_own)], state_bits, (low, limit))
    drive, end, win, cst = call(
        functools.partial(project_kernel, parts, own, group),
        [
            ((rows, 2 * channels), F32),
            ((SUB, 2 * channels), F32),
            ((2 * channels, feats), BF16),
            ((SUB, 2 * channels), F32),
        ],
        [low, limit] + b_blocks,
        [flat],
        12,
        full,
        "project",
    )
    ends = gather_ends(end, state_bits)
    (cot,) = call(cotangent_kernel, [((rows, feats), BF16)], [tie(cot4, end)], [], 8, MIB, "cotangent")
    (cw,) = call(
        weights_kernel,
        [((2 * channels, feats), BF16)],
        [tie(c_blocks[0], end)] + c_blocks[1:],
        [flat],
        8,
        MIB,
        "weights",
    )
    all_bits = state_bits + [parts]
    all_groups = [all_bits[:1]] + [all_bits[k : k + 2] for k in range(1, len(all_bits), 2)]
    all_orders = stage_orders(all_groups)
    glu_rows = feats // (2 * parts)
    block_outs = lambda rows, width, orders: [
        ((len(o), rows, width), BF16 if k == 0 else F32) for k, o in enumerate(orders)
    ]
    states, slow, branch, d_glu, slope, *glu_parts = call(
        functools.partial(mix_kernel, parts, own, group, all_orders),
        [
            ((rows + SUB, 2 * channels), F32),
            ((rows, 2 * channels), BF16),
            ((rows, feats), F32),
            ((rows, 2 * feats), BF16),
            ((rows, feats), F32),
        ]
        + block_outs(glu_rows, 2 * feats, all_orders),
        [drive, end, cst, ends, cw, unit, cot, limit, vec, glu_weight],
        [pltpu.VMEM((rows, feats), BF16), pltpu.VMEM((feats, 2 * feats), F32)],
        20,
        5 * full,
        "mix",
    )
    d_pre, d_mixed, skip_sum, *out_parts = call(
        functools.partial(back_kernel, own, all_orders),
        [((rows, feats), F32), ((rows, feats), BF16), ((SUB, feats), F32)]
        + block_outs(own, feats, all_orders),
        [d_glu, slope, unit, vec, glu_weight, slow],
        [pltpu.VMEM((2 * channels, feats), F32)],
        16,
        3 * full,
        "back",
    )
    d_states, start = call(
        functools.partial(starts_kernel, group),
        [((rows, 2 * channels), F32), ((SUB, 2 * channels), F32)],
        [d_mixed, cw, cst],
        [],
        12,
        full,
        "starts",
    )
    got = swap(glu_parts, all_groups[0])
    more = swap(out_parts, all_groups[0])
    starts = gather_ends(tie(start, got, more), state_bits)
    got, more = tie((got, more), start)
    glu_parts, out_parts = add_up(glu_parts, got), add_up(out_parts, more)
    both = [jnp.concatenate(p, axis=-1) for p in zip(glu_parts, out_parts)]
    state_groups = [[b] for b in state_bits]
    pair_orders = stage_orders(state_groups)
    d_proj, channel_sums, *in_parts = call(
        functools.partial(adjoint_kernel, own, group, pair_orders),
        [((rows, 2 * channels), BF16), ((SUB, 3 * channels), F32)]
        + block_outs(2 * own, feats, pair_orders),
        [tie(d_states, both), start, cst, starts, states, drive, low, limit],
        [pltpu.VMEM((rows, 2 * channels), F32), pltpu.VMEM((2 * channels, feats), F32)],
        16,
        2 * full,
        "adjoint",
    )
    d_normed, sums = call(
        normed_kernel,
        [((rows, feats), F32), ((SUB, feats), F32)],
        [d_proj, win, d_pre, unit, vec, channel_sums, skip_sum],
        [],
        12,
        full,
        "normed",
    )
    class chain:
        parts, total, held = in_parts, None, sums
        masks = state_bits + seq_masks
        sent = []

        def send(after=()):
            chain.two = two_parts(chain.held)
            if len(chain.parts) > 1:
                chain.low = chain.parts[0].astype(BF16).reshape(-1, feats)
            else:
                chain.low = rounded(chain.parts[0][0]).astype(BF16)
            chain.sent.append(tie(jnp.concatenate([chain.low] + chain.two, axis=0), after))

        def take(after=()):
            got = tie(exchange(chain.sent[-1], chain.masks[len(chain.sent) - 1]), after)
            chain.got, rest, off = got, [], 0
            if len(chain.parts) > 1:
                for p in chain.parts[1:]:
                    n = p.shape[0] * p.shape[1]
                    rest.append(p + got[off : off + n].reshape(p.shape).astype(F32))
                    off += n
            else:
                off = 2 * own
                rest.append((chain.low.astype(F32) + got[:off].astype(F32))[None])
            chain.parts = rest
            chain.held = sum_of(chain.two) + sum_of([got[off : off + SUB], got[off + SUB :]])

    chain.send()
    (out4,) = call(
        out_kernel,
        [(x4.shape, BF16)],
        [x_rows, tie(branch, chain.sent[-1])],
        [held(x4), pltpu.SemaphoreType.DMA((8,))],
        8,
        4096 * MIB,
        "out",
        sent=True,
    )
    chain.take(out4)
    chain.send()
    for g in all_groups[1:]:
        got = swap(both, g)
        both = add_up(both, tie(got, chain.sent[-1]))
    both = both[0][0]
    (grad4,) = call(
        tokens_kernel,
        [(cot4.shape, F32)],
        [cot, tie(d_normed, both, chain.sent[-1]), unit, inv, vec],
        [pltpu.VMEM(cot4.shape, F32), pltpu.SemaphoreType.DMA((8,))],
        12,
        4096 * MIB,
        "tokens",
        sent=True,
    )
    chain.take()
    chain.send()
    glu_masks = seq_masks[1:]
    for n, m in enumerate(glu_masks):
        mine = rounded(both).astype(BF16)
        got = exchange(mine, m)
        if n:
            chain.take()
            chain.send(mine)
        got = tie(got, chain.sent[-1], grad4)
        both = mine.astype(F32) + got.astype(F32)
    both = rounded(both).astype(BF16)
    while len(chain.sent) < len(chain.masks):
        chain.take()
        chain.send(both)
    chain.take()
    blocks = {0: both[:, : 2 * feats]}
    for g in reversed(all_groups[1:]):
        for m in list(blocks):
            for p in submasks(g):
                if m == 0 and p == parts:
                    got = exchange(both, p)
                    blocks[p] = got[:, : 2 * feats]
                    other_half = got[:, 2 * feats :]
                else:
                    blocks[m ^ p] = exchange(blocks[m], p)
    far_own = [exchange(blocks[0][None], p) for p in submasks(all_groups[0])]
    (grad_out,) = call(
        halves_kernel,
        [((own, 2, feats), F32)],
        [both[:, 2 * feats :], other_half],
        [flat],
        8,
        MIB,
        "halves",
    )
    rest = [m for m in blocks if m]
    near = [blocks[0][None], jnp.stack(tie([blocks[m] for m in rest], grad_out, chain.sent[-1]))]
    outer = submasks(all_groups[0])
    far = [exchange(near[1], p) for p in outer]
    first_masks = [[0], rest] + [[p] for p in outer]
    far_masks = [[m ^ p for m in rest] for p in outer]
    grad_glu = place_blocks(near + far_own, first_masks, parts, (feats, 2 * feats))
    grad_glu, grad_in, grad_gain, grad_bias, grad_skip, grad_rate, grad_angle, grad_level = last_step(
        far, far_masks, parts, grad_glu, chain.parts[0][0], chain.held, vec, own
    )
    return (
        out4.reshape(tokens.shape),
        grad4.reshape(tokens.shape),
        grad_gain.reshape(feats),
        grad_bias.reshape(feats),
        grad_in.transpose(2, 0, 1),
        grad_out,
        grad_rate.reshape(own),
        grad_angle.reshape(own),
        grad_level.reshape(own),
        grad_skip.reshape(feats),
        grad_glu,
    )


def solution(mesh):
    placed = (
        P("state", "seq", None),
        P(),
        P(),
        P(None, "state", None),
        P("state", None, None),
        P("state"),
        P("state"),
        P("state"),
        P(),
        P(),
        P("seq"),
        P("state", "seq", None),
    )
    return jax.shard_map(
        shards,
        mesh=mesh,
        in_specs=placed,
        out_specs=(
            P("state", "seq", None),
            P("state", "seq", None),
            P(),
            P(),
            P(None, "state", None),
            P("state", None, None),
            P("state"),
            P("state"),
            P("state"),
            P(),
            P(),
        ),
        check_vma=False,
    )
```
